32 devices in a mesh: dp: 16 (over z, x, core), tensor: 2 (over y).
Axes of the slice: x: 2, y: 2, z: 4, core: 2. Of those that a mesh axis runs over, the one named last changes fastest.
Arguments:
- tokens: bfloat16 [4096, 1536], P(('dp', 'tensor')), may hold values from -6 to 6
- cotangent: bfloat16 [4096, 1536], P(('dp', 'tensor')), may hold values from -12 to 12
- doc_lengths: int32 [16, 4], P('dp'), may hold values from 1 to 128, 256 in all within a row
- norm_attn: bfloat16 [2, 1536], replicated, may hold values from 0.5 to 1.5
- norm_ffn: bfloat16 [2, 1536], replicated, may hold values from 0.5 to 1.5
- w_qkv: bfloat16 [2, 1536, 2048], P(None, 'dp', 'tensor'), may hold values from -0.15625 to 0.15625
- b_qkv: bfloat16 [2, 2048], P(None, 'tensor'), may hold values from -3 to 3
- w_out: bfloat16 [2, 1536, 1536], P(None, 'dp', 'tensor'), may hold values from -0.4375 to 0.4375
- w_gateup: bfloat16 [2, 1536, 17920], P(None, 'dp', 'tensor'), may hold values from -0.15625 to 0.15625
- w_down: bfloat16 [2, 1536, 8960], P(None, 'dp', 'tensor'), may hold values from -0.125 to 0.125
Outputs:
- output: bfloat16 [4096, 1536], P(('dp', 'tensor'))
- d_tokens: float32 [4096, 1536], P(('dp', 'tensor'))
- d_norm_attn: float32 [2, 1536], replicated
- d_norm_ffn: float32 [2, 1536], replicated
- d_w_qkv: float32 [2, 1536, 2048], P(None, 'dp', 'tensor')
- d_b_qkv: float32 [2, 2048], P(None, 'tensor')
- d_w_out: float32 [2, 1536, 1536], P(None, 'dp', 'tensor')
- d_w_gateup: float32 [2, 1536, 17920], P(None, 'dp', 'tensor')
- d_w_down: float32 [2, 1536, 8960], P(None, 'dp', 'tensor')
The draws below stay inside these ranges and needn't reach their ends.
Inputs may be any that keep to these rules, and one draw needn't show every extreme that they name: `doc_lengths`: each sequence's document lengths add up to 256; in every sequence the longest is 128.
All inputs are finite; a program needn't handle non-finite values.
Results may differ from the reference program's by a relative error of at most 0.02.
Values may be sent and summed in bfloat16 or wider, within the bound.
A program may use at most 448 MiB of HBM per device.

```python
import math
import jax
import jax.numpy as jnp
import numpy as np
from jax import lax

D = 1536
H = 12
KV = 2
HD = 128
FF = 8960
LAYERS = 2
DOCS = 4
LEN = 256
SEQS = 16
TOKENS = 4096
QKV = 2048
N_TENSOR = 2


def raised(result, rng, source, target, blocks, factor):
    owner, partner = [(jnp.arange(result.shape[axis_at]) // (result.shape[axis_at] // blocks)).reshape([-1 if axis == axis_at else 1 for axis in range(result.ndim)]) for axis_at in (source, target)]
    chosen = jax.random.permutation(rng, blocks)[partner]
    strong = (owner == chosen) | (owner == (partner + blocks // 2) % blocks)
    return jnp.where(strong, factor * result, result)


def level_of(own_key, shape, cuts, low, largest):
    def one(position, shards_of):
        heights = jax.random.uniform(jax.random.fold_in(jax.random.fold_in(own_key, 6), position), (shards_of,), jnp.float32, low / len(cuts), largest / len(cuts))
        return jnp.repeat(jnp.exp(heights), shape[position] // shards_of).reshape((-1,) + (1,) * (len(shape) - position - 1))

    loudness = one(*cuts[0])
    for cut in cuts[1:]:
        loudness = loudness * one(*cut)
    return loudness


def split_up(count, total, bound, lean):
    portions = [(1 << 20) // math.isqrt(grade ** lean) + 1 for grade in range(2, count + 1)]
    surplus, counts = total - bound - (count - 1), [1] * (count - 1)
    while surplus > 0:
        movable = [i for i in range(count - 1) if counts[i] < bound]
        pool, remaining = sum([portions[i] for i in movable]), surplus
        for i in movable:
            more = min(bound - counts[i], max(1, remaining * portions[i] // pool), surplus)
            counts[i] = counts[i] + more
            surplus = surplus - more
    return np.array([bound] + counts)


def uneven_parts(own_key, number_of, total, most, slope):
    if number_of == 2:
        one = jax.random.randint(own_key, (), max(1, total - most), min(most, total - 1) + 1)
        return jnp.stack([one, total - one])
    tallies = jnp.asarray(split_up(number_of, total, most, slope), jnp.int32)
    twos = (number_of - 1) // 2
    source_of, sink = tallies[1:1 + 2 * twos:2], tallies[2:2 + 2 * twos:2]
    slack = jnp.minimum(source_of - 1, most - sink)
    shifted = jax.random.randint(jax.random.fold_in(own_key, 1), (twos,), 0, 1 << 20) % (slack + 1)
    tallies = tallies.at[1:1 + 2 * twos:2].set(source_of - shifted).at[2:2 + 2 * twos:2].set(sink + shifted)
    return tallies[jax.random.permutation(jax.random.fold_in(own_key, 2), number_of)]


def centred(key, extent, deviation, limit, shards=(), held_as=jnp.bfloat16):
    array = jax.random.normal(key, extent, jnp.float32) * deviation
    if len(shards) > 0:
        array = level_of(key, extent, shards, -0.22, 0.18) * array
    return jnp.clip(array, min=-limit, max=limit).astype(held_as)


def heavy_noise(stream_key, extent, spread, limit, split, heavy, held_as=jnp.bfloat16):
    entries = spread * jax.random.normal(stream_key, extent, jnp.float32)
    if split:
        entries = entries * level_of(stream_key, extent, split, -0.22, 0.18)
    return jnp.clip(raised(entries, jax.random.fold_in(stream_key, 3), *heavy), -limit, limit).astype(held_as)


def setup_inputs(seed: int = 0) -> dict:
    key_of = jax.random.split(jax.random.key(seed), 11)
    return {
        "tokens": centred(key_of[0], (TOKENS, D), 1.0, 6.0, ((0, 32),)),
        "cotangent": heavy_noise(key_of[1], (TOKENS, D), 1.0, 12.0, ((0, 32),), (0, 1, 32, 2.75)),
        "doc_lengths": jax.vmap(lambda own: uneven_parts(own, DOCS, LEN, LEN // 2, 2))(jax.random.split(key_of[2], SEQS)).reshape((SEQS, DOCS)).astype(jnp.int32),
        "norm_attn": jnp.clip(1.0 + 0.1 * jax.random.normal(key_of[3], (LAYERS, D), jnp.float32), 0.5, 1.5).astype(jnp.bfloat16),
        "norm_ffn": jnp.clip(1.0 + 0.1 * jax.random.normal(key_of[4], (LAYERS, D), jnp.float32), 0.5, 1.5).astype(jnp.bfloat16),
        "w_qkv": centred(key_of[5], (LAYERS, D, QKV), D ** -0.5, 0.15625, ((1, 16), (2, 2))),
        "b_qkv": centred(key_of[6], (LAYERS, QKV), 0.5, 3.0, ((1, 2),)),
        "w_out": centred(key_of[7], (LAYERS, D, H * HD), (H * HD // 8) ** -0.5, 0.4375, ((1, 16), (2, 2))),
        "w_gateup": centred(key_of[8], (LAYERS, D, 2 * FF), D ** -0.5, 0.15625, ((1, 16), (2, 2))),
        "w_down": centred(key_of[9], (LAYERS, D, FF), (FF // 4) ** -0.5, 0.125, ((1, 16), (2, 2))),
    }


@jax.custom_vjp
def low(v):
    return lax.optimization_barrier(v.astype(jnp.bfloat16)).astype(jnp.float32)

@jax.custom_vjp
def low_back(v):
    return v

def low_keep(v):
    return (low(v), None)

def low_pass(kept, grad):
    return (grad,)

def back_keep(v):
    return (v, None)

def back_low(kept, grad):
    return (low(grad),)
low.defvjp(low_keep, low_pass)
low_back.defvjp(back_keep, back_low)

def hdot(left, right):
    return jnp.dot(left, right, precision=lax.Precision.HIGHEST, preferred_element_type=jnp.float32)

def tdot(left, right):
    return lax.dot_general(left, right, (((1,), (1,)), ((), ())), precision=lax.Precision.HIGHEST)

def rms_factor(rows):
    return lax.rsqrt(lax.optimization_barrier(jnp.mean(rows * rows, axis=-1, keepdims=True)) + 1e-06)

def rotate(values):
    half = values.shape[-1] // 2
    return jnp.concatenate([-values[..., half:], values[..., :half]], axis=-1)

def doc_layout(lens, count):
    bounds = jnp.cumsum(lens.astype(jnp.int32), dtype=jnp.int32).astype(jnp.int32)
    rows = jnp.arange(count, dtype=jnp.int32)
    after = (rows[:, None] >= bounds[None, :]).astype(jnp.int32)
    doc = lax.optimization_barrier(jnp.sum(after, axis=1, dtype=jnp.int32))
    start = lax.optimization_barrier(jnp.sum(after * lens.astype(jnp.int32)[None, :], axis=1, dtype=jnp.int32))
    positions = rows - start
    allowed = (doc[:, None] == doc[None, :]) & (rows[:, None] >= rows[None, :])
    return (positions, allowed)

def rope_tables(positions, width):
    index = jnp.arange(width // 2, dtype=jnp.float32)
    freq = jnp.exp(-(2.0 * index / width) * math.log(1000000.0))
    angle = positions.astype(jnp.float32)[:, None] * freq[None, :]
    return (jnp.concatenate([jnp.cos(angle)] * 2, axis=1), jnp.concatenate([jnp.sin(angle)] * 2, axis=1))

def one_sequence(x, lens, params):
    norm_attn, norm_ffn, w_qkv, b_qkv, w_out, w_gateup, w_down = params
    length = x.shape[0]
    positions, allowed = doc_layout(lens, length)
    cosine, sine = rope_tables(positions, HD)
    kv_local = KV // N_TENSOR
    groups = H // KV
    q_width = kv_local * groups * HD
    kv_width = kv_local * HD
    block = w_qkv.shape[2] // N_TENSOR
    scale = 1.0 / math.sqrt(HD)
    cos_q = cosine[:, None, None, None, :]
    sin_q = sine[:, None, None, None, :]
    cos_k = cosine[:, None, None, :]
    sin_k = sine[:, None, None, :]
    for layer in range(LAYERS):
        xa = low(x * rms_factor(x) * norm_attn[layer])
        lin = low_back(hdot(xa, w_qkv[layer])) + b_qkv[layer]
        lin = lin.reshape(length, N_TENSOR, block)
        query = lin[:, :, :q_width].reshape(length, N_TENSOR, kv_local, groups, HD)
        key = lin[:, :, q_width:q_width + kv_width].reshape(length, N_TENSOR, kv_local, HD)
        value = lin[:, :, q_width + kv_width:].reshape(length, N_TENSOR, kv_local, HD)
        query = low(query * cos_q + rotate(query) * sin_q)
        key = low(key * cos_k + rotate(key) * sin_k)
        value = low(value)
        raw = low_back(jnp.einsum('qtkgd,ptkd->tkgqp', query, key, precision=lax.Precision.HIGHEST))
        scores = jnp.where(allowed, raw * scale, -1e+30)
        probs = low(jax.nn.softmax(scores, axis=-1))
        attended = jnp.einsum('tkgqp,ptkd->qtkgd', probs, value, precision=lax.Precision.HIGHEST)
        attended = low(low_back(attended.reshape(length, N_TENSOR * q_width)))
        x = x + low_back(tdot(attended, w_out[layer]))
        xf = low(x * rms_factor(x) * norm_ffn[layer])
        gate_up = low_back(hdot(xf, w_gateup[layer])).reshape(length, N_TENSOR, 2, FF // N_TENSOR)
        act = low(jax.nn.silu(gate_up[:, :, 0]) * gate_up[:, :, 1]).reshape(length, FF)
        x = x + low_back(tdot(act, w_down[layer]))
    return x

def reference(tokens, cotangent, doc_lengths, norm_attn, norm_ffn, w_qkv, b_qkv, w_out, w_gateup, w_down):
    params = (norm_attn.astype(jnp.float32), norm_ffn.astype(jnp.float32), w_qkv.astype(jnp.float32), b_qkv.astype(jnp.float32), w_out.astype(jnp.float32), w_gateup.astype(jnp.float32), w_down.astype(jnp.float32))
    inputs = tokens.astype(jnp.float32).reshape(SEQS, LEN, D)
    step_fn = jax.checkpoint(one_sequence)

    def forward(xs, weights):

        def visit(carry, item):
            return (carry, step_fn(item[0], item[1], weights))
        _, outputs = lax.scan(visit, jnp.zeros((), jnp.float32), (xs, doc_lengths))
        return outputs
    outputs, pull = jax.vjp(forward, inputs, params)
    d_inputs, d_params = pull(cotangent.astype(jnp.float32).reshape(SEQS, LEN, D))
    return (outputs.reshape(TOKENS, D).astype(jnp.bfloat16), d_inputs.reshape(TOKENS, D), d_params[0], d_params[1], d_params[2], d_params[3], d_params[4], d_params[5], d_params[6])
```

```python
import math

import jax
import jax.numpy as jnp
from jax import lax
from jax.sharding import Mesh
from jax.sharding import PartitionSpec as P

H = 12
KV = 2
HD = 128
LINE = 4
LANES = 128
LOW = jnp.bfloat16
F32 = jnp.float32


def rms_factor(rows):
    return lax.rsqrt(jnp.mean(rows * rows, axis=-1, keepdims=True) + 1e-06)


def rotate(values):
    half = values.shape[-1] // 2
    return jnp.concatenate([-values[..., half:], values[..., :half]], axis=-1)


def rotate_back(values):
    half = values.shape[-1] // 2
    return jnp.concatenate([values[..., half:], -values[..., :half]], axis=-1)


def doc_layout(lens, count):
    rows = jnp.arange(count, dtype=jnp.int32)
    doc = jnp.zeros((count,), jnp.int32)
    start = jnp.zeros((count,), jnp.int32)
    bound = jnp.int32(0)
    for number in range(lens.shape[0]):
        bound = bound + lens[number]
        after = (rows >= bound).astype(jnp.int32)
        doc = doc + after
        start = start + after * lens[number]
    positions = rows - start
    allowed = (doc[:, None] == doc[None, :]) & (rows[:, None] >= rows[None, :])
    return (positions, allowed)


def rope_tables(positions, width):
    index = jnp.arange(width // 2, dtype=F32)
    freq = jnp.exp(-(2.0 * index / width) * math.log(1000000.0))
    angle = positions.astype(F32)[:, None] * freq[None, :]
    return (
        jnp.concatenate([jnp.cos(angle)] * 2, axis=1),
        jnp.concatenate([jnp.sin(angle)] * 2, axis=1),
    )


def contract_last(left, right, out=F32):
    return lax.dot_general(left, right, (((1,), (1,)), ((), ())), preferred_element_type=out)


def contract_first(left, right, out=F32):
    return lax.dot_general(left, right, (((0,), (0,)), ((), ())), preferred_element_type=out)


def norm_back(upstream, rows, factor, gain):
    scaled = upstream * gain
    gain_part = jnp.sum(upstream * rows * factor, axis=0)
    result = factor * scaled - rows * factor**3 * jnp.mean(scaled * rows, axis=-1, keepdims=True)
    return (result, gain_part)


SWAP = [(0, 1), (1, 0)]


def take(array, index, axis):
    return lax.dynamic_index_in_dim(array, index, axis, keepdims=False)


def join_pair(own, other, axis_name, axis):
    index = lax.axis_index(axis_name)
    return jnp.where(
        index == 0, jnp.stack([own, other], axis=axis), jnp.stack([other, own], axis=axis)
    )


def spread_pair(rows):
    other = lax.ppermute(rows, "t", SWAP)
    return join_pair(rows, other, "t", 0).reshape(2 * rows.shape[0], rows.shape[1])


def sum_pair(partial):
    index = lax.axis_index("t")
    halves = partial.reshape(2, partial.shape[0] // 2, partial.shape[1])
    other = lax.ppermute(take(halves, 1 - index, 0).astype(LOW), "t", SWAP)
    return take(halves, index, 0) + other.astype(F32)


def spread_group(rows):
    return lax.all_gather(rows, ("z", "t"), axis=0, tiled=True)


def sum_group(partial):
    return lax.psum_scatter(partial, ("z", "t"), scatter_dimension=0, tiled=True).astype(F32)


def block_width(half):
    return -(-half // (LINE * LANES)) * LANES


def to_blocks(weight, parts):
    rows = weight.shape[0]
    half = weight.shape[1] // parts
    block = block_width(half)
    padded = jnp.pad(weight.reshape(rows, parts, half), ((0, 0), (0, 0), (0, LINE * block - half)))
    return padded.reshape(rows, parts, LINE, block).transpose(2, 0, 1, 3).reshape(LINE, rows, parts * block)


def from_blocks(blocks, parts, half):
    rows = blocks.shape[1]
    block = blocks.shape[2] // parts
    joined = blocks.reshape(LINE, rows, parts, block).transpose(1, 2, 0, 3)
    return joined.reshape(rows, parts, LINE * block)[:, :, :half].reshape(rows, parts * half)


def gather_blocks(weight, parts, bits):
    blocks = lax.all_to_all(to_blocks(weight, parts), "z", 0, 0, tiled=True)
    rows, width = blocks.shape[1:]
    lead = [LINE]
    current = blocks
    for bit in bits:
        other = lax.ppermute(current, bit, SWAP)
        current = join_pair(current, other, bit, len(lead))
        lead.append(2)
    return current.reshape(-1, width)


def reduce_blocks(grad, parts, half, bits, rows):
    width = grad.shape[1]
    current = grad.reshape(*([LINE] + [2] * len(bits)), rows, width)
    for number in reversed(range(len(bits))):
        index = lax.axis_index(bits[number])
        own = take(current, index, 1 + number)
        other = lax.ppermute(take(current, 1 - index, 1 + number), bits[number], SWAP)
        current = (own.astype(F32) + other.astype(F32)).astype(LOW)
    blocks = lax.all_to_all(current, "z", 0, 0, tiled=True)
    return from_blocks(blocks, parts, half).astype(F32)


def local(
    bits, tokens, cotangent, doc_lengths, norm_attn, norm_ffn, w_qkv, b_qkv, w_out, w_gateup, w_down
):
    dp = ("z", *bits)
    tensor_size = lax.axis_size("t")
    count = tokens.shape[0]
    length = count * tensor_size
    layers = w_qkv.shape[0]
    kv_local = KV // tensor_size
    groups = H // KV
    q_width = kv_local * groups * HD
    kv_width = kv_local * HD
    qkv_width = w_qkv.shape[2]
    rows = w_qkv.shape[1]
    half = w_down.shape[2]
    block = block_width(half)
    scale = 1.0 / math.sqrt(HD)
    positions, allowed = doc_layout(doc_lengths[0], length)
    cosine, sine = rope_tables(positions, HD)
    cos_q = cosine[:, None, None, :]
    sin_q = sine[:, None, None, :]
    cos_k = cosine[:, None, :]
    sin_k = sine[:, None, :]
    gain_attn = norm_attn.astype(F32)
    gain_ffn = norm_ffn.astype(F32)
    attn_weights, ffn_weights = [], []
    for layer in range(layers):
        both = lax.all_gather(
            jnp.concatenate([w_qkv[layer], w_out[layer]], axis=1), dp, axis=0, tiled=True
        )
        attn_weights.append((both[:, :qkv_width], both[:, qkv_width:]))
        ffn_weights.append(
            (gather_blocks(w_gateup[layer], 2, bits), gather_blocks(w_down[layer], 1, bits))
        )
    saved = []
    state = tokens.astype(F32)
    for layer in range(layers):
        qkv_w, out_w = attn_weights[layer]
        factor_a = rms_factor(state)
        xa_all = spread_pair((state * factor_a * gain_attn[layer]).astype(LOW))
        lin = jnp.dot(xa_all, qkv_w, preferred_element_type=F32) + b_qkv[layer].astype(F32)
        query = lin[:, :q_width].reshape(length, kv_local, groups, HD)
        key = lin[:, q_width : q_width + kv_width].reshape(length, kv_local, HD)
        value = lin[:, q_width + kv_width :].reshape(length, kv_local, HD).astype(LOW)
        query = (query * cos_q + rotate(query) * sin_q).astype(LOW)
        key = (key * cos_k + rotate(key) * sin_k).astype(LOW)
        raw = jnp.einsum("qkgd,pkd->kgqp", query, key, preferred_element_type=F32)
        scores = jnp.where(allowed, raw * scale, -1e30)
        top = jnp.max(scores, axis=-1, keepdims=True)
        expo = jnp.exp(scores - top)
        total = jnp.sum(expo, axis=-1, keepdims=True)
        probs = expo / total
        log_total = top + jnp.log(total)
        attended = (
            jnp.einsum("kgqp,pkd->qkgd", probs.astype(LOW), value, preferred_element_type=F32)
            .reshape(length, q_width)
            .astype(LOW)
        )
        middle = state + sum_pair(contract_last(attended, out_w))
        gu_w, down_w = ffn_weights[layer]
        factor_f = rms_factor(middle)
        xf_all = spread_group((middle * factor_f * gain_ffn[layer]).astype(LOW))
        gate_up = jnp.dot(xf_all, gu_w, preferred_element_type=F32)
        gate = gate_up[:, :block]
        up = gate_up[:, block:]
        act = (jax.nn.silu(gate) * up).astype(LOW)
        after = middle + sum_group(contract_last(act, down_w, LOW))
        saved.append(
            (state, factor_a, xa_all, query, key, value, log_total, attended)
            + (middle, factor_f, xf_all, gate, up, act)
        )
        state = after
    output = state.astype(LOW)
    grad = cotangent.astype(F32)
    grads_attn, grads_gu, grads_down, grads_bias, grads_ga, grads_gf = ([] for _ in range(6))
    for layer in reversed(range(layers)):
        (state_in, factor_a, xa_all, query, key, value, log_total, attended) = saved[layer][:8]
        (middle, factor_f, xf_all, gate, up, act) = saved[layer][8:]
        gu_w, down_w = ffn_weights[layer]
        qkv_w, out_w = attn_weights[layer]
        gm_all = spread_group(grad.astype(LOW))
        d_down = contract_first(gm_all, act, LOW)
        d_act = jnp.dot(gm_all, down_w, preferred_element_type=F32)
        sig = jax.nn.sigmoid(gate)
        d_gate = d_act * up * sig * (1.0 + gate * (1.0 - sig))
        d_up = d_act * gate * sig
        d_gu = jnp.concatenate([d_gate, d_up], axis=1).astype(LOW)
        d_xf = sum_group(contract_last(d_gu, gu_w, LOW))
        d_mid, part_f = norm_back(d_xf, middle, factor_f, gain_ffn[layer])
        grad = grad + d_mid
        d_gateup = contract_first(xf_all, d_gu, LOW)
        grads_gu.append(reduce_blocks(d_gateup, 2, half, bits, rows))
        grads_down.append(reduce_blocks(d_down, 1, half, bits, rows))
        ga_all = spread_pair(grad.astype(LOW))
        d_att = jnp.dot(ga_all, out_w, preferred_element_type=F32).astype(LOW)
        raw = jnp.einsum("qkgd,pkd->kgqp", query, key, preferred_element_type=F32)
        scores = jnp.where(allowed, raw * scale, -1e30)
        probs = jnp.exp(scores - log_total)
        d_att4 = d_att.reshape(length, kv_local, groups, HD)
        d_probs = jnp.einsum("qkgd,pkd->kgqp", d_att4, value, preferred_element_type=F32)
        centre = jnp.sum(probs * d_probs, axis=-1, keepdims=True)
        d_raw = (probs * (d_probs - centre) * scale).astype(LOW)
        d_query = jnp.einsum("kgqp,pkd->qkgd", d_raw, key, preferred_element_type=F32)
        d_key = jnp.einsum("kgqp,qkgd->pkd", d_raw, query, preferred_element_type=F32)
        d_value = jnp.einsum(
            "kgqp,qkgd->pkd", probs.astype(LOW), d_att4, preferred_element_type=F32
        )
        d_query = d_query * cos_q + rotate_back(d_query * sin_q)
        d_key = d_key * cos_k + rotate_back(d_key * sin_k)
        d_lin = jnp.concatenate(
            [
                d_query.reshape(length, q_width),
                d_key.reshape(length, kv_width),
                d_value.reshape(length, kv_width),
            ],
            axis=1,
        )
        grads_bias.append(jnp.sum(d_lin, axis=0))
        d_lin_low = d_lin.astype(LOW)
        d_xa = sum_pair(contract_last(d_lin_low, qkv_w))
        d_in, part_a = norm_back(d_xa, state_in, factor_a, gain_attn[layer])
        grad = grad + d_in
        d_both = jnp.concatenate(
            [contract_first(xa_all, d_lin_low, LOW), contract_first(ga_all, attended, LOW)], axis=1
        )
        grads_attn.append(
            lax.psum_scatter(d_both, dp, scatter_dimension=0, tiled=True).astype(F32)
        )
        grads_ga.append(part_a)
        grads_gf.append(part_f)

    def ordered(items):
        return jnp.stack(items[::-1], axis=0)

    side = lax.axis_index("t")
    bias = ordered(grads_bias)
    spread = jnp.where(
        (jnp.arange(tensor_size) == side)[:, None, None], bias[None], jnp.zeros_like(bias)[None]
    )
    full_ga, full_gf, full_bias = lax.psum(
        (ordered(grads_ga), ordered(grads_gf), spread), (*dp, "t")
    )
    both = ordered(grads_attn)
    return (
        output,
        grad,
        full_ga,
        full_gf,
        both[:, :, :qkv_width],
        take(full_bias, side, 0),
        both[:, :, qkv_width:],
        ordered(grads_gu),
        ordered(grads_down),
    )


def solution(mesh):
    dp_size, tensor_size = mesh.devices.shape
    rest = dp_size // LINE
    bits = tuple(f"r{number}" for number in range(rest.bit_length() - 1))
    shape = (LINE, *([2] * len(bits)), tensor_size)
    fine = Mesh(mesh.devices.reshape(shape), ("z", *bits, "t"))
    dp = ("z", *bits)
    rows = P((*dp, "t"), None)
    weight = P(None, dp, "t")

    def step(*args):
        return local(bits, *args)

    return jax.shard_map(
        step,
        mesh=fine,
        in_specs=(rows, rows, P(dp, None), P(), P(), weight, P(None, "t"), weight, weight, weight),
        out_specs=(rows, rows, P(), P(), weight, P(None, "t"), weight, weight, weight),
        check_vma=False,
    )
```

```python
import functools
import math

import jax
import jax.numpy as jnp
from jax import lax
from jax.experimental import pallas as pl
from jax.experimental.pallas import tpu as pltpu
from jax.sharding import Mesh
from jax.sharding import PartitionSpec as P

H = 12
KV = 2
HD = 128
LINE = 4
LANES = 128
LOW = jnp.bfloat16
F32 = jnp.float32
MESH = pl.DeviceIdType.MESH


def rms_factor(rows):
    return lax.rsqrt(jnp.mean(rows * rows, axis=-1, keepdims=True) + 1e-06)


def rotate(values):
    half = values.shape[-1] // 2
    return jnp.concatenate([-values[..., half:], values[..., :half]], axis=-1)


def rotate_back(values):
    half = values.shape[-1] // 2
    return jnp.concatenate([values[..., half:], -values[..., :half]], axis=-1)


def doc_layout(lens, count):
    rows = jnp.arange(count, dtype=jnp.int32)
    doc = jnp.zeros((count,), jnp.int32)
    start = jnp.zeros((count,), jnp.int32)
    bound = jnp.int32(0)
    for number in range(lens.shape[0]):
        bound = bound + lens[number]
        after = (rows >= bound).astype(jnp.int32)
        doc = doc + after
        start = start + after * lens[number]
    positions = rows - start
    allowed = (doc[:, None] == doc[None, :]) & (rows[:, None] >= rows[None, :])
    return (positions, allowed)


def rope_tables(positions, width):
    index = jnp.arange(width // 2, dtype=F32)
    freq = jnp.exp(-(2.0 * index / width) * math.log(1000000.0))
    angle = positions.astype(F32)[:, None] * freq[None, :]
    return (
        jnp.concatenate([jnp.cos(angle)] * 2, axis=1),
        jnp.concatenate([jnp.sin(angle)] * 2, axis=1),
    )


def contract_last(left, right, out=F32):
    return lax.dot_general(left, right, (((1,), (1,)), ((), ())), preferred_element_type=out)


def contract_first(left, right, out=F32):
    return lax.dot_general(left, right, (((0,), (0,)), ((), ())), preferred_element_type=out)


def norm_back(upstream, rows, factor, gain):
    scaled = upstream * gain
    gain_part = jnp.sum(upstream * rows * factor, axis=0)
    result = factor * scaled - rows * factor**3 * jnp.mean(scaled * rows, axis=-1, keepdims=True)
    return (result, gain_part)


SWAP = [(0, 1), (1, 0)]


def take(array, index, axis):
    return lax.dynamic_index_in_dim(array, index, axis, keepdims=False)


def join_pair(own, other, axis_name, axis):
    index = lax.axis_index(axis_name)
    return jnp.where(
        index == 0, jnp.stack([own, other], axis=axis), jnp.stack([other, own], axis=axis)
    )


def spread_pair(rows):
    other = lax.ppermute(rows, "t", SWAP)
    return join_pair(rows, other, "t", 0).reshape(2 * rows.shape[0], rows.shape[1])


def sum_pair(partial):
    index = lax.axis_index("t")
    halves = partial.reshape(2, partial.shape[0] // 2, partial.shape[1])
    other = lax.ppermute(take(halves, 1 - index, 0).astype(LOW), "t", SWAP)
    return take(halves, index, 0) + other.astype(F32)


def greet(axes_targets, conditions):
    barrier = pltpu.get_barrier_semaphore()
    for (axis, target), condition in zip(axes_targets, conditions):
        def signal(axis=axis, target=target):
            pl.semaphore_signal(barrier, inc=1, device_id={axis: target}, device_id_type=MESH)
        if condition is None:
            signal()
        else:
            pl.when(condition)(signal)
    amount = sum(1 if c is None else c.astype(jnp.int32) for c in conditions)
    pl.semaphore_wait(barrier, amount)


def slot_of(line, values):
    slot = line
    for value in values:
        slot = slot * 2 + value
    return slot


def both(*conditions):
    given = [c for c in conditions if c is not None]
    return functools.reduce(jnp.logical_and, given) if given else None


def guarded(condition, action):
    if condition is None:
        action()
    else:
        pl.when(condition)(action)


def bit_flips(variant, stage, count):
    return [(variant >> b) & 1 for b in range(stage)] + [1] + [0] * (count - stage - 1)


class Gather:
    def __init__(self, size, bits, x_ref, out_ref, own_sem, line_sems, bit_sems, recv_sems):
        self.size, self.bits, self.count = size, bits, len(bits)
        self.x_ref, self.out_ref, self.own_sem = x_ref, out_ref, own_sem
        self.line_sems, self.bit_sems, self.recv_sems = line_sems, bit_sems, recv_sems
        self.z = lax.axis_index("z")
        self.mine = [lax.axis_index(bit) for bit in bits]
        self.own = slot_of(self.z, self.mine)
        self.pending = []

    def copy(self, slot, first, axis, target, send_sem):
        return pltpu.make_async_remote_copy(
            src_ref=self.x_ref if first else self.out_ref.at[slot],
            dst_ref=self.out_ref.at[slot],
            send_sem=send_sem,
            recv_sem=self.recv_sems.at[slot],
            device_id={axis: target},
            device_id_type=MESH,
        )

    def start(self, condition, make):
        self.pending.append((condition, make))
        guarded(condition, lambda: make().start())

    def arrived(self, condition, slot, axis, target):
        guarded(
            condition,
            lambda: self.copy(slot, False, axis, target, self.line_sems.at[0, 0]).wait_recv(),
        )

    def spread(self, condition, slot, first, number, side, variant, after):
        for stage in range(after, self.count):
            self.start(
                condition,
                functools.partial(
                    self.copy,
                    slot,
                    first,
                    self.bits[stage],
                    1 - self.mine[stage],
                    self.bit_sems.at[number, side, variant, stage],
                ),
            )

    def line_of(self, number, side):
        line = self.z - number if side == 0 else self.z + number
        if number == 0:
            return line, None
        return line, (line >= 0 if side == 0 else line < self.size)

    def on_bits(self, number):
        for side in range(1 if number == 0 else 2):
            line, condition = self.line_of(number, side)
            for stage in range(self.count):
                for variant in range(2**stage):
                    flips = bit_flips(variant, stage, self.count)
                    slot = slot_of(line, [1 - m if f else m for m, f in zip(self.mine, flips)])
                    self.arrived(condition, slot, self.bits[stage], 1 - self.mine[stage])
                    code = sum(f << b for b, f in enumerate(flips))
                    self.spread(condition, slot, False, number, side, code, stage + 1)

    def begin(self):
        pltpu.make_async_copy(self.x_ref, self.out_ref.at[self.own], self.own_sem).start()
        z, size = self.z, self.size
        first = functools.partial(self.copy, self.own, True, "z")
        self.start(z < size - 1, functools.partial(first, z + 1, self.line_sems.at[0, 0]))
        self.start(z > 0, functools.partial(first, z - 1, self.line_sems.at[0, 1]))
        self.spread(None, self.own, True, 0, 0, 0, 0)

    def step(self, number):
        z, size = self.z, self.size
        for side in range(2):
            line, condition = self.line_of(number, side)
            slot = slot_of(line, self.mine)
            back = z - 1 if side == 0 else z + 1
            onto = z + 1 if side == 0 else z - 1
            self.arrived(condition, slot, "z", back)
            self.start(
                both(condition, onto < size if side == 0 else onto >= 0),
                functools.partial(self.copy, slot, False, "z", onto, self.line_sems.at[number, side]),
            )
            self.spread(condition, slot, False, number, side, 0, 0)

    def middle(self):
        for number in range(1, self.size):
            self.step(number)
            self.on_bits(number - 1)
        self.on_bits(self.size - 1)

    def end(self):
        pltpu.make_async_copy(self.x_ref, self.out_ref.at[self.own], self.own_sem).wait()
        for condition, make in self.pending:
            guarded(condition, lambda make=make: make().wait_send())


def gather_kernel(size, bits, *refs):
    z = lax.axis_index("z")
    mine = [lax.axis_index(bit) for bit in bits]
    greet(
        [("z", z + 1), ("z", z - 1)] + [(bit, 1 - m) for bit, m in zip(bits, mine)],
        [z < size - 1, z > 0] + [None] * len(bits),
    )
    steps = Gather(size, bits, *refs)
    steps.begin()
    steps.middle()
    steps.end()


def gather_semaphores(size, bits):
    slots = size * 2 ** len(bits)
    return [
        pltpu.SemaphoreType.DMA,
        pltpu.SemaphoreType.DMA((size, 2)),
        pltpu.SemaphoreType.DMA((size, 2, 2 ** len(bits), len(bits))),
        pltpu.SemaphoreType.DMA((slots,)),
    ]


def gather(x, size, bits, collective_id):
    slots = size * 2 ** len(bits)
    return pl.pallas_call(
        functools.partial(gather_kernel, size, bits),
        out_shape=jax.ShapeDtypeStruct((slots, *x.shape), x.dtype),
        in_specs=[pl.BlockSpec(memory_space=pl.ANY)],
        out_specs=pl.BlockSpec(memory_space=pl.ANY),
        scratch_shapes=gather_semaphores(size, bits),
        compiler_params=pltpu.CompilerParams(collective_id=collective_id, has_side_effects=True),
        cost_estimate=pl.CostEstimate(
            flops=0, transcendentals=0, bytes_accessed=slots * x.size * 100
        ),
    )(x)


class Exchange:
    def __init__(self, size, bits, block, half, gu_ref, dn_ref, gu_out, dn_out, sems):
        self.size, self.bits, self.count = size, bits, len(bits)
        self.block, self.half = block, half
        self.gu_ref, self.dn_ref, self.gu_out, self.dn_out = gu_ref, dn_ref, gu_out, dn_out
        self.own_sems, self.line_sems, self.bit_sems, self.recv_sems = sems
        self.z = lax.axis_index("z")
        self.mine = [lax.axis_index(bit) for bit in bits]
        self.own = slot_of(self.z, self.mine)
        self.others = [lax.rem(self.z + o, size) for o in range(1, size)]
        self.pending = []

    def pieces(self, target, slot):
        low = pl.multiple_of(jnp.minimum(target * self.block, self.half - self.block), LANES)
        high = pl.multiple_of(low + self.half, LANES)
        width = self.block
        return [
            (self.gu_ref.at[:, pl.ds(low, width)], self.gu_out.at[slot, :, pl.ds(0, width)]),
            (self.gu_ref.at[:, pl.ds(high, width)], self.gu_out.at[slot, :, pl.ds(width, width)]),
            (self.dn_ref.at[:, pl.ds(low, width)], self.dn_out.at[slot]),
        ]

    def line_copy(self, place, piece, slot):
        source, landing = self.pieces(self.others[place], slot)[piece]
        return pltpu.make_async_remote_copy(
            src_ref=source,
            dst_ref=landing,
            send_sem=self.line_sems.at[place, piece],
            recv_sem=self.recv_sems.at[slot, piece],
            device_id={"z": self.others[place]},
            device_id_type=MESH,
        )

    def own_copy(self, piece):
        source, landing = self.pieces(self.z, self.own)[piece]
        return pltpu.make_async_copy(source, landing, self.own_sems.at[piece])

    def bit_copy(self, slot, piece, stage, send_sem):
        ref = (self.gu_out, None, self.dn_out)[piece]
        return pltpu.make_async_remote_copy(
            src_ref=ref.at[slot],
            dst_ref=ref.at[slot],
            send_sem=send_sem,
            recv_sem=self.recv_sems.at[slot, piece],
            device_id={self.bits[stage]: 1 - self.mine[stage]},
            device_id_type=MESH,
        )

    def first_copy(self, slot, piece, stage, send_sem):
        source, landing = self.pieces(self.z, slot)[piece]
        return pltpu.make_async_remote_copy(
            src_ref=source,
            dst_ref=landing,
            send_sem=send_sem,
            recv_sem=self.recv_sems.at[slot, piece],
            device_id={self.bits[stage]: 1 - self.mine[stage]},
            device_id_type=MESH,
        )

    def spread(self, slot, number, variant, after):
        for stage in range(after, self.count):
            for piece in (0, 2):
                make = functools.partial(
                    self.bit_copy, slot, piece, stage, self.bit_sems.at[number, variant, stage, piece]
                )
                self.pending.append(make)
                make().start()

    def on_bits(self, number):
        line = lax.rem(self.z - number + self.size, self.size)
        for stage in range(self.count):
            for variant in range(2**stage):
                flips = bit_flips(variant, stage, self.count)
                slot = slot_of(line, [1 - m if f else m for m, f in zip(self.mine, flips)])
                if number == 0 and variant == 0:
                    for piece in range(3):
                        self.first_copy(slot, piece, stage, self.own_sems.at[0]).wait_recv()
                else:
                    for piece in (0, 2):
                        self.bit_copy(slot, piece, stage, self.own_sems.at[0]).wait_recv()
                self.spread(slot, number, sum(f << b for b, f in enumerate(flips)), stage + 1)

    def begin(self):
        for stage in range(self.count):
            for piece in range(3):
                make = functools.partial(
                    self.first_copy, self.own, piece, stage, self.bit_sems.at[0, 0, stage, piece]
                )
                self.pending.append(make)
                make().start()
        for piece in range(3):
            self.own_copy(piece).start()

    def send(self, offset):
        for piece in range(3):
            self.line_copy(offset - 1, piece, self.own).start()

    def sent(self, offset):
        for piece in range(3):
            self.line_copy(offset - 1, piece, self.own).wait_send()

    def step(self, offset):
        slot = slot_of(lax.rem(self.z - offset + self.size, self.size), self.mine)
        for piece in range(3):
            self.line_copy(0, piece, slot).wait_recv()
        self.spread(slot, offset, 0, 0)

    def end(self):
        for piece in range(3):
            self.own_copy(piece).wait()
        for make in self.pending:
            make().wait_send()


def weights_kernel(
    size, bits, block, half, at_ref, gu_ref, dn_ref, gm_ref, at_out, gu_out, dn_out, gm_out, *sems
):
    z = lax.axis_index("z")
    mine = [lax.axis_index(bit) for bit in bits]
    others = [lax.rem(z + o, size) for o in range(1, size)]
    greet(
        [("z", other) for other in others]
        + [(bit, 1 - m) for bit, m in zip(bits, mine)]
        + [("t", 1 - lax.axis_index("t"))],
        [None] * (size + len(bits)),
    )
    rows = Gather(size, ("t",), gm_ref, gm_out, *sems[8:])
    attention = Gather(size, bits, at_ref, at_out, *sems[:4])
    feed = Exchange(size, bits, block, half, gu_ref, dn_ref, gu_out, dn_out, sems[4:8])
    attention.begin()
    rows.begin()
    feed.begin()
    attention.step(1)
    rows.step(1)
    attention.step(2)
    attention.on_bits(0)
    rows.on_bits(0)
    rows.step(2)
    feed.send(1)
    attention.step(3)
    attention.on_bits(1)
    rows.on_bits(1)
    rows.step(3)
    feed.on_bits(0)
    attention.on_bits(2)
    feed.sent(1)
    feed.send(3)
    feed.step(1)
    attention.on_bits(3)
    rows.on_bits(2)
    feed.sent(3)
    feed.send(2)
    feed.step(3)
    feed.on_bits(1)
    rows.on_bits(3)
    feed.sent(2)
    feed.step(2)
    feed.on_bits(3)
    feed.on_bits(2)
    attention.end()
    feed.end()
    rows.end()


def weights(at, gu, dn, gm, size, bits, block, collective_id):
    slots = size * 2 ** len(bits)
    rows, half = dn.shape
    return pl.pallas_call(
        functools.partial(weights_kernel, size, bits, block, half),
        out_shape=(
            jax.ShapeDtypeStruct((slots, *at.shape), at.dtype),
            jax.ShapeDtypeStruct((slots, rows, 2 * block), gu.dtype),
            jax.ShapeDtypeStruct((slots, rows, block), dn.dtype),
            jax.ShapeDtypeStruct((2 * size, *gm.shape), gm.dtype),
        ),
        in_specs=[pl.BlockSpec(memory_space=pl.ANY)] * 4,
        out_specs=[pl.BlockSpec(memory_space=pl.ANY)] * 4,
        scratch_shapes=[
            *gather_semaphores(size, bits),
            pltpu.SemaphoreType.DMA((3,)),
            pltpu.SemaphoreType.DMA((size - 1, 3)),
            pltpu.SemaphoreType.DMA((size, 2 ** len(bits), len(bits), 3)),
            pltpu.SemaphoreType.DMA((slots, 3)),
            *gather_semaphores(size, ("t",)),
        ],
        compiler_params=pltpu.CompilerParams(collective_id=collective_id, has_side_effects=True),
        cost_estimate=pl.CostEstimate(
            flops=0, transcendentals=0, bytes_accessed=slots * gu.size * 27
        ),
    )(at, gu, dn, gm)


class Fold:
    def __init__(self, size, bits, order, p_ref, own_buf, sums, stage_in, stage_out, own_sems, send_sems, recv_sems):
        self.size, self.bits, self.count, self.order = size, bits, len(bits), order
        self.last = self.count - 1
        self.p_ref, self.own_buf, self.sums = p_ref, own_buf, sums
        self.stage_in, self.stage_out = stage_in, stage_out
        self.own_sems, self.send_sems, self.recv_sems = own_sems, send_sems, recv_sems
        self.z = lax.axis_index("z")
        self.mine = [lax.axis_index(bit) for bit in bits]

    def line(self, place):
        return lax.rem(self.z + self.order[place], self.size)

    def index(self, place, stage, variant):
        return place * (2**self.count - 1) + 2**stage - 1 + variant

    def slot(self, place, variant, flip):
        flips = [(variant >> b) & 1 for b in range(self.last)] + [flip]
        return slot_of(self.line(place), [1 - m if f else m for m, f in zip(self.mine, flips)])

    def copy(self, place, stage, variant):
        index = self.index(place, stage, variant)
        if stage == self.last:
            source = self.p_ref.at[self.slot(place, variant, 1)]
        else:
            source = self.stage_out.at[place * (2**self.last - 1) + 2**stage - 1 + variant]
        return pltpu.make_async_remote_copy(
            src_ref=source,
            dst_ref=self.stage_in.at[index],
            send_sem=self.send_sems.at[index],
            recv_sem=self.recv_sems.at[index],
            device_id={self.bits[stage]: 1 - self.mine[stage]},
            device_id_type=MESH,
        )

    def own_copy(self, place, variant):
        number = place * 2**self.last + variant
        return pltpu.make_async_copy(
            self.p_ref.at[self.slot(place, variant, 0)], self.own_buf.at[number], self.own_sems.at[number]
        )

    def begin(self, places=None):
        for place in range(self.size) if places is None else places:
            for variant in reversed(range(2**self.last)):
                self.copy(place, self.last, variant).start()
                self.own_copy(place, variant).start()

    def stage(self, place, stage, done=None):
        for variant in reversed(range(2**stage)):
            if stage == self.last:
                self.own_copy(place, variant).wait()
                held = self.own_buf[place * 2**self.last + variant].astype(F32)
            else:
                held = self.sums[place * (2**self.last - 1) + 2**stage - 1 + variant]
            self.copy(place, stage, variant).wait_recv()
            total = held + self.stage_in[self.index(place, stage, variant)].astype(F32)
            if stage == 0:
                done(place, total)
                continue
            lower = variant & (2 ** (stage - 1) - 1)
            number = place * (2**self.last - 1) + 2 ** (stage - 1) - 1 + lower
            if variant >> (stage - 1):
                self.stage_out[number] = total.astype(LOW)
                self.copy(place, stage - 1, lower).start()
            else:
                self.sums[number] = total

    def end(self):
        for place in range(self.size):
            for stage in range(self.count):
                for variant in range(2**stage):
                    self.copy(place, stage, variant).wait_send()


def fold_scratch(size, bits, rows, columns):
    count = len(bits)
    inner, lower = size * (2**count - 1), size * (2 ** (count - 1) - 1)
    return [
        pltpu.VMEM((size * 2 ** (count - 1), rows, columns), LOW),
        pltpu.VMEM((max(lower, 1), rows, columns) if lower else (1, 8, LANES), F32),
        pltpu.VMEM((inner, rows, columns), LOW),
        pltpu.VMEM((max(lower, 1), rows, columns) if lower else (1, 16, LANES), LOW),
        pltpu.SemaphoreType.DMA((size * 2 ** (count - 1),)),
        pltpu.SemaphoreType.DMA((inner,)),
        pltpu.SemaphoreType.DMA((inner,)),
    ]


class Scatter:
    def __init__(self, size, bits, p_ref, out_ref, line_out, line_in, line_send, line_recv, *fold):
        order = list(range(1, size)) + [0]
        self.fold = Fold(size, bits, order, p_ref, *fold)
        self.size, self.out_ref = size, out_ref
        self.line_out, self.line_in, self.line_send, self.line_recv = line_out, line_in, line_send, line_recv

    def line_copy(self, place):
        return pltpu.make_async_remote_copy(
            src_ref=self.line_out.at[place],
            dst_ref=self.line_in.at[place],
            send_sem=self.line_send.at[place],
            recv_sem=self.line_recv.at[place],
            device_id={"z": self.fold.line(place)},
            device_id_type=MESH,
        )

    def done(self, place, total):
        if place < self.size - 1:
            self.line_out[place] = total.astype(LOW)
            self.line_copy(place).start()
        else:
            self.out_ref[...] = total

    def begin(self):
        self.fold.begin()

    def place(self, place):
        for stage in reversed(range(self.fold.count)):
            self.fold.stage(place, stage, self.done)

    def finish(self):
        for place in range(self.size - 1):
            self.line_copy(place).wait_recv()
            self.out_ref[...] += self.line_in[place].astype(F32)

    def end(self):
        self.fold.end()
        for place in range(self.size - 1):
            self.line_copy(place).wait_send()


def scatter_scratch(size, bits, rows, columns):
    return [
        pltpu.VMEM((size - 1, rows, columns), LOW),
        pltpu.VMEM((size - 1, rows, columns), LOW),
        pltpu.SemaphoreType.DMA((size - 1,)),
        pltpu.SemaphoreType.DMA((size - 1,)),
        *fold_scratch(size, bits, rows, columns),
    ]


SCATTER_REFS = 11


class Total:
    def __init__(self, size, bits, x_ref, out_ref, held, landed, send_sems, recv_sems):
        self.size, self.bits, self.count = size, bits, len(bits)
        self.x_ref, self.out_ref, self.held, self.landed = x_ref, out_ref, held, landed
        self.send_sems, self.recv_sems = send_sems, recv_sems
        self.z = lax.axis_index("z")
        self.others = [lax.rem(self.z + o, size) for o in range(1, size)]

    def copy(self, number):
        if number < self.count:
            axis = self.bits[number]
            source, target = self.held.at[number], {axis: 1 - lax.axis_index(axis)}
        else:
            source, target = self.held.at[self.count], {"z": self.others[number - self.count]}
        return pltpu.make_async_remote_copy(
            src_ref=source,
            dst_ref=self.landed.at[number],
            send_sem=self.send_sems.at[number],
            recv_sem=self.recv_sems.at[number],
            device_id=target,
            device_id_type=MESH,
        )

    def begin(self):
        self.held[0] = self.x_ref[...]
        self.copy(0).start()

    def pair(self, number):
        self.copy(number).wait_recv()
        self.held[number + 1] = self.held[number] + self.landed[number]
        if number + 1 < self.count:
            self.copy(number + 1).start()
        else:
            for place in range(self.size - 1):
                self.copy(self.count + place).start()

    def finish(self):
        for place in range(self.size - 1):
            self.copy(self.count + place).wait_recv()
        total = jnp.zeros(self.out_ref.shape, self.out_ref.dtype)
        for line in range(self.size):
            offset = lax.rem(line - self.z + self.size, self.size)
            part = self.held[self.count]
            for o in range(1, self.size):
                part = jnp.where(offset == o, self.landed[self.count + self.size - o - 1], part)
            total = total + part
        self.out_ref[...] = total

    def end(self):
        for number in range(self.count + self.size - 1):
            self.copy(number).wait_send()


def greet_all(size, axes):
    z = lax.axis_index("z")
    greet(
        [("z", lax.rem(z + o, size)) for o in range(1, size)]
        + [(axis, 1 - lax.axis_index(axis)) for axis in axes],
        [None] * (size - 1 + len(axes)),
    )


def in_groups(refs, sizes):
    groups, at = [], 0
    for number in sizes:
        groups.append(refs[at : at + number])
        at += number
    return groups


def comm_params(collective_id):
    return pltpu.CompilerParams(
        collective_id=collective_id, has_side_effects=True, vmem_limit_bytes=56 * 2**20
    )


def at_microseconds(time):
    return pl.CostEstimate(flops=0, transcendentals=0, bytes_accessed=time * 3500000)


def scatter_kernel(size, bits, p_ref, out_ref, *refs):
    greet_all(size, bits)
    steps = Scatter(size, bits, p_ref, out_ref, *refs)
    steps.begin()
    for place in range(size):
        steps.place(place)
    steps.finish()
    steps.end()


def scatter(partial, size, bits, collective_id):
    slots, rows, columns = partial.shape
    return pl.pallas_call(
        functools.partial(scatter_kernel, size, bits),
        out_shape=jax.ShapeDtypeStruct((rows, columns), F32),
        in_specs=[pl.BlockSpec(memory_space=pl.ANY)],
        out_specs=pl.BlockSpec(memory_space=pltpu.VMEM),
        scratch_shapes=scatter_scratch(size, bits, rows, columns),
        compiler_params=comm_params(collective_id),
        cost_estimate=at_microseconds(48),
    )(partial)


def last_kernel(size, bits, p_ref, x_ref, out_ref, sum_ref, *refs):
    greet_all(size, ("t", *bits))
    given, rest = in_groups(refs, [SCATTER_REFS, 4])
    small = Total(size, ("t", *bits), x_ref, sum_ref, *rest)
    steps = Scatter(size, bits, p_ref, out_ref, *given)
    small.begin()
    steps.begin()
    for place in range(size):
        steps.place(place)
        if place <= len(bits):
            small.pair(place)
    for number in range(size, len(bits) + 1):
        small.pair(number)
    steps.finish()
    small.finish()
    steps.end()
    small.end()


def last(partial, x, size, bits, collective_id):
    slots, rows, columns = partial.shape
    number = len(bits) + 1
    return pl.pallas_call(
        functools.partial(last_kernel, size, bits),
        out_shape=(jax.ShapeDtypeStruct((rows, columns), F32), jax.ShapeDtypeStruct(x.shape, F32)),
        in_specs=[pl.BlockSpec(memory_space=pl.ANY), pl.BlockSpec(memory_space=pltpu.VMEM)],
        out_specs=[pl.BlockSpec(memory_space=pltpu.VMEM)] * 2,
        scratch_shapes=[
            *scatter_scratch(size, bits, rows, columns),
            pltpu.VMEM((number + 1, *x.shape), F32),
            pltpu.VMEM((number + size - 1, *x.shape), F32),
            pltpu.SemaphoreType.DMA((number + size - 1,)),
            pltpu.SemaphoreType.DMA((number + size - 1,)),
        ],
        compiler_params=comm_params(collective_id),
        cost_estimate=at_microseconds(60),
    )(partial, x)


def back_kernel(size, bits, branches, *refs):
    p_refs, (gu_ref, dn_ref), outs, (folded,), refs = in_groups(
        refs, [branches, 2, branches, 1, len(refs)]
    )
    greet_all(size, ("t", *bits))
    *scatters, gu_scratch, dn_scratch, (gu_done, dn_done, done_sems) = in_groups(
        refs, [SCATTER_REFS] * branches + [7, 7, 3]
    )
    scatters = [
        Scatter(size, ("t",), p, out, *scratch) for p, out, scratch in zip(p_refs, outs, scatters)
    ]
    order = list(range(size))
    gu = Fold(size, bits, order, gu_ref, *gu_scratch)
    dn = Fold(size, bits, order, dn_ref, *dn_scratch)
    width, narrow = gu_ref.shape[2], dn_ref.shape[2]

    def out_copy(number, place, line):
        source = (gu_done, dn_done)[number].at[place]
        low, count = ((0, width), (width, narrow))[number]
        return pltpu.make_async_copy(
            source, folded.at[line, :, pl.ds(low, count)], done_sems.at[number, place]
        )

    def done(number):
        def keep(place, total):
            (gu_done, dn_done)[number][place] = total.astype(LOW)
            out_copy(number, place, gu.line(place)).start()

        return keep

    for steps in scatters:
        steps.begin()
    gu.begin()
    dn.begin()
    for place in range(size):
        for stage in reversed(range(1, len(bits))):
            gu.stage(place, stage)
            dn.stage(place, stage)
        for steps in scatters:
            steps.place(place)
    for steps in scatters:
        steps.finish()
    for place in range(size):
        gu.stage(place, 0, done(0))
        dn.stage(place, 0, done(1))
    for place in range(size):
        for number in range(2):
            out_copy(number, place, gu.line(place)).wait()
    for steps in (*scatters, gu, dn):
        steps.end()


def back(partials, gu, dn, size, bits, collective_id):
    _, rows, columns = partials[0].shape
    slots, few, width = gu.shape
    narrow = dn.shape[2]
    branches = len(partials)
    out = pl.pallas_call(
        functools.partial(back_kernel, size, bits, branches),
        out_shape=(
            *([jax.ShapeDtypeStruct((rows, columns), F32)] * branches),
            jax.ShapeDtypeStruct((size, few, width + narrow), LOW),
        ),
        in_specs=[pl.BlockSpec(memory_space=pl.ANY)] * (branches + 2),
        out_specs=[pl.BlockSpec(memory_space=pltpu.VMEM)] * branches + [pl.BlockSpec(memory_space=pl.ANY)],
        scratch_shapes=[
            *(scatter_scratch(size, ("t",), rows, columns) * branches),
            *fold_scratch(size, bits, few, width),
            *fold_scratch(size, bits, few, narrow),
            pltpu.VMEM((size, few, width), LOW),
            pltpu.VMEM((size, few, narrow), LOW),
            pltpu.SemaphoreType.DMA((2, size)),
        ],
        compiler_params=comm_params(collective_id),
        cost_estimate=at_microseconds(80),
    )(*partials, gu, dn)
    return out[:branches], out[branches]


def spread_group(rows):
    return gather(rows, LINE, ("t",), 1).reshape(-1, rows.shape[1])


def in_slots(partial, slots):
    return partial.reshape(slots, -1, partial.shape[1])


def sum_group(partial):
    return scatter(in_slots(partial, 2 * LINE), LINE, ("t",), 2)


def block_width(half):
    return -(-half // (LINE * LANES)) * LANES


def block_start(line, block, half):
    return min(line * block, half - block)


def tie(value, *others):
    return lax.optimization_barrier((value, *others))


def column_sections(gu, dn, block):
    half = dn.shape[1]
    sections = []
    for line in range(LINE):
        low = block_start(line, block, half)
        parts = [gu[:, low : low + block], gu[:, half + low : half + low + block], dn[:, low : low + block]]
        sections.append(jnp.concatenate(parts, axis=1))
    return jnp.stack(sections)


def from_blocks(blocks, parts, half):
    block = blocks.shape[2] // 3
    pieces = []
    for part in parts:
        for line in range(LINE):
            skip = line * block - block_start(line, block, half)
            pieces.append(blocks[line, :, part * block + skip : (part + 1) * block])
    return jnp.concatenate(pieces, axis=1).astype(F32)


def local(
    bits, tokens, cotangent, doc_lengths, norm_attn, norm_ffn, w_qkv, b_qkv, w_out, w_gateup, w_down
):
    dp = ("z", *bits)
    tensor_size = lax.axis_size("t")
    count = tokens.shape[0]
    length = count * tensor_size
    layers = w_qkv.shape[0]
    kv_local = KV // tensor_size
    groups = H // KV
    q_width = kv_local * groups * HD
    kv_width = kv_local * HD
    qkv_width = w_qkv.shape[2]
    rows = w_qkv.shape[1]
    half = w_down.shape[2]
    block = block_width(half)
    scale = 1.0 / math.sqrt(HD)
    positions, allowed = doc_layout(doc_lengths[0], length)
    cosine, sine = rope_tables(positions, HD)
    cos_q = cosine[:, None, None, :]
    sin_q = sine[:, None, None, :]
    cos_k = cosine[:, None, :]
    sin_k = sine[:, None, :]
    gain_attn = norm_attn.astype(F32)
    gain_ffn = norm_ffn.astype(F32)
    flats = [jnp.concatenate([w_qkv[layer], w_out[layer]], axis=1) for layer in range(layers)]
    both_w, gu_w, down_w, gm_all = weights(
        flats[0], w_gateup[0], w_down[0], cotangent, LINE, bits, block, 3
    )
    attn_weights = [both_w.reshape(-1, flats[0].shape[1])]
    ffn_weights = [(gu_w.reshape(-1, 2 * block), down_w.reshape(-1, block))]
    gm_all = gm_all.reshape(-1, cotangent.shape[1])
    line = lax.axis_index("z")
    valid = jnp.arange(block) >= line * block - jnp.minimum(line * block, half - block)
    saved = []
    state = tokens.astype(F32)
    for layer in range(layers):
        both_w = attn_weights[layer]
        ahead = layer + 1 < layers
        if ahead:
            flat, sections = flats[layer + 1], column_sections(w_gateup[layer + 1], w_down[layer + 1], block)
            both_w, flat, sections = tie(both_w, flat, sections)
            coming = lax.all_gather(flat, dp, axis=0, tiled=True)
            sections = lax.all_to_all(sections, "z", 0, 0, tiled=True)
        attn_weights[layer] = both_w
        qkv_w, out_w = both_w[:, :qkv_width], both_w[:, qkv_width:]
        factor_a = rms_factor(state)
        xa_all = spread_pair((state * factor_a * gain_attn[layer]).astype(LOW))
        lin = jnp.dot(xa_all, qkv_w, preferred_element_type=F32) + b_qkv[layer].astype(F32)
        query = lin[:, :q_width].reshape(length, kv_local, groups, HD)
        key = lin[:, q_width : q_width + kv_width].reshape(length, kv_local, HD)
        value = lin[:, q_width + kv_width :].reshape(length, kv_local, HD).astype(LOW)
        query = (query * cos_q + rotate(query) * sin_q).astype(LOW)
        key = (key * cos_k + rotate(key) * sin_k).astype(LOW)
        raw = jnp.einsum("qkgd,pkd->kgqp", query, key, preferred_element_type=F32)
        scores = jnp.where(allowed, raw * scale, -1e30)
        top = jnp.max(scores, axis=-1, keepdims=True)
        expo = jnp.exp(scores - top)
        total = jnp.sum(expo, axis=-1, keepdims=True)
        probs = expo / total
        log_total = top + jnp.log(total)
        attended = (
            jnp.einsum("kgqp,pkd->qkgd", probs.astype(LOW), value, preferred_element_type=F32)
            .reshape(length, q_width)
            .astype(LOW)
        )
        middle = state + sum_pair(contract_last(attended, out_w))
        gu_w, down_w = ffn_weights[layer]
        factor_f = rms_factor(middle)
        xf_all = spread_group((middle * factor_f * gain_ffn[layer]).astype(LOW))
        if ahead:
            xf_all, sections = tie(xf_all, sections)
            sections = join_pair(sections, lax.ppermute(sections, bits[0], SWAP), bits[0], 1)
        gate_up = jnp.dot(xf_all, gu_w, preferred_element_type=F32)
        gate = gate_up[:, :block]
        up = gate_up[:, block:]
        act = jnp.where(valid, jax.nn.silu(gate) * up, 0.0).astype(LOW)
        partial = contract_last(act, down_w, LOW)
        if ahead:
            branch = sum_group(partial)
            branch, sections, coming = tie(branch, sections, coming)
            for number, bit in enumerate(bits[1:]):
                sections = join_pair(sections, lax.ppermute(sections, bit, SWAP), bit, 2 + number)
            sections = sections.reshape(-1, 3 * block)
            ffn_weights.append((sections[:, : 2 * block], sections[:, 2 * block :]))
            attn_weights.append(coming)
            after = middle + branch
        saved.append(
            (state, factor_a, xa_all, query, key, value, log_total, attended)
            + (middle, factor_f, xf_all, gate, up, act)
        )
        if ahead:
            state = after
    grad = cotangent.astype(F32)
    grads_attn, grads_bias, grads_ga, grads_gf = ([] for _ in range(4))
    waiting, branches = None, [in_slots(partial, 2 * LINE)]
    grads_blocks = []
    for layer in reversed(range(layers)):
        (state_in, factor_a, xa_all, query, key, value, log_total, attended) = saved[layer][:8]
        (middle, factor_f, xf_all, gate, up, act) = saved[layer][8:]
        gu_w, down_w = ffn_weights[layer]
        both_w = attn_weights[layer]
        qkv_w, out_w = both_w[:, :qkv_width], both_w[:, qkv_width:]
        if waiting is not None:
            gm_all = spread_group(grad.astype(LOW))
        d_down = contract_first(gm_all, act, LOW)
        d_act = jnp.dot(gm_all, down_w, preferred_element_type=F32)
        sig = jax.nn.sigmoid(gate)
        d_gate = d_act * up * sig * (1.0 + gate * (1.0 - sig))
        d_up = d_act * gate * sig
        d_gu = jnp.concatenate(
            [jnp.where(valid, d_gate, 0.0), jnp.where(valid, d_up, 0.0)], axis=1
        ).astype(LOW)
        d_gateup = contract_first(xf_all, d_gu, LOW)
        branches.insert(0, in_slots(contract_last(d_gu, gu_w, LOW), 2 * LINE))
        slots = in_slots(d_gateup, d_gateup.shape[0] // rows), in_slots(d_down, d_down.shape[0] // rows)
        (d_xf, *others), folded = back(branches, *slots, LINE, bits, 6 + layer)
        branches = []
        if others:
            output = (middle + others[0]).astype(LOW)
        waiting = lax.all_to_all(folded, "z", 0, 0, tiled=True)
        d_mid, part_f = norm_back(d_xf, middle, factor_f, gain_ffn[layer])
        grad = grad + d_mid
        ga_all = spread_pair(grad.astype(LOW))
        d_att = jnp.dot(ga_all, out_w, preferred_element_type=F32).astype(LOW)
        raw = jnp.einsum("qkgd,pkd->kgqp", query, key, preferred_element_type=F32)
        scores = jnp.where(allowed, raw * scale, -1e30)
        probs = jnp.exp(scores - log_total)
        d_att4 = d_att.reshape(length, kv_local, groups, HD)
        d_probs = jnp.einsum("qkgd,pkd->kgqp", d_att4, value, preferred_element_type=F32)
        centre = jnp.sum(probs * d_probs, axis=-1, keepdims=True)
        d_raw = (probs * (d_probs - centre) * scale).astype(LOW)
        d_query = jnp.einsum("kgqp,pkd->qkgd", d_raw, key, preferred_element_type=F32)
        d_key = jnp.einsum("kgqp,qkgd->pkd", d_raw, query, preferred_element_type=F32)
        d_value = jnp.einsum(
            "kgqp,qkgd->pkd", probs.astype(LOW), d_att4, preferred_element_type=F32
        )
        d_query = d_query * cos_q + rotate_back(d_query * sin_q)
        d_key = d_key * cos_k + rotate_back(d_key * sin_k)
        d_lin = jnp.concatenate(
            [
                d_query.reshape(length, q_width),
                d_key.reshape(length, kv_width),
                d_value.reshape(length, kv_width),
            ],
            axis=1,
        )
        grads_bias.append(jnp.sum(d_lin, axis=0))
        d_lin_low = d_lin.astype(LOW)
        d_xa = sum_pair(contract_last(d_lin_low, qkv_w))
        d_in, part_a = norm_back(d_xa, state_in, factor_a, gain_attn[layer])
        grad = grad + d_in
        if layer > 0:
            grad, waiting = tie(grad, waiting)
        grads_blocks.append(waiting)
        d_both = jnp.concatenate(
            [contract_first(xa_all, d_lin_low, LOW), contract_first(ga_all, attended, LOW)], axis=1
        )
        if layer == 0:
            d_both = in_slots(d_both, d_both.shape[0] // rows)
        else:
            grads_attn.append(
                lax.psum_scatter(d_both, dp, scatter_dimension=0, tiled=True).astype(F32)
            )
        grads_ga.append(part_a)
        grads_gf.append(part_f)

    def ordered(items):
        return jnp.stack(items[::-1], axis=0)

    side = lax.axis_index("t")
    bias = ordered(grads_bias)
    spread = jnp.where(
        (jnp.arange(tensor_size) == side)[:, None, None], bias[None], jnp.zeros_like(bias)[None]
    )
    small = (ordered(grads_ga), ordered(grads_gf), spread)
    flat = jnp.concatenate([item.reshape(-1, LANES) for item in small], axis=0)
    last_attn, flat = last(d_both, flat, LINE, bits, 4)
    grads_attn.append(last_attn)
    full_ga, full_gf, full_bias = (
        part.reshape(item.shape)
        for part, item in zip(
            jnp.split(flat, [small[0].size // LANES, 2 * small[0].size // LANES], axis=0), small
        )
    )
    both = ordered(grads_attn)
    return (
        output,
        grad,
        full_ga,
        full_gf,
        both[:, :, :qkv_width],
        take(full_bias, side, 0),
        both[:, :, qkv_width:],
        ordered([from_blocks(blocks, (0, 1), half) for blocks in grads_blocks]),
        ordered([from_blocks(blocks, (2,), half) for blocks in grads_blocks]),
    )


def solution(mesh):
    dp_size, tensor_size = mesh.devices.shape
    rest = dp_size // LINE
    bits = tuple(f"r{number}" for number in range(rest.bit_length() - 1))
    shape = (LINE, *([2] * len(bits)), tensor_size)
    fine = Mesh(mesh.devices.reshape(shape), ("z", *bits, "t"))
    dp = ("z", *bits)
    rows = P((*dp, "t"), None)
    weight = P(None, dp, "t")

    def step(*args):
        return local(bits, *args)

    return jax.shard_map(
        step,
        mesh=fine,
        in_specs=(rows, rows, P(dp, None), P(), P(), weight, P(None, "t"), weight, weight, weight),
        out_specs=(rows, rows, P(), P(), weight, P(None, "t"), weight, weight, weight),
        check_vma=False,
    )
```

```python
import functools
import math

import jax
import jax.numpy as jnp
from jax import lax
from jax.experimental import pallas as pl
from jax.experimental.pallas import tpu as pltpu
from jax.sharding import Mesh
from jax.sharding import PartitionSpec as P

H = 12
KV = 2
HD = 128
LINE = 4
LANES = 128
LOW = jnp.bfloat16
F32 = jnp.float32
MESH = pl.DeviceIdType.MESH


def rms_factor(rows):
    return lax.rsqrt(jnp.mean(rows * rows, axis=-1, keepdims=True) + 1e-06)


def rotate(values):
    half = values.shape[-1] // 2
    return jnp.concatenate([-values[..., half:], values[..., :half]], axis=-1)


def rotate_back(values):
    half = values.shape[-1] // 2
    return jnp.concatenate([values[..., half:], -values[..., :half]], axis=-1)


def doc_layout(lens, count):
    rows = jnp.arange(count, dtype=jnp.int32)
    doc = jnp.zeros((count,), jnp.int32)
    start = jnp.zeros((count,), jnp.int32)
    bound = jnp.int32(0)
    for number in range(lens.shape[0]):
        bound = bound + lens[number]
        after = (rows >= bound).astype(jnp.int32)
        doc = doc + after
        start = start + after * lens[number]
    positions = rows - start
    allowed = (doc[:, None] == doc[None, :]) & (rows[:, None] >= rows[None, :])
    return (positions, allowed)


def rope_tables(positions, width):
    index = jnp.arange(width // 2, dtype=F32)
    freq = jnp.exp(-(2.0 * index / width) * math.log(1000000.0))
    angle = positions.astype(F32)[:, None] * freq[None, :]
    return (
        jnp.concatenate([jnp.cos(angle)] * 2, axis=1),
        jnp.concatenate([jnp.sin(angle)] * 2, axis=1),
    )


def contract_last(left, right, out=F32):
    return lax.dot_general(left, right, (((1,), (1,)), ((), ())), preferred_element_type=out)


def contract_first(left, right, out=F32):
    return lax.dot_general(left, right, (((0,), (0,)), ((), ())), preferred_element_type=out)


def norm_back(upstream, rows, factor, gain):
    scaled = upstream * gain
    gain_part = jnp.sum(upstream * rows * factor, axis=0)
    result = factor * scaled - rows * factor**3 * jnp.mean(scaled * rows, axis=-1, keepdims=True)
    return (result, gain_part)


SWAP = [(0, 1), (1, 0)]


def take(array, index, axis):
    return lax.dynamic_index_in_dim(array, index, axis, keepdims=False)


def join_pair(own, other, axis_name, axis):
    index = lax.axis_index(axis_name)
    return jnp.where(
        index == 0, jnp.stack([own, other], axis=axis), jnp.stack([other, own], axis=axis)
    )


def spread_pair(rows):
    other = lax.ppermute(rows, "t", SWAP)
    return join_pair(rows, other, "t", 0).reshape(2 * rows.shape[0], rows.shape[1])


def sum_pair(partial):
    index = lax.axis_index("t")
    halves = partial.reshape(2, partial.shape[0] // 2, partial.shape[1])
    other = lax.ppermute(take(halves, 1 - index, 0).astype(LOW), "t", SWAP)
    return take(halves, index, 0) + other.astype(F32)


def greet(axes_targets, conditions):
    barrier = pltpu.get_barrier_semaphore()
    for (axis, target), condition in zip(axes_targets, conditions):
        def signal(axis=axis, target=target):
            pl.semaphore_signal(barrier, inc=1, device_id={axis: target}, device_id_type=MESH)
        if condition is None:
            signal()
        else:
            pl.when(condition)(signal)
    amount = sum(1 if c is None else c.astype(jnp.int32) for c in conditions)
    pl.semaphore_wait(barrier, amount)


def slot_of(line, values):
    slot = line
    for value in values:
        slot = slot * 2 + value
    return slot


def both(*conditions):
    given = [c for c in conditions if c is not None]
    return functools.reduce(jnp.logical_and, given) if given else None


def guarded(condition, action):
    if condition is None:
        action()
    else:
        pl.when(condition)(action)


def bit_flips(variant, stage, count):
    return [(variant >> b) & 1 for b in range(stage)] + [1] + [0] * (count - stage - 1)


class Gather:
    def __init__(self, size, bits, x_ref, out_ref, own_sem, line_sems, bit_sems, recv_sems):
        self.size, self.bits, self.count = size, bits, len(bits)
        self.x_ref, self.out_ref, self.own_sem = x_ref, out_ref, own_sem
        self.line_sems, self.bit_sems, self.recv_sems = line_sems, bit_sems, recv_sems
        self.z = lax.axis_index("z")
        self.mine = [lax.axis_index(bit) for bit in bits]
        self.own = slot_of(self.z, self.mine)
        self.pending, self.settled = [], False

    def copy(self, slot, first, axis, target, send_sem):
        return pltpu.make_async_remote_copy(
            src_ref=self.x_ref if first else self.out_ref.at[slot],
            dst_ref=self.out_ref.at[slot],
            send_sem=send_sem,
            recv_sem=self.recv_sems.at[slot],
            device_id={axis: target},
            device_id_type=MESH,
        )

    def start(self, condition, make):
        self.pending.append((condition, make))
        guarded(condition, lambda: make().start())

    def arrived(self, condition, slot, axis, target):
        guarded(
            condition,
            lambda: self.copy(slot, False, axis, target, self.line_sems.at[0, 0]).wait_recv(),
        )

    def spread(self, condition, slot, first, number, side, variant, after):
        for stage in range(after, self.count):
            self.start(
                condition,
                functools.partial(
                    self.copy,
                    slot,
                    first,
                    self.bits[stage],
                    1 - self.mine[stage],
                    self.bit_sems.at[number, side, variant, stage],
                ),
            )

    def line_of(self, number, side):
        line = self.z - number if side == 0 else self.z + number
        if number == 0:
            return line, None
        return line, (line >= 0 if side == 0 else line < self.size)

    def on_bits(self, number):
        for side in range(1 if number == 0 else 2):
            line, condition = self.line_of(number, side)
            for stage in range(self.count):
                for variant in range(2**stage):
                    flips = bit_flips(variant, stage, self.count)
                    slot = slot_of(line, [1 - m if f else m for m, f in zip(self.mine, flips)])
                    self.arrived(condition, slot, self.bits[stage], 1 - self.mine[stage])
                    code = sum(f << b for b, f in enumerate(flips))
                    self.spread(condition, slot, False, number, side, code, stage + 1)

    def begin(self):
        pltpu.make_async_copy(self.x_ref, self.out_ref.at[self.own], self.own_sem).start()
        z, size = self.z, self.size
        first = functools.partial(self.copy, self.own, True, "z")
        self.start(z < size - 1, functools.partial(first, z + 1, self.line_sems.at[0, 0]))
        self.start(z > 0, functools.partial(first, z - 1, self.line_sems.at[0, 1]))
        self.spread(None, self.own, True, 0, 0, 0, 0)

    def step(self, number):
        z, size = self.z, self.size
        for side in range(2):
            line, condition = self.line_of(number, side)
            slot = slot_of(line, self.mine)
            back = z - 1 if side == 0 else z + 1
            onto = z + 1 if side == 0 else z - 1
            self.arrived(condition, slot, "z", back)
            self.start(
                both(condition, onto < size if side == 0 else onto >= 0),
                functools.partial(self.copy, slot, False, "z", onto, self.line_sems.at[number, side]),
            )
            self.spread(condition, slot, False, number, side, 0, 0)

    def middle(self):
        for number in range(1, self.size):
            self.step(number)
            self.on_bits(number - 1)
        self.on_bits(self.size - 1)

    def settle(self):
        if not self.settled:
            pltpu.make_async_copy(self.x_ref, self.out_ref.at[self.own], self.own_sem).wait()
            self.settled = True

    def end(self):
        self.settle()
        for condition, make in self.pending:
            guarded(condition, lambda make=make: make().wait_send())


def gather_kernel(size, bits, *refs):
    z = lax.axis_index("z")
    mine = [lax.axis_index(bit) for bit in bits]
    greet(
        [("z", z + 1), ("z", z - 1)] + [(bit, 1 - m) for bit, m in zip(bits, mine)],
        [z < size - 1, z > 0] + [None] * len(bits),
    )
    steps = Gather(size, bits, *refs)
    steps.begin()
    steps.middle()
    steps.end()


def gather_semaphores(size, bits):
    slots = size * 2 ** len(bits)
    return [
        pltpu.SemaphoreType.DMA,
        pltpu.SemaphoreType.DMA((size, 2)),
        pltpu.SemaphoreType.DMA((size, 2, 2 ** len(bits), len(bits))),
        pltpu.SemaphoreType.DMA((slots,)),
    ]


def gather(x, size, bits, collective_id):
    slots = size * 2 ** len(bits)
    return pl.pallas_call(
        functools.partial(gather_kernel, size, bits),
        out_shape=jax.ShapeDtypeStruct((slots, *x.shape), x.dtype),
        in_specs=[pl.BlockSpec(memory_space=pl.ANY)],
        out_specs=pl.BlockSpec(memory_space=pl.ANY),
        scratch_shapes=gather_semaphores(size, bits),
        compiler_params=pltpu.CompilerParams(collective_id=collective_id, has_side_effects=True),
        cost_estimate=pl.CostEstimate(
            flops=0, transcendentals=0, bytes_accessed=slots * x.size * 100
        ),
    )(x)


class Exchange:
    def __init__(self, size, bits, block, half, gu_ref, dn_ref, gu_out, dn_out, sems):
        self.size, self.bits, self.count = size, bits, len(bits)
        self.block, self.half = block, half
        self.gu_ref, self.dn_ref, self.gu_out, self.dn_out = gu_ref, dn_ref, gu_out, dn_out
        self.own_sems, self.line_sems, self.bit_sems, self.recv_sems = sems
        self.z = lax.axis_index("z")
        self.mine = [lax.axis_index(bit) for bit in bits]
        self.own = slot_of(self.z, self.mine)
        self.others = [lax.rem(self.z + o, size) for o in range(1, size)]
        self.pending = []

    def pieces(self, target, slot):
        low = pl.multiple_of(jnp.minimum(target * self.block, self.half - self.block), LANES)
        high = pl.multiple_of(low + self.half, LANES)
        width = self.block
        return [
            (self.gu_ref.at[:, pl.ds(low, width)], self.gu_out.at[slot, :, pl.ds(0, width)]),
            (self.gu_ref.at[:, pl.ds(high, width)], self.gu_out.at[slot, :, pl.ds(width, width)]),
            (self.dn_ref.at[:, pl.ds(low, width)], self.dn_out.at[slot]),
        ]

    def line_copy(self, place, piece, slot):
        source, landing = self.pieces(self.others[place], slot)[piece]
        return pltpu.make_async_remote_copy(
            src_ref=source,
            dst_ref=landing,
            send_sem=self.line_sems.at[place, piece],
            recv_sem=self.recv_sems.at[slot, piece],
            device_id={"z": self.others[place]},
            device_id_type=MESH,
        )

    def own_copy(self, piece):
        source, landing = self.pieces(self.z, self.own)[piece]
        return pltpu.make_async_copy(source, landing, self.own_sems.at[piece])

    def bit_copy(self, slot, piece, stage, send_sem):
        ref = (self.gu_out, None, self.dn_out)[piece]
        return pltpu.make_async_remote_copy(
            src_ref=ref.at[slot],
            dst_ref=ref.at[slot],
            send_sem=send_sem,
            recv_sem=self.recv_sems.at[slot, piece],
            device_id={self.bits[stage]: 1 - self.mine[stage]},
            device_id_type=MESH,
        )

    def first_copy(self, slot, piece, stage, send_sem):
        source, landing = self.pieces(self.z, slot)[piece]
        return pltpu.make_async_remote_copy(
            src_ref=source,
            dst_ref=landing,
            send_sem=send_sem,
            recv_sem=self.recv_sems.at[slot, piece],
            device_id={self.bits[stage]: 1 - self.mine[stage]},
            device_id_type=MESH,
        )

    def spread(self, slot, number, variant, after):
        for stage in range(after, self.count):
            for piece in (0, 2):
                make = functools.partial(
                    self.bit_copy, slot, piece, stage, self.bit_sems.at[number, variant, stage, piece]
                )
                self.pending.append(make)
                make().start()

    def on_bits(self, number):
        line = lax.rem(self.z - number + self.size, self.size)
        for stage in range(self.count):
            for variant in range(2**stage):
                flips = bit_flips(variant, stage, self.count)
                slot = slot_of(line, [1 - m if f else m for m, f in zip(self.mine, flips)])
                if number == 0 and variant == 0:
                    for piece in range(3):
                        self.first_copy(slot, piece, stage, self.own_sems.at[0]).wait_recv()
                else:
                    for piece in (0, 2):
                        self.bit_copy(slot, piece, stage, self.own_sems.at[0]).wait_recv()
                self.spread(slot, number, sum(f << b for b, f in enumerate(flips)), stage + 1)

    def begin(self):
        for stage in range(self.count):
            for piece in range(3):
                make = functools.partial(
                    self.first_copy, self.own, piece, stage, self.bit_sems.at[0, 0, stage, piece]
                )
                self.pending.append(make)
                make().start()
        for piece in range(3):
            self.own_copy(piece).start()

    def send(self, offset):
        for piece in range(3):
            self.line_copy(offset - 1, piece, self.own).start()

    def sent(self, offset):
        for piece in range(3):
            self.line_copy(offset - 1, piece, self.own).wait_send()

    def step(self, offset):
        slot = slot_of(lax.rem(self.z - offset + self.size, self.size), self.mine)
        for piece in range(3):
            self.line_copy(0, piece, slot).wait_recv()
        self.spread(slot, offset, 0, 0)

    def end(self):
        for piece in range(3):
            self.own_copy(piece).wait()
        for make in self.pending:
            make().wait_send()


class Fold:
    def __init__(self, size, bits, order, p_ref, own_buf, sums, stage_in, stage_out, own_sems, send_sems, recv_sems):
        self.size, self.bits, self.count, self.order = size, bits, len(bits), order
        self.last = self.count - 1
        self.p_ref, self.own_buf, self.sums = p_ref, own_buf, sums
        self.stage_in, self.stage_out = stage_in, stage_out
        self.own_sems, self.send_sems, self.recv_sems = own_sems, send_sems, recv_sems
        self.z = lax.axis_index("z")
        self.mine = [lax.axis_index(bit) for bit in bits]

    def line(self, place):
        return lax.rem(self.z + self.order[place], self.size)

    def index(self, place, stage, variant):
        return place * (2**self.count - 1) + 2**stage - 1 + variant

    def slot(self, place, variant, flip):
        flips = [(variant >> b) & 1 for b in range(self.last)] + [flip]
        return slot_of(self.line(place), [1 - m if f else m for m, f in zip(self.mine, flips)])

    def copy(self, place, stage, variant):
        index = self.index(place, stage, variant)
        if stage == self.last:
            source = self.p_ref.at[self.slot(place, variant, 1)]
        else:
            source = self.stage_out.at[place * (2**self.last - 1) + 2**stage - 1 + variant]
        return pltpu.make_async_remote_copy(
            src_ref=source,
            dst_ref=self.stage_in.at[index],
            send_sem=self.send_sems.at[index],
            recv_sem=self.recv_sems.at[index],
            device_id={self.bits[stage]: 1 - self.mine[stage]},
            device_id_type=MESH,
        )

    def own_copy(self, place, variant):
        number = place * 2**self.last + variant
        return pltpu.make_async_copy(
            self.p_ref.at[self.slot(place, variant, 0)], self.own_buf.at[number], self.own_sems.at[number]
        )

    def begin(self, places=None):
        for place in range(self.size) if places is None else places:
            for variant in reversed(range(2**self.last)):
                self.copy(place, self.last, variant).start()
                self.own_copy(place, variant).start()

    def stage(self, place, stage, done=None):
        for variant in reversed(range(2**stage)):
            if stage == self.last:
                self.own_copy(place, variant).wait()
                held = self.own_buf[place * 2**self.last + variant].astype(F32)
            else:
                held = self.sums[place * (2**self.last - 1) + 2**stage - 1 + variant]
            self.copy(place, stage, variant).wait_recv()
            total = held + self.stage_in[self.index(place, stage, variant)].astype(F32)
            if stage == 0:
                done(place, total)
                continue
            lower = variant & (2 ** (stage - 1) - 1)
            number = place * (2**self.last - 1) + 2 ** (stage - 1) - 1 + lower
            if variant >> (stage - 1):
                self.stage_out[number] = total.astype(LOW)
                self.copy(place, stage - 1, lower).start()
            else:
                self.sums[number] = total

    def end(self):
        for place in range(self.size):
            for stage in range(self.count):
                for variant in range(2**stage):
                    self.copy(place, stage, variant).wait_send()


def fold_scratch(size, bits, rows, columns):
    count = len(bits)
    inner, lower = size * (2**count - 1), size * (2 ** (count - 1) - 1)
    return [
        pltpu.VMEM((size * 2 ** (count - 1), rows, columns), LOW),
        pltpu.VMEM((max(lower, 1), rows, columns) if lower else (1, 8, LANES), F32),
        pltpu.VMEM((inner, rows, columns), LOW),
        pltpu.VMEM((max(lower, 1), rows, columns) if lower else (1, 16, LANES), LOW),
        pltpu.SemaphoreType.DMA((size * 2 ** (count - 1),)),
        pltpu.SemaphoreType.DMA((inner,)),
        pltpu.SemaphoreType.DMA((inner,)),
    ]


class Scatter:
    def __init__(self, size, bits, p_ref, out_ref, line_out, line_in, line_send, line_recv, *fold):
        order = list(range(1, size)) + [0]
        self.fold = Fold(size, bits, order, p_ref, *fold)
        self.size, self.out_ref = size, out_ref
        self.line_out, self.line_in, self.line_send, self.line_recv = line_out, line_in, line_send, line_recv

    def line_copy(self, place):
        return pltpu.make_async_remote_copy(
            src_ref=self.line_out.at[place],
            dst_ref=self.line_in.at[place],
            send_sem=self.line_send.at[place],
            recv_sem=self.line_recv.at[place],
            device_id={"z": self.fold.line(place)},
            device_id_type=MESH,
        )

    def done(self, place, total):
        if place < self.size - 1:
            self.line_out[place] = total.astype(LOW)
            self.line_copy(place).start()
        else:
            self.out_ref[...] = total

    def begin(self):
        self.fold.begin()

    def place(self, place):
        for stage in reversed(range(self.fold.count)):
            self.fold.stage(place, stage, self.done)

    def finish(self):
        for place in range(self.size - 1):
            self.line_copy(place).wait_recv()
            self.out_ref[...] += self.line_in[place].astype(F32)

    def end(self):
        self.fold.end()
        for place in range(self.size - 1):
            self.line_copy(place).wait_send()


def scatter_scratch(size, bits, rows, columns):
    return [
        pltpu.VMEM((size - 1, rows, columns), LOW),
        pltpu.VMEM((size - 1, rows, columns), LOW),
        pltpu.SemaphoreType.DMA((size - 1,)),
        pltpu.SemaphoreType.DMA((size - 1,)),
        *fold_scratch(size, bits, rows, columns),
    ]


SCATTER_REFS = 11


class Total:
    def __init__(self, size, bits, x_ref, out_ref, held, landed, send_sems, recv_sems):
        self.size, self.bits, self.count = size, bits, len(bits)
        self.x_ref, self.out_ref, self.held, self.landed = x_ref, out_ref, held, landed
        self.send_sems, self.recv_sems = send_sems, recv_sems
        self.z = lax.axis_index("z")
        self.others = [lax.rem(self.z + o, size) for o in range(1, size)]

    def copy(self, number):
        if number < self.count:
            axis = self.bits[number]
            source, target = self.held.at[number], {axis: 1 - lax.axis_index(axis)}
        else:
            source, target = self.held.at[self.count], {"z": self.others[number - self.count]}
        return pltpu.make_async_remote_copy(
            src_ref=source,
            dst_ref=self.landed.at[number],
            send_sem=self.send_sems.at[number],
            recv_sem=self.recv_sems.at[number],
            device_id=target,
            device_id_type=MESH,
        )

    def begin(self):
        self.held[0] = self.x_ref[...]
        self.copy(0).start()

    def pair(self, number):
        self.copy(number).wait_recv()
        self.held[number + 1] = self.held[number] + self.landed[number]
        if number + 1 < self.count:
            self.copy(number + 1).start()
        else:
            for place in range(self.size - 1):
                self.copy(self.count + place).start()

    def finish(self):
        for place in range(self.size - 1):
            self.copy(self.count + place).wait_recv()
        total = jnp.zeros(self.out_ref.shape, self.out_ref.dtype)
        for line in range(self.size):
            offset = lax.rem(line - self.z + self.size, self.size)
            part = self.held[self.count]
            for o in range(1, self.size):
                part = jnp.where(offset == o, self.landed[self.count + self.size - o - 1], part)
            total = total + part
        self.out_ref[...] = total

    def end(self):
        for number in range(self.count + self.size - 1):
            self.copy(number).wait_send()


def greet_all(size, axes):
    z = lax.axis_index("z")
    greet(
        [("z", lax.rem(z + o, size)) for o in range(1, size)]
        + [(axis, 1 - lax.axis_index(axis)) for axis in axes],
        [None] * (size - 1 + len(axes)),
    )


def in_groups(refs, sizes):
    groups, at = [], 0
    for number in sizes:
        groups.append(refs[at : at + number])
        at += number
    return groups


def comm_params(collective_id):
    return pltpu.CompilerParams(
        collective_id=collective_id, has_side_effects=True, vmem_limit_bytes=56 * 2**20
    )


def at_microseconds(time):
    return pl.CostEstimate(flops=0, transcendentals=0, bytes_accessed=time * 3500000)


def last_kernel(size, bits, p_ref, x_ref, out_ref, sum_ref, *refs):
    greet_all(size, ("t", *bits))
    given, rest = in_groups(refs, [SCATTER_REFS, 4])
    small = Total(size, ("t", *bits), x_ref, sum_ref, *rest)
    steps = Scatter(size, bits, p_ref, out_ref, *given)
    small.begin()
    steps.begin()
    for place in range(size):
        steps.place(place)
        if place <= len(bits):
            small.pair(place)
    for number in range(size, len(bits) + 1):
        small.pair(number)
    steps.finish()
    small.finish()
    steps.end()
    small.end()


def last(partial, x, size, bits, collective_id):
    slots, rows, columns = partial.shape
    number = len(bits) + 1
    return pl.pallas_call(
        functools.partial(last_kernel, size, bits),
        out_shape=(jax.ShapeDtypeStruct((rows, columns), F32), jax.ShapeDtypeStruct(x.shape, F32)),
        in_specs=[pl.BlockSpec(memory_space=pl.ANY), pl.BlockSpec(memory_space=pltpu.VMEM)],
        out_specs=[pl.BlockSpec(memory_space=pltpu.VMEM)] * 2,
        scratch_shapes=[
            *scatter_scratch(size, bits, rows, columns),
            pltpu.VMEM((number + 1, *x.shape), F32),
            pltpu.VMEM((number + size - 1, *x.shape), F32),
            pltpu.SemaphoreType.DMA((number + size - 1,)),
            pltpu.SemaphoreType.DMA((number + size - 1,)),
        ],
        compiler_params=comm_params(collective_id),
        cost_estimate=at_microseconds(60),
    )(partial, x)


def back_kernel(size, bits, branches, *refs):
    p_refs, (gu_ref, dn_ref), outs, (folded,), refs = in_groups(
        refs, [branches, 2, branches, 1, len(refs)]
    )
    greet_all(size, ("t", *bits))
    *scatters, gu_scratch, dn_scratch, (gu_done, dn_done, done_sems) = in_groups(
        refs, [SCATTER_REFS] * branches + [7, 7, 3]
    )
    scatters = [
        Scatter(size, ("t",), p, out, *scratch) for p, out, scratch in zip(p_refs, outs, scatters)
    ]
    order = list(range(size))
    gu = Fold(size, bits, order, gu_ref, *gu_scratch)
    dn = Fold(size, bits, order, dn_ref, *dn_scratch)
    width, narrow = gu_ref.shape[2], dn_ref.shape[2]

    def out_copy(number, place, line):
        source = (gu_done, dn_done)[number].at[place]
        low, count = ((0, width), (width, narrow))[number]
        return pltpu.make_async_copy(
            source, folded.at[line, :, pl.ds(low, count)], done_sems.at[number, place]
        )

    def done(number):
        def keep(place, total):
            (gu_done, dn_done)[number][place] = total.astype(LOW)
            out_copy(number, place, gu.line(place)).start()

        return keep

    for steps in scatters:
        steps.begin()
    gu.begin()
    dn.begin()
    for place in range(size):
        for stage in reversed(range(1, len(bits))):
            gu.stage(place, stage)
            dn.stage(place, stage)
        for steps in scatters:
            steps.place(place)
    for steps in scatters:
        steps.finish()
    for place in range(size):
        gu.stage(place, 0, done(0))
        dn.stage(place, 0, done(1))
    for place in range(size):
        for number in range(2):
            out_copy(number, place, gu.line(place)).wait()
    for steps in (*scatters, gu, dn):
        steps.end()


def back(partials, gu, dn, size, bits, collective_id):
    _, rows, columns = partials[0].shape
    slots, few, width = gu.shape
    narrow = dn.shape[2]
    branches = len(partials)
    out = pl.pallas_call(
        functools.partial(back_kernel, size, bits, branches),
        out_shape=(
            *([jax.ShapeDtypeStruct((rows, columns), F32)] * branches),
            jax.ShapeDtypeStruct((size, few, width + narrow), LOW),
        ),
        in_specs=[pl.BlockSpec(memory_space=pl.ANY)] * (branches + 2),
        out_specs=[pl.BlockSpec(memory_space=pltpu.VMEM)] * branches + [pl.BlockSpec(memory_space=pl.ANY)],
        scratch_shapes=[
            *(scatter_scratch(size, ("t",), rows, columns) * branches),
            *fold_scratch(size, bits, few, width),
            *fold_scratch(size, bits, few, narrow),
            pltpu.VMEM((size, few, width), LOW),
            pltpu.VMEM((size, few, narrow), LOW),
            pltpu.SemaphoreType.DMA((2, size)),
        ],
        compiler_params=comm_params(collective_id),
        cost_estimate=at_microseconds(80),
    )(*partials, gu, dn)
    return out[:branches], out[branches]


class Attend:
    def __init__(self, rows_ref, gain_ref, bias_ref, cos_ref, sin_ref, mask_ref, w_ref, outs, scratch, width, epsilon=1e-06):
        self.gain_ref, self.bias_ref, self.w_ref = gain_ref, bias_ref, w_ref
        self.cos_ref, self.sin_ref, self.mask_ref = cos_ref, sin_ref, mask_ref
        self.state_ref, self.middle_ref, self.xa_ref, self.q_ref, self.k_ref, self.v_ref, self.lse_ref, self.o_ref = outs
        self.send_buf, self.land_buf, self.send_sems, self.recv_sems = scratch
        self.rows_ref = rows_ref
        self.t = lax.axis_index("t")
        self.slots, self.few = w_ref.shape[0], w_ref.shape[1]
        self.model = self.slots * self.few
        self.count = rows_ref.shape[0]
        self.q_width = self.q_ref.shape[1]
        self.width = width
        self.epsilon = epsilon

    def normed(self, rows, gain_ref):
        factor = lax.rsqrt(jnp.mean(rows * rows, axis=-1, keepdims=True) + self.epsilon)
        return (rows * factor * gain_ref[...]).astype(LOW)

    def xa_copy(self):
        return pltpu.make_async_remote_copy(
            src_ref=self.xa_ref.at[self.t],
            dst_ref=self.xa_ref.at[self.t],
            send_sem=self.send_sems.at[0],
            recv_sem=self.recv_sems.at[0],
            device_id={"t": 1 - self.t},
            device_id_type=MESH,
        )

    def xa_landing(self):
        return pltpu.make_async_remote_copy(
            src_ref=self.xa_ref.at[1 - self.t],
            dst_ref=self.xa_ref.at[1 - self.t],
            send_sem=self.send_sems.at[0],
            recv_sem=self.recv_sems.at[0],
            device_id={"t": 1 - self.t},
            device_id_type=MESH,
        )

    def half_copy(self):
        return pltpu.make_async_remote_copy(
            src_ref=self.send_buf,
            dst_ref=self.land_buf,
            send_sem=self.send_sems.at[1],
            recv_sem=self.recv_sems.at[1],
            device_id={"t": 1 - self.t},
            device_id_type=MESH,
        )

    def begin(self, state):
        self.state_ref[...] = state
        self.xa_ref[self.t] = self.normed(state, self.gain_ref)
        self.xa_copy().start()

    def columns(self, low, count):
        weight = self.w_ref[:, :, low : low + count].reshape(self.model, count)
        xa = self.xa_ref[...].reshape(2 * self.count, self.model)
        return jnp.dot(xa, weight, preferred_element_type=F32) + self.bias_ref[:, low : low + count]

    def rope(self, values):
        return (values * self.cos_ref[...] + pltpu.roll(values, HD // 2, 1) * self.sin_ref[...]).astype(LOW)

    def keys(self):
        self.xa_landing().wait_recv()
        both_kv = self.columns(self.q_width, 2 * HD)
        self.k_ref[...] = self.rope(both_kv[:, :HD])
        self.v_ref[...] = both_kv[:, HD:].astype(LOW)

    def heads(self, first):
        lin = self.columns(first * HD, 2 * HD)
        for number in range(2):
            head = first + number
            low = head * HD
            query = self.rope(lin[:, number * HD : (number + 1) * HD])
            self.q_ref[:, low : low + HD] = query
            raw = lax.dot_general(
                query, self.k_ref[...], (((1,), (1,)), ((), ())), preferred_element_type=F32
            )
            scores = jnp.where(self.mask_ref[...] > 0, raw * (1.0 / math.sqrt(HD)), -1e30)
            top = jnp.max(scores, axis=-1, keepdims=True)
            expo = jnp.exp(scores - top)
            whole = jnp.sum(expo, axis=-1, keepdims=True)
            probs = (expo / whole).astype(LOW)
            self.lse_ref[head] = top + jnp.log(whole)
            out = jnp.dot(probs, self.v_ref[...], preferred_element_type=F32).astype(LOW)
            self.o_ref[0, :, low : low + HD] = out[: self.count]
            self.o_ref[1, :, low : low + HD] = out[self.count :]

    def projected(self, half, step):
        left = self.o_ref[half]
        for low in range(0, self.slots, step):
            weight = self.w_ref[low : low + step, :, self.width :].reshape(step * self.few, self.q_width)
            yield low * self.few, lax.dot_general(
                left, weight, (((1,), (1,)), ((), ())), preferred_element_type=F32
            )

    def other_half(self):
        for low, part in self.projected(1 - self.t, self.slots // 4):
            self.send_buf[:, low : low + part.shape[1]] = part.astype(LOW)
        self.half_copy().start()

    def own_half(self):
        for low, part in self.projected(self.t, self.slots // 4):
            where = slice(low, low + part.shape[1])
            self.middle_ref[:, where] = self.state_ref[:, where] + part

    def finish(self, gain_ref, xf_ref):
        self.half_copy().wait_recv()
        middle = self.middle_ref[...] + self.land_buf[...].astype(F32)
        self.middle_ref[...] = middle
        xf_ref[...] = self.normed(middle, gain_ref)

    def end(self):
        self.xa_copy().wait_send()
        self.half_copy().wait_send()


def front_kernel(size, bits, block, half, layer, width, *refs):
    first = layer == 0
    inputs, outs, refs = in_groups(refs, [11, 13 if first else 12, len(refs)])
    (x_ref, more_ref, ga_ref, gf_ref, bias_ref, cos_ref, sin_ref, mask_ref, at_ref, gu_ref, dn_ref) = inputs
    xf_out, gu_out, dn_out, at_out = outs[8:12]
    (w_ref, xf_ref, at_sem), pair, at_sems, feed_sems, rows_sems, rest = in_groups(
        refs, [3, 4, 4, 4, 4, len(refs)]
    )
    greet_all(size, ("t", *bits))
    work = Attend(
        x_ref, ga_ref, bias_ref, cos_ref, sin_ref, mask_ref, w_ref, outs[:8], pair, width
    )
    attention = Gather(size, bits, at_ref, w_ref, *at_sems)
    feed = Exchange(
        size, bits, block, half, gu_ref.at[layer], dn_ref.at[layer], gu_out, dn_out, feed_sems
    )
    rows = Gather(size, ("t",), xf_ref, xf_out, *rows_sems)
    kept = pltpu.make_async_copy(w_ref, at_out, at_sem)
    if first:
        side = Gather(size, ("t",), more_ref, outs[12], *rest)
        attention.begin()
        side.begin()
        feed.begin()
        work.begin(x_ref[...].astype(F32))
        attention.step(1)
        side.step(1)
        attention.step(2)
        attention.on_bits(0)
        side.on_bits(0)
        side.step(2)
        feed.send(1)
        attention.step(3)
        attention.on_bits(1)
        side.on_bits(1)
        side.step(3)
        feed.on_bits(0)
        attention.on_bits(2)
        feed.sent(1)
        feed.send(3)
        feed.step(1)
        attention.on_bits(3)
        attention.settle()
        work.keys()
        work.heads(0)
        side.on_bits(2)
        side.on_bits(3)
    else:
        total_ref, *rest = rest
        side = Scatter(size, ("t",), more_ref, total_ref, *rest)
        attention.begin()
        side.begin()
        feed.begin()
        side.place(0)
        attention.step(1)
        side.place(1)
        attention.step(2)
        attention.on_bits(0)
        side.place(2)
        attention.step(3)
        attention.on_bits(1)
        side.place(3)
        feed.send(1)
        attention.on_bits(2)
        attention.on_bits(3)
        attention.settle()
        side.finish()
        work.begin(x_ref[...] + total_ref[...])
        feed.on_bits(0)
        feed.sent(1)
        feed.send(3)
        feed.step(1)
        work.keys()
        work.heads(0)
    kept.start()
    feed.sent(3)
    feed.send(2)
    feed.step(3)
    feed.on_bits(1)
    work.heads(2)
    work.heads(4)
    work.other_half()
    work.own_half()
    work.finish(gf_ref, xf_ref)
    rows.begin()
    rows.step(1)
    rows.on_bits(0)
    rows.step(2)
    feed.sent(2)
    feed.step(2)
    rows.on_bits(1)
    feed.on_bits(3)
    rows.step(3)
    rows.on_bits(2)
    feed.on_bits(2)
    rows.on_bits(3)
    kept.wait()
    for steps in (attention, side, feed, work, rows):
        steps.end()


def front(x, more, gains, bias, tables, at, gu, dn, layer, size, bits, block, width, collective_id):
    slots = size * 2 ** len(bits)
    count, model = x.shape
    few, half = dn.shape[1:]
    length = 2 * count
    q_width = at.shape[1] - width
    first = layer == 0
    held, far = pl.BlockSpec(memory_space=pltpu.VMEM), pl.BlockSpec(memory_space=pl.ANY)
    shape = jax.ShapeDtypeStruct
    more_scratch = (
        gather_semaphores(size, ("t",))
        if first
        else [pltpu.VMEM((count, model), F32), *scatter_scratch(size, ("t",), count, model)]
    )
    return pl.pallas_call(
        functools.partial(front_kernel, size, bits, block, half, layer, width),
        out_shape=(
            shape((count, model), F32),
            shape((count, model), F32),
            shape((2, count, model), LOW),
            shape((length, q_width), LOW),
            shape((length, HD), LOW),
            shape((length, HD), LOW),
            shape((q_width // HD, length, 1), F32),
            shape((2, count, q_width), LOW),
            shape((2 * size, count, model), LOW),
            shape((slots, few, 2 * block), LOW),
            shape((slots, few, block), LOW),
            shape((slots, few, at.shape[1]), LOW),
            *([shape((2 * size, count, model), LOW)] if first else []),
        ),
        in_specs=[held, far] + [held] * 6 + [far] * 3,
        out_specs=[held] * 8 + [far] * (5 if first else 4),
        scratch_shapes=[
            pltpu.VMEM((slots, few, at.shape[1]), LOW),
            pltpu.VMEM((count, model), LOW),
            pltpu.SemaphoreType.DMA,
            pltpu.VMEM((count, model), LOW),
            pltpu.VMEM((count, model), LOW),
            pltpu.SemaphoreType.DMA((2,)),
            pltpu.SemaphoreType.DMA((2,)),
            *gather_semaphores(size, bits),
            pltpu.SemaphoreType.DMA((3,)),
            pltpu.SemaphoreType.DMA((size - 1, 3)),
            pltpu.SemaphoreType.DMA((size, 2 ** len(bits), len(bits), 3)),
            pltpu.SemaphoreType.DMA((slots, 3)),
            *gather_semaphores(size, ("t",)),
            *more_scratch,
        ],
        compiler_params=comm_params(collective_id),
        cost_estimate=at_microseconds(150),
    )(x, more, *gains, bias, *tables, at, gu, dn)


def spread_group(rows):
    return gather(rows, LINE, ("t",), 1).reshape(-1, rows.shape[1])


def in_slots(partial, slots):
    return partial.reshape(slots, -1, partial.shape[1])


def block_width(half):
    return -(-half // (LINE * LANES)) * LANES


def block_start(line, block, half):
    return min(line * block, half - block)


def tie(value, *others):
    return lax.optimization_barrier((value, *others))


def from_blocks(blocks, parts, half):
    block = blocks.shape[2] // 3
    pieces = []
    for part in parts:
        for line in range(LINE):
            skip = line * block - block_start(line, block, half)
            pieces.append(blocks[line, :, part * block + skip : (part + 1) * block])
    return jnp.concatenate(pieces, axis=1).astype(F32)


def local(
    bits, tokens, cotangent, doc_lengths, norm_attn, norm_ffn, w_qkv, b_qkv, w_out, w_gateup, w_down
):
    dp = ("z", *bits)
    tensor_size = lax.axis_size("t")
    count = tokens.shape[0]
    length = count * tensor_size
    layers = w_qkv.shape[0]
    kv_local = KV // tensor_size
    groups = H // KV
    q_width = kv_local * groups * HD
    kv_width = kv_local * HD
    qkv_width = w_qkv.shape[2]
    rows = w_qkv.shape[1]
    half = w_down.shape[2]
    block = block_width(half)
    scale = 1.0 / math.sqrt(HD)
    positions, allowed = doc_layout(doc_lengths[0], length)
    cosine, sine = rope_tables(positions, HD)
    turned = jnp.where(jnp.arange(HD) < HD // 2, -sine, sine)
    tables = (cosine, turned, allowed.astype(F32))
    cos_q = cosine[:, None, None, :]
    sin_q = sine[:, None, None, :]
    cos_k = cosine[:, None, :]
    sin_k = sine[:, None, :]
    gain_attn = norm_attn.astype(F32)
    gain_ffn = norm_ffn.astype(F32)
    bias_all = b_qkv.astype(F32)
    line = lax.axis_index("z")
    valid = jnp.arange(block) >= line * block - jnp.minimum(line * block, half - block)
    saved = []
    for layer in range(layers):
        flat = jnp.concatenate([w_qkv[layer], w_out[layer]], axis=1)
        start, more = (tokens, cotangent) if layer == 0 else (middle, in_slots(partial, 2 * LINE))
        gains = (gain_attn[layer : layer + 1], gain_ffn[layer : layer + 1])
        out = front(
            start, more, gains, bias_all[layer : layer + 1], tables, flat, w_gateup, w_down,
            layer, LINE, bits, block, qkv_width, 8 + layer,
        )
        if layer == 0:
            gm_all = out[12].reshape(-1, cotangent.shape[1])
        (state, middle, xa_all, query, key, value, log_total, attended) = out[:8]
        xf_all, gu_w, down_w, both_w = (item.reshape(-1, item.shape[2]) for item in out[8:12])
        xa_all = xa_all.reshape(length, -1)
        attended = attended.reshape(length, -1)
        query = query.reshape(length, kv_local, groups, HD)
        key = key.reshape(length, kv_local, HD)
        value = value.reshape(length, kv_local, HD)
        log_total = log_total[None]
        gate_up = jnp.dot(xf_all, gu_w, preferred_element_type=F32)
        gate = gate_up[:, :block]
        up = gate_up[:, block:]
        act = jnp.where(valid, jax.nn.silu(gate) * up, 0.0).astype(LOW)
        partial = contract_last(act, down_w, LOW)
        saved.append(
            (state, xa_all, query, key, value, log_total, attended)
            + (middle, xf_all, gate, up, act, gu_w, down_w, both_w)
        )
    grad = cotangent.astype(F32)
    grads_attn, grads_bias, grads_ga, grads_gf = ([] for _ in range(4))
    waiting, branches = None, [in_slots(partial, 2 * LINE)]
    grads_blocks = []
    for layer in reversed(range(layers)):
        (state_in, xa_all, query, key, value, log_total, attended) = saved[layer][:7]
        (middle, xf_all, gate, up, act, gu_w, down_w, both_w) = saved[layer][7:]
        factor_a, factor_f = rms_factor(state_in), rms_factor(middle)
        qkv_w, out_w = both_w[:, :qkv_width], both_w[:, qkv_width:]
        if waiting is not None:
            gm_all = spread_group(grad.astype(LOW))
        d_down = contract_first(gm_all, act, LOW)
        d_act = jnp.dot(gm_all, down_w, preferred_element_type=F32)
        sig = jax.nn.sigmoid(gate)
        d_gate = d_act * up * sig * (1.0 + gate * (1.0 - sig))
        d_up = d_act * gate * sig
        d_gu = jnp.concatenate(
            [jnp.where(valid, d_gate, 0.0), jnp.where(valid, d_up, 0.0)], axis=1
        ).astype(LOW)
        d_gateup = contract_first(xf_all, d_gu, LOW)
        branches.insert(0, in_slots(contract_last(d_gu, gu_w, LOW), 2 * LINE))
        slots = in_slots(d_gateup, d_gateup.shape[0] // rows), in_slots(d_down, d_down.shape[0] // rows)
        (d_xf, *others), folded = back(branches, *slots, LINE, bits, 6 + layer)
        branches = []
        if others:
            output = (middle + others[0]).astype(LOW)
        waiting = lax.all_to_all(folded, "z", 0, 0, tiled=True)
        d_mid, part_f = norm_back(d_xf, middle, factor_f, gain_ffn[layer])
        grad = grad + d_mid
        ga_all = spread_pair(grad.astype(LOW))
        d_att = jnp.dot(ga_all, out_w, preferred_element_type=F32).astype(LOW)
        raw = jnp.einsum("qkgd,pkd->kgqp", query, key, preferred_element_type=F32)
        scores = jnp.where(allowed, raw * scale, -1e30)
        probs = jnp.exp(scores - log_total)
        d_att4 = d_att.reshape(length, kv_local, groups, HD)
        d_probs = jnp.einsum("qkgd,pkd->kgqp", d_att4, value, preferred_element_type=F32)
        centre = jnp.sum(probs * d_probs, axis=-1, keepdims=True)
        d_raw = (probs * (d_probs - centre) * scale).astype(LOW)
        d_query = jnp.einsum("kgqp,pkd->qkgd", d_raw, key, preferred_element_type=F32)
        d_key = jnp.einsum("kgqp,qkgd->pkd", d_raw, query, preferred_element_type=F32)
        d_value = jnp.einsum(
            "kgqp,qkgd->pkd", probs.astype(LOW), d_att4, preferred_element_type=F32
        )
        d_query = d_query * cos_q + rotate_back(d_query * sin_q)
        d_key = d_key * cos_k + rotate_back(d_key * sin_k)
        d_lin = jnp.concatenate(
            [
                d_query.reshape(length, q_width),
                d_key.reshape(length, kv_width),
                d_value.reshape(length, kv_width),
            ],
            axis=1,
        )
        grads_bias.append(jnp.sum(d_lin, axis=0))
        d_lin_low = d_lin.astype(LOW)
        d_xa = sum_pair(contract_last(d_lin_low, qkv_w))
        d_in, part_a = norm_back(d_xa, state_in, factor_a, gain_attn[layer])
        grad = grad + d_in
        if layer > 0:
            grad, waiting = tie(grad, waiting)
        grads_blocks.append(waiting)
        d_both = jnp.concatenate(
            [contract_first(xa_all, d_lin_low, LOW), contract_first(ga_all, attended, LOW)], axis=1
        )
        if layer == 0:
            d_both = in_slots(d_both, d_both.shape[0] // rows)
        else:
            grads_attn.append(
                lax.psum_scatter(d_both, dp, scatter_dimension=0, tiled=True).astype(F32)
            )
        grads_ga.append(part_a)
        grads_gf.append(part_f)

    def ordered(items):
        return jnp.stack(items[::-1], axis=0)

    side = lax.axis_index("t")
    bias = ordered(grads_bias)
    spread = jnp.where(
        (jnp.arange(tensor_size) == side)[:, None, None], bias[None], jnp.zeros_like(bias)[None]
    )
    small = (ordered(grads_ga), ordered(grads_gf), spread)
    flat = jnp.concatenate([item.reshape(-1, LANES) for item in small], axis=0)
    last_attn, flat = last(d_both, flat, LINE, bits, 4)
    grads_attn.append(last_attn)
    full_ga, full_gf, full_bias = (
        part.reshape(item.shape)
        for part, item in zip(
            jnp.split(flat, [small[0].size // LANES, 2 * small[0].size // LANES], axis=0), small
        )
    )
    both = ordered(grads_attn)
    return (
        output,
        grad,
        full_ga,
        full_gf,
        both[:, :, :qkv_width],
        take(full_bias, side, 0),
        both[:, :, qkv_width:],
        ordered([from_blocks(blocks, (0, 1), half) for blocks in grads_blocks]),
        ordered([from_blocks(blocks, (2,), half) for blocks in grads_blocks]),
    )


def solution(mesh):
    dp_size, tensor_size = mesh.devices.shape
    rest = dp_size // LINE
    bits = tuple(f"r{number}" for number in range(rest.bit_length() - 1))
    shape = (LINE, *([2] * len(bits)), tensor_size)
    fine = Mesh(mesh.devices.reshape(shape), ("z", *bits, "t"))
    dp = ("z", *bits)
    rows = P((*dp, "t"), None)
    weight = P(None, dp, "t")

    def step(*args):
        return local(bits, *args)

    return jax.shard_map(
        step,
        mesh=fine,
        in_specs=(rows, rows, P(dp, None), P(), P(), weight, P(None, "t"), weight, weight, weight),
        out_specs=(rows, rows, P(), P(), weight, P(None, "t"), weight, weight, weight),
        check_vma=False,
    )
```

```python
import functools
import math

import jax
import jax.numpy as jnp
from jax import lax
from jax.experimental import pallas as pl
from jax.experimental.pallas import tpu as pltpu
from jax.sharding import Mesh
from jax.sharding import PartitionSpec as P

HD = 128
LINE = 4
LANES = 128
LOW = jnp.bfloat16
F32 = jnp.float32
MESH = pl.DeviceIdType.MESH


def doc_layout(lens, count):
    rows = jnp.arange(count, dtype=jnp.int32)
    doc = jnp.zeros((count,), jnp.int32)
    start = jnp.zeros((count,), jnp.int32)
    bound = jnp.int32(0)
    for number in range(lens.shape[0]):
        bound = bound + lens[number]
        after = (rows >= bound).astype(jnp.int32)
        doc = doc + after
        start = start + after * lens[number]
    positions = rows - start
    allowed = (doc[:, None] == doc[None, :]) & (rows[:, None] >= rows[None, :])
    return (positions, allowed)


def rope_tables(positions, width):
    index = jnp.arange(width // 2, dtype=F32)
    freq = jnp.exp(-(2.0 * index / width) * math.log(1000000.0))
    angle = positions.astype(F32)[:, None] * freq[None, :]
    return (
        jnp.concatenate([jnp.cos(angle)] * 2, axis=1),
        jnp.concatenate([jnp.sin(angle)] * 2, axis=1),
    )


def contract_last(left, right, out=F32):
    return lax.dot_general(left, right, (((1,), (1,)), ((), ())), preferred_element_type=out)


def contract_first(left, right, out=F32):
    return lax.dot_general(left, right, (((0,), (0,)), ((), ())), preferred_element_type=out)


def take(array, index, axis):
    return lax.dynamic_index_in_dim(array, index, axis, keepdims=False)


def greet(axes_targets, conditions):
    barrier = pltpu.get_barrier_semaphore()
    for (axis, target), condition in zip(axes_targets, conditions):
        def signal(axis=axis, target=target):
            pl.semaphore_signal(barrier, inc=1, device_id={axis: target}, device_id_type=MESH)
        if condition is None:
            signal()
        else:
            pl.when(condition)(signal)
    amount = sum(1 if c is None else c.astype(jnp.int32) for c in conditions)
    pl.semaphore_wait(barrier, amount)


def slot_of(line, values):
    slot = line
    for value in values:
        slot = slot * 2 + value
    return slot


def both(*conditions):
    given = [c for c in conditions if c is not None]
    return functools.reduce(jnp.logical_and, given) if given else None


def guarded(condition, action):
    if condition is None:
        action()
    else:
        pl.when(condition)(action)


def bit_flips(variant, stage, count):
    return [(variant >> b) & 1 for b in range(stage)] + [1] + [0] * (count - stage - 1)


class Gather:
    def __init__(self, size, bits, x_ref, out_ref, own_sem, line_sems, bit_sems, recv_sems):
        self.size, self.bits, self.count = size, bits, len(bits)
        self.x_ref, self.out_ref, self.own_sem = x_ref, out_ref, own_sem
        self.line_sems, self.bit_sems, self.recv_sems = line_sems, bit_sems, recv_sems
        self.z = lax.axis_index("z")
        self.mine = [lax.axis_index(bit) for bit in bits]
        self.own = slot_of(self.z, self.mine)
        self.pending, self.settled = [], False

    def copy(self, slot, first, axis, target, send_sem):
        return pltpu.make_async_remote_copy(
            src_ref=self.x_ref if first else self.out_ref.at[slot],
            dst_ref=self.out_ref.at[slot],
            send_sem=send_sem,
            recv_sem=self.recv_sems.at[slot],
            device_id={axis: target},
            device_id_type=MESH,
        )

    def start(self, condition, make):
        self.pending.append((condition, make))
        guarded(condition, lambda: make().start())

    def arrived(self, condition, slot, axis, target):
        guarded(
            condition,
            lambda: self.copy(slot, False, axis, target, self.line_sems.at[0, 0]).wait_recv(),
        )

    def spread(self, condition, slot, first, number, side, variant, after):
        for stage in range(after, self.count):
            self.start(
                condition,
                functools.partial(
                    self.copy,
                    slot,
                    first,
                    self.bits[stage],
                    1 - self.mine[stage],
                    self.bit_sems.at[number, side, variant, stage],
                ),
            )

    def line_of(self, number, side):
        line = self.z - number if side == 0 else self.z + number
        if number == 0:
            return line, None
        return line, (line >= 0 if side == 0 else line < self.size)

    def on_bits(self, number):
        for side in range(1 if number == 0 else 2):
            line, condition = self.line_of(number, side)
            for stage in range(self.count):
                for variant in range(2**stage):
                    flips = bit_flips(variant, stage, self.count)
                    slot = slot_of(line, [1 - m if f else m for m, f in zip(self.mine, flips)])
                    self.arrived(condition, slot, self.bits[stage], 1 - self.mine[stage])
                    code = sum(f << b for b, f in enumerate(flips))
                    self.spread(condition, slot, False, number, side, code, stage + 1)

    def begin(self):
        pltpu.make_async_copy(self.x_ref, self.out_ref.at[self.own], self.own_sem).start()
        z, size = self.z, self.size
        first = functools.partial(self.copy, self.own, True, "z")
        self.start(z < size - 1, functools.partial(first, z + 1, self.line_sems.at[0, 0]))
        self.start(z > 0, functools.partial(first, z - 1, self.line_sems.at[0, 1]))
        self.spread(None, self.own, True, 0, 0, 0, 0)

    def step(self, number):
        z, size = self.z, self.size
        for side in range(2):
            line, condition = self.line_of(number, side)
            slot = slot_of(line, self.mine)
            back = z - 1 if side == 0 else z + 1
            onto = z + 1 if side == 0 else z - 1
            self.arrived(condition, slot, "z", back)
            self.start(
                both(condition, onto < size if side == 0 else onto >= 0),
                functools.partial(self.copy, slot, False, "z", onto, self.line_sems.at[number, side]),
            )
            self.spread(condition, slot, False, number, side, 0, 0)

    def middle(self):
        for number in range(1, self.size):
            self.step(number)
            self.on_bits(number - 1)
        self.on_bits(self.size - 1)

    def settle(self):
        if not self.settled:
            pltpu.make_async_copy(self.x_ref, self.out_ref.at[self.own], self.own_sem).wait()
            self.settled = True

    def end(self):
        self.settle()
        for condition, make in self.pending:
            guarded(condition, lambda make=make: make().wait_send())


def gather_semaphores(size, bits):
    slots = size * 2 ** len(bits)
    return [
        pltpu.SemaphoreType.DMA,
        pltpu.SemaphoreType.DMA((size, 2)),
        pltpu.SemaphoreType.DMA((size, 2, 2 ** len(bits), len(bits))),
        pltpu.SemaphoreType.DMA((slots,)),
    ]


class Exchange:
    def __init__(self, size, bits, block, half, gu_ref, dn_ref, gu_out, dn_out, sems):
        self.size, self.bits, self.count = size, bits, len(bits)
        self.block, self.half = block, half
        self.gu_ref, self.dn_ref, self.gu_out, self.dn_out = gu_ref, dn_ref, gu_out, dn_out
        self.own_sems, self.line_sems, self.bit_sems, self.recv_sems = sems
        self.z = lax.axis_index("z")
        self.mine = [lax.axis_index(bit) for bit in bits]
        self.own = slot_of(self.z, self.mine)
        self.others = [lax.rem(self.z + o, size) for o in range(1, size)]
        self.pending = []

    def pieces(self, target, slot):
        low = pl.multiple_of(jnp.minimum(target * self.block, self.half - self.block), LANES)
        high = pl.multiple_of(low + self.half, LANES)
        width = self.block
        return [
            (self.gu_ref.at[:, pl.ds(low, width)], self.gu_out.at[slot, :, pl.ds(0, width)]),
            (self.gu_ref.at[:, pl.ds(high, width)], self.gu_out.at[slot, :, pl.ds(width, width)]),
            (self.dn_ref.at[:, pl.ds(low, width)], self.dn_out.at[slot]),
        ]

    def line_copy(self, place, piece, slot):
        source, landing = self.pieces(self.others[place], slot)[piece]
        return pltpu.make_async_remote_copy(
            src_ref=source,
            dst_ref=landing,
            send_sem=self.line_sems.at[place, piece],
            recv_sem=self.recv_sems.at[slot, piece],
            device_id={"z": self.others[place]},
            device_id_type=MESH,
        )

    def own_copy(self, piece):
        source, landing = self.pieces(self.z, self.own)[piece]
        return pltpu.make_async_copy(source, landing, self.own_sems.at[piece])

    def bit_copy(self, slot, piece, stage, send_sem):
        ref = (self.gu_out, None, self.dn_out)[piece]
        return pltpu.make_async_remote_copy(
            src_ref=ref.at[slot],
            dst_ref=ref.at[slot],
            send_sem=send_sem,
            recv_sem=self.recv_sems.at[slot, piece],
            device_id={self.bits[stage]: 1 - self.mine[stage]},
            device_id_type=MESH,
        )

    def first_copy(self, slot, piece, stage, send_sem):
        source, landing = self.pieces(self.z, slot)[piece]
        return pltpu.make_async_remote_copy(
            src_ref=source,
            dst_ref=landing,
            send_sem=send_sem,
            recv_sem=self.recv_sems.at[slot, piece],
            device_id={self.bits[stage]: 1 - self.mine[stage]},
            device_id_type=MESH,
        )

    def spread(self, slot, number, variant, after):
        for stage in range(after, self.count):
            for piece in (0, 2):
                make = functools.partial(
                    self.bit_copy, slot, piece, stage, self.bit_sems.at[number, variant, stage, piece]
                )
                self.pending.append(make)
                make().start()

    def on_bits(self, number):
        line = lax.rem(self.z - number + self.size, self.size)
        for stage in range(self.count):
            for variant in range(2**stage):
                flips = bit_flips(variant, stage, self.count)
                slot = slot_of(line, [1 - m if f else m for m, f in zip(self.mine, flips)])
                if number == 0 and variant == 0:
                    for piece in range(3):
                        self.first_copy(slot, piece, stage, self.own_sems.at[0]).wait_recv()
                else:
                    for piece in (0, 2):
                        self.bit_copy(slot, piece, stage, self.own_sems.at[0]).wait_recv()
                self.spread(slot, number, sum(f << b for b, f in enumerate(flips)), stage + 1)

    def begin(self):
        for stage in range(self.count):
            for piece in range(3):
                make = functools.partial(
                    self.first_copy, self.own, piece, stage, self.bit_sems.at[0, 0, stage, piece]
                )
                self.pending.append(make)
                make().start()
        for piece in range(3):
            self.own_copy(piece).start()

    def send(self, offset):
        for piece in range(3):
            self.line_copy(offset - 1, piece, self.own).start()

    def sent(self, offset):
        for piece in range(3):
            self.line_copy(offset - 1, piece, self.own).wait_send()

    def step(self, offset):
        slot = slot_of(lax.rem(self.z - offset + self.size, self.size), self.mine)
        for piece in range(3):
            self.line_copy(0, piece, slot).wait_recv()
        self.spread(slot, offset, 0, 0)

    def end(self):
        for piece in range(3):
            self.own_copy(piece).wait()
        for make in self.pending:
            make().wait_send()


class Fold:
    def __init__(self, size, bits, order, p_ref, own_buf, sums, stage_in, stage_out, own_sems, send_sems, recv_sems):
        self.size, self.bits, self.count, self.order = size, bits, len(bits), order
        self.last = self.count - 1
        self.p_ref, self.own_buf, self.sums = p_ref, own_buf, sums
        self.stage_in, self.stage_out = stage_in, stage_out
        self.own_sems, self.send_sems, self.recv_sems = own_sems, send_sems, recv_sems
        self.z = lax.axis_index("z")
        self.mine = [lax.axis_index(bit) for bit in bits]

    def line(self, place):
        return lax.rem(self.z + self.order[place], self.size)

    def index(self, place, stage, variant):
        return place * (2**self.count - 1) + 2**stage - 1 + variant

    def slot(self, place, variant, flip):
        flips = [(variant >> b) & 1 for b in range(self.last)] + [flip]
        return slot_of(self.line(place), [1 - m if f else m for m, f in zip(self.mine, flips)])

    def copy(self, place, stage, variant):
        index = self.index(place, stage, variant)
        if stage == self.last:
            source = self.p_ref.at[self.slot(place, variant, 1)]
        else:
            source = self.stage_out.at[place * (2**self.last - 1) + 2**stage - 1 + variant]
        return pltpu.make_async_remote_copy(
            src_ref=source,
            dst_ref=self.stage_in.at[index],
            send_sem=self.send_sems.at[index],
            recv_sem=self.recv_sems.at[index],
            device_id={self.bits[stage]: 1 - self.mine[stage]},
            device_id_type=MESH,
        )

    def own_copy(self, place, variant):
        number = place * 2**self.last + variant
        return pltpu.make_async_copy(
            self.p_ref.at[self.slot(place, variant, 0)], self.own_buf.at[number], self.own_sems.at[number]
        )

    def begin(self, places=None):
        for place in range(self.size) if places is None else places:
            for variant in reversed(range(2**self.last)):
                self.copy(place, self.last, variant).start()
                self.own_copy(place, variant).start()

    def stage(self, place, stage, done=None):
        for variant in reversed(range(2**stage)):
            if stage == self.last:
                self.own_copy(place, variant).wait()
                held = self.own_buf[place * 2**self.last + variant].astype(F32)
            else:
                held = self.sums[place * (2**self.last - 1) + 2**stage - 1 + variant]
            self.copy(place, stage, variant).wait_recv()
            total = held + self.stage_in[self.index(place, stage, variant)].astype(F32)
            if stage == 0:
                done(place, total)
                continue
            lower = variant & (2 ** (stage - 1) - 1)
            number = place * (2**self.last - 1) + 2 ** (stage - 1) - 1 + lower
            if variant >> (stage - 1):
                self.stage_out[number] = total.astype(LOW)
                self.copy(place, stage - 1, lower).start()
            else:
                self.sums[number] = total

    def end(self):
        for place in range(self.size):
            for stage in range(self.count):
                for variant in range(2**stage):
                    self.copy(place, stage, variant).wait_send()


def fold_scratch(size, bits, rows, columns):
    count = len(bits)
    inner, lower = size * (2**count - 1), size * (2 ** (count - 1) - 1)
    return [
        pltpu.VMEM((size * 2 ** (count - 1), rows, columns), LOW),
        pltpu.VMEM((max(lower, 1), rows, columns) if lower else (1, 8, LANES), F32),
        pltpu.VMEM((inner, rows, columns), LOW),
        pltpu.VMEM((max(lower, 1), rows, columns) if lower else (1, 16, LANES), LOW),
        pltpu.SemaphoreType.DMA((size * 2 ** (count - 1),)),
        pltpu.SemaphoreType.DMA((inner,)),
        pltpu.SemaphoreType.DMA((inner,)),
    ]


class Scatter:
    def __init__(self, size, bits, p_ref, out_ref, line_out, line_in, line_send, line_recv, *fold):
        order = list(range(1, size)) + [0]
        self.fold = Fold(size, bits, order, p_ref, *fold)
        self.size, self.out_ref = size, out_ref
        self.line_out, self.line_in, self.line_send, self.line_recv = line_out, line_in, line_send, line_recv

    def line_copy(self, place):
        return pltpu.make_async_remote_copy(
            src_ref=self.line_out.at[place],
            dst_ref=self.line_in.at[place],
            send_sem=self.line_send.at[place],
            recv_sem=self.line_recv.at[place],
            device_id={"z": self.fold.line(place)},
            device_id_type=MESH,
        )

    def done(self, place, total):
        if place < self.size - 1:
            self.line_out[place] = total.astype(LOW)
            self.line_copy(place).start()
        else:
            self.out_ref[...] = total

    def begin(self, places=None):
        self.fold.begin(places)

    def place(self, place):
        for stage in reversed(range(self.fold.count)):
            self.fold.stage(place, stage, self.done)

    def finish(self):
        for place in range(self.size - 1):
            self.line_copy(place).wait_recv()
            self.out_ref[...] += self.line_in[place].astype(F32)

    def end(self):
        self.fold.end()
        for place in range(self.size - 1):
            self.line_copy(place).wait_send()


def scatter_scratch(size, bits, rows, columns):
    return [
        pltpu.VMEM((size - 1, rows, columns), LOW),
        pltpu.VMEM((size - 1, rows, columns), LOW),
        pltpu.SemaphoreType.DMA((size - 1,)),
        pltpu.SemaphoreType.DMA((size - 1,)),
        *fold_scratch(size, bits, rows, columns),
    ]


SCATTER_REFS = 11


class Total:
    def __init__(self, size, bits, x_ref, out_ref, held, landed, send_sems, recv_sems):
        self.size, self.bits, self.count = size, bits, len(bits)
        self.x_ref, self.out_ref, self.held, self.landed = x_ref, out_ref, held, landed
        self.send_sems, self.recv_sems = send_sems, recv_sems
        self.z = lax.axis_index("z")
        self.others = [lax.rem(self.z + o, size) for o in range(1, size)]

    def copy(self, number):
        if number < self.count:
            axis = self.bits[number]
            source, target = self.held.at[number], {axis: 1 - lax.axis_index(axis)}
        else:
            source, target = self.held.at[self.count], {"z": self.others[number - self.count]}
        return pltpu.make_async_remote_copy(
            src_ref=source,
            dst_ref=self.landed.at[number],
            send_sem=self.send_sems.at[number],
            recv_sem=self.recv_sems.at[number],
            device_id=target,
            device_id_type=MESH,
        )

    def begin(self):
        self.held[0] = self.x_ref[...]
        self.copy(0).start()

    def pair(self, number):
        self.copy(number).wait_recv()
        self.held[number + 1] = self.held[number] + self.landed[number]
        if number + 1 < self.count:
            self.copy(number + 1).start()
        else:
            for place in range(self.size - 1):
                self.copy(self.count + place).start()

    def finish(self):
        for place in range(self.size - 1):
            self.copy(self.count + place).wait_recv()
        total = jnp.zeros(self.out_ref.shape, self.out_ref.dtype)
        for line in range(self.size):
            offset = lax.rem(line - self.z + self.size, self.size)
            part = self.held[self.count]
            for o in range(1, self.size):
                part = jnp.where(offset == o, self.landed[self.count + self.size - o - 1], part)
            total = total + part
        self.out_ref[...] = total

    def end(self):
        for number in range(self.count + self.size - 1):
            self.copy(number).wait_send()


def greet_all(size, axes):
    z = lax.axis_index("z")
    greet(
        [("z", lax.rem(z + o, size)) for o in range(1, size)]
        + [(axis, 1 - lax.axis_index(axis)) for axis in axes],
        [None] * (size - 1 + len(axes)),
    )


def in_groups(refs, sizes):
    groups, at = [], 0
    for number in sizes:
        groups.append(refs[at : at + number])
        at += number
    return groups


def comm_params(collective_id):
    return pltpu.CompilerParams(
        collective_id=collective_id, has_side_effects=True, vmem_limit_bytes=60 * 2**20
    )


def at_microseconds(time):
    return pl.CostEstimate(flops=0, transcendentals=0, bytes_accessed=time * 3500000)


def last_kernel(size, bits, p_ref, x_ref, out_ref, sum_ref, *refs):
    greet_all(size, ("t", *bits))
    given, rest = in_groups(refs, [SCATTER_REFS, 4])
    small = Total(size, ("t", *bits), x_ref, sum_ref, *rest)
    steps = Scatter(size, bits, p_ref, out_ref, *given)
    small.begin()
    steps.begin()
    for place in range(size):
        steps.place(place)
        if place <= len(bits):
            small.pair(place)
    for number in range(size, len(bits) + 1):
        small.pair(number)
    steps.finish()
    small.finish()
    steps.end()
    small.end()


def last(partial, x, size, bits, collective_id):
    slots, rows, columns = partial.shape
    number = len(bits) + 1
    return pl.pallas_call(
        functools.partial(last_kernel, size, bits),
        out_shape=(jax.ShapeDtypeStruct((rows, columns), F32), jax.ShapeDtypeStruct(x.shape, F32)),
        in_specs=[pl.BlockSpec(memory_space=pl.ANY), pl.BlockSpec(memory_space=pltpu.VMEM)],
        out_specs=[pl.BlockSpec(memory_space=pltpu.VMEM)] * 2,
        scratch_shapes=[
            *scatter_scratch(size, bits, rows, columns),
            pltpu.VMEM((number + 1, *x.shape), F32),
            pltpu.VMEM((number + size - 1, *x.shape), F32),
            pltpu.SemaphoreType.DMA((number + size - 1,)),
            pltpu.SemaphoreType.DMA((number + size - 1,)),
        ],
        compiler_params=comm_params(collective_id),
        cost_estimate=at_microseconds(60),
    )(partial, x)


class Attend:
    def __init__(self, rows_ref, gain_ref, bias_ref, cos_ref, sin_ref, mask_ref, w_ref, outs, scratch, width, epsilon=1e-06):
        self.gain_ref, self.bias_ref, self.w_ref = gain_ref, bias_ref, w_ref
        self.cos_ref, self.sin_ref, self.mask_ref = cos_ref, sin_ref, mask_ref
        self.state_ref, self.middle_ref, self.xa_ref, self.q_ref, self.k_ref, self.v_ref, self.lse_ref, self.o_ref = outs
        self.send_buf, self.land_buf, self.send_sems, self.recv_sems = scratch
        self.rows_ref = rows_ref
        self.t = lax.axis_index("t")
        self.slots, self.few = w_ref.shape[0], w_ref.shape[1]
        self.model = self.slots * self.few
        self.count = rows_ref.shape[0]
        self.q_width = self.q_ref.shape[1]
        self.width = width
        self.epsilon = epsilon

    def normed(self, rows, gain_ref):
        factor = lax.rsqrt(jnp.mean(rows * rows, axis=-1, keepdims=True) + self.epsilon)
        return (rows * factor * gain_ref[...]).astype(LOW)

    def xa_copy(self):
        return pltpu.make_async_remote_copy(
            src_ref=self.xa_ref.at[self.t],
            dst_ref=self.xa_ref.at[self.t],
            send_sem=self.send_sems.at[0],
            recv_sem=self.recv_sems.at[0],
            device_id={"t": 1 - self.t},
            device_id_type=MESH,
        )

    def xa_landing(self):
        return pltpu.make_async_remote_copy(
            src_ref=self.xa_ref.at[1 - self.t],
            dst_ref=self.xa_ref.at[1 - self.t],
            send_sem=self.send_sems.at[0],
            recv_sem=self.recv_sems.at[0],
            device_id={"t": 1 - self.t},
            device_id_type=MESH,
        )

    def half_copy(self):
        return pltpu.make_async_remote_copy(
            src_ref=self.send_buf,
            dst_ref=self.land_buf,
            send_sem=self.send_sems.at[1],
            recv_sem=self.recv_sems.at[1],
            device_id={"t": 1 - self.t},
            device_id_type=MESH,
        )

    def begin(self, state):
        self.state_ref[...] = state
        self.xa_ref[self.t] = self.normed(state, self.gain_ref)
        self.xa_copy().start()

    def columns(self, low, count):
        weight = self.w_ref[:, :, low : low + count].reshape(self.model, count)
        xa = self.xa_ref[...].reshape(2 * self.count, self.model)
        return jnp.dot(xa, weight, preferred_element_type=F32) + self.bias_ref[:, low : low + count]

    def rope(self, values):
        return (values * self.cos_ref[...] + pltpu.roll(values, HD // 2, 1) * self.sin_ref[...]).astype(LOW)

    def keys(self):
        self.xa_landing().wait_recv()
        both_kv = self.columns(self.q_width, 2 * HD)
        self.k_ref[...] = self.rope(both_kv[:, :HD])
        self.v_ref[...] = both_kv[:, HD:].astype(LOW)

    def heads(self, first):
        lin = self.columns(first * HD, 2 * HD)
        for number in range(2):
            head = first + number
            low = head * HD
            query = self.rope(lin[:, number * HD : (number + 1) * HD])
            self.q_ref[:, low : low + HD] = query
            raw = lax.dot_general(
                query, self.k_ref[...], (((1,), (1,)), ((), ())), preferred_element_type=F32
            )
            scores = jnp.where(self.mask_ref[...] > 0, raw * (1.0 / math.sqrt(HD)), -1e30)
            top = jnp.max(scores, axis=-1, keepdims=True)
            expo = jnp.exp(scores - top)
            whole = jnp.sum(expo, axis=-1, keepdims=True)
            probs = (expo / whole).astype(LOW)
            self.lse_ref[head] = top + jnp.log(whole)
            out = jnp.dot(probs, self.v_ref[...], preferred_element_type=F32).astype(LOW)
            self.o_ref[0, :, low : low + HD] = out[: self.count]
            self.o_ref[1, :, low : low + HD] = out[self.count :]

    def projected(self, half, step):
        left = self.o_ref[half]
        for low in range(0, self.slots, step):
            weight = self.w_ref[low : low + step, :, self.width :].reshape(step * self.few, self.q_width)
            yield low * self.few, lax.dot_general(
                left, weight, (((1,), (1,)), ((), ())), preferred_element_type=F32
            )

    def other_half(self):
        for low, part in self.projected(1 - self.t, self.slots // 4):
            self.send_buf[:, low : low + part.shape[1]] = part.astype(LOW)
        self.half_copy().start()

    def own_half(self):
        for low, part in self.projected(self.t, self.slots // 4):
            where = slice(low, low + part.shape[1])
            self.middle_ref[:, where] = self.state_ref[:, where] + part

    def finish(self, gain_ref, xf_ref):
        self.half_copy().wait_recv()
        middle = self.middle_ref[...] + self.land_buf[...].astype(F32)
        self.middle_ref[...] = middle
        xf_ref[...] = self.normed(middle, gain_ref)

    def end(self):
        self.xa_copy().wait_send()
        self.half_copy().wait_send()


def front_kernel(size, bits, block, half, layer, width, *refs):
    first = layer == 0
    inputs, outs, refs = in_groups(refs, [11, 13 if first else 12, len(refs)])
    (x_ref, more_ref, ga_ref, gf_ref, bias_ref, cos_ref, sin_ref, mask_ref, at_ref, gu_ref, dn_ref) = inputs
    xf_out, gu_out, dn_out, at_out = outs[8:12]
    (w_ref, xf_ref, at_sem), pair, at_sems, feed_sems, rows_sems, rest = in_groups(
        refs, [3, 4, 4, 4, 4, len(refs)]
    )
    greet_all(size, ("t", *bits))
    work = Attend(
        x_ref, ga_ref, bias_ref, cos_ref, sin_ref, mask_ref, w_ref, outs[:8], pair, width
    )
    attention = Gather(size, bits, at_ref, w_ref, *at_sems)
    feed = Exchange(
        size, bits, block, half, gu_ref.at[layer], dn_ref.at[layer], gu_out, dn_out, feed_sems
    )
    rows = Gather(size, ("t",), xf_ref, xf_out, *rows_sems)
    kept = pltpu.make_async_copy(w_ref, at_out, at_sem)
    if first:
        side = Gather(size, ("t",), more_ref, outs[12], *rest)
        attention.begin()
        side.begin()
        feed.begin()
        work.begin(x_ref[...].astype(F32))
        attention.step(1)
        side.step(1)
        attention.step(2)
        attention.on_bits(0)
        side.on_bits(0)
        side.step(2)
        feed.send(1)
        attention.step(3)
        attention.on_bits(1)
        side.on_bits(1)
        side.step(3)
        feed.on_bits(0)
        attention.on_bits(2)
        feed.sent(1)
        feed.send(3)
        feed.step(1)
        attention.on_bits(3)
        attention.settle()
        work.keys()
        work.heads(0)
        side.on_bits(2)
        side.on_bits(3)
    else:
        total_ref, *rest = rest
        side = Scatter(size, ("t",), more_ref, total_ref, *rest)
        attention.begin()
        side.begin()
        feed.begin()
        side.place(0)
        attention.step(1)
        side.place(1)
        attention.step(2)
        attention.on_bits(0)
        side.place(2)
        attention.step(3)
        attention.on_bits(1)
        side.place(3)
        feed.send(1)
        attention.on_bits(2)
        attention.on_bits(3)
        attention.settle()
        side.finish()
        work.begin(x_ref[...] + total_ref[...])
        feed.on_bits(0)
        feed.sent(1)
        feed.send(3)
        feed.step(1)
        work.keys()
        work.heads(0)
    kept.start()
    feed.sent(3)
    feed.send(2)
    feed.step(3)
    feed.on_bits(1)
    work.heads(2)
    work.heads(4)
    work.other_half()
    work.own_half()
    work.finish(gf_ref, xf_ref)
    rows.begin()
    rows.step(1)
    rows.on_bits(0)
    rows.step(2)
    feed.sent(2)
    feed.step(2)
    rows.on_bits(1)
    feed.on_bits(3)
    rows.step(3)
    rows.on_bits(2)
    feed.on_bits(2)
    rows.on_bits(3)
    kept.wait()
    for steps in (attention, side, feed, work, rows):
        steps.end()


def front(x, more, gains, bias, tables, at, gu, dn, layer, size, bits, block, width, collective_id):
    slots = size * 2 ** len(bits)
    count, model = x.shape
    few, half = dn.shape[1:]
    length = 2 * count
    q_width = at.shape[1] - width
    first = layer == 0
    held, far = pl.BlockSpec(memory_space=pltpu.VMEM), pl.BlockSpec(memory_space=pl.ANY)
    shape = jax.ShapeDtypeStruct
    more_scratch = (
        gather_semaphores(size, ("t",))
        if first
        else [pltpu.VMEM((count, model), F32), *scatter_scratch(size, ("t",), count, model)]
    )
    return pl.pallas_call(
        functools.partial(front_kernel, size, bits, block, half, layer, width),
        out_shape=(
            shape((count, model), F32),
            shape((count, model), F32),
            shape((2, count, model), LOW),
            shape((length, q_width), LOW),
            shape((length, HD), LOW),
            shape((length, HD), LOW),
            shape((q_width // HD, length, 1), F32),
            shape((2, count, q_width), LOW),
            shape((2 * size, count, model), LOW),
            shape((slots, few, 2 * block), LOW),
            shape((slots, few, block), LOW),
            shape((slots, few, at.shape[1]), LOW),
            *([shape((2 * size, count, model), LOW)] if first else []),
        ),
        in_specs=[held, far] + [held] * 6 + [far] * 3,
        out_specs=[held] * 8 + [far] * (5 if first else 4),
        scratch_shapes=[
            pltpu.VMEM((slots, few, at.shape[1]), LOW),
            pltpu.VMEM((count, model), LOW),
            pltpu.SemaphoreType.DMA,
            pltpu.VMEM((count, model), LOW),
            pltpu.VMEM((count, model), LOW),
            pltpu.SemaphoreType.DMA((2,)),
            pltpu.SemaphoreType.DMA((2,)),
            *gather_semaphores(size, bits),
            pltpu.SemaphoreType.DMA((3,)),
            pltpu.SemaphoreType.DMA((size - 1, 3)),
            pltpu.SemaphoreType.DMA((size, 2 ** len(bits), len(bits), 3)),
            pltpu.SemaphoreType.DMA((slots, 3)),
            *gather_semaphores(size, ("t",)),
            *more_scratch,
        ],
        compiler_params=comm_params(collective_id),
        cost_estimate=at_microseconds(150),
    )(x, more, *gains, bias, *tables, at, gu, dn)


class AttendBack:
    def __init__(self, ins, outs, scratch, width, epsilon=1e-06):
        (self.g_ref, self.state_ref, self.middle_ref, self.ga_gain, self.gf_gain, self.cos_ref, self.sin_ref) = ins[:7]
        (self.mask_ref, self.q_ref, self.k_ref, self.v_ref, self.lse_ref, self.far_w) = ins[7:]
        (self.grad_ref, self.ga_ref, self.lin_ref, self.bias_ref, self.pa_ref, self.pf_ref) = outs
        (self.w_ref, self.w_sem, self.dk, self.dv, self.sum_buf, self.send_buf, self.land_buf) = scratch[:7]
        (self.send_sems, self.recv_sems) = scratch[7:]
        self.t = lax.axis_index("t")
        self.slots, self.few = self.w_ref.shape[:2]
        self.model = self.slots * self.few
        self.count = self.state_ref.shape[0]
        self.q_width = self.q_ref.shape[1]
        self.width, self.epsilon = width, epsilon

    def pair_copy(self, number, source, landing):
        return pltpu.make_async_remote_copy(
            src_ref=source,
            dst_ref=landing,
            send_sem=self.send_sems.at[number],
            recv_sem=self.recv_sems.at[number],
            device_id={"t": 1 - self.t},
            device_id_type=MESH,
        )

    def ga_copy(self, side):
        return self.pair_copy(0, self.ga_ref.at[side], self.ga_ref.at[side])

    def half_copy(self):
        return self.pair_copy(1, self.send_buf, self.land_buf)

    def weight_copy(self):
        return pltpu.make_async_copy(self.far_w, self.w_ref, self.w_sem)

    def norm_back(self, upstream, rows, gain):
        factor = lax.rsqrt(jnp.mean(rows * rows, axis=-1, keepdims=True) + self.epsilon)
        scaled = upstream * gain
        part = jnp.sum(upstream * rows * factor, axis=0, keepdims=True)
        inner = jnp.mean(scaled * rows, axis=-1, keepdims=True)
        return factor * scaled - rows * factor**3 * inner, part

    def prepare(self):
        self.weight_copy().start()

    def begin(self, d_xf):
        d_mid, part = self.norm_back(d_xf, self.middle_ref[...], self.gf_gain[...])
        self.pf_ref[...] = part
        grad = self.g_ref[...].astype(F32) + d_mid
        self.grad_ref[...] = grad
        self.ga_ref[self.t] = grad.astype(LOW)
        self.ga_copy(self.t).start()
        self.dk[...] = jnp.zeros_like(self.dk)
        self.dv[...] = jnp.zeros_like(self.dv)

    def arrive(self):
        self.weight_copy().wait()
        self.ga_copy(1 - self.t).wait_recv()

    def unrope(self, values):
        return values * self.cos_ref[...] - pltpu.roll(values, HD // 2, 1) * self.sin_ref[...]

    def keep(self, low, values):
        count = values.shape[1]
        self.bias_ref[:, low : low + count] = jnp.sum(values, axis=0, keepdims=True)
        values = values.astype(LOW)
        self.lin_ref[0, :, low : low + count] = values[: self.count]
        self.lin_ref[1, :, low : low + count] = values[self.count :]

    def heads(self, first):
        low, count = self.width + first * HD, 2 * HD
        weight = self.w_ref[:, :, low : low + count].reshape(self.model, count)
        above = self.ga_ref[...].reshape(2 * self.count, self.model)
        d_out = jnp.dot(above, weight, preferred_element_type=F32).astype(LOW)
        key, value = self.k_ref[...], self.v_ref[...]
        last = (((1,), (1,)), ((), ()))
        early = (((0,), (0,)), ((), ()))
        scale = 1.0 / math.sqrt(HD)
        for number in range(2):
            head = first + number
            query = self.q_ref[:, head * HD : (head + 1) * HD]
            d_head = d_out[:, number * HD : (number + 1) * HD]
            raw = lax.dot_general(query, key, last, preferred_element_type=F32)
            scores = jnp.where(self.mask_ref[...] > 0, raw * scale, -1e30)
            probs = jnp.exp(scores - self.lse_ref[head])
            d_probs = lax.dot_general(d_head, value, last, preferred_element_type=F32)
            centre = jnp.sum(probs * d_probs, axis=-1, keepdims=True)
            d_raw = (probs * (d_probs - centre) * scale).astype(LOW)
            d_query = jnp.dot(d_raw, key, preferred_element_type=F32)
            self.dk[...] += lax.dot_general(d_raw, query, early, preferred_element_type=F32)
            self.dv[...] += lax.dot_general(
                probs.astype(LOW), d_head, early, preferred_element_type=F32
            )
            self.keep(head * HD, self.unrope(d_query))

    def keys(self):
        self.keep(self.q_width, self.unrope(self.dk[...]))
        self.keep(self.q_width + HD, self.dv[...])

    def projected(self, half):
        left, step = self.lin_ref[half], self.slots // 4
        for low in range(0, self.slots, step):
            weight = self.w_ref[low : low + step, :, : self.width].reshape(step * self.few, self.width)
            yield slice(low * self.few, (low + step) * self.few), lax.dot_general(
                left, weight, (((1,), (1,)), ((), ())), preferred_element_type=F32
            )

    def other_half(self):
        for where, part in self.projected(1 - self.t):
            self.send_buf[:, where] = part.astype(LOW)
        self.half_copy().start()

    def own_half(self):
        for where, part in self.projected(self.t):
            self.sum_buf[:, where] = part

    def finish(self):
        self.half_copy().wait_recv()
        d_xa = self.sum_buf[...] + self.land_buf[...].astype(F32)
        d_in, part = self.norm_back(d_xa, self.state_ref[...], self.ga_gain[...])
        self.pa_ref[...] = part
        grad = self.grad_ref[...] + d_in
        self.grad_ref[...] = grad
        return grad

    def end(self):
        self.ga_copy(self.t).wait_send()
        self.half_copy().wait_send()


class Blocks:
    def __init__(self, size, bits, gu_ref, dn_ref, out_ref, gu_fold, dn_fold, done, sems):
        self.size, self.out_ref = size, out_ref
        order = list(range(1, size)) + [0]
        self.folds = [Fold(size, bits, order, gu_ref, *gu_fold), Fold(size, bits, order, dn_ref, *dn_fold)]
        self.done = done
        self.own_sems, self.send_sems, self.recv_sems = sems
        self.width, self.narrow = gu_ref.shape[2], dn_ref.shape[2]
        self.z = lax.axis_index("z")

    def landing(self, number, slot):
        low, count = ((0, self.width), (self.width, self.narrow))[number]
        return self.out_ref.at[slot, :, pl.ds(low, count)]

    def line_copy(self, number, place, slot):
        return pltpu.make_async_remote_copy(
            src_ref=self.done[number].at[place],
            dst_ref=self.landing(number, slot),
            send_sem=self.send_sems.at[number, place],
            recv_sem=self.recv_sems.at[number, slot],
            device_id={"z": self.folds[0].line(place)},
            device_id_type=MESH,
        )

    def own_copy(self, number):
        return pltpu.make_async_copy(
            self.done[number].at[self.size - 1], self.landing(number, self.z), self.own_sems.at[number]
        )

    def begin(self):
        for fold in self.folds:
            fold.begin()

    def inner(self, place):
        for stage in reversed(range(1, self.folds[0].count)):
            for fold in self.folds:
                fold.stage(place, stage)

    def send(self, place):
        for number, fold in enumerate(self.folds):

            def keep(place, total, number=number):
                self.done[number][place] = total.astype(LOW)
                if place < self.size - 1:
                    self.line_copy(number, place, self.z).start()
                else:
                    self.own_copy(number).start()

            fold.stage(place, 0, keep)

    def end(self):
        for number, fold in enumerate(self.folds):
            for offset in range(1, self.size):
                slot = lax.rem(self.z - offset + self.size, self.size)
                self.line_copy(number, 0, slot).wait_recv()
            for place in range(self.size - 1):
                self.line_copy(number, place, self.z).wait_send()
            self.own_copy(number).wait()
            fold.end()


def back_kernel(size, bits, width, final, *refs):
    top, bottom = final
    counts = [1, 1 if top else 0, 2, 13, 6, 1, 1 if top else 0, 0 if bottom else 1]
    p_ref, branch_ref, wide, ins, outs, (blocks_ref,), branch_out, gm_out, refs = in_groups(
        refs, counts + [len(refs)]
    )
    (dxf_ref,), dxf_scratch, gu_fold, dn_fold, done, sems, work_scratch, refs = in_groups(
        refs, [1, SCATTER_REFS, 7, 7, 2, 3, 9, len(refs)]
    )
    greet_all(size, ("t", *bits))
    rows = Scatter(size, ("t",), p_ref[0], dxf_ref, *dxf_scratch)
    blocks = Blocks(size, bits, *wide, blocks_ref, gu_fold, dn_fold, done, sems)
    work = AttendBack(ins, outs, work_scratch, width)
    branch = onward = None
    if top:
        branch_scratch, refs = in_groups(refs, [SCATTER_REFS, len(refs)])
        branch = Scatter(size, ("t",), branch_ref[0], branch_out[0], *branch_scratch)
    if not bottom:
        gm_ref, *gm_sems = refs
        onward = Gather(size, ("t",), gm_ref, gm_out[0], *gm_sems)
    rows.begin()
    blocks.begin()
    work.prepare()
    blocks.inner(0)
    rows.place(0)
    blocks.inner(1)
    blocks.inner(2)
    rows.place(1)
    blocks.inner(3)
    blocks.send(0)
    rows.place(2)
    rows.place(3)
    if top:
        branch.begin([0])
    rows.finish()
    blocks.send(1)
    work.begin(dxf_ref[...])
    if top:
        branch.begin([1])
    work.arrive()
    work.heads(0)
    if top:
        branch.place(0)
    work.heads(2)
    blocks.send(2)
    work.heads(4)
    work.keys()
    work.other_half()
    if top:
        branch.place(1)
        branch.begin([2])
    work.own_half()
    blocks.send(3)
    grad = work.finish()
    if not bottom:
        gm_ref[...] = grad.astype(LOW)
        onward.begin()
    if top:
        branch.begin([3])
        branch.place(2)
    if not bottom:
        onward.step(1)
        onward.on_bits(0)
    if top:
        branch.place(3)
    if not bottom:
        onward.step(2)
        onward.on_bits(1)
        onward.step(3)
        onward.on_bits(2)
        onward.on_bits(3)
    if top:
        branch.finish()
    for steps in (rows, blocks, work, branch, onward):
        if steps is not None:
            steps.end()


def back(partial, branch, gu, dn, ins, size, bits, width, bottom, collective_id):
    count, model = ins[1].shape
    length, q_width = ins[8].shape
    slots, few, wide = gu.shape
    narrow = dn.shape[2]
    top = branch is not None
    held, far = pl.BlockSpec(memory_space=pltpu.VMEM), pl.BlockSpec(memory_space=pl.ANY)
    shape = jax.ShapeDtypeStruct
    rows_scratch = scatter_scratch(size, ("t",), count, model)
    return pl.pallas_call(
        functools.partial(back_kernel, size, bits, width, (top, bottom)),
        out_shape=(
            shape((count, model), F32),
            shape((2, count, model), LOW),
            shape((2, count, width), LOW),
            shape((1, width), F32),
            shape((1, model), F32),
            shape((1, model), F32),
            shape((size, few, wide + narrow), LOW),
            *([shape((count, model), F32)] if top else []),
            *([] if bottom else [shape((2 * size, count, model), LOW)]),
        ),
        in_specs=[far] * (4 if top else 3) + [held] * 12 + [far],
        out_specs=[held] * 6 + [far] + [held] * top + [far] * (not bottom),
        scratch_shapes=[
            pltpu.VMEM((count, model), F32),
            *rows_scratch,
            *fold_scratch(size, bits, few, wide),
            *fold_scratch(size, bits, few, narrow),
            pltpu.VMEM((size, few, wide), LOW),
            pltpu.VMEM((size, few, narrow), LOW),
            pltpu.SemaphoreType.DMA((2,)),
            pltpu.SemaphoreType.DMA((2, size)),
            pltpu.SemaphoreType.DMA((2, size)),
            pltpu.VMEM(ins[12].shape, LOW),
            pltpu.SemaphoreType.DMA,
            pltpu.VMEM((length, HD), F32),
            pltpu.VMEM((length, HD), F32),
            pltpu.VMEM((count, model), F32),
            pltpu.VMEM((count, model), LOW),
            pltpu.VMEM((count, model), LOW),
            pltpu.SemaphoreType.DMA((2,)),
            pltpu.SemaphoreType.DMA((2,)),
            *(rows_scratch if top else []),
            *([] if bottom else [pltpu.VMEM((count, model), LOW), *gather_semaphores(size, ("t",))]),
        ],
        compiler_params=comm_params(collective_id),
        cost_estimate=at_microseconds(120),
    )(partial, *([branch] if top else []), gu, dn, *ins)


def in_slots(partial, slots):
    return partial.reshape(slots, -1, partial.shape[1])


def block_width(half):
    return -(-half // (LINE * LANES)) * LANES


def block_start(line, block, half):
    return min(line * block, half - block)


def from_blocks(blocks, parts, half):
    block = blocks.shape[2] // 3
    pieces = []
    for part in parts:
        for line in range(LINE):
            skip = line * block - block_start(line, block, half)
            pieces.append(blocks[line, :, part * block + skip : (part + 1) * block])
    return jnp.concatenate(pieces, axis=1).astype(F32)


def local(
    bits, tokens, cotangent, doc_lengths, norm_attn, norm_ffn, w_qkv, b_qkv, w_out, w_gateup, w_down
):
    dp = ("z", *bits)
    tensor_size = lax.axis_size("t")
    count = tokens.shape[0]
    length = count * tensor_size
    layers = w_qkv.shape[0]
    qkv_width = w_qkv.shape[2]
    rows = w_qkv.shape[1]
    half = w_down.shape[2]
    block = block_width(half)
    positions, allowed = doc_layout(doc_lengths[0], length)
    cosine, sine = rope_tables(positions, HD)
    turned = jnp.where(jnp.arange(HD) < HD // 2, -sine, sine)
    tables = (cosine, turned, allowed.astype(F32))
    gain_attn = norm_attn.astype(F32)
    gain_ffn = norm_ffn.astype(F32)
    bias_all = b_qkv.astype(F32)
    line = lax.axis_index("z")
    valid = jnp.arange(block) >= line * block - jnp.minimum(line * block, half - block)
    saved = []
    for layer in range(layers):
        flat = jnp.concatenate([w_qkv[layer], w_out[layer]], axis=1)
        start, more = (tokens, cotangent) if layer == 0 else (middle, in_slots(partial, 2 * LINE))
        gains = (gain_attn[layer : layer + 1], gain_ffn[layer : layer + 1])
        out = front(
            start, more, gains, bias_all[layer : layer + 1], tables, flat, w_gateup, w_down,
            layer, LINE, bits, block, qkv_width, 8 + layer,
        )
        if layer == 0:
            gm_all = out[12].reshape(-1, cotangent.shape[1])
        (state, middle, xa_all, query, key, value, log_total, attended) = out[:8]
        xf_all, gu_w, down_w = (item.reshape(-1, item.shape[2]) for item in out[8:11])
        both_w = out[11]
        xa_all = xa_all.reshape(length, -1)
        attended = attended.reshape(length, -1)
        gate_up = jnp.dot(xf_all, gu_w, preferred_element_type=F32)
        gate = gate_up[:, :block]
        up = gate_up[:, block:]
        act = jnp.where(valid, jax.nn.silu(gate) * up, 0.0).astype(LOW)
        partial = contract_last(act, down_w, LOW)
        saved.append(
            (state, xa_all, query, key, value, log_total, attended)
            + (middle, xf_all, gate, up, act, gu_w, down_w, both_w)
        )
    grad, branch = cotangent, in_slots(partial, 2 * LINE)
    grads_attn, grads_bias, grads_ga, grads_gf, grads_blocks = ([] for _ in range(5))
    for layer in reversed(range(layers)):
        (state_in, xa_all, query, key, value, log_total, attended) = saved[layer][:7]
        (middle, xf_all, gate, up, act, gu_w, down_w, both_w) = saved[layer][7:]
        d_down = contract_first(gm_all, act, LOW)
        d_act = jnp.dot(gm_all, down_w, preferred_element_type=F32)
        sig = jax.nn.sigmoid(gate)
        d_gate = d_act * up * sig * (1.0 + gate * (1.0 - sig))
        d_up = d_act * gate * sig
        d_gu = jnp.concatenate(
            [jnp.where(valid, d_gate, 0.0), jnp.where(valid, d_up, 0.0)], axis=1
        ).astype(LOW)
        d_gateup = contract_first(xf_all, d_gu, LOW)
        partial = in_slots(contract_last(d_gu, gu_w, LOW), 2 * LINE)
        wide = (in_slots(d_gateup, d_gateup.shape[0] // rows), in_slots(d_down, d_down.shape[0] // rows))
        gains = (gain_attn[layer : layer + 1], gain_ffn[layer : layer + 1])
        ins = (grad, state_in, middle, *gains, *tables, query, key, value, log_total, both_w)
        out = back(partial, branch, *wide, ins, LINE, bits, qkv_width, layer == 0, 16 + layer)
        (grad, ga_all, d_lin, d_bias, part_a, part_f, blocks), rest = out[:7], list(out[7:])
        if branch is not None:
            output = (middle + rest.pop(0)).astype(LOW)
            branch = None
        if rest:
            gm_all = rest[0].reshape(-1, rest[0].shape[2])
        grads_bias.append(d_bias[0])
        grads_blocks.append(blocks)
        d_lin, ga_all = d_lin.reshape(length, -1), ga_all.reshape(length, -1)
        d_both = jnp.concatenate(
            [contract_first(xa_all, d_lin, LOW), contract_first(ga_all, attended, LOW)], axis=1
        )
        if layer == 0:
            d_both = in_slots(d_both, d_both.shape[0] // rows)
        else:
            grads_attn.append(
                lax.psum_scatter(d_both, dp, scatter_dimension=0, tiled=True).astype(F32)
            )
        grads_ga.append(part_a[0])
        grads_gf.append(part_f[0])

    def ordered(items):
        return jnp.stack(items[::-1], axis=0)

    side = lax.axis_index("t")
    bias = ordered(grads_bias)
    spread = jnp.where(
        (jnp.arange(tensor_size) == side)[:, None, None], bias[None], jnp.zeros_like(bias)[None]
    )
    small = (ordered(grads_ga), ordered(grads_gf), spread)
    flat = jnp.concatenate([item.reshape(-1, LANES) for item in small], axis=0)
    last_attn, flat = last(d_both, flat, LINE, bits, 4)
    grads_attn.append(last_attn)
    full_ga, full_gf, full_bias = (
        part.reshape(item.shape)
        for part, item in zip(
            jnp.split(flat, [small[0].size // LANES, 2 * small[0].size // LANES], axis=0), small
        )
    )
    both = ordered(grads_attn)
    return (
        output,
        grad,
        full_ga,
        full_gf,
        both[:, :, :qkv_width],
        take(full_bias, side, 0),
        both[:, :, qkv_width:],
        ordered([from_blocks(blocks, (0, 1), half) for blocks in grads_blocks]),
        ordered([from_blocks(blocks, (2,), half) for blocks in grads_blocks]),
    )


def solution(mesh):
    dp_size, tensor_size = mesh.devices.shape
    rest = dp_size // LINE
    bits = tuple(f"r{number}" for number in range(rest.bit_length() - 1))
    shape = (LINE, *([2] * len(bits)), tensor_size)
    fine = Mesh(mesh.devices.reshape(shape), ("z", *bits, "t"))
    dp = ("z", *bits)
    rows = P((*dp, "t"), None)
    weight = P(None, dp, "t")

    def step(*args):
        return local(bits, *args)

    return jax.shard_map(
        step,
        mesh=fine,
        in_specs=(rows, rows, P(dp, None), P(), P(), weight, P(None, "t"), weight, weight, weight),
        out_specs=(rows, rows, P(), P(), weight, P(None, "t"), weight, weight, weight),
        check_vma=False,
    )
```

```python
import functools
import math

import jax
import jax.numpy as jnp
from jax import lax
from jax.experimental import pallas as pl
from jax.experimental.pallas import tpu as pltpu
from jax.sharding import Mesh
from jax.sharding import PartitionSpec as P

HD = 128
LINE = 4
LANES = 128
LOW = jnp.bfloat16
F32 = jnp.float32
MESH = pl.DeviceIdType.MESH


def doc_layout(lens, count):
    rows = jnp.arange(count, dtype=jnp.int32)
    doc = jnp.zeros((count,), jnp.int32)
    start = jnp.zeros((count,), jnp.int32)
    bound = jnp.int32(0)
    for number in range(lens.shape[0]):
        bound = bound + lens[number]
        after = (rows >= bound).astype(jnp.int32)
        doc = doc + after
        start = start + after * lens[number]
    positions = rows - start
    allowed = (doc[:, None] == doc[None, :]) & (rows[:, None] >= rows[None, :])
    return (positions, allowed)


def rope_tables(positions, width):
    index = jnp.arange(width // 2, dtype=F32)
    freq = jnp.exp(-(2.0 * index / width) * math.log(1000000.0))
    angle = positions.astype(F32)[:, None] * freq[None, :]
    return (
        jnp.concatenate([jnp.cos(angle)] * 2, axis=1),
        jnp.concatenate([jnp.sin(angle)] * 2, axis=1),
    )


def contract_last(left, right, out=F32):
    return lax.dot_general(left, right, (((1,), (1,)), ((), ())), preferred_element_type=out)


def contract_first(left, right, out=F32):
    return lax.dot_general(left, right, (((0,), (0,)), ((), ())), preferred_element_type=out)


def take(array, index, axis):
    return lax.dynamic_index_in_dim(array, index, axis, keepdims=False)


def greet(axes_targets, conditions):
    barrier = pltpu.get_barrier_semaphore()
    for (axis, target), condition in zip(axes_targets, conditions):
        def signal(axis=axis, target=target):
            pl.semaphore_signal(barrier, inc=1, device_id={axis: target}, device_id_type=MESH)
        if condition is None:
            signal()
        else:
            pl.when(condition)(signal)
    amount = sum(1 if c is None else c.astype(jnp.int32) for c in conditions)
    pl.semaphore_wait(barrier, amount)


def slot_of(line, values):
    slot = line
    for value in values:
        slot = slot * 2 + value
    return slot


def both(*conditions):
    given = [c for c in conditions if c is not None]
    return functools.reduce(jnp.logical_and, given) if given else None


def guarded(condition, action):
    if condition is None:
        action()
    else:
        pl.when(condition)(action)


def bit_flips(variant, stage, count):
    return [(variant >> b) & 1 for b in range(stage)] + [1] + [0] * (count - stage - 1)


class Gather:
    def __init__(self, size, bits, x_ref, out_ref, own_sem, line_sems, bit_sems, recv_sems):
        self.size, self.bits, self.count = size, bits, len(bits)
        self.x_ref, self.out_ref, self.own_sem = x_ref, out_ref, own_sem
        self.line_sems, self.bit_sems, self.recv_sems = line_sems, bit_sems, recv_sems
        self.z = lax.axis_index("z")
        self.mine = [lax.axis_index(bit) for bit in bits]
        self.own = slot_of(self.z, self.mine)
        self.pending, self.settled = [], False

    def copy(self, slot, first, axis, target, send_sem):
        return pltpu.make_async_remote_copy(
            src_ref=self.x_ref if first else self.out_ref.at[slot],
            dst_ref=self.out_ref.at[slot],
            send_sem=send_sem,
            recv_sem=self.recv_sems.at[slot],
            device_id={axis: target},
            device_id_type=MESH,
        )

    def start(self, condition, make):
        self.pending.append((condition, make))
        guarded(condition, lambda: make().start())

    def arrived(self, condition, slot, axis, target):
        guarded(
            condition,
            lambda: self.copy(slot, False, axis, target, self.line_sems.at[0, 0]).wait_recv(),
        )

    def spread(self, condition, slot, first, number, side, variant, after):
        for stage in range(after, self.count):
            self.start(
                condition,
                functools.partial(
                    self.copy,
                    slot,
                    first,
                    self.bits[stage],
                    1 - self.mine[stage],
                    self.bit_sems.at[number, side, variant, stage],
                ),
            )

    def line_of(self, number, side):
        line = self.z - number if side == 0 else self.z + number
        if number == 0:
            return line, None
        return line, (line >= 0 if side == 0 else line < self.size)

    def on_bits(self, number):
        for side in range(1 if number == 0 else 2):
            line, condition = self.line_of(number, side)
            for stage in range(self.count):
                for variant in range(2**stage):
                    flips = bit_flips(variant, stage, self.count)
                    slot = slot_of(line, [1 - m if f else m for m, f in zip(self.mine, flips)])
                    self.arrived(condition, slot, self.bits[stage], 1 - self.mine[stage])
                    code = sum(f << b for b, f in enumerate(flips))
                    self.spread(condition, slot, False, number, side, code, stage + 1)

    def begin(self):
        pltpu.make_async_copy(self.x_ref, self.out_ref.at[self.own], self.own_sem).start()
        z, size = self.z, self.size
        first = functools.partial(self.copy, self.own, True, "z")
        self.start(z < size - 1, functools.partial(first, z + 1, self.line_sems.at[0, 0]))
        self.start(z > 0, functools.partial(first, z - 1, self.line_sems.at[0, 1]))
        self.spread(None, self.own, True, 0, 0, 0, 0)

    def step(self, number):
        z, size = self.z, self.size
        for side in range(2):
            line, condition = self.line_of(number, side)
            slot = slot_of(line, self.mine)
            back = z - 1 if side == 0 else z + 1
            onto = z + 1 if side == 0 else z - 1
            self.arrived(condition, slot, "z", back)
            self.start(
                both(condition, onto < size if side == 0 else onto >= 0),
                functools.partial(self.copy, slot, False, "z", onto, self.line_sems.at[number, side]),
            )
            self.spread(condition, slot, False, number, side, 0, 0)

    def middle(self):
        for number in range(1, self.size):
            self.step(number)
            self.on_bits(number - 1)
        self.on_bits(self.size - 1)

    def settle(self):
        if not self.settled:
            pltpu.make_async_copy(self.x_ref, self.out_ref.at[self.own], self.own_sem).wait()
            self.settled = True

    def end(self):
        self.settle()
        for condition, make in self.pending:
            guarded(condition, lambda make=make: make().wait_send())


def gather_semaphores(size, bits):
    slots = size * 2 ** len(bits)
    return [
        pltpu.SemaphoreType.DMA,
        pltpu.SemaphoreType.DMA((size, 2)),
        pltpu.SemaphoreType.DMA((size, 2, 2 ** len(bits), len(bits))),
        pltpu.SemaphoreType.DMA((slots,)),
    ]


class Exchange:
    def __init__(self, size, bits, block, half, gu_ref, dn_ref, gu_out, dn_out, sems):
        self.size, self.bits, self.count = size, bits, len(bits)
        self.block, self.half = block, half
        self.gu_ref, self.dn_ref, self.gu_out, self.dn_out = gu_ref, dn_ref, gu_out, dn_out
        self.own_sems, self.line_sems, self.bit_sems, self.recv_sems = sems
        self.z = lax.axis_index("z")
        self.mine = [lax.axis_index(bit) for bit in bits]
        self.own = slot_of(self.z, self.mine)
        self.others = [lax.rem(self.z + o, size) for o in range(1, size)]
        self.pending = []

    def pieces(self, target, slot):
        low = pl.multiple_of(jnp.minimum(target * self.block, self.half - self.block), LANES)
        high = pl.multiple_of(low + self.half, LANES)
        width = self.block
        return [
            (self.gu_ref.at[:, pl.ds(low, width)], self.gu_out.at[slot, :, pl.ds(0, width)]),
            (self.gu_ref.at[:, pl.ds(high, width)], self.gu_out.at[slot, :, pl.ds(width, width)]),
            (self.dn_ref.at[:, pl.ds(low, width)], self.dn_out.at[slot]),
        ]

    def line_copy(self, place, piece, slot):
        source, landing = self.pieces(self.others[place], slot)[piece]
        return pltpu.make_async_remote_copy(
            src_ref=source,
            dst_ref=landing,
            send_sem=self.line_sems.at[place, piece],
            recv_sem=self.recv_sems.at[slot, piece],
            device_id={"z": self.others[place]},
            device_id_type=MESH,
        )

    def own_copy(self, piece):
        source, landing = self.pieces(self.z, self.own)[piece]
        return pltpu.make_async_copy(source, landing, self.own_sems.at[piece])

    def bit_copy(self, slot, piece, stage, send_sem):
        ref = (self.gu_out, None, self.dn_out)[piece]
        return pltpu.make_async_remote_copy(
            src_ref=ref.at[slot],
            dst_ref=ref.at[slot],
            send_sem=send_sem,
            recv_sem=self.recv_sems.at[slot, piece],
            device_id={self.bits[stage]: 1 - self.mine[stage]},
            device_id_type=MESH,
        )

    def first_copy(self, slot, piece, stage, send_sem):
        source, landing = self.pieces(self.z, slot)[piece]
        return pltpu.make_async_remote_copy(
            src_ref=source,
            dst_ref=landing,
            send_sem=send_sem,
            recv_sem=self.recv_sems.at[slot, piece],
            device_id={self.bits[stage]: 1 - self.mine[stage]},
            device_id_type=MESH,
        )

    def spread(self, slot, number, variant, after):
        for stage in range(after, self.count):
            for piece in (0, 2):
                make = functools.partial(
                    self.bit_copy, slot, piece, stage, self.bit_sems.at[number, variant, stage, piece]
                )
                self.pending.append(make)
                make().start()

    def on_bits(self, number):
        line = lax.rem(self.z - number + self.size, self.size)
        for stage in range(self.count):
            for variant in range(2**stage):
                flips = bit_flips(variant, stage, self.count)
                slot = slot_of(line, [1 - m if f else m for m, f in zip(self.mine, flips)])
                if number == 0 and variant == 0:
                    for piece in range(3):
                        self.first_copy(slot, piece, stage, self.own_sems.at[0]).wait_recv()
                else:
                    for piece in (0, 2):
                        self.bit_copy(slot, piece, stage, self.own_sems.at[0]).wait_recv()
                self.spread(slot, number, sum(f << b for b, f in enumerate(flips)), stage + 1)

    def begin(self):
        for stage in range(self.count):
            for piece in range(3):
                make = functools.partial(
                    self.first_copy, self.own, piece, stage, self.bit_sems.at[0, 0, stage, piece]
                )
                self.pending.append(make)
                make().start()
        for piece in range(3):
            self.own_copy(piece).start()

    def send(self, offset):
        for piece in range(3):
            self.line_copy(offset - 1, piece, self.own).start()

    def sent(self, offset):
        for piece in range(3):
            self.line_copy(offset - 1, piece, self.own).wait_send()

    def step(self, offset):
        slot = slot_of(lax.rem(self.z - offset + self.size, self.size), self.mine)
        for piece in range(3):
            self.line_copy(0, piece, slot).wait_recv()
        self.spread(slot, offset, 0, 0)

    def end(self):
        for piece in range(3):
            self.own_copy(piece).wait()
        for make in self.pending:
            make().wait_send()


class Fold:
    def __init__(self, size, bits, order, p_ref, own_buf, sums, stage_in, stage_out, own_sems, send_sems, recv_sems):
        self.size, self.bits, self.count, self.order = size, bits, len(bits), order
        self.last = self.count - 1
        self.p_ref, self.own_buf, self.sums = p_ref, own_buf, sums
        self.stage_in, self.stage_out = stage_in, stage_out
        self.own_sems, self.send_sems, self.recv_sems = own_sems, send_sems, recv_sems
        self.z = lax.axis_index("z")
        self.mine = [lax.axis_index(bit) for bit in bits]

    def line(self, place):
        return lax.rem(self.z + self.order[place], self.size)

    def index(self, place, stage, variant):
        return place * (2**self.count - 1) + 2**stage - 1 + variant

    def slot(self, place, variant, flip):
        flips = [(variant >> b) & 1 for b in range(self.last)] + [flip]
        return slot_of(self.line(place), [1 - m if f else m for m, f in zip(self.mine, flips)])

    def copy(self, place, stage, variant):
        index = self.index(place, stage, variant)
        if stage == self.last:
            source = self.p_ref.at[self.slot(place, variant, 1)]
        else:
            source = self.stage_out.at[place * (2**self.last - 1) + 2**stage - 1 + variant]
        return pltpu.make_async_remote_copy(
            src_ref=source,
            dst_ref=self.stage_in.at[index],
            send_sem=self.send_sems.at[index],
            recv_sem=self.recv_sems.at[index],
            device_id={self.bits[stage]: 1 - self.mine[stage]},
            device_id_type=MESH,
        )

    def own_copy(self, place, variant):
        number = place * 2**self.last + variant
        return pltpu.make_async_copy(
            self.p_ref.at[self.slot(place, variant, 0)], self.own_buf.at[number], self.own_sems.at[number]
        )

    def begin(self, places=None):
        for place in range(self.size) if places is None else places:
            for variant in reversed(range(2**self.last)):
                self.copy(place, self.last, variant).start()
                self.own_copy(place, variant).start()

    def stage(self, place, stage, done=None):
        for variant in reversed(range(2**stage)):
            if stage == self.last:
                self.own_copy(place, variant).wait()
                held = self.own_buf[place * 2**self.last + variant].astype(F32)
            else:
                held = self.sums[place * (2**self.last - 1) + 2**stage - 1 + variant]
            self.copy(place, stage, variant).wait_recv()
            total = held + self.stage_in[self.index(place, stage, variant)].astype(F32)
            if stage == 0:
                done(place, total)
                continue
            lower = variant & (2 ** (stage - 1) - 1)
            number = place * (2**self.last - 1) + 2 ** (stage - 1) - 1 + lower
            if variant >> (stage - 1):
                self.stage_out[number] = total.astype(LOW)
                self.copy(place, stage - 1, lower).start()
            else:
                self.sums[number] = total

    def end(self):
        for place in range(self.size):
            for stage in range(self.count):
                for variant in range(2**stage):
                    self.copy(place, stage, variant).wait_send()


def fold_scratch(size, bits, rows, columns):
    count = len(bits)
    inner, lower = size * (2**count - 1), size * (2 ** (count - 1) - 1)
    return [
        pltpu.VMEM((size * 2 ** (count - 1), rows, columns), LOW),
        pltpu.VMEM((max(lower, 1), rows, columns) if lower else (1, 8, LANES), F32),
        pltpu.VMEM((inner, rows, columns), LOW),
        pltpu.VMEM((max(lower, 1), rows, columns) if lower else (1, 16, LANES), LOW),
        pltpu.SemaphoreType.DMA((size * 2 ** (count - 1),)),
        pltpu.SemaphoreType.DMA((inner,)),
        pltpu.SemaphoreType.DMA((inner,)),
    ]


class Scatter:
    def __init__(self, size, bits, p_ref, out_ref, line_out, line_in, line_send, line_recv, *fold):
        order = list(range(1, size)) + [0]
        self.fold = Fold(size, bits, order, p_ref, *fold)
        self.size, self.out_ref = size, out_ref
        self.line_out, self.line_in, self.line_send, self.line_recv = line_out, line_in, line_send, line_recv

    def line_copy(self, place):
        return pltpu.make_async_remote_copy(
            src_ref=self.line_out.at[place],
            dst_ref=self.line_in.at[place],
            send_sem=self.line_send.at[place],
            recv_sem=self.line_recv.at[place],
            device_id={"z": self.fold.line(place)},
            device_id_type=MESH,
        )

    def done(self, place, total):
        if place < self.size - 1:
            self.line_out[place] = total.astype(LOW)
            self.line_copy(place).start()
        else:
            self.out_ref[...] = total

    def begin(self, places=None):
        self.fold.begin(places)

    def place(self, place):
        for stage in reversed(range(self.fold.count)):
            self.fold.stage(place, stage, self.done)

    def finish(self):
        for place in range(self.size - 1):
            self.line_copy(place).wait_recv()
            self.out_ref[...] += self.line_in[place].astype(F32)

    def end(self):
        self.fold.end()
        for place in range(self.size - 1):
            self.line_copy(place).wait_send()


def scatter_scratch(size, bits, rows, columns):
    return [
        pltpu.VMEM((size - 1, rows, columns), LOW),
        pltpu.VMEM((size - 1, rows, columns), LOW),
        pltpu.SemaphoreType.DMA((size - 1,)),
        pltpu.SemaphoreType.DMA((size - 1,)),
        *fold_scratch(size, bits, rows, columns),
    ]


SCATTER_REFS = 11


class Total:
    def __init__(self, size, bits, x_ref, out_ref, held, landed, send_sems, recv_sems):
        self.size, self.bits, self.count = size, bits, len(bits)
        self.x_ref, self.out_ref, self.held, self.landed = x_ref, out_ref, held, landed
        self.send_sems, self.recv_sems = send_sems, recv_sems
        self.z = lax.axis_index("z")
        self.others = [lax.rem(self.z + o, size) for o in range(1, size)]

    def copy(self, number):
        if number < self.count:
            axis = self.bits[number]
            source, target = self.held.at[number], {axis: 1 - lax.axis_index(axis)}
        else:
            source, target = self.held.at[self.count], {"z": self.others[number - self.count]}
        return pltpu.make_async_remote_copy(
            src_ref=source,
            dst_ref=self.landed.at[number],
            send_sem=self.send_sems.at[number],
            recv_sem=self.recv_sems.at[number],
            device_id=target,
            device_id_type=MESH,
        )

    def begin(self):
        self.held[0] = self.x_ref[...]
        self.copy(0).start()

    def pair(self, number):
        self.copy(number).wait_recv()
        self.held[number + 1] = self.held[number] + self.landed[number]
        if number + 1 < self.count:
            self.copy(number + 1).start()
        else:
            for place in range(self.size - 1):
                self.copy(self.count + place).start()

    def finish(self):
        for place in range(self.size - 1):
            self.copy(self.count + place).wait_recv()
        total = jnp.zeros(self.out_ref.shape, self.out_ref.dtype)
        for line in range(self.size):
            offset = lax.rem(line - self.z + self.size, self.size)
            part = self.held[self.count]
            for o in range(1, self.size):
                part = jnp.where(offset == o, self.landed[self.count + self.size - o - 1], part)
            total = total + part
        self.out_ref[...] = total

    def end(self):
        for number in range(self.count + self.size - 1):
            self.copy(number).wait_send()


def greet_all(size, axes):
    z = lax.axis_index("z")
    greet(
        [("z", lax.rem(z + o, size)) for o in range(1, size)]
        + [(axis, 1 - lax.axis_index(axis)) for axis in axes],
        [None] * (size - 1 + len(axes)),
    )


def in_groups(refs, sizes):
    groups, at = [], 0
    for number in sizes:
        groups.append(refs[at : at + number])
        at += number
    return groups


def comm_params(collective_id):
    return pltpu.CompilerParams(
        collective_id=collective_id, has_side_effects=True, vmem_limit_bytes=60 * 2**20
    )


def at_microseconds(time):
    return pl.CostEstimate(flops=0, transcendentals=0, bytes_accessed=time * 3500000)


class Attend:
    def __init__(self, rows_ref, gain_ref, bias_ref, cos_ref, sin_ref, mask_ref, w_ref, outs, scratch, width, epsilon=1e-06):
        self.gain_ref, self.bias_ref, self.w_ref = gain_ref, bias_ref, w_ref
        self.cos_ref, self.sin_ref, self.mask_ref = cos_ref, sin_ref, mask_ref
        self.state_ref, self.middle_ref, self.xa_ref, self.q_ref, self.k_ref, self.v_ref, self.lse_ref, self.o_ref = outs
        self.send_buf, self.land_buf, self.send_sems, self.recv_sems = scratch
        self.rows_ref = rows_ref
        self.t = lax.axis_index("t")
        self.slots, self.few = w_ref.shape[0], w_ref.shape[1]
        self.model = self.slots * self.few
        self.count = rows_ref.shape[0]
        self.q_width = self.q_ref.shape[1]
        self.width = width
        self.epsilon = epsilon

    def normed(self, rows, gain_ref):
        factor = lax.rsqrt(jnp.mean(rows * rows, axis=-1, keepdims=True) + self.epsilon)
        return (rows * factor * gain_ref[...]).astype(LOW)

    def xa_copy(self):
        return pltpu.make_async_remote_copy(
            src_ref=self.xa_ref.at[self.t],
            dst_ref=self.xa_ref.at[self.t],
            send_sem=self.send_sems.at[0],
            recv_sem=self.recv_sems.at[0],
            device_id={"t": 1 - self.t},
            device_id_type=MESH,
        )

    def xa_landing(self):
        return pltpu.make_async_remote_copy(
            src_ref=self.xa_ref.at[1 - self.t],
            dst_ref=self.xa_ref.at[1 - self.t],
            send_sem=self.send_sems.at[0],
            recv_sem=self.recv_sems.at[0],
            device_id={"t": 1 - self.t},
            device_id_type=MESH,
        )

    def half_copy(self):
        return pltpu.make_async_remote_copy(
            src_ref=self.send_buf,
            dst_ref=self.land_buf,
            send_sem=self.send_sems.at[1],
            recv_sem=self.recv_sems.at[1],
            device_id={"t": 1 - self.t},
            device_id_type=MESH,
        )

    def begin(self, state):
        self.state_ref[...] = state
        self.xa_ref[self.t] = self.normed(state, self.gain_ref)
        self.xa_copy().start()

    def columns(self, low, count):
        weight = self.w_ref[:, :, low : low + count].reshape(self.model, count)
        xa = self.xa_ref[...].reshape(2 * self.count, self.model)
        return jnp.dot(xa, weight, preferred_element_type=F32) + self.bias_ref[:, low : low + count]

    def rope(self, values):
        return (values * self.cos_ref[...] + pltpu.roll(values, HD // 2, 1) * self.sin_ref[...]).astype(LOW)

    def keys(self):
        self.xa_landing().wait_recv()
        both_kv = self.columns(self.q_width, 2 * HD)
        self.k_ref[...] = self.rope(both_kv[:, :HD])
        self.v_ref[...] = both_kv[:, HD:].astype(LOW)

    def heads(self, first):
        lin = self.columns(first * HD, 2 * HD)
        for number in range(2):
            head = first + number
            low = head * HD
            query = self.rope(lin[:, number * HD : (number + 1) * HD])
            self.q_ref[:, low : low + HD] = query
            raw = lax.dot_general(
                query, self.k_ref[...], (((1,), (1,)), ((), ())), preferred_element_type=F32
            )
            scores = jnp.where(self.mask_ref[...] > 0, raw * (1.0 / math.sqrt(HD)), -1e30)
            top = jnp.max(scores, axis=-1, keepdims=True)
            expo = jnp.exp(scores - top)
            whole = jnp.sum(expo, axis=-1, keepdims=True)
            probs = (expo / whole).astype(LOW)
            self.lse_ref[head] = top + jnp.log(whole)
            out = jnp.dot(probs, self.v_ref[...], preferred_element_type=F32).astype(LOW)
            self.o_ref[0, :, low : low + HD] = out[: self.count]
            self.o_ref[1, :, low : low + HD] = out[self.count :]

    def projected(self, half, step):
        left = self.o_ref[half]
        for low in range(0, self.slots, step):
            weight = self.w_ref[low : low + step, :, self.width :].reshape(step * self.few, self.q_width)
            yield low * self.few, lax.dot_general(
                left, weight, (((1,), (1,)), ((), ())), preferred_element_type=F32
            )

    def other_half(self):
        for low, part in self.projected(1 - self.t, self.slots // 4):
            self.send_buf[:, low : low + part.shape[1]] = part.astype(LOW)
        self.half_copy().start()

    def own_half(self):
        for low, part in self.projected(self.t, self.slots // 4):
            where = slice(low, low + part.shape[1])
            self.middle_ref[:, where] = self.state_ref[:, where] + part

    def finish(self, gain_ref, xf_ref):
        self.half_copy().wait_recv()
        middle = self.middle_ref[...] + self.land_buf[...].astype(F32)
        self.middle_ref[...] = middle
        xf_ref[...] = self.normed(middle, gain_ref)

    def end(self):
        self.xa_copy().wait_send()
        self.half_copy().wait_send()


def front_kernel(size, bits, block, half, layer, width, *refs):
    first = layer == 0
    inputs, outs, refs = in_groups(refs, [11, 13 if first else 12, len(refs)])
    (x_ref, more_ref, ga_ref, gf_ref, bias_ref, cos_ref, sin_ref, mask_ref, at_ref, gu_ref, dn_ref) = inputs
    xf_out, gu_out, dn_out, at_out = outs[8:12]
    (w_ref, xf_ref, at_sem), pair, at_sems, feed_sems, rows_sems, rest = in_groups(
        refs, [3, 4, 4, 4, 4, len(refs)]
    )
    greet_all(size, ("t", *bits))
    work = Attend(
        x_ref, ga_ref, bias_ref, cos_ref, sin_ref, mask_ref, w_ref, outs[:8], pair, width
    )
    attention = Gather(size, bits, at_ref, w_ref, *at_sems)
    feed = Exchange(
        size, bits, block, half, gu_ref.at[layer], dn_ref.at[layer], gu_out, dn_out, feed_sems
    )
    rows = Gather(size, ("t",), xf_ref, xf_out, *rows_sems)
    kept = pltpu.make_async_copy(w_ref, at_out, at_sem)
    if first:
        side = Gather(size, ("t",), more_ref, outs[12], *rest)
        attention.begin()
        side.begin()
        feed.begin()
        work.begin(x_ref[...].astype(F32))
        attention.step(1)
        side.step(1)
        attention.step(2)
        attention.on_bits(0)
        side.on_bits(0)
        side.step(2)
        feed.send(1)
        attention.step(3)
        attention.on_bits(1)
        side.on_bits(1)
        side.step(3)
        feed.on_bits(0)
        attention.on_bits(2)
        feed.sent(1)
        feed.send(3)
        feed.step(1)
        attention.on_bits(3)
        attention.settle()
        work.keys()
        work.heads(0)
        side.on_bits(2)
        side.on_bits(3)
    else:
        total_ref, *rest = rest
        side = Scatter(size, ("t",), more_ref, total_ref, *rest)
        attention.begin()
        side.begin()
        feed.begin()
        side.place(0)
        attention.step(1)
        side.place(1)
        attention.step(2)
        attention.on_bits(0)
        side.place(2)
        attention.step(3)
        attention.on_bits(1)
        side.place(3)
        feed.send(1)
        attention.on_bits(2)
        attention.on_bits(3)
        attention.settle()
        side.finish()
        work.begin(x_ref[...] + total_ref[...])
        feed.on_bits(0)
        feed.sent(1)
        feed.send(3)
        feed.step(1)
        work.keys()
        work.heads(0)
    kept.start()
    feed.sent(3)
    feed.send(2)
    feed.step(3)
    feed.on_bits(1)
    work.heads(2)
    work.heads(4)
    work.other_half()
    work.own_half()
    work.finish(gf_ref, xf_ref)
    rows.begin()
    rows.step(1)
    rows.on_bits(0)
    rows.step(2)
    feed.sent(2)
    feed.step(2)
    rows.on_bits(1)
    feed.on_bits(3)
    rows.step(3)
    rows.on_bits(2)
    feed.on_bits(2)
    rows.on_bits(3)
    kept.wait()
    for steps in (attention, side, feed, work, rows):
        steps.end()


def front(x, more, gains, bias, tables, at, gu, dn, layer, size, bits, block, width, collective_id):
    slots = size * 2 ** len(bits)
    count, model = x.shape
    few, half = dn.shape[1:]
    length = 2 * count
    q_width = at.shape[1] - width
    first = layer == 0
    held, far = pl.BlockSpec(memory_space=pltpu.VMEM), pl.BlockSpec(memory_space=pl.ANY)
    shape = jax.ShapeDtypeStruct
    more_scratch = (
        gather_semaphores(size, ("t",))
        if first
        else [pltpu.VMEM((count, model), F32), *scatter_scratch(size, ("t",), count, model)]
    )
    return pl.pallas_call(
        functools.partial(front_kernel, size, bits, block, half, layer, width),
        out_shape=(
            shape((count, model), F32),
            shape((count, model), F32),
            shape((2, count, model), LOW),
            shape((length, q_width), LOW),
            shape((length, HD), LOW),
            shape((length, HD), LOW),
            shape((q_width // HD, length, 1), F32),
            shape((2, count, q_width), LOW),
            shape((2 * size, count, model), LOW),
            shape((slots, few, 2 * block), LOW),
            shape((slots, few, block), LOW),
            shape((slots, few, at.shape[1]), LOW),
            *([shape((2 * size, count, model), LOW)] if first else []),
        ),
        in_specs=[held, far] + [held] * 6 + [far] * 3,
        out_specs=[held] * 8 + [far] * (5 if first else 4),
        scratch_shapes=[
            pltpu.VMEM((slots, few, at.shape[1]), LOW),
            pltpu.VMEM((count, model), LOW),
            pltpu.SemaphoreType.DMA,
            pltpu.VMEM((count, model), LOW),
            pltpu.VMEM((count, model), LOW),
            pltpu.SemaphoreType.DMA((2,)),
            pltpu.SemaphoreType.DMA((2,)),
            *gather_semaphores(size, bits),
            pltpu.SemaphoreType.DMA((3,)),
            pltpu.SemaphoreType.DMA((size - 1, 3)),
            pltpu.SemaphoreType.DMA((size, 2 ** len(bits), len(bits), 3)),
            pltpu.SemaphoreType.DMA((slots, 3)),
            *gather_semaphores(size, ("t",)),
            *more_scratch,
        ],
        compiler_params=comm_params(collective_id),
        cost_estimate=at_microseconds(150),
    )(x, more, *gains, bias, *tables, at, gu, dn)


class AttendBack:
    def __init__(self, ins, outs, scratch, width, epsilon=1e-06):
        (self.g_ref, self.state_ref, self.middle_ref, self.ga_gain, self.gf_gain, self.cos_ref, self.sin_ref) = ins[:7]
        (self.mask_ref, self.q_ref, self.k_ref, self.v_ref, self.lse_ref, self.xa_ref, self.o_ref, self.far_w) = ins[7:]
        (self.grad_ref, self.ga_ref, self.lin_ref, self.bias_ref, self.pa_ref, self.pf_ref) = outs
        (self.w_ref, self.w_sem, self.dk, self.dv, self.sum_buf, self.send_buf, self.land_buf) = scratch[:7]
        (self.send_sems, self.recv_sems) = scratch[7:]
        self.t = lax.axis_index("t")
        self.slots, self.few = self.w_ref.shape[:2]
        self.model = self.slots * self.few
        self.count = self.state_ref.shape[0]
        self.q_width = self.q_ref.shape[1]
        self.width, self.epsilon = width, epsilon

    def pair_copy(self, number, source, landing):
        return pltpu.make_async_remote_copy(
            src_ref=source,
            dst_ref=landing,
            send_sem=self.send_sems.at[number],
            recv_sem=self.recv_sems.at[number],
            device_id={"t": 1 - self.t},
            device_id_type=MESH,
        )

    def ga_copy(self, side):
        return self.pair_copy(0, self.ga_ref.at[side], self.ga_ref.at[side])

    def half_copy(self):
        return self.pair_copy(1, self.send_buf, self.land_buf)

    def weight_copy(self):
        return pltpu.make_async_copy(self.far_w, self.w_ref, self.w_sem)

    def norm_back(self, upstream, rows, gain):
        factor = lax.rsqrt(jnp.mean(rows * rows, axis=-1, keepdims=True) + self.epsilon)
        scaled = upstream * gain
        part = jnp.sum(upstream * rows * factor, axis=0, keepdims=True)
        inner = jnp.mean(scaled * rows, axis=-1, keepdims=True)
        return factor * scaled - rows * factor**3 * inner, part

    def prepare(self):
        self.weight_copy().start()

    def begin(self, d_xf):
        d_mid, part = self.norm_back(d_xf, self.middle_ref[...], self.gf_gain[...])
        self.pf_ref[...] = part
        grad = self.g_ref[...].astype(F32) + d_mid
        self.grad_ref[...] = grad
        self.ga_ref[self.t] = grad.astype(LOW)
        self.ga_copy(self.t).start()
        self.dk[...] = jnp.zeros_like(self.dk)
        self.dv[...] = jnp.zeros_like(self.dv)

    def arrive(self):
        self.weight_copy().wait()
        self.ga_copy(1 - self.t).wait_recv()

    def unrope(self, values):
        return values * self.cos_ref[...] - pltpu.roll(values, HD // 2, 1) * self.sin_ref[...]

    def keep(self, low, values):
        count = values.shape[1]
        self.bias_ref[:, low : low + count] = jnp.sum(values, axis=0, keepdims=True)
        values = values.astype(LOW)
        self.lin_ref[0, :, low : low + count] = values[: self.count]
        self.lin_ref[1, :, low : low + count] = values[self.count :]

    def heads(self, first):
        low, count = self.width + first * HD, 2 * HD
        weight = self.w_ref[:, :, low : low + count].reshape(self.model, count)
        above = self.ga_ref[...].reshape(2 * self.count, self.model)
        d_out = jnp.dot(above, weight, preferred_element_type=F32).astype(LOW)
        key, value = self.k_ref[...], self.v_ref[...]
        last = (((1,), (1,)), ((), ()))
        early = (((0,), (0,)), ((), ()))
        scale = 1.0 / math.sqrt(HD)
        for number in range(2):
            head = first + number
            query = self.q_ref[:, head * HD : (head + 1) * HD]
            d_head = d_out[:, number * HD : (number + 1) * HD]
            raw = lax.dot_general(query, key, last, preferred_element_type=F32)
            scores = jnp.where(self.mask_ref[...] > 0, raw * scale, -1e30)
            probs = jnp.exp(scores - self.lse_ref[head])
            d_probs = lax.dot_general(d_head, value, last, preferred_element_type=F32)
            centre = jnp.sum(probs * d_probs, axis=-1, keepdims=True)
            d_raw = (probs * (d_probs - centre) * scale).astype(LOW)
            d_query = jnp.dot(d_raw, key, preferred_element_type=F32)
            self.dk[...] += lax.dot_general(d_raw, query, early, preferred_element_type=F32)
            self.dv[...] += lax.dot_general(
                probs.astype(LOW), d_head, early, preferred_element_type=F32
            )
            self.keep(head * HD, self.unrope(d_query))

    def keys(self):
        self.keep(self.q_width, self.unrope(self.dk[...]))
        self.keep(self.q_width + HD, self.dv[...])

    def projected(self, half):
        left, step = self.lin_ref[half], self.slots // 4
        for low in range(0, self.slots, step):
            weight = self.w_ref[low : low + step, :, : self.width].reshape(step * self.few, self.width)
            yield slice(low * self.few, (low + step) * self.few), lax.dot_general(
                left, weight, (((1,), (1,)), ((), ())), preferred_element_type=F32
            )

    def other_half(self):
        for where, part in self.projected(1 - self.t):
            self.send_buf[:, where] = part.astype(LOW)
        self.half_copy().start()

    def own_half(self):
        for where, part in self.projected(self.t):
            self.sum_buf[:, where] = part

    def gradients(self):
        step = self.slots // 4
        early = (((0,), (0,)), ((), ()))
        pairs = ((self.xa_ref, self.lin_ref, 0, self.width), (self.ga_ref, self.o_ref, self.width, self.q_width))
        for left_ref, right_ref, low, count in pairs:
            right = right_ref[...].reshape(2 * self.count, count)
            for slot in range(0, self.slots, step):
                where = slice(slot * self.few, (slot + step) * self.few)
                left = left_ref[:, :, where].reshape(2 * self.count, step * self.few)
                part = lax.dot_general(left, right, early, preferred_element_type=F32)
                self.w_ref[slot : slot + step, :, low : low + count] = part.astype(LOW).reshape(
                    step, self.few, count
                )

    def finish(self):
        self.half_copy().wait_recv()
        d_xa = self.sum_buf[...] + self.land_buf[...].astype(F32)
        d_in, part = self.norm_back(d_xa, self.state_ref[...], self.ga_gain[...])
        self.pa_ref[...] = part
        grad = self.grad_ref[...] + d_in
        self.grad_ref[...] = grad
        return grad

    def end(self):
        self.ga_copy(self.t).wait_send()
        self.half_copy().wait_send()


class Blocks:
    def __init__(self, size, bits, gu_ref, dn_ref, out_ref, gu_fold, dn_fold, done, sems):
        self.size, self.out_ref = size, out_ref
        order = list(range(1, size)) + [0]
        self.folds = [Fold(size, bits, order, gu_ref, *gu_fold), Fold(size, bits, order, dn_ref, *dn_fold)]
        self.done = done
        self.own_sems, self.send_sems, self.recv_sems = sems
        self.width, self.narrow = gu_ref.shape[2], dn_ref.shape[2]
        self.z = lax.axis_index("z")

    def landing(self, number, slot):
        low, count = ((0, self.width), (self.width, self.narrow))[number]
        return self.out_ref.at[slot, :, pl.ds(low, count)]

    def line_copy(self, number, place, slot):
        return pltpu.make_async_remote_copy(
            src_ref=self.done[number].at[place],
            dst_ref=self.landing(number, slot),
            send_sem=self.send_sems.at[number, place],
            recv_sem=self.recv_sems.at[number, slot],
            device_id={"z": self.folds[0].line(place)},
            device_id_type=MESH,
        )

    def own_copy(self, number):
        return pltpu.make_async_copy(
            self.done[number].at[self.size - 1], self.landing(number, self.z), self.own_sems.at[number]
        )

    def begin(self):
        for fold in self.folds:
            fold.begin()

    def inner(self, place):
        for stage in reversed(range(1, self.folds[0].count)):
            for fold in self.folds:
                fold.stage(place, stage)

    def send(self, place):
        for number, fold in enumerate(self.folds):

            def keep(place, total, number=number):
                self.done[number][place] = total.astype(LOW)
                if place < self.size - 1:
                    self.line_copy(number, place, self.z).start()
                else:
                    self.own_copy(number).start()

            fold.stage(place, 0, keep)

    def end(self):
        for number, fold in enumerate(self.folds):
            for offset in range(1, self.size):
                slot = lax.rem(self.z - offset + self.size, self.size)
                self.line_copy(number, 0, slot).wait_recv()
            for place in range(self.size - 1):
                self.line_copy(number, place, self.z).wait_send()
            self.own_copy(number).wait()
            fold.end()


def back_kernel(size, bits, width, final, *refs):
    top, bottom = final
    counts = [1, 1 if top else 0, 2, 15, 3 if bottom else 0, 6, 2, 1 if top else 0, 1]
    p_ref, branch_ref, wide, ins, above, outs, (blocks_ref, attn_ref), branch_out, more_out, refs = (
        in_groups(refs, counts + [len(refs)])
    )
    (dxf_ref,), dxf_scratch, gu_fold, dn_fold, done, sems, work_scratch, refs = in_groups(
        refs, [1, SCATTER_REFS, 7, 7, 2, 3, 9, len(refs)]
    )
    greet_all(size, ("t", *bits))
    rows = Scatter(size, ("t",), p_ref[0], dxf_ref, *dxf_scratch)
    blocks = Blocks(size, bits, *wide, blocks_ref, gu_fold, dn_fold, done, sems)
    work = AttendBack(ins, outs, work_scratch, width)
    branch = None
    if top:
        branch_scratch, refs = in_groups(refs, [SCATTER_REFS, len(refs)])
        branch = Scatter(size, ("t",), branch_ref[0], branch_out[0], *branch_scratch)
    if not bottom:
        gm_ref, kept_sem, *gm_sems = refs
        onward = Gather(size, ("t",), gm_ref, more_out[0], *gm_sems)
        kept = pltpu.make_async_copy(work.w_ref, attn_ref, kept_sem)
    else:
        attn_scratch, (x_ref, *small_scratch) = in_groups(refs, [SCATTER_REFS, len(refs)])
        final = Scatter(size, bits, work.w_ref, attn_ref, *attn_scratch)
        small = Total(size, ("t", *bits), x_ref, more_out[0], *small_scratch)
    rows.begin()
    blocks.begin()
    work.prepare()
    blocks.inner(0)
    rows.place(0)
    blocks.inner(1)
    blocks.inner(2)
    rows.place(1)
    blocks.inner(3)
    blocks.send(0)
    rows.place(2)
    rows.place(3)
    if top:
        branch.begin([0])
    rows.finish()
    blocks.send(1)
    work.begin(dxf_ref[...])
    if top:
        branch.begin([1])
    work.arrive()
    work.heads(0)
    if top:
        branch.place(0)
    work.heads(2)
    blocks.send(2)
    work.heads(4)
    work.keys()
    work.other_half()
    if top:
        branch.place(1)
        branch.begin([2])
    work.own_half()
    blocks.send(3)
    work.gradients()
    if bottom:
        final.begin()
    else:
        kept.start()
    grad = work.finish()
    if bottom:
        pa_above, pf_above, bias_above = above
        x_ref[...] = jnp.zeros_like(x_ref)
        x_ref[0:1, :] = work.pa_ref[...]
        x_ref[1:2, :] = pa_above[...]
        x_ref[2:3, :] = work.pf_ref[...]
        x_ref[3:4, :] = pf_above[...]
        for side in range(2):
            mine = (work.t == side).astype(F32)
            x_ref[4 + 2 * side : 5 + 2 * side, : work.width] = work.bias_ref[...] * mine
            x_ref[5 + 2 * side : 6 + 2 * side, : work.width] = bias_above[...] * mine
        small.begin()
        for place in range(size):
            final.place(place)
            if place <= len(bits):
                small.pair(place)
        for number in range(size, len(bits) + 1):
            small.pair(number)
        final.finish()
        small.finish()
    if not bottom:
        gm_ref[...] = grad.astype(LOW)
        onward.begin()
    if top:
        branch.begin([3])
        branch.place(2)
    if not bottom:
        onward.step(1)
        onward.on_bits(0)
    if top:
        branch.place(3)
    if not bottom:
        onward.step(2)
        onward.on_bits(1)
        onward.step(3)
        onward.on_bits(2)
        onward.on_bits(3)
    if top:
        branch.finish()
    for steps in (rows, blocks, work, *((final, small) if bottom else (onward,)), branch):
        if steps is not None:
            steps.end()
    if not bottom:
        kept.wait()


def back(partial, branch, gu, dn, ins, above, size, bits, width, collective_id):
    count, model = ins[1].shape
    length, q_width = ins[8].shape
    slots, few, wide = gu.shape
    narrow = dn.shape[2]
    top, bottom = branch is not None, bool(above)
    number = len(bits) + 1
    weight = ins[14].shape
    held, far = pl.BlockSpec(memory_space=pltpu.VMEM), pl.BlockSpec(memory_space=pl.ANY)
    shape = jax.ShapeDtypeStruct
    rows_scratch = scatter_scratch(size, ("t",), count, model)
    return pl.pallas_call(
        functools.partial(back_kernel, size, bits, width, (top, bottom)),
        out_shape=(
            shape((count, model), F32),
            shape((2, count, model), LOW),
            shape((2, count, width), LOW),
            shape((1, width), F32),
            shape((1, model), F32),
            shape((1, model), F32),
            shape((size, few, wide + narrow), LOW),
            shape(weight[1:], F32) if bottom else shape(weight, LOW),
            *([shape((count, model), F32)] if top else []),
            shape((8, model), F32) if bottom else shape((2 * size, count, model), LOW),
        ),
        in_specs=[far] * (4 if top else 3) + [held] * 14 + [far] + [held] * len(above),
        out_specs=[held] * 6 + [far, held if bottom else far] + [held] * top + [held if bottom else far],
        scratch_shapes=[
            pltpu.VMEM((count, model), F32),
            *rows_scratch,
            *fold_scratch(size, bits, few, wide),
            *fold_scratch(size, bits, few, narrow),
            pltpu.VMEM((size, few, wide), LOW),
            pltpu.VMEM((size, few, narrow), LOW),
            pltpu.SemaphoreType.DMA((2,)),
            pltpu.SemaphoreType.DMA((2, size)),
            pltpu.SemaphoreType.DMA((2, size)),
            pltpu.VMEM(weight, LOW),
            pltpu.SemaphoreType.DMA,
            pltpu.VMEM((length, HD), F32),
            pltpu.VMEM((length, HD), F32),
            pltpu.VMEM((count, model), F32),
            pltpu.VMEM((count, model), LOW),
            pltpu.VMEM((count, model), LOW),
            pltpu.SemaphoreType.DMA((2,)),
            pltpu.SemaphoreType.DMA((2,)),
            *(rows_scratch if top else []),
            *(
                [
                    *scatter_scratch(size, bits, *weight[1:]),
                    pltpu.VMEM((8, model), F32),
                    pltpu.VMEM((number + 1, 8, model), F32),
                    pltpu.VMEM((number + size - 1, 8, model), F32),
                    pltpu.SemaphoreType.DMA((number + size - 1,)),
                    pltpu.SemaphoreType.DMA((number + size - 1,)),
                ]
                if bottom
                else [
                    pltpu.VMEM((count, model), LOW),
                    pltpu.SemaphoreType.DMA,
                    *gather_semaphores(size, ("t",)),
                ]
            ),
        ],
        compiler_params=comm_params(collective_id),
        cost_estimate=at_microseconds(120),
    )(partial, *([branch] if top else []), gu, dn, *ins, *above)


def settle_kernel(half, width, *refs):
    *blocks, attn_low, attn_high, gu_ref, dn_ref, qkv_ref, out_ref = refs
    block = blocks[0].shape[2] // 3
    for layer, ref in enumerate(blocks):
        for line in range(LINE):
            low = block_start(line, block, half)
            skip = line * block - low
            for part in range(2):
                piece = ref[line, :, part * block + skip : (part + 1) * block].astype(F32)
                gu_ref[layer, :, part * half + low + skip : part * half + low + block] = piece
            dn_ref[layer, :, low + skip : low + block] = ref[line, :, 2 * block + skip :].astype(F32)
    for layer, ref in enumerate((attn_low, attn_high)):
        qkv_ref[layer] = ref[:, :width].astype(F32)
        out_ref[layer] = ref[:, width:].astype(F32)


def settle(blocks, attn, half, width):
    few = attn[0].shape[0]
    shape = jax.ShapeDtypeStruct
    return pl.pallas_call(
        functools.partial(settle_kernel, half, width),
        out_shape=(
            shape((2, few, 2 * half), F32),
            shape((2, few, half), F32),
            shape((2, few, width), F32),
            shape((2, few, attn[0].shape[1] - width), F32),
        ),
        compiler_params=pltpu.CompilerParams(vmem_limit_bytes=56 * 2**20),
    )(*blocks, *attn)


def in_slots(partial, slots):
    return partial.reshape(slots, -1, partial.shape[1])


def block_width(half):
    return -(-half // (LINE * LANES)) * LANES


def block_start(line, block, half):
    return min(line * block, half - block)


def local(
    bits, tokens, cotangent, doc_lengths, norm_attn, norm_ffn, w_qkv, b_qkv, w_out, w_gateup, w_down
):
    dp = ("z", *bits)
    tensor_size = lax.axis_size("t")
    count = tokens.shape[0]
    length = count * tensor_size
    layers = w_qkv.shape[0]
    qkv_width = w_qkv.shape[2]
    rows = w_qkv.shape[1]
    half = w_down.shape[2]
    block = block_width(half)
    positions, allowed = doc_layout(doc_lengths[0], length)
    cosine, sine = rope_tables(positions, HD)
    turned = jnp.where(jnp.arange(HD) < HD // 2, -sine, sine)
    tables = (cosine, turned, allowed.astype(F32))
    gain_attn = norm_attn.astype(F32)
    gain_ffn = norm_ffn.astype(F32)
    bias_all = b_qkv.astype(F32)
    line = lax.axis_index("z")
    valid = jnp.arange(block) >= line * block - jnp.minimum(line * block, half - block)
    saved = []
    for layer in range(layers):
        flat = jnp.concatenate([w_qkv[layer], w_out[layer]], axis=1)
        start, more = (tokens, cotangent) if layer == 0 else (middle, in_slots(partial, 2 * LINE))
        gains = (gain_attn[layer : layer + 1], gain_ffn[layer : layer + 1])
        out = front(
            start, more, gains, bias_all[layer : layer + 1], tables, flat, w_gateup, w_down,
            layer, LINE, bits, block, qkv_width, 8 + layer,
        )
        if layer == 0:
            gm_all = out[12].reshape(-1, cotangent.shape[1])
        (state, middle, xa_all, query, key, value, log_total, attended) = out[:8]
        xf_all, gu_w, down_w = (item.reshape(-1, item.shape[2]) for item in out[8:11])
        both_w = out[11]
        gate_up = jnp.dot(xf_all, gu_w, preferred_element_type=F32)
        gate = gate_up[:, :block]
        up = gate_up[:, block:]
        act = jnp.where(valid, jax.nn.silu(gate) * up, 0.0).astype(LOW)
        partial = contract_last(act, down_w, LOW)
        saved.append(
            (state, xa_all, query, key, value, log_total, attended)
            + (middle, xf_all, gate, up, act, gu_w, down_w, both_w)
        )
    grad, branch, above = cotangent, in_slots(partial, 2 * LINE), []
    grads_attn, grads_blocks = [], []
    for layer in reversed(range(layers)):
        (state_in, xa_all, query, key, value, log_total, attended) = saved[layer][:7]
        (middle, xf_all, gate, up, act, gu_w, down_w, both_w) = saved[layer][7:]
        d_down = contract_first(gm_all, act, LOW)
        d_act = jnp.dot(gm_all, down_w, preferred_element_type=F32)
        sig = jax.nn.sigmoid(gate)
        d_gate = d_act * up * sig * (1.0 + gate * (1.0 - sig))
        d_up = d_act * gate * sig
        d_gu = jnp.concatenate(
            [jnp.where(valid, d_gate, 0.0), jnp.where(valid, d_up, 0.0)], axis=1
        ).astype(LOW)
        d_gateup = contract_first(xf_all, d_gu, LOW)
        partial = in_slots(contract_last(d_gu, gu_w, LOW), 2 * LINE)
        wide = (in_slots(d_gateup, d_gateup.shape[0] // rows), in_slots(d_down, d_down.shape[0] // rows))
        gains = (gain_attn[layer : layer + 1], gain_ffn[layer : layer + 1])
        ins = (grad, state_in, middle, *gains, *tables, query, key, value, log_total, xa_all, attended, both_w)
        out = back(
            partial, branch, *wide, ins, above if layer == 0 else [], LINE, bits, qkv_width, 16 + layer
        )
        (grad, _, _, d_bias, part_a, part_f, blocks, d_attn), rest = out[:8], out[8:]
        grads_blocks.append(blocks)
        if branch is not None:
            output = (middle + rest[0]).astype(LOW)
            branch = None
        if layer > 0:
            gm_all = rest[-1].reshape(-1, rest[-1].shape[2])
            above = [part_a, part_f, d_bias]
            d_attn = lax.psum_scatter(
                d_attn.reshape(-1, d_attn.shape[2]), dp, scatter_dimension=0, tiled=True
            )
        grads_attn.append(d_attn)
    sums = rest[-1]
    side = lax.axis_index("t")
    d_gu_all, d_dn_all, d_qkv_all, d_out_all = settle(grads_blocks[::-1], grads_attn[::-1], half, qkv_width)
    return (
        output,
        grad,
        sums[0:2],
        sums[2:4],
        d_qkv_all,
        lax.dynamic_slice_in_dim(sums, 4 + 2 * side, 2, 0)[:, :qkv_width],
        d_out_all,
        d_gu_all,
        d_dn_all,
    )


def solution(mesh):
    dp_size, tensor_size = mesh.devices.shape
    rest = dp_size // LINE
    bits = tuple(f"r{number}" for number in range(rest.bit_length() - 1))
    shape = (LINE, *([2] * len(bits)), tensor_size)
    fine = Mesh(mesh.devices.reshape(shape), ("z", *bits, "t"))
    dp = ("z", *bits)
    rows = P((*dp, "t"), None)
    weight = P(None, dp, "t")

    def step(*args):
        return local(bits, *args)

    return jax.shard_map(
        step,
        mesh=fine,
        in_specs=(rows, rows, P(dp, None), P(), P(), weight, P(None, "t"), weight, weight, weight),
        out_specs=(rows, rows, P(), P(), weight, P(None, "t"), weight, weight, weight),
        check_vma=False,
    )
```

```python
import functools
import math

import jax
import jax.numpy as jnp
from jax import lax
from jax.experimental import pallas as pl
from jax.experimental.pallas import tpu as pltpu
from jax.sharding import Mesh
from jax.sharding import PartitionSpec as P

HD = 128
LINE = 4
LANES = 128
LOW = jnp.bfloat16
F32 = jnp.float32
MESH = pl.DeviceIdType.MESH


def doc_layout(lens, count):
    rows = jnp.arange(count, dtype=jnp.int32)
    doc = jnp.zeros((count,), jnp.int32)
    start = jnp.zeros((count,), jnp.int32)
    bound = jnp.int32(0)
    for number in range(lens.shape[0]):
        bound = bound + lens[number]
        after = (rows >= bound).astype(jnp.int32)
        doc = doc + after
        start = start + after * lens[number]
    positions = rows - start
    allowed = (doc[:, None] == doc[None, :]) & (rows[:, None] >= rows[None, :])
    return (positions, allowed)


def rope_tables(positions, width):
    index = jnp.arange(width // 2, dtype=F32)
    freq = jnp.exp(-(2.0 * index / width) * math.log(1000000.0))
    angle = positions.astype(F32)[:, None] * freq[None, :]
    return (
        jnp.concatenate([jnp.cos(angle)] * 2, axis=1),
        jnp.concatenate([jnp.sin(angle)] * 2, axis=1),
    )


def contract_last(left, right, out=F32):
    return lax.dot_general(left, right, (((1,), (1,)), ((), ())), preferred_element_type=out)


def contract_first(left, right, out=F32):
    return lax.dot_general(left, right, (((0,), (0,)), ((), ())), preferred_element_type=out)


def take(array, index, axis):
    return lax.dynamic_index_in_dim(array, index, axis, keepdims=False)


def greet(axes_targets, conditions):
    barrier = pltpu.get_barrier_semaphore()
    for (axis, target), condition in zip(axes_targets, conditions):
        def signal(axis=axis, target=target):
            pl.semaphore_signal(barrier, inc=1, device_id={axis: target}, device_id_type=MESH)
        if condition is None:
            signal()
        else:
            pl.when(condition)(signal)
    amount = sum(1 if c is None else c.astype(jnp.int32) for c in conditions)
    pl.semaphore_wait(barrier, amount)


def slot_of(line, values):
    slot = line
    for value in values:
        slot = slot * 2 + value
    return slot


def both(*conditions):
    given = [c for c in conditions if c is not None]
    return functools.reduce(jnp.logical_and, given) if given else None


def guarded(condition, action):
    if condition is None:
        action()
    else:
        pl.when(condition)(action)


def bit_flips(variant, stage, count):
    return [(variant >> b) & 1 for b in range(stage)] + [1] + [0] * (count - stage - 1)


class Gather:
    def __init__(self, size, bits, x_ref, out_ref, own_sem, line_sems, bit_sems, recv_sems):
        self.size, self.bits, self.count = size, bits, len(bits)
        self.x_ref, self.out_ref, self.own_sem = x_ref, out_ref, own_sem
        self.line_sems, self.bit_sems, self.recv_sems = line_sems, bit_sems, recv_sems
        self.z = lax.axis_index("z")
        self.mine = [lax.axis_index(bit) for bit in bits]
        self.own = slot_of(self.z, self.mine)
        self.pending, self.settled = [], False

    def copy(self, slot, first, axis, target, send_sem):
        return pltpu.make_async_remote_copy(
            src_ref=self.x_ref if first else self.out_ref.at[slot],
            dst_ref=self.out_ref.at[slot],
            send_sem=send_sem,
            recv_sem=self.recv_sems.at[slot],
            device_id={axis: target},
            device_id_type=MESH,
        )

    def start(self, condition, make):
        self.pending.append((condition, make))
        guarded(condition, lambda: make().start())

    def arrived(self, condition, slot, axis, target):
        guarded(
            condition,
            lambda: self.copy(slot, False, axis, target, self.line_sems.at[0, 0]).wait_recv(),
        )

    def spread(self, condition, slot, first, number, side, variant, after):
        for stage in range(after, self.count):
            self.start(
                condition,
                functools.partial(
                    self.copy,
                    slot,
                    first,
                    self.bits[stage],
                    1 - self.mine[stage],
                    self.bit_sems.at[number, side, variant, stage],
                ),
            )

    def line_of(self, number, side):
        line = self.z - number if side == 0 else self.z + number
        if number == 0:
            return line, None
        return line, (line >= 0 if side == 0 else line < self.size)

    def on_bits(self, number):
        for side in range(1 if number == 0 else 2):
            line, condition = self.line_of(number, side)
            for stage in range(self.count):
                for variant in range(2**stage):
                    flips = bit_flips(variant, stage, self.count)
                    slot = slot_of(line, [1 - m if f else m for m, f in zip(self.mine, flips)])
                    self.arrived(condition, slot, self.bits[stage], 1 - self.mine[stage])
                    code = sum(f << b for b, f in enumerate(flips))
                    self.spread(condition, slot, False, number, side, code, stage + 1)

    def begin(self):
        pltpu.make_async_copy(self.x_ref, self.out_ref.at[self.own], self.own_sem).start()
        z, size = self.z, self.size
        first = functools.partial(self.copy, self.own, True, "z")
        self.start(z < size - 1, functools.partial(first, z + 1, self.line_sems.at[0, 0]))
        self.start(z > 0, functools.partial(first, z - 1, self.line_sems.at[0, 1]))
        self.spread(None, self.own, True, 0, 0, 0, 0)

    def step(self, number):
        z, size = self.z, self.size
        for side in range(2):
            line, condition = self.line_of(number, side)
            slot = slot_of(line, self.mine)
            back = z - 1 if side == 0 else z + 1
            onto = z + 1 if side == 0 else z - 1
            self.arrived(condition, slot, "z", back)
            self.start(
                both(condition, onto < size if side == 0 else onto >= 0),
                functools.partial(self.copy, slot, False, "z", onto, self.line_sems.at[number, side]),
            )
            self.spread(condition, slot, False, number, side, 0, 0)

    def middle(self):
        for number in range(1, self.size):
            self.step(number)
            self.on_bits(number - 1)
        self.on_bits(self.size - 1)

    def settle(self):
        if not self.settled:
            pltpu.make_async_copy(self.x_ref, self.out_ref.at[self.own], self.own_sem).wait()
            self.settled = True

    def end(self):
        self.settle()
        for condition, make in self.pending:
            guarded(condition, lambda make=make: make().wait_send())


def gather_semaphores(size, bits):
    slots = size * 2 ** len(bits)
    return [
        pltpu.SemaphoreType.DMA,
        pltpu.SemaphoreType.DMA((size, 2)),
        pltpu.SemaphoreType.DMA((size, 2, 2 ** len(bits), len(bits))),
        pltpu.SemaphoreType.DMA((slots,)),
    ]


class Exchange:
    def __init__(self, size, bits, block, half, gu_ref, dn_ref, gu_out, dn_out, sems):
        self.size, self.bits, self.count = size, bits, len(bits)
        self.block, self.half = block, half
        self.gu_ref, self.dn_ref, self.gu_out, self.dn_out = gu_ref, dn_ref, gu_out, dn_out
        self.own_sems, self.line_sems, self.bit_sems, self.recv_sems = sems
        self.z = lax.axis_index("z")
        self.mine = [lax.axis_index(bit) for bit in bits]
        self.own = slot_of(self.z, self.mine)
        self.others = [lax.rem(self.z + o, size) for o in range(1, size)]
        self.pending = []

    def pieces(self, target, slot):
        low = pl.multiple_of(jnp.minimum(target * self.block, self.half - self.block), LANES)
        high = pl.multiple_of(low + self.half, LANES)
        width = self.block
        return [
            (self.gu_ref.at[:, pl.ds(low, width)], self.gu_out.at[slot, :, pl.ds(0, width)]),
            (self.gu_ref.at[:, pl.ds(high, width)], self.gu_out.at[slot, :, pl.ds(width, width)]),
            (self.dn_ref.at[:, pl.ds(low, width)], self.dn_out.at[slot]),
        ]

    def line_copy(self, place, piece, slot):
        source, landing = self.pieces(self.others[place], slot)[piece]
        return pltpu.make_async_remote_copy(
            src_ref=source,
            dst_ref=landing,
            send_sem=self.line_sems.at[place, piece],
            recv_sem=self.recv_sems.at[slot, piece],
            device_id={"z": self.others[place]},
            device_id_type=MESH,
        )

    def own_copy(self, piece):
        source, landing = self.pieces(self.z, self.own)[piece]
        return pltpu.make_async_copy(source, landing, self.own_sems.at[piece])

    def bit_copy(self, slot, piece, stage, send_sem):
        ref = (self.gu_out, None, self.dn_out)[piece]
        return pltpu.make_async_remote_copy(
            src_ref=ref.at[slot],
            dst_ref=ref.at[slot],
            send_sem=send_sem,
            recv_sem=self.recv_sems.at[slot, piece],
            device_id={self.bits[stage]: 1 - self.mine[stage]},
            device_id_type=MESH,
        )

    def first_copy(self, slot, piece, stage, send_sem):
        source, landing = self.pieces(self.z, slot)[piece]
        return pltpu.make_async_remote_copy(
            src_ref=source,
            dst_ref=landing,
            send_sem=send_sem,
            recv_sem=self.recv_sems.at[slot, piece],
            device_id={self.bits[stage]: 1 - self.mine[stage]},
            device_id_type=MESH,
        )

    def spread(self, slot, number, variant, after):
        for stage in range(after, self.count):
            for piece in (0, 2):
                make = functools.partial(
                    self.bit_copy, slot, piece, stage, self.bit_sems.at[number, variant, stage, piece]
                )
                self.pending.append(make)
                make().start()

    def on_bits(self, number):
        line = lax.rem(self.z - number + self.size, self.size)
        for stage in range(self.count):
            for variant in range(2**stage):
                flips = bit_flips(variant, stage, self.count)
                slot = slot_of(line, [1 - m if f else m for m, f in zip(self.mine, flips)])
                if number == 0 and variant == 0:
                    for piece in range(3):
                        self.first_copy(slot, piece, stage, self.own_sems.at[0]).wait_recv()
                else:
                    for piece in (0, 2):
                        self.bit_copy(slot, piece, stage, self.own_sems.at[0]).wait_recv()
                self.spread(slot, number, sum(f << b for b, f in enumerate(flips)), stage + 1)

    def begin(self):
        for stage in range(self.count):
            for piece in range(3):
                make = functools.partial(
                    self.first_copy, self.own, piece, stage, self.bit_sems.at[0, 0, stage, piece]
                )
                self.pending.append(make)
                make().start()
        for piece in range(3):
            self.own_copy(piece).start()

    def send(self, offset):
        for piece in range(3):
            self.line_copy(offset - 1, piece, self.own).start()

    def sent(self, offset):
        for piece in range(3):
            self.line_copy(offset - 1, piece, self.own).wait_send()

    def step(self, offset):
        slot = slot_of(lax.rem(self.z - offset + self.size, self.size), self.mine)
        for piece in range(3):
            self.line_copy(0, piece, slot).wait_recv()
        self.spread(slot, offset, 0, 0)

    def end(self):
        for piece in range(3):
            self.own_copy(piece).wait()
        for make in self.pending:
            make().wait_send()


class Fold:
    def __init__(self, size, bits, order, p_ref, own_buf, sums, stage_in, stage_out, own_sems, send_sems, recv_sems):
        self.size, self.bits, self.count, self.order = size, bits, len(bits), order
        self.last = self.count - 1
        self.p_ref, self.own_buf, self.sums = p_ref, own_buf, sums
        self.stage_in, self.stage_out = stage_in, stage_out
        self.own_sems, self.send_sems, self.recv_sems = own_sems, send_sems, recv_sems
        self.z = lax.axis_index("z")
        self.mine = [lax.axis_index(bit) for bit in bits]

    def line(self, place):
        if self.order is None:
            return relay_line(self.z, place, self.size)
        return lax.rem(self.z + self.order[place], self.size)

    def index(self, place, stage, variant):
        return place * (2**self.count - 1) + 2**stage - 1 + variant

    def slot(self, place, variant, flip):
        flips = [(variant >> b) & 1 for b in range(self.last)] + [flip]
        return slot_of(self.line(place), [1 - m if f else m for m, f in zip(self.mine, flips)])

    def copy(self, place, stage, variant):
        index = self.index(place, stage, variant)
        if stage == self.last:
            source = self.p_ref.at[self.slot(place, variant, 1)]
        else:
            source = self.stage_out.at[place * (2**self.last - 1) + 2**stage - 1 + variant]
        return pltpu.make_async_remote_copy(
            src_ref=source,
            dst_ref=self.stage_in.at[index],
            send_sem=self.send_sems.at[index],
            recv_sem=self.recv_sems.at[index],
            device_id={self.bits[stage]: 1 - self.mine[stage]},
            device_id_type=MESH,
        )

    def own_copy(self, place, variant):
        number = place * 2**self.last + variant
        return pltpu.make_async_copy(
            self.p_ref.at[self.slot(place, variant, 0)], self.own_buf.at[number], self.own_sems.at[number]
        )

    def begin(self, places=None):
        for place in range(self.size) if places is None else places:
            for variant in reversed(range(2**self.last)):
                self.copy(place, self.last, variant).start()
                self.own_copy(place, variant).start()

    def stage(self, place, stage, done=None):
        for variant in reversed(range(2**stage)):
            if stage == self.last:
                self.own_copy(place, variant).wait()
                held = self.own_buf[place * 2**self.last + variant].astype(F32)
            else:
                held = self.sums[place * (2**self.last - 1) + 2**stage - 1 + variant]
            self.copy(place, stage, variant).wait_recv()
            total = held + self.stage_in[self.index(place, stage, variant)].astype(F32)
            if stage == 0:
                done(place, total)
                continue
            lower = variant & (2 ** (stage - 1) - 1)
            number = place * (2**self.last - 1) + 2 ** (stage - 1) - 1 + lower
            if variant >> (stage - 1):
                self.stage_out[number] = total.astype(LOW)
                self.copy(place, stage - 1, lower).start()
            else:
                self.sums[number] = total

    def end(self):
        for place in range(self.size):
            for stage in range(self.count):
                for variant in range(2**stage):
                    self.copy(place, stage, variant).wait_send()


def fold_scratch(size, bits, rows, columns):
    count = len(bits)
    inner, lower = size * (2**count - 1), size * (2 ** (count - 1) - 1)
    return [
        pltpu.VMEM((size * 2 ** (count - 1), rows, columns), LOW),
        pltpu.VMEM((max(lower, 1), rows, columns) if lower else (1, 8, LANES), F32),
        pltpu.VMEM((inner, rows, columns), LOW),
        pltpu.VMEM((max(lower, 1), rows, columns) if lower else (1, 16, LANES), LOW),
        pltpu.SemaphoreType.DMA((size * 2 ** (count - 1),)),
        pltpu.SemaphoreType.DMA((inner,)),
        pltpu.SemaphoreType.DMA((inner,)),
    ]


def relay_line(z, place, size):
    order = []
    for line in range(size):
        others = sorted((other for other in range(size) if other != line), key=lambda other: -abs(other - line))
        order.append([*others, line])
    return sum(jnp.where(z == line, order[line][place], 0) for line in range(size))


class Scatter:
    def __init__(self, size, bits, p_ref, out_ref, line_out, line_in, line_send, line_recv, *fold):
        order = list(range(1, size)) + [0]
        self.fold = Fold(size, bits, order, p_ref, *fold)
        self.size, self.out_ref = size, out_ref
        self.line_out, self.line_in, self.line_send, self.line_recv = line_out, line_in, line_send, line_recv

    def line_copy(self, place):
        return pltpu.make_async_remote_copy(
            src_ref=self.line_out.at[place],
            dst_ref=self.line_in.at[place],
            send_sem=self.line_send.at[place],
            recv_sem=self.line_recv.at[place],
            device_id={"z": self.fold.line(place)},
            device_id_type=MESH,
        )

    def done(self, place, total):
        if place < self.size - 1:
            self.line_out[place] = total.astype(LOW)
            self.line_copy(place).start()
        else:
            self.out_ref[...] = total

    def begin(self, places=None):
        self.fold.begin(places)

    def place(self, place):
        for stage in reversed(range(self.fold.count)):
            self.fold.stage(place, stage, self.done)

    def finish(self):
        for place in range(self.size - 1):
            self.line_copy(place).wait_recv()
            self.out_ref[...] += self.line_in[place].astype(F32)

    def end(self):
        self.fold.end()
        for place in range(self.size - 1):
            self.line_copy(place).wait_send()


class Relay:
    def __init__(self, size, bits, p_ref, out_ref, line_out, line_in, line_send, line_recv, *fold):
        self.fold = Fold(size, bits, None, p_ref, *fold)
        self.size, self.out_ref, self.z = size, out_ref, lax.axis_index("z")
        self.line_out, self.line_in, self.line_send, self.line_recv = line_out, line_in, line_send, line_recv

    def line_copy(self, place, line):
        right = (line > self.z).astype(jnp.int32)
        slot = (1 - right) * (self.size - 1) + jnp.abs(line - self.z) - 1
        return pltpu.make_async_remote_copy(
            src_ref=self.line_out.at[place],
            dst_ref=self.line_in.at[slot],
            send_sem=self.line_send.at[place],
            recv_sem=self.line_recv.at[slot],
            device_id={"z": self.z + 2 * right - 1},
            device_id_type=MESH,
        )

    def landed(self, slot):
        pltpu.make_async_remote_copy(
            src_ref=self.line_in.at[slot],
            dst_ref=self.line_in.at[slot],
            send_sem=self.line_send.at[0],
            recv_sem=self.line_recv.at[slot],
            device_id={"z": lax.rem(self.z + 1, self.size)},
            device_id_type=MESH,
        ).wait_recv()

    def done(self, place, total):
        if place == self.size - 1:
            self.out_ref[...] = total
            return
        line = self.fold.line(place)
        right = line > self.z
        self.line_out[place] = total.astype(LOW)
        slot = (1 - right.astype(jnp.int32)) * (self.size - 1) + jnp.abs(line - self.z)

        @pl.when(jnp.where(right, self.z > 0, self.z < self.size - 1))
        def _():
            self.landed(slot)
            self.line_out[place] = (total + self.line_in[slot].astype(F32)).astype(LOW)

        self.line_copy(place, line).start()

    def begin(self, places=None):
        self.fold.begin(places)

    def place(self, place):
        for stage in reversed(range(self.fold.count)):
            self.fold.stage(place, stage, self.done)

    def finish(self):
        for slot, there in ((0, self.z > 0), (self.size - 1, self.z < self.size - 1)):

            @pl.when(there)
            def _(slot=slot):
                self.landed(slot)
                self.out_ref[...] += self.line_in[slot].astype(F32)

    def end(self):
        self.fold.end()
        for place in range(self.size - 1):
            self.line_copy(place, self.fold.line(place)).wait_send()


def scatter_scratch(size, bits, rows, columns, relay=False):
    lands = (size - 1) * (2 if relay else 1)
    return [
        pltpu.VMEM((size - 1, rows, columns), LOW),
        pltpu.VMEM((lands, rows, columns), LOW),
        pltpu.SemaphoreType.DMA((size - 1,)),
        pltpu.SemaphoreType.DMA((lands,)),
        *fold_scratch(size, bits, rows, columns),
    ]


SCATTER_REFS = 11


class Total:
    def __init__(self, size, bits, x_ref, out_ref, held, landed, send_sems, recv_sems):
        self.size, self.bits, self.count = size, bits, len(bits)
        self.x_ref, self.out_ref, self.held, self.landed = x_ref, out_ref, held, landed
        self.send_sems, self.recv_sems = send_sems, recv_sems
        self.z = lax.axis_index("z")
        self.others = [lax.rem(self.z + o, size) for o in range(1, size)]

    def copy(self, number):
        if number < self.count:
            axis = self.bits[number]
            source, target = self.held.at[number], {axis: 1 - lax.axis_index(axis)}
        else:
            source, target = self.held.at[self.count], {"z": self.others[number - self.count]}
        return pltpu.make_async_remote_copy(
            src_ref=source,
            dst_ref=self.landed.at[number],
            send_sem=self.send_sems.at[number],
            recv_sem=self.recv_sems.at[number],
            device_id=target,
            device_id_type=MESH,
        )

    def begin(self):
        self.held[0] = self.x_ref[...]
        self.copy(0).start()

    def pair(self, number):
        self.copy(number).wait_recv()
        self.held[number + 1] = self.held[number] + self.landed[number]
        if number + 1 < self.count:
            self.copy(number + 1).start()
        else:
            for place in range(self.size - 1):
                self.copy(self.count + place).start()

    def finish(self):
        for place in range(self.size - 1):
            self.copy(self.count + place).wait_recv()
        total = jnp.zeros(self.out_ref.shape, self.out_ref.dtype)
        for line in range(self.size):
            offset = lax.rem(line - self.z + self.size, self.size)
            part = self.held[self.count]
            for o in range(1, self.size):
                part = jnp.where(offset == o, self.landed[self.count + self.size - o - 1], part)
            total = total + part
        self.out_ref[...] = total

    def end(self):
        for number in range(self.count + self.size - 1):
            self.copy(number).wait_send()


def greet_all(size, axes):
    z = lax.axis_index("z")
    greet(
        [("z", lax.rem(z + o, size)) for o in range(1, size)]
        + [(axis, 1 - lax.axis_index(axis)) for axis in axes],
        [None] * (size - 1 + len(axes)),
    )


def in_groups(refs, sizes):
    groups, at = [], 0
    for number in sizes:
        groups.append(refs[at : at + number])
        at += number
    return groups


def comm_params(collective_id):
    return pltpu.CompilerParams(
        collective_id=collective_id, has_side_effects=True, vmem_limit_bytes=60 * 2**20
    )


def at_microseconds(time):
    return pl.CostEstimate(flops=0, transcendentals=0, bytes_accessed=time * 3500000)


class Attend:
    def __init__(self, rows_ref, gain_ref, bias_ref, cos_ref, sin_ref, mask_ref, w_ref, outs, scratch, width, epsilon=1e-06):
        self.gain_ref, self.bias_ref, self.w_ref = gain_ref, bias_ref, w_ref
        self.cos_ref, self.sin_ref, self.mask_ref = cos_ref, sin_ref, mask_ref
        self.state_ref, self.middle_ref, self.xa_ref, self.q_ref, self.k_ref, self.v_ref, self.lse_ref, self.o_ref = outs
        self.send_buf, self.land_buf, self.send_sems, self.recv_sems = scratch
        self.rows_ref = rows_ref
        self.t = lax.axis_index("t")
        self.slots, self.few = w_ref.shape[0], w_ref.shape[1]
        self.model = self.slots * self.few
        self.count = rows_ref.shape[0]
        self.q_width = self.q_ref.shape[1]
        self.width = width
        self.epsilon = epsilon

    def normed(self, rows, gain_ref):
        factor = lax.rsqrt(jnp.mean(rows * rows, axis=-1, keepdims=True) + self.epsilon)
        return (rows * factor * gain_ref[...]).astype(LOW)

    def xa_copy(self):
        return pltpu.make_async_remote_copy(
            src_ref=self.xa_ref.at[self.t],
            dst_ref=self.xa_ref.at[self.t],
            send_sem=self.send_sems.at[0],
            recv_sem=self.recv_sems.at[0],
            device_id={"t": 1 - self.t},
            device_id_type=MESH,
        )

    def xa_landing(self):
        return pltpu.make_async_remote_copy(
            src_ref=self.xa_ref.at[1 - self.t],
            dst_ref=self.xa_ref.at[1 - self.t],
            send_sem=self.send_sems.at[0],
            recv_sem=self.recv_sems.at[0],
            device_id={"t": 1 - self.t},
            device_id_type=MESH,
        )

    def half_copy(self):
        return pltpu.make_async_remote_copy(
            src_ref=self.send_buf,
            dst_ref=self.land_buf,
            send_sem=self.send_sems.at[1],
            recv_sem=self.recv_sems.at[1],
            device_id={"t": 1 - self.t},
            device_id_type=MESH,
        )

    def begin(self, state):
        self.state_ref[...] = state
        self.xa_ref[self.t] = self.normed(state, self.gain_ref)
        self.xa_copy().start()

    def columns(self, low, count):
        weight = self.w_ref[:, :, low : low + count].reshape(self.model, count)
        xa = self.xa_ref[...].reshape(2 * self.count, self.model)
        return jnp.dot(xa, weight, preferred_element_type=F32) + self.bias_ref[:, low : low + count]

    def rope(self, values):
        return (values * self.cos_ref[...] + pltpu.roll(values, HD // 2, 1) * self.sin_ref[...]).astype(LOW)

    def keys(self):
        self.xa_landing().wait_recv()
        both_kv = self.columns(self.q_width, 2 * HD)
        self.k_ref[...] = self.rope(both_kv[:, :HD])
        self.v_ref[...] = both_kv[:, HD:].astype(LOW)

    def heads(self, first):
        lin = self.columns(first * HD, 2 * HD)
        for number in range(2):
            head = first + number
            low = head * HD
            query = self.rope(lin[:, number * HD : (number + 1) * HD])
            self.q_ref[:, low : low + HD] = query
            raw = lax.dot_general(
                query, self.k_ref[...], (((1,), (1,)), ((), ())), preferred_element_type=F32
            )
            scores = jnp.where(self.mask_ref[...] > 0, raw * (1.0 / math.sqrt(HD)), -1e30)
            top = jnp.max(scores, axis=-1, keepdims=True)
            expo = jnp.exp(scores - top)
            whole = jnp.sum(expo, axis=-1, keepdims=True)
            probs = (expo / whole).astype(LOW)
            self.lse_ref[head] = top + jnp.log(whole)
            out = jnp.dot(probs, self.v_ref[...], preferred_element_type=F32).astype(LOW)
            self.o_ref[0, :, low : low + HD] = out[: self.count]
            self.o_ref[1, :, low : low + HD] = out[self.count :]

    def projected(self, half, step):
        left = self.o_ref[half]
        for low in range(0, self.slots, step):
            weight = self.w_ref[low : low + step, :, self.width :].reshape(step * self.few, self.q_width)
            yield low * self.few, lax.dot_general(
                left, weight, (((1,), (1,)), ((), ())), preferred_element_type=F32
            )

    def other_half(self):
        for low, part in self.projected(1 - self.t, self.slots // 4):
            self.send_buf[:, low : low + part.shape[1]] = part.astype(LOW)
        self.half_copy().start()

    def own_half(self):
        for low, part in self.projected(self.t, self.slots // 4):
            where = slice(low, low + part.shape[1])
            self.middle_ref[:, where] = self.state_ref[:, where] + part

    def finish(self, gain_ref, xf_ref):
        self.half_copy().wait_recv()
        middle = self.middle_ref[...] + self.land_buf[...].astype(F32)
        self.middle_ref[...] = middle
        xf_ref[...] = self.normed(middle, gain_ref)

    def end(self):
        self.xa_copy().wait_send()
        self.half_copy().wait_send()


def front_kernel(size, bits, block, half, layer, width, *refs):
    first = layer == 0
    inputs, outs, refs = in_groups(refs, [11, 13 if first else 11, len(refs)])
    (x_ref, more_ref, ga_ref, gf_ref, bias_ref, cos_ref, sin_ref, mask_ref, at_ref, gu_ref, dn_ref) = inputs
    xf_out, gu_out, dn_out = outs[8:11]
    (w_ref, xf_ref, at_sem), pair, feed_sems, rows_sems, rest = in_groups(refs, [3, 4, 4, 4, len(refs)])
    greet_all(size, ("t", *bits))
    work = Attend(
        x_ref, ga_ref, bias_ref, cos_ref, sin_ref, mask_ref, w_ref, outs[:8], pair, width
    )
    feed = Exchange(
        size, bits, block, half, gu_ref.at[layer], dn_ref.at[layer], gu_out, dn_out, feed_sems
    )
    rows = Gather(size, ("t",), xf_ref, xf_out, *rows_sems)
    if first:
        at_sems, next_sems = in_groups(rest, [4, 4])
        attention = Gather(size, bits, at_ref, w_ref, *at_sems)
        ahead = Gather(size, bits, more_ref, outs[12], *next_sems)
        moved = pltpu.make_async_copy(w_ref, outs[11], at_sem)
        attention.begin()
        feed.begin()
        work.begin(x_ref[...].astype(F32))
        attention.step(1)
        attention.step(2)
        attention.on_bits(0)
        attention.step(3)
        feed.send(1)
        attention.on_bits(1)
        attention.on_bits(2)
        attention.on_bits(3)
        attention.settle()
        moved.start()
        feed.on_bits(0)
        feed.sent(1)
        feed.send(3)
        feed.step(1)
        steps = (attention, ahead)
    else:
        total_ref, *rest = rest
        side = Scatter(size, ("t",), more_ref, total_ref, *rest)
        moved = pltpu.make_async_copy(at_ref, w_ref, at_sem)
        moved.start()
        side.begin()
        feed.begin()
        for place in range(size):
            side.place(place)
        feed.send(1)
        side.finish()
        work.begin(x_ref[...] + total_ref[...])
        moved.wait()
        feed.on_bits(0)
        feed.sent(1)
        feed.send(3)
        feed.step(1)
        steps = (side,)
    work.keys()
    work.heads(0)
    work.heads(2)
    work.heads(4)
    work.other_half()
    work.own_half()
    feed.sent(3)
    feed.send(2)
    feed.step(3)
    feed.on_bits(1)
    work.finish(gf_ref, xf_ref)
    rows.begin()
    if first:
        ahead.begin()
    rows.step(1)
    rows.on_bits(0)
    if first:
        ahead.step(1)
    rows.step(2)
    feed.sent(2)
    feed.step(2)
    rows.on_bits(1)
    if first:
        ahead.on_bits(0)
    feed.on_bits(3)
    rows.step(3)
    if first:
        ahead.step(2)
    rows.on_bits(2)
    feed.on_bits(2)
    rows.on_bits(3)
    if first:
        ahead.on_bits(1)
        ahead.step(3)
        ahead.on_bits(2)
        ahead.on_bits(3)
        moved.wait()
    for item in (*steps, feed, work, rows):
        item.end()


def front(x, more, gains, bias, tables, at, gu, dn, layer, size, bits, block, width, collective_id):
    slots = size * 2 ** len(bits)
    count, model = x.shape
    few, half = dn.shape[1:]
    length = 2 * count
    q_width = at.shape[-1] - width
    first = layer == 0
    held, far = pl.BlockSpec(memory_space=pltpu.VMEM), pl.BlockSpec(memory_space=pl.ANY)
    shape = jax.ShapeDtypeStruct
    weight = (slots, few, at.shape[-1])
    more_scratch = (
        gather_semaphores(size, bits) * 2
        if first
        else [pltpu.VMEM((count, model), F32), *scatter_scratch(size, ("t",), count, model)]
    )
    return pl.pallas_call(
        functools.partial(front_kernel, size, bits, block, half, layer, width),
        out_shape=(
            shape((count, model), F32),
            shape((count, model), F32),
            shape((2, count, model), LOW),
            shape((length, q_width), LOW),
            shape((length, HD), LOW),
            shape((length, HD), LOW),
            shape((q_width // HD, length, 1), F32),
            shape((2, count, q_width), LOW),
            shape((2 * size, count, model), LOW),
            shape((slots, few, 2 * block), LOW),
            shape((slots, few, block), LOW),
            *([shape(weight, LOW)] * 2 if first else []),
        ),
        in_specs=[held, far] + [held] * 6 + [far] * 3,
        out_specs=[held] * 8 + [far] * (5 if first else 3),
        scratch_shapes=[
            pltpu.VMEM(weight, LOW),
            pltpu.VMEM((count, model), LOW),
            pltpu.SemaphoreType.DMA,
            pltpu.VMEM((count, model), LOW),
            pltpu.VMEM((count, model), LOW),
            pltpu.SemaphoreType.DMA((2,)),
            pltpu.SemaphoreType.DMA((2,)),
            pltpu.SemaphoreType.DMA((3,)),
            pltpu.SemaphoreType.DMA((size - 1, 3)),
            pltpu.SemaphoreType.DMA((size, 2 ** len(bits), len(bits), 3)),
            pltpu.SemaphoreType.DMA((slots, 3)),
            *gather_semaphores(size, ("t",)),
            *more_scratch,
        ],
        compiler_params=comm_params(collective_id),
        cost_estimate=at_microseconds(150),
    )(x, more, *gains, bias, *tables, at, gu, dn)


class AttendBack:
    def __init__(self, ins, outs, scratch, width, epsilon=1e-06):
        (self.g_ref, self.state_ref, self.middle_ref, self.ga_gain, self.gf_gain, self.cos_ref, self.sin_ref) = ins[:7]
        (self.mask_ref, self.q_ref, self.k_ref, self.v_ref, self.lse_ref, self.xa_ref, self.o_ref, self.far_w) = ins[7:]
        (self.grad_ref, self.ga_ref, self.lin_ref, self.bias_ref, self.pa_ref, self.pf_ref) = outs
        (self.w_ref, self.w_sem, self.dk, self.dv, self.sum_buf, self.send_buf, self.land_buf) = scratch[:7]
        (self.send_sems, self.recv_sems) = scratch[7:]
        self.t = lax.axis_index("t")
        self.slots, self.few = self.w_ref.shape[:2]
        self.model = self.slots * self.few
        self.count = self.state_ref.shape[0]
        self.q_width = self.q_ref.shape[1]
        self.width, self.epsilon = width, epsilon

    def pair_copy(self, number, source, landing):
        return pltpu.make_async_remote_copy(
            src_ref=source,
            dst_ref=landing,
            send_sem=self.send_sems.at[number],
            recv_sem=self.recv_sems.at[number],
            device_id={"t": 1 - self.t},
            device_id_type=MESH,
        )

    def ga_copy(self, side):
        return self.pair_copy(0, self.ga_ref.at[side], self.ga_ref.at[side])

    def half_copy(self):
        return self.pair_copy(1, self.send_buf, self.land_buf)

    def weight_copy(self):
        return pltpu.make_async_copy(self.far_w, self.w_ref, self.w_sem)

    def norm_back(self, upstream, rows, gain):
        factor = lax.rsqrt(jnp.mean(rows * rows, axis=-1, keepdims=True) + self.epsilon)
        scaled = upstream * gain
        part = jnp.sum(upstream * rows * factor, axis=0, keepdims=True)
        inner = jnp.mean(scaled * rows, axis=-1, keepdims=True)
        return factor * scaled - rows * factor**3 * inner, part

    def prepare(self):
        self.weight_copy().start()

    def begin(self, d_xf):
        d_mid, part = self.norm_back(d_xf, self.middle_ref[...], self.gf_gain[...])
        self.pf_ref[...] = part
        grad = self.g_ref[...].astype(F32) + d_mid
        self.grad_ref[...] = grad
        self.ga_ref[self.t] = grad.astype(LOW)
        self.ga_copy(self.t).start()
        self.dk[...] = jnp.zeros_like(self.dk)
        self.dv[...] = jnp.zeros_like(self.dv)

    def arrive(self):
        self.weight_copy().wait()
        self.ga_copy(1 - self.t).wait_recv()

    def unrope(self, values):
        return values * self.cos_ref[...] - pltpu.roll(values, HD // 2, 1) * self.sin_ref[...]

    def keep(self, low, values):
        count = values.shape[1]
        self.bias_ref[:, low : low + count] = jnp.sum(values, axis=0, keepdims=True)
        values = values.astype(LOW)
        self.lin_ref[0, :, low : low + count] = values[: self.count]
        self.lin_ref[1, :, low : low + count] = values[self.count :]

    def heads(self, first):
        low, count = self.width + first * HD, 2 * HD
        weight = self.w_ref[:, :, low : low + count].reshape(self.model, count)
        above = self.ga_ref[...].reshape(2 * self.count, self.model)
        d_out = jnp.dot(above, weight, preferred_element_type=F32).astype(LOW)
        key, value = self.k_ref[...], self.v_ref[...]
        last = (((1,), (1,)), ((), ()))
        early = (((0,), (0,)), ((), ()))
        scale = 1.0 / math.sqrt(HD)
        for number in range(2):
            head = first + number
            query = self.q_ref[:, head * HD : (head + 1) * HD]
            d_head = d_out[:, number * HD : (number + 1) * HD]
            raw = lax.dot_general(query, key, last, preferred_element_type=F32)
            scores = jnp.where(self.mask_ref[...] > 0, raw * scale, -1e30)
            probs = jnp.exp(scores - self.lse_ref[head])
            d_probs = lax.dot_general(d_head, value, last, preferred_element_type=F32)
            centre = jnp.sum(probs * d_probs, axis=-1, keepdims=True)
            d_raw = (probs * (d_probs - centre) * scale).astype(LOW)
            d_query = jnp.dot(d_raw, key, preferred_element_type=F32)
            self.dk[...] += lax.dot_general(d_raw, query, early, preferred_element_type=F32)
            self.dv[...] += lax.dot_general(
                probs.astype(LOW), d_head, early, preferred_element_type=F32
            )
            self.keep(head * HD, self.unrope(d_query))

    def keys(self):
        self.keep(self.q_width, self.unrope(self.dk[...]))
        self.keep(self.q_width + HD, self.dv[...])

    def projected(self, half):
        left, step = self.lin_ref[half], self.slots // 4
        for low in range(0, self.slots, step):
            weight = self.w_ref[low : low + step, :, : self.width].reshape(step * self.few, self.width)
            yield slice(low * self.few, (low + step) * self.few), lax.dot_general(
                left, weight, (((1,), (1,)), ((), ())), preferred_element_type=F32
            )

    def other_half(self):
        for where, part in self.projected(1 - self.t):
            self.send_buf[:, where] = part.astype(LOW)
        self.half_copy().start()

    def own_half(self):
        for where, part in self.projected(self.t):
            self.sum_buf[:, where] = part

    def gradients(self):
        step = self.slots // 4
        early = (((0,), (0,)), ((), ()))
        pairs = ((self.xa_ref, self.lin_ref, 0, self.width), (self.ga_ref, self.o_ref, self.width, self.q_width))
        for left_ref, right_ref, low, count in pairs:
            right = right_ref[...].reshape(2 * self.count, count)
            for slot in range(0, self.slots, step):
                where = slice(slot * self.few, (slot + step) * self.few)
                left = left_ref[:, :, where].reshape(2 * self.count, step * self.few)
                part = lax.dot_general(left, right, early, preferred_element_type=F32)
                self.w_ref[slot : slot + step, :, low : low + count] = part.astype(LOW).reshape(
                    step, self.few, count
                )

    def finish(self):
        self.half_copy().wait_recv()
        d_xa = self.sum_buf[...] + self.land_buf[...].astype(F32)
        d_in, part = self.norm_back(d_xa, self.state_ref[...], self.ga_gain[...])
        self.pa_ref[...] = part
        grad = self.grad_ref[...] + d_in
        self.grad_ref[...] = grad
        return grad

    def end(self):
        self.ga_copy(self.t).wait_send()
        self.half_copy().wait_send()


class Blocks:
    def __init__(self, size, bits, gu_ref, dn_ref, outs, gu_fold, dn_fold, done, sems):
        self.size, self.outs, self.sending = size, outs, len(outs) == 1
        order = list(range(1, size)) + [0]
        self.folds = [Fold(size, bits, order, gu_ref, *gu_fold), Fold(size, bits, order, dn_ref, *dn_fold)]
        self.done = done
        self.own_sems, self.send_sems, self.recv_sems = sems
        self.width, self.narrow = gu_ref.shape[2], dn_ref.shape[2]
        self.z = lax.axis_index("z")

    def columns(self, number):
        return pl.ds(*((0, self.width), (self.width, self.narrow))[number])

    def landing(self, number, slot):
        return self.outs[0].at[slot, :, self.columns(number)]

    def line_copy(self, number, place, slot):
        return pltpu.make_async_remote_copy(
            src_ref=self.done[number].at[place],
            dst_ref=self.landing(number, slot),
            send_sem=self.send_sems.at[number, place],
            recv_sem=self.recv_sems.at[number, slot],
            device_id={"z": self.folds[0].line(place)},
            device_id_type=MESH,
        )

    def own_copy(self, number, place):
        landing = (
            self.landing(number, self.z)
            if self.sending
            else self.outs[place].at[:, self.columns(number)]
        )
        return pltpu.make_async_copy(
            self.done[number].at[place], landing, self.own_sems.at[number, place]
        )

    def begin(self):
        for fold in self.folds:
            fold.begin()

    def inner(self, place):
        for stage in reversed(range(1, self.folds[0].count)):
            for fold in self.folds:
                fold.stage(place, stage)

    def send(self, place):
        for number, fold in enumerate(self.folds):

            def keep(place, total, number=number):
                self.done[number][place] = total.astype(LOW)
                if self.sending and place < self.size - 1:
                    self.line_copy(number, place, self.z).start()
                else:
                    self.own_copy(number, place).start()

            fold.stage(place, 0, keep)

    def end(self):
        for number, fold in enumerate(self.folds):
            for place in range(self.size):
                if not self.sending or place == self.size - 1:
                    self.own_copy(number, place).wait()
                    continue
                slot = lax.rem(self.z - place - 1 + self.size, self.size)
                self.line_copy(number, 0, slot).wait_recv()
                self.line_copy(number, place, self.z).wait_send()
            fold.end()


def back_kernel(size, bits, width, final, *refs):
    top, bottom = final
    counts = [1, 1 if top else 0, 2, 15, 3 if bottom else 0, 6, 1 if bottom else size, 1, 1 if top else 0, 1]
    p_ref, branch_ref, wide, ins, above, outs, folded, (attn_ref,), branch_out, more_out, refs = (
        in_groups(refs, counts + [len(refs)])
    )
    (dxf_ref,), dxf_scratch, gu_fold, dn_fold, done, sems, work_scratch, refs = in_groups(
        refs, [1, SCATTER_REFS, 7, 7, 2, 3, 9, len(refs)]
    )
    greet_all(size, ("t", *bits))
    rows = Scatter(size, ("t",), p_ref[0], dxf_ref, *dxf_scratch)
    blocks = Blocks(size, bits, *wide, folded, gu_fold, dn_fold, done, sems)
    work = AttendBack(ins, outs, work_scratch, width)
    branch = None
    if top:
        branch_scratch, refs = in_groups(refs, [SCATTER_REFS, len(refs)])
        branch = Relay(size, ("t",), branch_ref[0], branch_out[0], *branch_scratch)
    if not bottom:
        gm_ref, kept_sem, *gm_sems = refs
        onward = Gather(size, ("t",), gm_ref, more_out[0], *gm_sems)
        kept = pltpu.make_async_copy(work.w_ref, attn_ref, kept_sem)
    else:
        attn_scratch, (x_ref, *small_scratch) = in_groups(refs, [SCATTER_REFS, len(refs)])
        final = Scatter(size, bits, work.w_ref, attn_ref, *attn_scratch)
        small = Total(size, ("t", *bits), x_ref, more_out[0], *small_scratch)
    rows.begin()
    blocks.begin()
    work.prepare()
    blocks.inner(0)
    rows.place(0)
    blocks.inner(1)
    blocks.inner(2)
    rows.place(1)
    blocks.inner(3)
    blocks.send(0)
    rows.place(2)
    rows.place(3)
    if top:
        branch.begin([0])
    rows.finish()
    blocks.send(1)
    work.begin(dxf_ref[...])
    if top:
        branch.begin([1])
    work.arrive()
    work.heads(0)
    if top:
        branch.place(0)
    work.heads(2)
    blocks.send(2)
    work.heads(4)
    work.keys()
    work.other_half()
    if top:
        branch.place(1)
        branch.begin([2])
    work.own_half()
    blocks.send(3)
    work.gradients()
    if bottom:
        final.begin()
    else:
        kept.start()
    grad = work.finish()
    if bottom:
        pa_above, pf_above, bias_above = above
        x_ref[...] = jnp.zeros_like(x_ref)
        x_ref[0:1, :] = work.pa_ref[...]
        x_ref[1:2, :] = pa_above[...]
        x_ref[2:3, :] = work.pf_ref[...]
        x_ref[3:4, :] = pf_above[...]
        for side in range(2):
            mine = (work.t == side).astype(F32)
            x_ref[4 + 2 * side : 5 + 2 * side, : work.width] = work.bias_ref[...] * mine
            x_ref[5 + 2 * side : 6 + 2 * side, : work.width] = bias_above[...] * mine
        small.begin()
        for place in range(size):
            final.place(place)
            if place <= len(bits):
                small.pair(place)
        for number in range(size, len(bits) + 1):
            small.pair(number)
        final.finish()
        small.finish()
    if not bottom:
        gm_ref[...] = grad.astype(LOW)
        onward.begin()
    if top:
        branch.begin([3])
        branch.place(2)
    if not bottom:
        onward.step(1)
        onward.on_bits(0)
    if top:
        branch.place(3)
    if not bottom:
        onward.step(2)
        onward.on_bits(1)
        onward.step(3)
        onward.on_bits(2)
        onward.on_bits(3)
    if top:
        branch.finish()
    for steps in (rows, blocks, work, *((final, small) if bottom else (onward,)), branch):
        if steps is not None:
            steps.end()
    if not bottom:
        kept.wait()


def back(partial, branch, gu, dn, ins, above, size, bits, width, collective_id):
    count, model = ins[1].shape
    length, q_width = ins[8].shape
    slots, few, wide = gu.shape
    narrow = dn.shape[2]
    top, bottom = branch is not None, bool(above)
    number = len(bits) + 1
    weight = ins[14].shape
    held, far = pl.BlockSpec(memory_space=pltpu.VMEM), pl.BlockSpec(memory_space=pl.ANY)
    shape = jax.ShapeDtypeStruct
    rows_scratch = scatter_scratch(size, ("t",), count, model)
    branch_scratch = scatter_scratch(size, ("t",), count, model, relay=True)
    return pl.pallas_call(
        functools.partial(back_kernel, size, bits, width, (top, bottom)),
        out_shape=(
            shape((count, model), F32),
            shape((2, count, model), LOW),
            shape((2, count, width), LOW),
            shape((1, width), F32),
            shape((1, model), F32),
            shape((1, model), F32),
            *(
                [shape((size, few, wide + narrow), LOW)]
                if bottom
                else [shape((few, wide + narrow), LOW)] * size
            ),
            shape(weight[1:], F32) if bottom else shape(weight, LOW),
            *([shape((count, model), F32)] if top else []),
            shape((8, model), F32) if bottom else shape((2 * size, count, model), LOW),
        ),
        in_specs=[far] * (4 if top else 3) + [held] * 14 + [far] + [held] * len(above),
        out_specs=[held] * 6
        + ([far, held] if bottom else [far] * (size + 1))
        + [held] * top + [held if bottom else far],
        scratch_shapes=[
            pltpu.VMEM((count, model), F32),
            *rows_scratch,
            *fold_scratch(size, bits, few, wide),
            *fold_scratch(size, bits, few, narrow),
            pltpu.VMEM((size, few, wide), LOW),
            pltpu.VMEM((size, few, narrow), LOW),
            *([pltpu.SemaphoreType.DMA((2, size))] * 3),
            pltpu.VMEM(weight, LOW),
            pltpu.SemaphoreType.DMA,
            pltpu.VMEM((length, HD), F32),
            pltpu.VMEM((length, HD), F32),
            pltpu.VMEM((count, model), F32),
            pltpu.VMEM((count, model), LOW),
            pltpu.VMEM((count, model), LOW),
            pltpu.SemaphoreType.DMA((2,)),
            pltpu.SemaphoreType.DMA((2,)),
            *(branch_scratch if top else []),
            *(
                [
                    *scatter_scratch(size, bits, *weight[1:]),
                    pltpu.VMEM((8, model), F32),
                    pltpu.VMEM((number + 1, 8, model), F32),
                    pltpu.VMEM((number + size - 1, 8, model), F32),
                    pltpu.SemaphoreType.DMA((number + size - 1,)),
                    pltpu.SemaphoreType.DMA((number + size - 1,)),
                ]
                if bottom
                else [
                    pltpu.VMEM((count, model), LOW),
                    pltpu.SemaphoreType.DMA,
                    *gather_semaphores(size, ("t",)),
                ]
            ),
        ],
        compiler_params=comm_params(collective_id),
        cost_estimate=at_microseconds(5 if bottom else 150),
    )(partial, *([branch] if top else []), gu, dn, *ins, *above)


def settle_kernel(half, width, *refs):
    low_ref, *high_refs = refs[: LINE + 1]
    attn_low, attn_high, gu_ref, dn_ref, qkv_ref, out_ref = refs[LINE + 1 :]
    block = low_ref.shape[2] // 3
    z = lax.axis_index("z")
    for layer in range(2):
        for line in range(LINE):
            low = block_start(line, block, half)
            skip = line * block - low
            for part in range(3):
                where = slice(part * block + skip, (part + 1) * block)
                if layer == 0:
                    piece = low_ref[line, :, where]
                else:
                    offset = lax.rem(z - line + LINE, LINE)
                    piece = high_refs[LINE - 1][:, where]
                    for o in range(1, LINE):
                        piece = jnp.where(offset == o, high_refs[o - 1][:, where], piece)
                piece = piece.astype(F32)
                if part < 2:
                    gu_ref[layer, :, part * half + low + skip : part * half + low + block] = piece
                else:
                    dn_ref[layer, :, low + skip : low + block] = piece
    for layer, ref in enumerate((attn_low, attn_high)):
        qkv_ref[layer] = ref[:, :width].astype(F32)
        out_ref[layer] = ref[:, width:].astype(F32)


def settle(blocks, arrived, attn, half, width):
    few = attn[0].shape[0]
    shape = jax.ShapeDtypeStruct
    return pl.pallas_call(
        functools.partial(settle_kernel, half, width),
        out_shape=(
            shape((2, few, 2 * half), F32),
            shape((2, few, half), F32),
            shape((2, few, width), F32),
            shape((2, few, attn[0].shape[1] - width), F32),
        ),
        compiler_params=pltpu.CompilerParams(vmem_limit_bytes=56 * 2**20),
    )(blocks, *arrived, *attn)


def in_slots(partial, slots):
    return partial.reshape(slots, -1, partial.shape[1])


def block_width(half):
    return -(-half // (LINE * LANES)) * LANES


def block_start(line, block, half):
    return min(line * block, half - block)


def local(
    bits, tokens, cotangent, doc_lengths, norm_attn, norm_ffn, w_qkv, b_qkv, w_out, w_gateup, w_down
):
    dp = ("z", *bits)
    tensor_size = lax.axis_size("t")
    count = tokens.shape[0]
    length = count * tensor_size
    layers = w_qkv.shape[0]
    qkv_width = w_qkv.shape[2]
    rows = w_qkv.shape[1]
    half = w_down.shape[2]
    block = block_width(half)
    positions, allowed = doc_layout(doc_lengths[0], length)
    cosine, sine = rope_tables(positions, HD)
    turned = jnp.where(jnp.arange(HD) < HD // 2, -sine, sine)
    tables = (cosine, turned, allowed.astype(F32))
    gain_attn = norm_attn.astype(F32)
    gain_ffn = norm_ffn.astype(F32)
    bias_all = b_qkv.astype(F32)
    line = lax.axis_index("z")
    valid = jnp.arange(block) >= line * block - jnp.minimum(line * block, half - block)
    flats = [jnp.concatenate([w_qkv[layer], w_out[layer]], axis=1) for layer in range(layers)]
    saved = []
    for layer in range(layers):
        gains = (gain_attn[layer : layer + 1], gain_ffn[layer : layer + 1])
        if layer == 0:
            start, more, weight = tokens, flats[1], flats[0]
        else:
            start, more, weight = middle, in_slots(partial, 2 * LINE), attn_weights[layer]
        out = front(
            start, more, gains, bias_all[layer : layer + 1], tables, weight, w_gateup, w_down,
            layer, LINE, bits, block, qkv_width, 8 + layer,
        )
        (state, middle, xa_all, query, key, value, log_total, attended) = out[:8]
        xf_all, gu_w, down_w = (item.reshape(-1, item.shape[2]) for item in out[8:11])
        if layer == 0:
            attn_weights = out[11:]
            xf_all, late = lax.optimization_barrier((xf_all, cotangent))
            gm_all = lax.all_gather(late, ("z", "t"), axis=0, tiled=True)
        both_w = attn_weights[layer]
        gate_up = jnp.dot(xf_all, gu_w, preferred_element_type=F32)
        gate = gate_up[:, :block]
        up = gate_up[:, block:]
        act = jnp.where(valid, jax.nn.silu(gate) * up, 0.0).astype(LOW)
        partial = contract_last(act, down_w, LOW)
        saved.append(
            (state, xa_all, query, key, value, log_total, attended)
            + (middle, xf_all, gate, up, act, gu_w, down_w, both_w)
        )
    grad, branch, above = cotangent, in_slots(partial, 2 * LINE), []
    grads_attn = []
    for layer in reversed(range(layers)):
        (state_in, xa_all, query, key, value, log_total, attended) = saved[layer][:7]
        (middle, xf_all, gate, up, act, gu_w, down_w, both_w) = saved[layer][7:]
        d_down = contract_first(gm_all, act, LOW)
        d_act = jnp.dot(gm_all, down_w, preferred_element_type=F32)
        sig = jax.nn.sigmoid(gate)
        d_gate = d_act * up * sig * (1.0 + gate * (1.0 - sig))
        d_up = d_act * gate * sig
        d_gu = jnp.concatenate(
            [jnp.where(valid, d_gate, 0.0), jnp.where(valid, d_up, 0.0)], axis=1
        ).astype(LOW)
        d_gateup = contract_first(xf_all, d_gu, LOW)
        partial = in_slots(contract_last(d_gu, gu_w, LOW), 2 * LINE)
        wide = (in_slots(d_gateup, d_gateup.shape[0] // rows), in_slots(d_down, d_down.shape[0] // rows))
        gains = (gain_attn[layer : layer + 1], gain_ffn[layer : layer + 1])
        ins = (grad, state_in, middle, *gains, *tables, query, key, value, log_total, xa_all, attended, both_w)
        out = back(
            partial, branch, *wide, ins, above if layer == 0 else [], LINE, bits, qkv_width, 16 + layer
        )
        (grad, _, _, d_bias, part_a, part_f), rest = out[:6], out[6:]
        if layer > 0:
            (*folded, d_attn), rest = rest[: LINE + 1], rest[LINE + 1 :]
            arrived = [
                lax.ppermute(folded[o - 1], "z", [(i, (i + o) % LINE) for i in range(LINE)])
                for o in range(1, LINE)
            ]
            arrived.append(folded[LINE - 1])
        else:
            (blocks, d_attn), rest = rest[:2], rest[2:]
        if branch is not None:
            output = (middle + rest[0]).astype(LOW)
            branch = None
        if layer > 0:
            gm_all = rest[-1].reshape(-1, rest[-1].shape[2])
            above = [part_a, part_f, d_bias]
            d_attn = lax.psum_scatter(
                d_attn.reshape(-1, d_attn.shape[2]), dp, scatter_dimension=0, tiled=True
            )
        grads_attn.append(d_attn)
    sums = rest[-1]
    side = lax.axis_index("t")
    d_gu_all, d_dn_all, d_qkv_all, d_out_all = settle(blocks, arrived, grads_attn[::-1], half, qkv_width)
    return (
        output,
        grad,
        sums[0:2],
        sums[2:4],
        d_qkv_all,
        lax.dynamic_slice_in_dim(sums, 4 + 2 * side, 2, 0)[:, :qkv_width],
        d_out_all,
        d_gu_all,
        d_dn_all,
    )


def solution(mesh):
    dp_size, tensor_size = mesh.devices.shape
    rest = dp_size // LINE
    bits = tuple(f"r{number}" for number in range(rest.bit_length() - 1))
    shape = (LINE, *([2] * len(bits)), tensor_size)
    fine = Mesh(mesh.devices.reshape(shape), ("z", *bits, "t"))
    dp = ("z", *bits)
    rows = P((*dp, "t"), None)
    weight = P(None, dp, "t")

    def step(*args):
        return local(bits, *args)

    return jax.shard_map(
        step,
        mesh=fine,
        in_specs=(rows, rows, P(dp, None), P(), P(), weight, P(None, "t"), weight, weight, weight),
        out_specs=(rows, rows, P(), P(), weight, P(None, "t"), weight, weight, weight),
        check_vma=False,
    )
```

```python
import functools
import math

import jax
import jax.numpy as jnp
from jax import lax
from jax.experimental import pallas as pl
from jax.experimental.pallas import tpu as pltpu
from jax.sharding import Mesh
from jax.sharding import PartitionSpec as P

HD = 128
LINE = 4
LANES = 128
LOW = jnp.bfloat16
F32 = jnp.float32
MESH = pl.DeviceIdType.MESH


def doc_layout(lens, count):
    rows = jnp.arange(count, dtype=jnp.int32)
    doc = jnp.zeros((count,), jnp.int32)
    start = jnp.zeros((count,), jnp.int32)
    bound = jnp.int32(0)
    for number in range(lens.shape[0]):
        bound = bound + lens[number]
        after = (rows >= bound).astype(jnp.int32)
        doc = doc + after
        start = start + after * lens[number]
    positions = rows - start
    allowed = (doc[:, None] == doc[None, :]) & (rows[:, None] >= rows[None, :])
    return (positions, allowed)


def rope_tables(positions, width):
    index = jnp.arange(width // 2, dtype=F32)
    freq = jnp.exp(-(2.0 * index / width) * math.log(1000000.0))
    angle = positions.astype(F32)[:, None] * freq[None, :]
    return (
        jnp.concatenate([jnp.cos(angle)] * 2, axis=1),
        jnp.concatenate([jnp.sin(angle)] * 2, axis=1),
    )


def contract_last(left, right, out=F32):
    return lax.dot_general(left, right, (((1,), (1,)), ((), ())), preferred_element_type=out)


def contract_first(left, right, out=F32):
    return lax.dot_general(left, right, (((0,), (0,)), ((), ())), preferred_element_type=out)


def take(array, index, axis):
    return lax.dynamic_index_in_dim(array, index, axis, keepdims=False)


def greet(axes_targets, conditions):
    barrier = pltpu.get_barrier_semaphore()
    for (axis, target), condition in zip(axes_targets, conditions):
        def signal(axis=axis, target=target):
            pl.semaphore_signal(barrier, inc=1, device_id={axis: target}, device_id_type=MESH)
        if condition is None:
            signal()
        else:
            pl.when(condition)(signal)
    amount = sum(1 if c is None else c.astype(jnp.int32) for c in conditions)
    pl.semaphore_wait(barrier, amount)


def slot_of(line, values):
    slot = line
    for value in values:
        slot = slot * 2 + value
    return slot


def both(*conditions):
    given = [c for c in conditions if c is not None]
    return functools.reduce(jnp.logical_and, given) if given else None


def guarded(condition, action):
    if condition is None:
        action()
    else:
        pl.when(condition)(action)


def bit_flips(variant, stage, count):
    return [(variant >> b) & 1 for b in range(stage)] + [1] + [0] * (count - stage - 1)


class Gather:
    def __init__(self, size, bits, x_ref, out_ref, own_sem, line_sems, bit_sems, recv_sems):
        self.size, self.bits, self.count = size, bits, len(bits)
        self.x_ref, self.out_ref, self.own_sem = x_ref, out_ref, own_sem
        self.line_sems, self.bit_sems, self.recv_sems = line_sems, bit_sems, recv_sems
        self.z = lax.axis_index("z")
        self.mine = [lax.axis_index(bit) for bit in bits]
        self.own = slot_of(self.z, self.mine)
        self.pending, self.settled = [], False

    def copy(self, slot, first, axis, target, send_sem):
        return pltpu.make_async_remote_copy(
            src_ref=self.x_ref if first else self.out_ref.at[slot],
            dst_ref=self.out_ref.at[slot],
            send_sem=send_sem,
            recv_sem=self.recv_sems.at[slot],
            device_id={axis: target},
            device_id_type=MESH,
        )

    def start(self, condition, make):
        self.pending.append((condition, make))
        guarded(condition, lambda: make().start())

    def arrived(self, condition, slot, axis, target):
        guarded(
            condition,
            lambda: self.copy(slot, False, axis, target, self.line_sems.at[0, 0]).wait_recv(),
        )

    def spread(self, condition, slot, first, number, side, variant, after):
        for stage in range(after, self.count):
            self.start(
                condition,
                functools.partial(
                    self.copy,
                    slot,
                    first,
                    self.bits[stage],
                    1 - self.mine[stage],
                    self.bit_sems.at[number, side, variant, stage],
                ),
            )

    def line_of(self, number, side):
        line = self.z - number if side == 0 else self.z + number
        if number == 0:
            return line, None
        return line, (line >= 0 if side == 0 else line < self.size)

    def on_bits(self, number):
        for side in range(1 if number == 0 else 2):
            line, condition = self.line_of(number, side)
            for stage in range(self.count):
                for variant in range(2**stage):
                    flips = bit_flips(variant, stage, self.count)
                    slot = slot_of(line, [1 - m if f else m for m, f in zip(self.mine, flips)])
                    self.arrived(condition, slot, self.bits[stage], 1 - self.mine[stage])
                    code = sum(f << b for b, f in enumerate(flips))
                    self.spread(condition, slot, False, number, side, code, stage + 1)

    def begin(self):
        pltpu.make_async_copy(self.x_ref, self.out_ref.at[self.own], self.own_sem).start()
        z, size = self.z, self.size
        first = functools.partial(self.copy, self.own, True, "z")
        self.start(z < size - 1, functools.partial(first, z + 1, self.line_sems.at[0, 0]))
        self.start(z > 0, functools.partial(first, z - 1, self.line_sems.at[0, 1]))
        self.spread(None, self.own, True, 0, 0, 0, 0)

    def step(self, number):
        z, size = self.z, self.size
        for side in range(2):
            line, condition = self.line_of(number, side)
            slot = slot_of(line, self.mine)
            back = z - 1 if side == 0 else z + 1
            onto = z + 1 if side == 0 else z - 1
            self.arrived(condition, slot, "z", back)
            self.start(
                both(condition, onto < size if side == 0 else onto >= 0),
                functools.partial(self.copy, slot, False, "z", onto, self.line_sems.at[number, side]),
            )
            self.spread(condition, slot, False, number, side, 0, 0)

    def middle(self):
        for number in range(1, self.size):
            self.step(number)
            self.on_bits(number - 1)
        self.on_bits(self.size - 1)

    def settle(self):
        if not self.settled:
            pltpu.make_async_copy(self.x_ref, self.out_ref.at[self.own], self.own_sem).wait()
            self.settled = True

    def end(self):
        self.settle()
        for condition, make in self.pending:
            guarded(condition, lambda make=make: make().wait_send())


def gather_semaphores(size, bits):
    slots = size * 2 ** len(bits)
    return [
        pltpu.SemaphoreType.DMA,
        pltpu.SemaphoreType.DMA((size, 2)),
        pltpu.SemaphoreType.DMA((size, 2, 2 ** len(bits), len(bits))),
        pltpu.SemaphoreType.DMA((slots,)),
    ]


class Exchange:
    def __init__(self, size, bits, block, half, gu_ref, dn_ref, gu_out, dn_out, sems):
        self.size, self.bits, self.count = size, bits, len(bits)
        self.block, self.half = block, half
        self.gu_ref, self.dn_ref, self.gu_out, self.dn_out = gu_ref, dn_ref, gu_out, dn_out
        self.own_sems, self.line_sems, self.bit_sems, self.recv_sems = sems
        self.z = lax.axis_index("z")
        self.mine = [lax.axis_index(bit) for bit in bits]
        self.own = slot_of(self.z, self.mine)
        self.others = [lax.rem(self.z + o, size) for o in range(1, size)]
        self.pending = []

    def pieces(self, target, slot):
        low = pl.multiple_of(jnp.minimum(target * self.block, self.half - self.block), LANES)
        high = pl.multiple_of(low + self.half, LANES)
        width = self.block
        return [
            (self.gu_ref.at[:, pl.ds(low, width)], self.gu_out.at[slot, :, pl.ds(0, width)]),
            (self.gu_ref.at[:, pl.ds(high, width)], self.gu_out.at[slot, :, pl.ds(width, width)]),
            (self.dn_ref.at[:, pl.ds(low, width)], self.dn_out.at[slot]),
        ]

    def line_copy(self, place, piece, slot):
        source, landing = self.pieces(self.others[place], slot)[piece]
        return pltpu.make_async_remote_copy(
            src_ref=source,
            dst_ref=landing,
            send_sem=self.line_sems.at[place, piece],
            recv_sem=self.recv_sems.at[slot, piece],
            device_id={"z": self.others[place]},
            device_id_type=MESH,
        )

    def own_copy(self, piece):
        source, landing = self.pieces(self.z, self.own)[piece]
        return pltpu.make_async_copy(source, landing, self.own_sems.at[piece])

    def bit_copy(self, slot, piece, stage, send_sem):
        ref = (self.gu_out, None, self.dn_out)[piece]
        return pltpu.make_async_remote_copy(
            src_ref=ref.at[slot],
            dst_ref=ref.at[slot],
            send_sem=send_sem,
            recv_sem=self.recv_sems.at[slot, piece],
            device_id={self.bits[stage]: 1 - self.mine[stage]},
            device_id_type=MESH,
        )

    def first_copy(self, slot, piece, stage, send_sem):
        source, landing = self.pieces(self.z, slot)[piece]
        return pltpu.make_async_remote_copy(
            src_ref=source,
            dst_ref=landing,
            send_sem=send_sem,
            recv_sem=self.recv_sems.at[slot, piece],
            device_id={self.bits[stage]: 1 - self.mine[stage]},
            device_id_type=MESH,
        )

    def spread(self, slot, number, variant, after):
        for stage in range(after, self.count):
            for piece in (0, 2):
                make = functools.partial(
                    self.bit_copy, slot, piece, stage, self.bit_sems.at[number, variant, stage, piece]
                )
                self.pending.append(make)
                make().start()

    def on_bits(self, number):
        line = lax.rem(self.z - number + self.size, self.size)
        for stage in range(self.count):
            for variant in range(2**stage):
                flips = bit_flips(variant, stage, self.count)
                slot = slot_of(line, [1 - m if f else m for m, f in zip(self.mine, flips)])
                if number == 0 and variant == 0:
                    for piece in range(3):
                        self.first_copy(slot, piece, stage, self.own_sems.at[0]).wait_recv()
                else:
                    for piece in (0, 2):
                        self.bit_copy(slot, piece, stage, self.own_sems.at[0]).wait_recv()
                self.spread(slot, number, sum(f << b for b, f in enumerate(flips)), stage + 1)

    def begin(self):
        for stage in range(self.count):
            for piece in range(3):
                make = functools.partial(
                    self.first_copy, self.own, piece, stage, self.bit_sems.at[0, 0, stage, piece]
                )
                self.pending.append(make)
                make().start()
        for piece in range(3):
            self.own_copy(piece).start()

    def send(self, offset):
        for piece in range(3):
            self.line_copy(offset - 1, piece, self.own).start()

    def sent(self, offset):
        for piece in range(3):
            self.line_copy(offset - 1, piece, self.own).wait_send()

    def step(self, offset):
        slot = slot_of(lax.rem(self.z - offset + self.size, self.size), self.mine)
        for piece in range(3):
            self.line_copy(0, piece, slot).wait_recv()
        self.spread(slot, offset, 0, 0)

    def end(self):
        for piece in range(3):
            self.own_copy(piece).wait()
        for make in self.pending:
            make().wait_send()


class Fold:
    def __init__(self, size, bits, order, p_ref, own_buf, sums, stage_in, stage_out, own_sems, send_sems, recv_sems):
        self.size, self.bits, self.count, self.order = size, bits, len(bits), order
        self.last = self.count - 1
        self.p_ref, self.own_buf, self.sums = p_ref, own_buf, sums
        self.stage_in, self.stage_out = stage_in, stage_out
        self.own_sems, self.send_sems, self.recv_sems = own_sems, send_sems, recv_sems
        self.z = lax.axis_index("z")
        self.mine = [lax.axis_index(bit) for bit in bits]

    def line(self, place):
        if self.order is None:
            return relay_line(self.z, place, self.size)
        return lax.rem(self.z + self.order[place], self.size)

    def index(self, place, stage, variant):
        return place * (2**self.count - 1) + 2**stage - 1 + variant

    def slot(self, place, variant, flip):
        flips = [(variant >> b) & 1 for b in range(self.last)] + [flip]
        return slot_of(self.line(place), [1 - m if f else m for m, f in zip(self.mine, flips)])

    def copy(self, place, stage, variant):
        index = self.index(place, stage, variant)
        if stage == self.last:
            source = self.p_ref.at[self.slot(place, variant, 1)]
        else:
            source = self.stage_out.at[place * (2**self.last - 1) + 2**stage - 1 + variant]
        return pltpu.make_async_remote_copy(
            src_ref=source,
            dst_ref=self.stage_in.at[index],
            send_sem=self.send_sems.at[index],
            recv_sem=self.recv_sems.at[index],
            device_id={self.bits[stage]: 1 - self.mine[stage]},
            device_id_type=MESH,
        )

    def own_copy(self, place, variant):
        number = place * 2**self.last + variant
        return pltpu.make_async_copy(
            self.p_ref.at[self.slot(place, variant, 0)], self.own_buf.at[number], self.own_sems.at[number]
        )

    def begin(self, places=None):
        for place in range(self.size) if places is None else places:
            for variant in reversed(range(2**self.last)):
                self.copy(place, self.last, variant).start()
                self.own_copy(place, variant).start()

    def stage(self, place, stage, done=None):
        for variant in reversed(range(2**stage)):
            if stage == self.last:
                self.own_copy(place, variant).wait()
                held = self.own_buf[place * 2**self.last + variant].astype(F32)
            else:
                held = self.sums[place * (2**self.last - 1) + 2**stage - 1 + variant].astype(F32)
            self.copy(place, stage, variant).wait_recv()
            total = held + self.stage_in[self.index(place, stage, variant)].astype(F32)
            if stage == 0:
                done(place, total)
                continue
            lower = variant & (2 ** (stage - 1) - 1)
            number = place * (2**self.last - 1) + 2 ** (stage - 1) - 1 + lower
            if variant >> (stage - 1):
                self.stage_out[number] = total.astype(LOW)
                self.copy(place, stage - 1, lower).start()
            else:
                self.sums[number] = total.astype(LOW)

    def end(self):
        for place in range(self.size):
            for stage in range(self.count):
                for variant in range(2**stage):
                    self.copy(place, stage, variant).wait_send()


def fold_scratch(size, bits, rows, columns):
    count = len(bits)
    inner, lower = size * (2**count - 1), size * (2 ** (count - 1) - 1)
    return [
        pltpu.VMEM((size * 2 ** (count - 1), rows, columns), LOW),
        pltpu.VMEM((max(lower, 1), rows, columns) if lower else (1, 16, LANES), LOW),
        pltpu.VMEM((inner, rows, columns), LOW),
        pltpu.VMEM((max(lower, 1), rows, columns) if lower else (1, 16, LANES), LOW),
        pltpu.SemaphoreType.DMA((size * 2 ** (count - 1),)),
        pltpu.SemaphoreType.DMA((inner,)),
        pltpu.SemaphoreType.DMA((inner,)),
    ]


def relay_line(z, place, size):
    order = []
    for line in range(size):
        others = sorted((other for other in range(size) if other != line), key=lambda other: -abs(other - line))
        order.append([*others, line])
    return sum(jnp.where(z == line, order[line][place], 0) for line in range(size))


class Relay:
    def __init__(self, size, bits, p_ref, out_ref, line_out, line_in, line_send, line_recv, *fold):
        self.fold = Fold(size, bits, None, p_ref, *fold)
        self.size, self.out_ref, self.z = size, out_ref, lax.axis_index("z")
        self.line_out, self.line_in, self.line_send, self.line_recv = line_out, line_in, line_send, line_recv

    def line_copy(self, place, line):
        right = (line > self.z).astype(jnp.int32)
        slot = (1 - right) * (self.size - 1) + jnp.abs(line - self.z) - 1
        return pltpu.make_async_remote_copy(
            src_ref=self.line_out.at[place],
            dst_ref=self.line_in.at[slot],
            send_sem=self.line_send.at[place],
            recv_sem=self.line_recv.at[slot],
            device_id={"z": self.z + 2 * right - 1},
            device_id_type=MESH,
        )

    def landed(self, slot):
        pltpu.make_async_remote_copy(
            src_ref=self.line_in.at[slot],
            dst_ref=self.line_in.at[slot],
            send_sem=self.line_send.at[0],
            recv_sem=self.line_recv.at[slot],
            device_id={"z": lax.rem(self.z + 1, self.size)},
            device_id_type=MESH,
        ).wait_recv()

    def done(self, place, total):
        if place == self.size - 1:
            self.out_ref[...] = total
            return
        line = self.fold.line(place)
        right = line > self.z
        self.line_out[place] = total.astype(LOW)
        slot = (1 - right.astype(jnp.int32)) * (self.size - 1) + jnp.abs(line - self.z)

        @pl.when(jnp.where(right, self.z > 0, self.z < self.size - 1))
        def _():
            self.landed(slot)
            self.line_out[place] = (total + self.line_in[slot].astype(F32)).astype(LOW)

        self.line_copy(place, line).start()

    def begin(self, places=None):
        self.fold.begin(places)

    def place(self, place):
        for stage in reversed(range(self.fold.count)):
            self.fold.stage(place, stage, self.done)

    def finish(self):
        for slot, there in ((0, self.z > 0), (self.size - 1, self.z < self.size - 1)):

            @pl.when(there)
            def _(slot=slot):
                self.landed(slot)
                self.out_ref[...] += self.line_in[slot].astype(F32)

    def end(self):
        self.fold.end()
        for place in range(self.size - 1):
            self.line_copy(place, self.fold.line(place)).wait_send()


def scatter_scratch(size, bits, rows, columns):
    lands = 2 * (size - 1)
    return [
        pltpu.VMEM((size - 1, rows, columns), LOW),
        pltpu.VMEM((lands, rows, columns), LOW),
        pltpu.SemaphoreType.DMA((size - 1,)),
        pltpu.SemaphoreType.DMA((lands,)),
        *fold_scratch(size, bits, rows, columns),
    ]


SCATTER_REFS = 11


class Total:
    def __init__(self, size, bits, x_ref, out_ref, held, landed, send_sems, recv_sems):
        self.size, self.bits, self.count = size, bits, len(bits)
        self.x_ref, self.out_ref, self.held, self.landed = x_ref, out_ref, held, landed
        self.send_sems, self.recv_sems = send_sems, recv_sems
        self.z = lax.axis_index("z")
        self.others = [lax.rem(self.z + o, size) for o in range(1, size)]

    def copy(self, number):
        if number < self.count:
            axis = self.bits[number]
            source, target = self.held.at[number], {axis: 1 - lax.axis_index(axis)}
        else:
            source, target = self.held.at[self.count], {"z": self.others[number - self.count]}
        return pltpu.make_async_remote_copy(
            src_ref=source,
            dst_ref=self.landed.at[number],
            send_sem=self.send_sems.at[number],
            recv_sem=self.recv_sems.at[number],
            device_id=target,
            device_id_type=MESH,
        )

    def begin(self):
        self.held[0] = self.x_ref[...]
        self.copy(0).start()

    def pair(self, number):
        self.copy(number).wait_recv()
        self.held[number + 1] = self.held[number] + self.landed[number]
        if number + 1 < self.count:
            self.copy(number + 1).start()
        else:
            for place in range(self.size - 1):
                self.copy(self.count + place).start()

    def finish(self):
        for place in range(self.size - 1):
            self.copy(self.count + place).wait_recv()
        total = jnp.zeros(self.out_ref.shape, self.out_ref.dtype)
        for line in range(self.size):
            offset = lax.rem(line - self.z + self.size, self.size)
            part = self.held[self.count]
            for o in range(1, self.size):
                part = jnp.where(offset == o, self.landed[self.count + self.size - o - 1], part)
            total = total + part
        self.out_ref[...] = total

    def end(self):
        for number in range(self.count + self.size - 1):
            self.copy(number).wait_send()


def greet_all(size, axes):
    z = lax.axis_index("z")
    greet(
        [("z", lax.rem(z + o, size)) for o in range(1, size)]
        + [(axis, 1 - lax.axis_index(axis)) for axis in axes],
        [None] * (size - 1 + len(axes)),
    )


def in_groups(refs, sizes):
    groups, at = [], 0
    for number in sizes:
        groups.append(refs[at : at + number])
        at += number
    return groups


def comm_params(collective_id):
    return pltpu.CompilerParams(
        collective_id=collective_id, has_side_effects=True, vmem_limit_bytes=61 * 2**20
    )


def at_microseconds(time):
    return pl.CostEstimate(flops=0, transcendentals=0, bytes_accessed=time * 3500000)


class Attend:
    def __init__(self, rows_ref, gain_ref, bias_ref, cos_ref, sin_ref, mask_ref, w_ref, outs, scratch, width, epsilon=1e-06):
        self.gain_ref, self.bias_ref, self.w_ref = gain_ref, bias_ref, w_ref
        self.cos_ref, self.sin_ref, self.mask_ref = cos_ref, sin_ref, mask_ref
        self.state_ref, self.middle_ref, self.xa_ref, self.q_ref, self.k_ref, self.v_ref, self.lse_ref, self.o_ref = outs
        self.send_buf, self.land_buf, self.send_sems, self.recv_sems = scratch
        self.rows_ref = rows_ref
        self.t = lax.axis_index("t")
        self.slots, self.few = w_ref.shape[0], w_ref.shape[1]
        self.model = self.slots * self.few
        self.count = rows_ref.shape[0]
        self.q_width = self.q_ref.shape[1]
        self.width = width
        self.epsilon = epsilon

    def normed(self, rows, gain_ref):
        factor = lax.rsqrt(jnp.mean(rows * rows, axis=-1, keepdims=True) + self.epsilon)
        return (rows * factor * gain_ref[...]).astype(LOW)

    def xa_copy(self):
        return pltpu.make_async_remote_copy(
            src_ref=self.xa_ref.at[self.t],
            dst_ref=self.xa_ref.at[self.t],
            send_sem=self.send_sems.at[0],
            recv_sem=self.recv_sems.at[0],
            device_id={"t": 1 - self.t},
            device_id_type=MESH,
        )

    def xa_landing(self):
        return pltpu.make_async_remote_copy(
            src_ref=self.xa_ref.at[1 - self.t],
            dst_ref=self.xa_ref.at[1 - self.t],
            send_sem=self.send_sems.at[0],
            recv_sem=self.recv_sems.at[0],
            device_id={"t": 1 - self.t},
            device_id_type=MESH,
        )

    def half_copy(self):
        return pltpu.make_async_remote_copy(
            src_ref=self.send_buf,
            dst_ref=self.land_buf,
            send_sem=self.send_sems.at[1],
            recv_sem=self.recv_sems.at[1],
            device_id={"t": 1 - self.t},
            device_id_type=MESH,
        )

    def begin(self, state):
        self.state_ref[...] = state
        self.xa_ref[self.t] = self.normed(state, self.gain_ref)
        self.xa_copy().start()

    def columns(self, low, count):
        weight = self.w_ref[:, :, low : low + count].reshape(self.model, count)
        xa = self.xa_ref[...].reshape(2 * self.count, self.model)
        return jnp.dot(xa, weight, preferred_element_type=F32) + self.bias_ref[:, low : low + count]

    def rope(self, values):
        return (values * self.cos_ref[...] + pltpu.roll(values, HD // 2, 1) * self.sin_ref[...]).astype(LOW)

    def keys(self):
        self.xa_landing().wait_recv()
        both_kv = self.columns(self.q_width, 2 * HD)
        self.k_ref[...] = self.rope(both_kv[:, :HD])
        self.v_ref[...] = both_kv[:, HD:].astype(LOW)

    def heads(self, first):
        lin = self.columns(first * HD, 2 * HD)
        for number in range(2):
            head = first + number
            low = head * HD
            query = self.rope(lin[:, number * HD : (number + 1) * HD])
            self.q_ref[:, low : low + HD] = query
            raw = lax.dot_general(
                query, self.k_ref[...], (((1,), (1,)), ((), ())), preferred_element_type=F32
            )
            scores = jnp.where(self.mask_ref[...] > 0, raw * (1.0 / math.sqrt(HD)), -1e30)
            top = jnp.max(scores, axis=-1, keepdims=True)
            expo = jnp.exp(scores - top)
            whole = jnp.sum(expo, axis=-1, keepdims=True)
            probs = (expo / whole).astype(LOW)
            self.lse_ref[head] = top + jnp.log(whole)
            out = jnp.dot(probs, self.v_ref[...], preferred_element_type=F32).astype(LOW)
            self.o_ref[0, :, low : low + HD] = out[: self.count]
            self.o_ref[1, :, low : low + HD] = out[self.count :]

    def projected(self, half, step):
        left = self.o_ref[half]
        for low in range(0, self.slots, step):
            weight = self.w_ref[low : low + step, :, self.width :].reshape(step * self.few, self.q_width)
            yield low * self.few, lax.dot_general(
                left, weight, (((1,), (1,)), ((), ())), preferred_element_type=F32
            )

    def other_half(self):
        for low, part in self.projected(1 - self.t, self.slots // 4):
            self.send_buf[:, low : low + part.shape[1]] = part.astype(LOW)
        self.half_copy().start()

    def own_half(self):
        for low, part in self.projected(self.t, self.slots // 4):
            where = slice(low, low + part.shape[1])
            self.middle_ref[:, where] = self.state_ref[:, where] + part

    def finish(self, gain_ref, xf_ref):
        self.half_copy().wait_recv()
        middle = self.middle_ref[...] + self.land_buf[...].astype(F32)
        self.middle_ref[...] = middle
        xf_ref[...] = self.normed(middle, gain_ref)

    def end(self):
        self.xa_copy().wait_send()
        self.half_copy().wait_send()


def front_kernel(size, bits, block, half, layer, width, *refs):
    first = layer == 0
    inputs, outs, refs = in_groups(refs, [11, 13 if first else 11, len(refs)])
    (x_ref, more_ref, ga_ref, gf_ref, bias_ref, cos_ref, sin_ref, mask_ref, at_ref, gu_ref, dn_ref) = inputs
    xf_out, gu_out, dn_out = outs[8:11]
    (w_ref, xf_ref, at_sem), pair, feed_sems, rows_sems, rest = in_groups(refs, [3, 4, 4, 4, len(refs)])
    greet_all(size, ("t", *bits))
    work = Attend(
        x_ref, ga_ref, bias_ref, cos_ref, sin_ref, mask_ref, w_ref, outs[:8], pair, width
    )
    feed = Exchange(
        size, bits, block, half, gu_ref.at[layer], dn_ref.at[layer], gu_out, dn_out, feed_sems
    )
    rows = Gather(size, ("t",), xf_ref, xf_out, *rows_sems)
    if first:
        at_sems, next_sems = in_groups(rest, [4, 4])
        attention = Gather(size, bits, at_ref, w_ref, *at_sems)
        ahead = Gather(size, bits, more_ref, outs[12], *next_sems)
        moved = pltpu.make_async_copy(w_ref, outs[11], at_sem)
        attention.begin()
        feed.begin()
        work.begin(x_ref[...].astype(F32))
        attention.step(1)
        attention.step(2)
        attention.on_bits(0)
        attention.step(3)
        feed.send(1)
        attention.on_bits(1)
        attention.on_bits(2)
        attention.on_bits(3)
        attention.settle()
        moved.start()
        feed.on_bits(0)
        feed.sent(1)
        feed.send(3)
        feed.step(1)
        steps = (attention, ahead)
    else:
        total_ref, *rest = rest
        side = Relay(size, ("t",), more_ref, total_ref, *rest)
        moved = pltpu.make_async_copy(at_ref, w_ref, at_sem)
        moved.start()
        side.begin()
        feed.begin()
        for place in range(size):
            side.place(place)
        feed.send(1)
        side.finish()
        work.begin(x_ref[...] + total_ref[...])
        moved.wait()
        feed.on_bits(0)
        feed.sent(1)
        feed.send(3)
        feed.step(1)
        steps = (side,)
    work.keys()
    work.heads(0)
    work.heads(2)
    work.heads(4)
    work.other_half()
    work.own_half()
    feed.sent(3)
    feed.send(2)
    feed.step(3)
    feed.on_bits(1)
    work.finish(gf_ref, xf_ref)
    rows.begin()
    if first:
        ahead.begin()
    rows.step(1)
    rows.on_bits(0)
    if first:
        ahead.step(1)
    rows.step(2)
    feed.sent(2)
    feed.step(2)
    rows.on_bits(1)
    if first:
        ahead.on_bits(0)
    feed.on_bits(3)
    rows.step(3)
    if first:
        ahead.step(2)
    rows.on_bits(2)
    feed.on_bits(2)
    rows.on_bits(3)
    if first:
        ahead.on_bits(1)
        ahead.step(3)
        ahead.on_bits(2)
        ahead.on_bits(3)
        moved.wait()
    for item in (*steps, feed, work, rows):
        item.end()


def front(x, more, gains, bias, tables, at, gu, dn, layer, size, bits, block, width, collective_id):
    slots = size * 2 ** len(bits)
    count, model = x.shape
    few, half = dn.shape[1:]
    length = 2 * count
    q_width = at.shape[-1] - width
    first = layer == 0
    held, far = pl.BlockSpec(memory_space=pltpu.VMEM), pl.BlockSpec(memory_space=pl.ANY)
    shape = jax.ShapeDtypeStruct
    weight = (slots, few, at.shape[-1])
    more_scratch = (
        gather_semaphores(size, bits) * 2
        if first
        else [pltpu.VMEM((count, model), F32), *scatter_scratch(size, ("t",), count, model)]
    )
    return pl.pallas_call(
        functools.partial(front_kernel, size, bits, block, half, layer, width),
        out_shape=(
            shape((count, model), F32),
            shape((count, model), F32),
            shape((2, count, model), LOW),
            shape((length, q_width), LOW),
            shape((length, HD), LOW),
            shape((length, HD), LOW),
            shape((q_width // HD, length, 1), F32),
            shape((2, count, q_width), LOW),
            shape((2 * size, count, model), LOW),
            shape((slots, few, 2 * block), LOW),
            shape((slots, few, block), LOW),
            *([shape(weight, LOW)] * 2 if first else []),
        ),
        in_specs=[held, far] + [held] * 6 + [far] * 3,
        out_specs=[held] * 8 + [far] * (5 if first else 3),
        scratch_shapes=[
            pltpu.VMEM(weight, LOW),
            pltpu.VMEM((count, model), LOW),
            pltpu.SemaphoreType.DMA,
            pltpu.VMEM((count, model), LOW),
            pltpu.VMEM((count, model), LOW),
            pltpu.SemaphoreType.DMA((2,)),
            pltpu.SemaphoreType.DMA((2,)),
            pltpu.SemaphoreType.DMA((3,)),
            pltpu.SemaphoreType.DMA((size - 1, 3)),
            pltpu.SemaphoreType.DMA((size, 2 ** len(bits), len(bits), 3)),
            pltpu.SemaphoreType.DMA((slots, 3)),
            *gather_semaphores(size, ("t",)),
            *more_scratch,
        ],
        compiler_params=comm_params(collective_id),
        cost_estimate=at_microseconds(150),
    )(x, more, *gains, bias, *tables, at, gu, dn)


class AttendBack:
    def __init__(self, ins, outs, scratch, width, epsilon=1e-06):
        (self.g_ref, self.state_ref, self.middle_ref, self.ga_gain, self.gf_gain, self.cos_ref, self.sin_ref) = ins[:7]
        (self.mask_ref, self.q_ref, self.k_ref, self.v_ref, self.lse_ref, self.xa_ref, self.o_ref, self.far_w) = ins[7:]
        (self.grad_ref, self.ga_ref, self.lin_ref, self.bias_ref, self.pa_ref, self.pf_ref) = outs
        (self.w_ref, self.w_sem, self.dk, self.dv, self.sum_buf, self.send_buf, self.land_buf) = scratch[:7]
        (self.send_sems, self.recv_sems) = scratch[7:]
        self.t = lax.axis_index("t")
        self.slots, self.few = self.w_ref.shape[:2]
        self.model = self.slots * self.few
        self.count = self.state_ref.shape[0]
        self.q_width = self.q_ref.shape[1]
        self.width, self.epsilon = width, epsilon

    def pair_copy(self, number, source, landing):
        return pltpu.make_async_remote_copy(
            src_ref=source,
            dst_ref=landing,
            send_sem=self.send_sems.at[number],
            recv_sem=self.recv_sems.at[number],
            device_id={"t": 1 - self.t},
            device_id_type=MESH,
        )

    def ga_copy(self, side):
        return self.pair_copy(0, self.ga_ref.at[side], self.ga_ref.at[side])

    def half_copy(self):
        return self.pair_copy(1, self.send_buf, self.land_buf)

    def weight_copy(self):
        return pltpu.make_async_copy(self.far_w, self.w_ref, self.w_sem)

    def norm_back(self, upstream, rows, gain):
        factor = lax.rsqrt(jnp.mean(rows * rows, axis=-1, keepdims=True) + self.epsilon)
        scaled = upstream * gain
        part = jnp.sum(upstream * rows * factor, axis=0, keepdims=True)
        inner = jnp.mean(scaled * rows, axis=-1, keepdims=True)
        return factor * scaled - rows * factor**3 * inner, part

    def prepare(self):
        self.weight_copy().start()

    def begin(self, d_xf):
        d_mid, part = self.norm_back(d_xf, self.middle_ref[...], self.gf_gain[...])
        self.pf_ref[...] = part
        grad = self.g_ref[...].astype(F32) + d_mid
        self.grad_ref[...] = grad
        self.ga_ref[self.t] = grad.astype(LOW)
        self.ga_copy(self.t).start()
        self.dk[...] = jnp.zeros_like(self.dk)
        self.dv[...] = jnp.zeros_like(self.dv)

    def arrive(self):
        self.weight_copy().wait()
        self.ga_copy(1 - self.t).wait_recv()

    def unrope(self, values):
        return values * self.cos_ref[...] - pltpu.roll(values, HD // 2, 1) * self.sin_ref[...]

    def keep(self, low, values):
        count = values.shape[1]
        self.bias_ref[:, low : low + count] = jnp.sum(values, axis=0, keepdims=True)
        values = values.astype(LOW)
        self.lin_ref[0, :, low : low + count] = values[: self.count]
        self.lin_ref[1, :, low : low + count] = values[self.count :]

    def heads(self, first):
        low, count = self.width + first * HD, 2 * HD
        weight = self.w_ref[:, :, low : low + count].reshape(self.model, count)
        above = self.ga_ref[...].reshape(2 * self.count, self.model)
        d_out = jnp.dot(above, weight, preferred_element_type=F32).astype(LOW)
        key, value = self.k_ref[...], self.v_ref[...]
        last = (((1,), (1,)), ((), ()))
        early = (((0,), (0,)), ((), ()))
        scale = 1.0 / math.sqrt(HD)
        for number in range(2):
            head = first + number
            query = self.q_ref[:, head * HD : (head + 1) * HD]
            d_head = d_out[:, number * HD : (number + 1) * HD]
            raw = lax.dot_general(query, key, last, preferred_element_type=F32)
            scores = jnp.where(self.mask_ref[...] > 0, raw * scale, -1e30)
            probs = jnp.exp(scores - self.lse_ref[head])
            d_probs = lax.dot_general(d_head, value, last, preferred_element_type=F32)
            centre = jnp.sum(probs * d_probs, axis=-1, keepdims=True)
            d_raw = (probs * (d_probs - centre) * scale).astype(LOW)
            d_query = jnp.dot(d_raw, key, preferred_element_type=F32)
            self.dk[...] += lax.dot_general(d_raw, query, early, preferred_element_type=F32)
            self.dv[...] += lax.dot_general(
                probs.astype(LOW), d_head, early, preferred_element_type=F32
            )
            self.keep(head * HD, self.unrope(d_query))

    def keys(self):
        self.keep(self.q_width, self.unrope(self.dk[...]))
        self.keep(self.q_width + HD, self.dv[...])

    def projected(self, half):
        left, step = self.lin_ref[half], self.slots // 4
        for low in range(0, self.slots, step):
            weight = self.w_ref[low : low + step, :, : self.width].reshape(step * self.few, self.width)
            yield slice(low * self.few, (low + step) * self.few), lax.dot_general(
                left, weight, (((1,), (1,)), ((), ())), preferred_element_type=F32
            )

    def other_half(self):
        for where, part in self.projected(1 - self.t):
            self.send_buf[:, where] = part.astype(LOW)
        self.half_copy().start()

    def own_half(self):
        for where, part in self.projected(self.t):
            self.sum_buf[:, where] = part

    def gradients(self):
        step = self.slots // 4
        early = (((0,), (0,)), ((), ()))
        pairs = ((self.xa_ref, self.lin_ref, 0, self.width), (self.ga_ref, self.o_ref, self.width, self.q_width))
        for left_ref, right_ref, low, count in pairs:
            right = right_ref[...].reshape(2 * self.count, count)
            for slot in range(0, self.slots, step):
                where = slice(slot * self.few, (slot + step) * self.few)
                left = left_ref[:, :, where].reshape(2 * self.count, step * self.few)
                part = lax.dot_general(left, right, early, preferred_element_type=F32)
                self.w_ref[slot : slot + step, :, low : low + count] = part.astype(LOW).reshape(
                    step, self.few, count
                )

    def finish(self):
        self.half_copy().wait_recv()
        d_xa = self.sum_buf[...] + self.land_buf[...].astype(F32)
        d_in, part = self.norm_back(d_xa, self.state_ref[...], self.ga_gain[...])
        self.pa_ref[...] = part
        grad = self.grad_ref[...] + d_in
        self.grad_ref[...] = grad
        return grad

    def end(self):
        self.ga_copy(self.t).wait_send()
        self.half_copy().wait_send()


class Blocks:
    def __init__(self, size, bits, gu_ref, dn_ref, outs, gu_fold, dn_fold, done, sems):
        self.size, self.outs, self.sending = size, outs, len(outs) == 1
        order = list(range(1, size)) + [0]
        self.folds = [Fold(size, bits, order, gu_ref, *gu_fold), Fold(size, bits, order, dn_ref, *dn_fold)]
        self.done = done
        self.own_sems, self.send_sems, self.recv_sems = sems
        self.width, self.narrow = gu_ref.shape[2], dn_ref.shape[2]
        self.z = lax.axis_index("z")

    def columns(self, number):
        return pl.ds(*((0, self.width), (self.width, self.narrow))[number])

    def landing(self, number, slot):
        return self.outs[0].at[slot, :, self.columns(number)]

    def line_copy(self, number, place, slot):
        return pltpu.make_async_remote_copy(
            src_ref=self.done[number].at[place],
            dst_ref=self.landing(number, slot),
            send_sem=self.send_sems.at[number, place],
            recv_sem=self.recv_sems.at[number, slot],
            device_id={"z": self.folds[0].line(place)},
            device_id_type=MESH,
        )

    def own_copy(self, number, place):
        landing = (
            self.landing(number, self.z)
            if self.sending
            else self.outs[place].at[:, self.columns(number)]
        )
        return pltpu.make_async_copy(
            self.done[number].at[place], landing, self.own_sems.at[number, place]
        )

    def begin(self):
        for fold in self.folds:
            fold.begin()

    def inner(self, place):
        for stage in reversed(range(1, self.folds[0].count)):
            for fold in self.folds:
                fold.stage(place, stage)

    def send(self, place):
        for number, fold in enumerate(self.folds):

            def keep(place, total, number=number):
                self.done[number][place] = total.astype(LOW)
                if self.sending and place < self.size - 1:
                    self.line_copy(number, place, self.z).start()
                else:
                    self.own_copy(number, place).start()

            fold.stage(place, 0, keep)

    def end(self):
        for number, fold in enumerate(self.folds):
            for place in range(self.size):
                if not self.sending or place == self.size - 1:
                    self.own_copy(number, place).wait()
                    continue
                slot = lax.rem(self.z - place - 1 + self.size, self.size)
                self.line_copy(number, 0, slot).wait_recv()
                self.line_copy(number, place, self.z).wait_send()
            fold.end()


def back_kernel(size, bits, width, final, *refs):
    top, bottom = final
    counts = [1, 1 if top else 0, 2, 15, 3 if bottom else 0, 6, 1 if bottom else size, 1, 1 if top else 0, 1]
    p_ref, branch_ref, wide, ins, above, outs, folded, (attn_ref,), branch_out, more_out, refs = (
        in_groups(refs, counts + [len(refs)])
    )
    (dxf_ref,), dxf_scratch, gu_fold, dn_fold, done, sems, work_scratch, refs = in_groups(
        refs, [1, SCATTER_REFS, 7, 7, 2, 3, 9, len(refs)]
    )
    greet_all(size, ("t", *bits))
    rows = Relay(size, ("t",), p_ref[0], dxf_ref, *dxf_scratch)
    blocks = Blocks(size, bits, *wide, folded, gu_fold, dn_fold, done, sems)
    work = AttendBack(ins, outs, work_scratch, width)
    branch = None
    if top:
        branch_scratch, refs = in_groups(refs, [SCATTER_REFS, len(refs)])
        branch = Relay(size, ("t",), branch_ref[0], branch_out[0], *branch_scratch)
    if not bottom:
        gm_ref, kept_sem, *gm_sems = refs
        onward = Gather(size, ("t",), gm_ref, more_out[0], *gm_sems)
        kept = pltpu.make_async_copy(work.w_ref, attn_ref, kept_sem)
    else:
        attn_scratch, (x_ref, *small_scratch) = in_groups(refs, [SCATTER_REFS, len(refs)])
        final = Relay(size, bits, work.w_ref, attn_ref, *attn_scratch)
        small = Total(size, ("t", *bits), x_ref, more_out[0], *small_scratch)
    rows.begin()
    blocks.begin()
    work.prepare()
    blocks.inner(0)
    rows.place(0)
    blocks.inner(1)
    blocks.inner(2)
    rows.place(1)
    blocks.inner(3)
    rows.place(2)
    rows.place(3)
    if top:
        branch.begin([0])
    rows.finish()
    work.begin(dxf_ref[...])
    blocks.send(0)
    blocks.send(1)
    if top:
        branch.begin([1])
    work.arrive()
    work.heads(0)
    if top:
        branch.place(0)
    work.heads(2)
    blocks.send(2)
    work.heads(4)
    work.keys()
    work.other_half()
    if top:
        branch.place(1)
        branch.begin([2])
    work.own_half()
    blocks.send(3)
    work.gradients()
    if bottom:
        final.begin()
    else:
        kept.start()
    grad = work.finish()
    if bottom:
        pa_above, pf_above, bias_above = above
        x_ref[...] = jnp.zeros_like(x_ref)
        x_ref[0:1, :] = work.pa_ref[...]
        x_ref[1:2, :] = pa_above[...]
        x_ref[2:3, :] = work.pf_ref[...]
        x_ref[3:4, :] = pf_above[...]
        for side in range(2):
            mine = (work.t == side).astype(F32)
            x_ref[4 + 2 * side : 5 + 2 * side, : work.width] = work.bias_ref[...] * mine
            x_ref[5 + 2 * side : 6 + 2 * side, : work.width] = bias_above[...] * mine
        small.begin()
        for place in range(size):
            final.place(place)
            if place <= len(bits):
                small.pair(place)
        for number in range(size, len(bits) + 1):
            small.pair(number)
        final.finish()
        small.finish()
    if not bottom:
        gm_ref[...] = grad.astype(LOW)
        onward.begin()
    if top:
        branch.begin([3])
        branch.place(2)
    if not bottom:
        onward.step(1)
        onward.on_bits(0)
    if top:
        branch.place(3)
    if not bottom:
        onward.step(2)
        onward.on_bits(1)
        onward.step(3)
        onward.on_bits(2)
        onward.on_bits(3)
    if top:
        branch.finish()
    for steps in (rows, blocks, work, *((final, small) if bottom else (onward,)), branch):
        if steps is not None:
            steps.end()
    if not bottom:
        kept.wait()


def back(partial, branch, gu, dn, ins, above, size, bits, width, collective_id):
    count, model = ins[1].shape
    length, q_width = ins[8].shape
    slots, few, wide = gu.shape
    narrow = dn.shape[2]
    top, bottom = branch is not None, bool(above)
    number = len(bits) + 1
    weight = ins[14].shape
    held, far = pl.BlockSpec(memory_space=pltpu.VMEM), pl.BlockSpec(memory_space=pl.ANY)
    shape = jax.ShapeDtypeStruct
    rows_scratch = scatter_scratch(size, ("t",), count, model)
    return pl.pallas_call(
        functools.partial(back_kernel, size, bits, width, (top, bottom)),
        out_shape=(
            shape((count, model), F32),
            shape((2, count, model), LOW),
            shape((2, count, width), LOW),
            shape((1, width), F32),
            shape((1, model), F32),
            shape((1, model), F32),
            *(
                [shape((size, few, wide + narrow), LOW)]
                if bottom
                else [shape((few, wide + narrow), LOW)] * size
            ),
            shape(weight[1:], F32) if bottom else shape(weight, LOW),
            *([shape((count, model), F32)] if top else []),
            shape((8, model), F32) if bottom else shape((2 * size, count, model), LOW),
        ),
        in_specs=[far] * (4 if top else 3) + [held] * 14 + [far] + [held] * len(above),
        out_specs=[held] * 6
        + ([far, held] if bottom else [far] * (size + 1))
        + [held] * top + [held if bottom else far],
        scratch_shapes=[
            pltpu.VMEM((count, model), F32),
            *rows_scratch,
            *fold_scratch(size, bits, few, wide),
            *fold_scratch(size, bits, few, narrow),
            pltpu.VMEM((size, few, wide), LOW),
            pltpu.VMEM((size, few, narrow), LOW),
            *([pltpu.SemaphoreType.DMA((2, size))] * 3),
            pltpu.VMEM(weight, LOW),
            pltpu.SemaphoreType.DMA,
            pltpu.VMEM((length, HD), F32),
            pltpu.VMEM((length, HD), F32),
            pltpu.VMEM((count, model), F32),
            pltpu.VMEM((count, model), LOW),
            pltpu.VMEM((count, model), LOW),
            pltpu.SemaphoreType.DMA((2,)),
            pltpu.SemaphoreType.DMA((2,)),
            *(rows_scratch if top else []),
            *(
                [
                    *scatter_scratch(size, bits, *weight[1:]),
                    pltpu.VMEM((8, model), F32),
                    pltpu.VMEM((number + 1, 8, model), F32),
                    pltpu.VMEM((number + size - 1, 8, model), F32),
                    pltpu.SemaphoreType.DMA((number + size - 1,)),
                    pltpu.SemaphoreType.DMA((number + size - 1,)),
                ]
                if bottom
                else [
                    pltpu.VMEM((count, model), LOW),
                    pltpu.SemaphoreType.DMA,
                    *gather_semaphores(size, ("t",)),
                ]
            ),
        ],
        compiler_params=comm_params(collective_id),
        cost_estimate=at_microseconds(5 if bottom else 150),
    )(partial, *([branch] if top else []), gu, dn, *ins, *above)


def settle_kernel(half, width, *refs):
    low_ref, *high_refs = refs[: LINE + 1]
    attn_low, attn_high, gu_ref, dn_ref, qkv_ref, out_ref = refs[LINE + 1 :]
    block = low_ref.shape[2] // 3
    z = lax.axis_index("z")
    for layer in range(2):
        for line in range(LINE):
            low = block_start(line, block, half)
            skip = line * block - low
            for part in range(3):
                where = slice(part * block + skip, (part + 1) * block)
                if layer == 0:
                    piece = low_ref[line, :, where]
                else:
                    offset = lax.rem(z - line + LINE, LINE)
                    piece = high_refs[LINE - 1][:, where]
                    for o in range(1, LINE):
                        piece = jnp.where(offset == o, high_refs[o - 1][:, where], piece)
                piece = piece.astype(F32)
                if part < 2:
                    gu_ref[layer, :, part * half + low + skip : part * half + low + block] = piece
                else:
                    dn_ref[layer, :, low + skip : low + block] = piece
    for layer, ref in enumerate((attn_low, attn_high)):
        qkv_ref[layer] = ref[:, :width].astype(F32)
        out_ref[layer] = ref[:, width:].astype(F32)


def settle(blocks, arrived, attn, half, width):
    few = attn[0].shape[0]
    shape = jax.ShapeDtypeStruct
    return pl.pallas_call(
        functools.partial(settle_kernel, half, width),
        out_shape=(
            shape((2, few, 2 * half), F32),
            shape((2, few, half), F32),
            shape((2, few, width), F32),
            shape((2, few, attn[0].shape[1] - width), F32),
        ),
        compiler_params=pltpu.CompilerParams(vmem_limit_bytes=56 * 2**20),
    )(blocks, *arrived, *attn)


def in_slots(partial, slots):
    return partial.reshape(slots, -1, partial.shape[1])


def block_width(half):
    return -(-half // (LINE * LANES)) * LANES


def block_start(line, block, half):
    return min(line * block, half - block)


def local(
    bits, tokens, cotangent, doc_lengths, norm_attn, norm_ffn, w_qkv, b_qkv, w_out, w_gateup, w_down
):
    dp = ("z", *bits)
    tensor_size = lax.axis_size("t")
    count = tokens.shape[0]
    length = count * tensor_size
    layers = w_qkv.shape[0]
    qkv_width = w_qkv.shape[2]
    rows = w_qkv.shape[1]
    half = w_down.shape[2]
    block = block_width(half)
    positions, allowed = doc_layout(doc_lengths[0], length)
    cosine, sine = rope_tables(positions, HD)
    turned = jnp.where(jnp.arange(HD) < HD // 2, -sine, sine)
    tables = (cosine, turned, allowed.astype(F32))
    gain_attn = norm_attn.astype(F32)
    gain_ffn = norm_ffn.astype(F32)
    bias_all = b_qkv.astype(F32)
    line = lax.axis_index("z")
    valid = jnp.arange(block) >= line * block - jnp.minimum(line * block, half - block)
    flats = [jnp.concatenate([w_qkv[layer], w_out[layer]], axis=1) for layer in range(layers)]
    saved = []
    for layer in range(layers):
        gains = (gain_attn[layer : layer + 1], gain_ffn[layer : layer + 1])
        if layer == 0:
            start, more, weight = tokens, flats[1], flats[0]
        else:
            start, more, weight = middle, in_slots(partial, 2 * LINE), attn_weights[layer]
        out = front(
            start, more, gains, bias_all[layer : layer + 1], tables, weight, w_gateup, w_down,
            layer, LINE, bits, block, qkv_width, 8 + layer,
        )
        (state, middle, xa_all, query, key, value, log_total, attended) = out[:8]
        xf_all, gu_w, down_w = (item.reshape(-1, item.shape[2]) for item in out[8:11])
        if layer == 0:
            attn_weights = out[11:]
            xf_all, late = lax.optimization_barrier((xf_all, cotangent))
            gm_all = lax.all_gather(late, ("z", "t"), axis=0, tiled=True)
        both_w = attn_weights[layer]
        gate_up = jnp.dot(xf_all, gu_w, preferred_element_type=F32)
        gate = gate_up[:, :block]
        up = gate_up[:, block:]
        act = jnp.where(valid, jax.nn.silu(gate) * up, 0.0).astype(LOW)
        partial = contract_last(act, down_w, LOW)
        saved.append(
            (state, xa_all, query, key, value, log_total, attended)
            + (middle, xf_all, gate, up, act, gu_w, down_w, both_w)
        )
    grad, branch, above = cotangent, in_slots(partial, 2 * LINE), []
    grads_attn = []
    for layer in reversed(range(layers)):
        (state_in, xa_all, query, key, value, log_total, attended) = saved[layer][:7]
        (middle, xf_all, gate, up, act, gu_w, down_w, both_w) = saved[layer][7:]
        d_down = contract_first(gm_all, act, LOW)
        d_act = jnp.dot(gm_all, down_w, preferred_element_type=F32)
        sig = jax.nn.sigmoid(gate)
        d_gate = d_act * up * sig * (1.0 + gate * (1.0 - sig))
        d_up = d_act * gate * sig
        d_gu = jnp.concatenate(
            [jnp.where(valid, d_gate, 0.0), jnp.where(valid, d_up, 0.0)], axis=1
        ).astype(LOW)
        d_gateup = contract_first(xf_all, d_gu, LOW)
        partial = in_slots(contract_last(d_gu, gu_w, LOW), 2 * LINE)
        wide = (in_slots(d_gateup, d_gateup.shape[0] // rows), in_slots(d_down, d_down.shape[0] // rows))
        gains = (gain_attn[layer : layer + 1], gain_ffn[layer : layer + 1])
        ins = (grad, state_in, middle, *gains, *tables, query, key, value, log_total, xa_all, attended, both_w)
        out = back(
            partial, branch, *wide, ins, above if layer == 0 else [], LINE, bits, qkv_width, 16 + layer
        )
        (grad, _, _, d_bias, part_a, part_f), rest = out[:6], out[6:]
        if layer > 0:
            (*folded, d_attn), rest = rest[: LINE + 1], rest[LINE + 1 :]
            arrived = [
                lax.ppermute(folded[o - 1], "z", [(i, (i + o) % LINE) for i in range(LINE)])
                for o in range(1, LINE)
            ]
            arrived.append(folded[LINE - 1])
        else:
            (blocks, d_attn), rest = rest[:2], rest[2:]
        if branch is not None:
            output = (middle + rest[0]).astype(LOW)
            branch = None
        if layer > 0:
            gm_all = rest[-1].reshape(-1, rest[-1].shape[2])
            above = [part_a, part_f, d_bias]
            d_attn = lax.psum_scatter(
                d_attn.reshape(-1, d_attn.shape[2]), dp, scatter_dimension=0, tiled=True
            )
        grads_attn.append(d_attn)
    sums = rest[-1]
    side = lax.axis_index("t")
    d_gu_all, d_dn_all, d_qkv_all, d_out_all = settle(blocks, arrived, grads_attn[::-1], half, qkv_width)
    return (
        output,
        grad,
        sums[0:2],
        sums[2:4],
        d_qkv_all,
        lax.dynamic_slice_in_dim(sums, 4 + 2 * side, 2, 0)[:, :qkv_width],
        d_out_all,
        d_gu_all,
        d_dn_all,
    )


def solution(mesh):
    dp_size, tensor_size = mesh.devices.shape
    rest = dp_size // LINE
    bits = tuple(f"r{number}" for number in range(rest.bit_length() - 1))
    shape = (LINE, *([2] * len(bits)), tensor_size)
    fine = Mesh(mesh.devices.reshape(shape), ("z", *bits, "t"))
    dp = ("z", *bits)
    rows = P((*dp, "t"), None)
    weight = P(None, dp, "t")

    def step(*args):
        return local(bits, *args)

    return jax.shard_map(
        step,
        mesh=fine,
        in_specs=(rows, rows, P(dp, None), P(), P(), weight, P(None, "t"), weight, weight, weight),
        out_specs=(rows, rows, P(), P(), weight, P(None, "t"), weight, weight, weight),
        check_vma=False,
    )
```

```python
import functools
import math

import jax
import jax.numpy as jnp
from jax import lax
from jax.experimental import pallas as pl
from jax.experimental.pallas import tpu as pltpu
from jax.sharding import Mesh
from jax.sharding import PartitionSpec as P

HD = 128
LINE = 4
LANES = 128
LOW = jnp.bfloat16
F32 = jnp.float32
MESH = pl.DeviceIdType.MESH


def doc_layout(lens, count):
    rows = jnp.arange(count, dtype=jnp.int32)
    doc = jnp.zeros((count,), jnp.int32)
    start = jnp.zeros((count,), jnp.int32)
    bound = jnp.int32(0)
    for number in range(lens.shape[0]):
        bound = bound + lens[number]
        after = (rows >= bound).astype(jnp.int32)
        doc = doc + after
        start = start + after * lens[number]
    positions = rows - start
    allowed = (doc[:, None] == doc[None, :]) & (rows[:, None] >= rows[None, :])
    return (positions, allowed)


def rope_tables(positions, width):
    index = jnp.arange(width // 2, dtype=F32)
    freq = jnp.exp(-(2.0 * index / width) * math.log(1000000.0))
    angle = positions.astype(F32)[:, None] * freq[None, :]
    return (
        jnp.concatenate([jnp.cos(angle)] * 2, axis=1),
        jnp.concatenate([jnp.sin(angle)] * 2, axis=1),
    )


def contract_last(left, right, out=F32):
    return lax.dot_general(left, right, (((1,), (1,)), ((), ())), preferred_element_type=out)


def contract_first(left, right, out=F32):
    return lax.dot_general(left, right, (((0,), (0,)), ((), ())), preferred_element_type=out)


def take(array, index, axis):
    return lax.dynamic_index_in_dim(array, index, axis, keepdims=False)


def greet(axes_targets, conditions):
    barrier = pltpu.get_barrier_semaphore()
    for (axis, target), condition in zip(axes_targets, conditions):
        def signal(axis=axis, target=target):
            pl.semaphore_signal(barrier, inc=1, device_id={axis: target}, device_id_type=MESH)
        if condition is None:
            signal()
        else:
            pl.when(condition)(signal)
    amount = sum(1 if c is None else c.astype(jnp.int32) for c in conditions)
    pl.semaphore_wait(barrier, amount)


def slot_of(line, values):
    slot = line
    for value in values:
        slot = slot * 2 + value
    return slot


def both(*conditions):
    given = [c for c in conditions if c is not None]
    return functools.reduce(jnp.logical_and, given) if given else None


def guarded(condition, action):
    if condition is None:
        action()
    else:
        pl.when(condition)(action)


def bit_flips(variant, stage, count):
    return [(variant >> b) & 1 for b in range(stage)] + [1] + [0] * (count - stage - 1)


class Gather:
    def __init__(self, size, bits, x_ref, out_ref, own_sem, line_sems, bit_sems, recv_sems):
        self.size, self.bits, self.count = size, bits, len(bits)
        self.x_ref, self.out_ref, self.own_sem = x_ref, out_ref, own_sem
        self.line_sems, self.bit_sems, self.recv_sems = line_sems, bit_sems, recv_sems
        self.z = lax.axis_index("z")
        self.mine = [lax.axis_index(bit) for bit in bits]
        self.own = slot_of(self.z, self.mine)
        self.pending, self.settled = [], False

    def copy(self, slot, first, axis, target, send_sem):
        return pltpu.make_async_remote_copy(
            src_ref=self.x_ref if first else self.out_ref.at[slot],
            dst_ref=self.out_ref.at[slot],
            send_sem=send_sem,
            recv_sem=self.recv_sems.at[slot],
            device_id={axis: target},
            device_id_type=MESH,
        )

    def start(self, condition, make):
        self.pending.append((condition, make))
        guarded(condition, lambda: make().start())

    def arrived(self, condition, slot, axis, target):
        guarded(
            condition,
            lambda: self.copy(slot, False, axis, target, self.line_sems.at[0, 0]).wait_recv(),
        )

    def spread(self, condition, slot, first, number, side, variant, after):
        for stage in range(after, self.count):
            self.start(
                condition,
                functools.partial(
                    self.copy,
                    slot,
                    first,
                    self.bits[stage],
                    1 - self.mine[stage],
                    self.bit_sems.at[number, side, variant, stage],
                ),
            )

    def line_of(self, number, side):
        line = self.z - number if side == 0 else self.z + number
        if number == 0:
            return line, None
        return line, (line >= 0 if side == 0 else line < self.size)

    def on_bits(self, number):
        for side in range(1 if number == 0 else 2):
            line, condition = self.line_of(number, side)
            for stage in range(self.count):
                for variant in range(2**stage):
                    flips = bit_flips(variant, stage, self.count)
                    slot = slot_of(line, [1 - m if f else m for m, f in zip(self.mine, flips)])
                    self.arrived(condition, slot, self.bits[stage], 1 - self.mine[stage])
                    code = sum(f << b for b, f in enumerate(flips))
                    self.spread(condition, slot, False, number, side, code, stage + 1)

    def begin(self):
        pltpu.make_async_copy(self.x_ref, self.out_ref.at[self.own], self.own_sem).start()
        z, size = self.z, self.size
        first = functools.partial(self.copy, self.own, True, "z")
        self.start(z < size - 1, functools.partial(first, z + 1, self.line_sems.at[0, 0]))
        self.start(z > 0, functools.partial(first, z - 1, self.line_sems.at[0, 1]))
        self.spread(None, self.own, True, 0, 0, 0, 0)

    def step(self, number):
        z, size = self.z, self.size
        for side in range(2):
            line, condition = self.line_of(number, side)
            slot = slot_of(line, self.mine)
            back = z - 1 if side == 0 else z + 1
            onto = z + 1 if side == 0 else z - 1
            self.arrived(condition, slot, "z", back)
            self.start(
                both(condition, onto < size if side == 0 else onto >= 0),
                functools.partial(self.copy, slot, False, "z", onto, self.line_sems.at[number, side]),
            )
            self.spread(condition, slot, False, number, side, 0, 0)

    def middle(self):
        for number in range(1, self.size):
            self.step(number)
            self.on_bits(number - 1)
        self.on_bits(self.size - 1)

    def settle(self):
        if not self.settled:
            pltpu.make_async_copy(self.x_ref, self.out_ref.at[self.own], self.own_sem).wait()
            self.settled = True

    def end(self):
        self.settle()
        for condition, make in self.pending:
            guarded(condition, lambda make=make: make().wait_send())


def gather_semaphores(size, bits):
    slots = size * 2 ** len(bits)
    return [
        pltpu.SemaphoreType.DMA,
        pltpu.SemaphoreType.DMA((size, 2)),
        pltpu.SemaphoreType.DMA((size, 2, 2 ** len(bits), len(bits))),
        pltpu.SemaphoreType.DMA((slots,)),
    ]


class Exchange:
    def __init__(self, size, bits, block, half, gu_ref, dn_ref, gu_out, dn_out, sems):
        self.size, self.bits, self.count = size, bits, len(bits)
        self.block, self.half = block, half
        self.gu_ref, self.dn_ref, self.gu_out, self.dn_out = gu_ref, dn_ref, gu_out, dn_out
        self.own_sems, self.line_sems, self.bit_sems, self.recv_sems = sems
        self.z = lax.axis_index("z")
        self.mine = [lax.axis_index(bit) for bit in bits]
        self.own = slot_of(self.z, self.mine)
        self.others = [lax.rem(self.z + o, size) for o in range(1, size)]
        self.pending = []

    def pieces(self, target, slot):
        low = pl.multiple_of(jnp.minimum(target * self.block, self.half - self.block), LANES)
        high = pl.multiple_of(low + self.half, LANES)
        width = self.block
        return [
            (self.gu_ref.at[:, pl.ds(low, width)], self.gu_out.at[slot, :, pl.ds(0, width)]),
            (self.gu_ref.at[:, pl.ds(high, width)], self.gu_out.at[slot, :, pl.ds(width, width)]),
            (self.dn_ref.at[:, pl.ds(low, width)], self.dn_out.at[slot]),
        ]

    def line_copy(self, place, piece, slot):
        source, landing = self.pieces(self.others[place], slot)[piece]
        return pltpu.make_async_remote_copy(
            src_ref=source,
            dst_ref=landing,
            send_sem=self.line_sems.at[place, piece],
            recv_sem=self.recv_sems.at[slot, piece],
            device_id={"z": self.others[place]},
            device_id_type=MESH,
        )

    def own_copy(self, piece):
        source, landing = self.pieces(self.z, self.own)[piece]
        return pltpu.make_async_copy(source, landing, self.own_sems.at[piece])

    def bit_copy(self, slot, piece, stage, send_sem):
        ref = (self.gu_out, None, self.dn_out)[piece]
        return pltpu.make_async_remote_copy(
            src_ref=ref.at[slot],
            dst_ref=ref.at[slot],
            send_sem=send_sem,
            recv_sem=self.recv_sems.at[slot, piece],
            device_id={self.bits[stage]: 1 - self.mine[stage]},
            device_id_type=MESH,
        )

    def first_copy(self, slot, piece, stage, send_sem):
        source, landing = self.pieces(self.z, slot)[piece]
        return pltpu.make_async_remote_copy(
            src_ref=source,
            dst_ref=landing,
            send_sem=send_sem,
            recv_sem=self.recv_sems.at[slot, piece],
            device_id={self.bits[stage]: 1 - self.mine[stage]},
            device_id_type=MESH,
        )

    def spread(self, slot, number, variant, after):
        for stage in range(after, self.count):
            for piece in (0, 2):
                make = functools.partial(
                    self.bit_copy, slot, piece, stage, self.bit_sems.at[number, variant, stage, piece]
                )
                self.pending.append(make)
                make().start()

    def on_bits(self, number):
        line = lax.rem(self.z - number + self.size, self.size)
        for stage in range(self.count):
            for variant in range(2**stage):
                flips = bit_flips(variant, stage, self.count)
                slot = slot_of(line, [1 - m if f else m for m, f in zip(self.mine, flips)])
                if number == 0 and variant == 0:
                    for piece in range(3):
                        self.first_copy(slot, piece, stage, self.own_sems.at[0]).wait_recv()
                else:
                    for piece in (0, 2):
                        self.bit_copy(slot, piece, stage, self.own_sems.at[0]).wait_recv()
                self.spread(slot, number, sum(f << b for b, f in enumerate(flips)), stage + 1)

    def begin(self):
        for stage in range(self.count):
            for piece in range(3):
                make = functools.partial(
                    self.first_copy, self.own, piece, stage, self.bit_sems.at[0, 0, stage, piece]
                )
                self.pending.append(make)
                make().start()
        for piece in range(3):
            self.own_copy(piece).start()

    def send(self, offset):
        for piece in range(3):
            self.line_copy(offset - 1, piece, self.own).start()

    def sent(self, offset):
        for piece in range(3):
            self.line_copy(offset - 1, piece, self.own).wait_send()

    def step(self, offset):
        slot = slot_of(lax.rem(self.z - offset + self.size, self.size), self.mine)
        for piece in range(3):
            self.line_copy(0, piece, slot).wait_recv()
        self.spread(slot, offset, 0, 0)

    def end(self):
        for piece in range(3):
            self.own_copy(piece).wait()
        for make in self.pending:
            make().wait_send()


class Fold:
    def __init__(self, size, bits, order, p_ref, own_buf, sums, stage_in, stage_out, own_sems, send_sems, recv_sems):
        self.size, self.bits, self.count, self.order = size, bits, len(bits), order
        self.last = self.count - 1
        self.p_ref, self.own_buf, self.sums = p_ref, own_buf, sums
        self.stage_in, self.stage_out = stage_in, stage_out
        self.own_sems, self.send_sems, self.recv_sems = own_sems, send_sems, recv_sems
        self.z = lax.axis_index("z")
        self.mine = [lax.axis_index(bit) for bit in bits]

    def line(self, place):
        if self.order is None:
            return relay_line(self.z, place, self.size)
        return lax.rem(self.z + self.order[place], self.size)

    def index(self, place, stage, variant):
        return place * (2**self.count - 1) + 2**stage - 1 + variant

    def slot(self, place, variant, flip):
        flips = [(variant >> b) & 1 for b in range(self.last)] + [flip]
        return slot_of(self.line(place), [1 - m if f else m for m, f in zip(self.mine, flips)])

    def copy(self, place, stage, variant):
        index = self.index(place, stage, variant)
        if stage == self.last:
            source = self.p_ref.at[self.slot(place, variant, 1)]
        else:
            source = self.stage_out.at[place * (2**self.last - 1) + 2**stage - 1 + variant]
        return pltpu.make_async_remote_copy(
            src_ref=source,
            dst_ref=self.stage_in.at[index],
            send_sem=self.send_sems.at[index],
            recv_sem=self.recv_sems.at[index],
            device_id={self.bits[stage]: 1 - self.mine[stage]},
            device_id_type=MESH,
        )

    def own_copy(self, place, variant):
        number = place * 2**self.last + variant
        return pltpu.make_async_copy(
            self.p_ref.at[self.slot(place, variant, 0)], self.own_buf.at[number], self.own_sems.at[number]
        )

    def begin(self, places=None):
        for place in range(self.size) if places is None else places:
            for variant in reversed(range(2**self.last)):
                self.copy(place, self.last, variant).start()
                self.own_copy(place, variant).start()

    def stage(self, place, stage, done=None):
        for variant in reversed(range(2**stage)):
            if stage == self.last:
                self.own_copy(place, variant).wait()
                held = self.own_buf[place * 2**self.last + variant].astype(F32)
            else:
                held = self.sums[place * (2**self.last - 1) + 2**stage - 1 + variant].astype(F32)
            self.copy(place, stage, variant).wait_recv()
            total = held + self.stage_in[self.index(place, stage, variant)].astype(F32)
            if stage == 0:
                done(place, total)
                continue
            lower = variant & (2 ** (stage - 1) - 1)
            number = place * (2**self.last - 1) + 2 ** (stage - 1) - 1 + lower
            if variant >> (stage - 1):
                self.stage_out[number] = total.astype(LOW)
                self.copy(place, stage - 1, lower).start()
            else:
                self.sums[number] = total.astype(LOW)

    def end(self):
        for place in range(self.size):
            for stage in range(self.count):
                for variant in range(2**stage):
                    self.copy(place, stage, variant).wait_send()


def fold_scratch(size, bits, rows, columns):
    count = len(bits)
    inner, lower = size * (2**count - 1), size * (2 ** (count - 1) - 1)
    return [
        pltpu.VMEM((size * 2 ** (count - 1), rows, columns), LOW),
        pltpu.VMEM((max(lower, 1), rows, columns) if lower else (1, 16, LANES), LOW),
        pltpu.VMEM((inner, rows, columns), LOW),
        pltpu.VMEM((max(lower, 1), rows, columns) if lower else (1, 16, LANES), LOW),
        pltpu.SemaphoreType.DMA((size * 2 ** (count - 1),)),
        pltpu.SemaphoreType.DMA((inner,)),
        pltpu.SemaphoreType.DMA((inner,)),
    ]


def relay_line(z, place, size):
    order = []
    for line in range(size):
        others = sorted((other for other in range(size) if other != line), key=lambda other: -abs(other - line))
        order.append([*others, line])
    return sum(jnp.where(z == line, order[line][place], 0) for line in range(size))


class Relay:
    def __init__(self, size, bits, p_ref, out_ref, line_out, line_in, line_send, line_recv, *fold):
        self.fold = Fold(size, bits, None, p_ref, *fold)
        self.size, self.out_ref, self.z = size, out_ref, lax.axis_index("z")
        self.line_out, self.line_in, self.line_send, self.line_recv = line_out, line_in, line_send, line_recv

    def line_copy(self, place, line):
        right = (line > self.z).astype(jnp.int32)
        slot = (1 - right) * (self.size - 1) + jnp.abs(line - self.z) - 1
        return pltpu.make_async_remote_copy(
            src_ref=self.line_out.at[place],
            dst_ref=self.line_in.at[slot],
            send_sem=self.line_send.at[place],
            recv_sem=self.line_recv.at[slot],
            device_id={"z": self.z + 2 * right - 1},
            device_id_type=MESH,
        )

    def landed(self, slot):
        pltpu.make_async_remote_copy(
            src_ref=self.line_in.at[slot],
            dst_ref=self.line_in.at[slot],
            send_sem=self.line_send.at[0],
            recv_sem=self.line_recv.at[slot],
            device_id={"z": lax.rem(self.z + 1, self.size)},
            device_id_type=MESH,
        ).wait_recv()

    def done(self, place, total):
        if place == self.size - 1:
            self.out_ref[...] = total
            return
        line = self.fold.line(place)
        right = line > self.z
        self.line_out[place] = total.astype(LOW)
        slot = (1 - right.astype(jnp.int32)) * (self.size - 1) + jnp.abs(line - self.z)

        @pl.when(jnp.where(right, self.z > 0, self.z < self.size - 1))
        def _():
            self.landed(slot)
            self.line_out[place] = (total + self.line_in[slot].astype(F32)).astype(LOW)

        self.line_copy(place, line).start()

    def begin(self, places=None):
        self.fold.begin(places)

    def place(self, place):
        for stage in reversed(range(self.fold.count)):
            self.fold.stage(place, stage, self.done)

    def finish(self):
        for slot, there in ((0, self.z > 0), (self.size - 1, self.z < self.size - 1)):

            @pl.when(there)
            def _(slot=slot):
                self.landed(slot)
                self.out_ref[...] += self.line_in[slot].astype(F32)

    def end(self):
        self.fold.end()
        for place in range(self.size - 1):
            self.line_copy(place, self.fold.line(place)).wait_send()


def scatter_scratch(size, bits, rows, columns):
    lands = 2 * (size - 1)
    return [
        pltpu.VMEM((size - 1, rows, columns), LOW),
        pltpu.VMEM((lands, rows, columns), LOW),
        pltpu.SemaphoreType.DMA((size - 1,)),
        pltpu.SemaphoreType.DMA((lands,)),
        *fold_scratch(size, bits, rows, columns),
    ]


SCATTER_REFS = 11


class Total:
    def __init__(self, size, bits, x_ref, out_ref, held, landed, send_sems, recv_sems):
        self.size, self.bits, self.count = size, bits, len(bits)
        self.x_ref, self.out_ref, self.held, self.landed = x_ref, out_ref, held, landed
        self.send_sems, self.recv_sems = send_sems, recv_sems
        self.z = lax.axis_index("z")
        self.others = [lax.rem(self.z + o, size) for o in range(1, size)]

    def copy(self, number):
        if number < self.count:
            axis = self.bits[number]
            source, target = self.held.at[number], {axis: 1 - lax.axis_index(axis)}
        else:
            source, target = self.held.at[self.count], {"z": self.others[number - self.count]}
        return pltpu.make_async_remote_copy(
            src_ref=source,
            dst_ref=self.landed.at[number],
            send_sem=self.send_sems.at[number],
            recv_sem=self.recv_sems.at[number],
            device_id=target,
            device_id_type=MESH,
        )

    def begin(self):
        self.held[0] = self.x_ref[...]
        self.copy(0).start()

    def pair(self, number):
        self.copy(number).wait_recv()
        self.held[number + 1] = self.held[number] + self.landed[number]
        if number + 1 < self.count:
            self.copy(number + 1).start()
        else:
            for place in range(self.size - 1):
                self.copy(self.count + place).start()

    def finish(self):
        for place in range(self.size - 1):
            self.copy(self.count + place).wait_recv()
        total = jnp.zeros(self.out_ref.shape, self.out_ref.dtype)
        for line in range(self.size):
            offset = lax.rem(line - self.z + self.size, self.size)
            part = self.held[self.count]
            for o in range(1, self.size):
                part = jnp.where(offset == o, self.landed[self.count + self.size - o - 1], part)
            total = total + part
        self.out_ref[...] = total

    def end(self):
        for number in range(self.count + self.size - 1):
            self.copy(number).wait_send()


def greet_all(size, axes):
    z = lax.axis_index("z")
    greet(
        [("z", lax.rem(z + o, size)) for o in range(1, size)]
        + [(axis, 1 - lax.axis_index(axis)) for axis in axes],
        [None] * (size - 1 + len(axes)),
    )


def in_groups(refs, sizes):
    groups, at = [], 0
    for number in sizes:
        groups.append(refs[at : at + number])
        at += number
    return groups


def comm_params(collective_id):
    return pltpu.CompilerParams(
        collective_id=collective_id, has_side_effects=True, vmem_limit_bytes=61 * 2**20
    )


def at_microseconds(time):
    return pl.CostEstimate(flops=0, transcendentals=0, bytes_accessed=time * 3500000)


class Attend:
    def __init__(self, rows_ref, gain_ref, bias_ref, cos_ref, sin_ref, mask_ref, w_ref, outs, scratch, width, epsilon=1e-06):
        self.gain_ref, self.bias_ref, self.w_ref = gain_ref, bias_ref, w_ref
        self.cos_ref, self.sin_ref, self.mask_ref = cos_ref, sin_ref, mask_ref
        self.state_ref, self.middle_ref, self.xa_ref, self.q_ref, self.k_ref, self.v_ref, self.lse_ref, self.o_ref = outs
        self.send_buf, self.land_buf, self.send_sems, self.recv_sems = scratch
        self.rows_ref = rows_ref
        self.t = lax.axis_index("t")
        self.slots, self.few = w_ref.shape[0], w_ref.shape[1]
        self.model = self.slots * self.few
        self.count = rows_ref.shape[0]
        self.q_width = self.q_ref.shape[1]
        self.width = width
        self.epsilon = epsilon

    def normed(self, rows, gain_ref):
        factor = lax.rsqrt(jnp.mean(rows * rows, axis=-1, keepdims=True) + self.epsilon)
        return (rows * factor * gain_ref[...]).astype(LOW)

    def xa_copy(self):
        return pltpu.make_async_remote_copy(
            src_ref=self.xa_ref.at[self.t],
            dst_ref=self.xa_ref.at[self.t],
            send_sem=self.send_sems.at[0],
            recv_sem=self.recv_sems.at[0],
            device_id={"t": 1 - self.t},
            device_id_type=MESH,
        )

    def xa_landing(self):
        return pltpu.make_async_remote_copy(
            src_ref=self.xa_ref.at[1 - self.t],
            dst_ref=self.xa_ref.at[1 - self.t],
            send_sem=self.send_sems.at[0],
            recv_sem=self.recv_sems.at[0],
            device_id={"t": 1 - self.t},
            device_id_type=MESH,
        )

    def half_copy(self):
        return pltpu.make_async_remote_copy(
            src_ref=self.send_buf,
            dst_ref=self.land_buf,
            send_sem=self.send_sems.at[1],
            recv_sem=self.recv_sems.at[1],
            device_id={"t": 1 - self.t},
            device_id_type=MESH,
        )

    def begin(self, state):
        self.state_ref[...] = state
        self.xa_ref[self.t] = self.normed(state, self.gain_ref)
        self.xa_copy().start()

    def columns(self, low, count):
        weight = self.w_ref[:, :, low : low + count].reshape(self.model, count)
        xa = self.xa_ref[...].reshape(2 * self.count, self.model)
        return jnp.dot(xa, weight, preferred_element_type=F32) + self.bias_ref[:, low : low + count]

    def rope(self, values):
        return (values * self.cos_ref[...] + pltpu.roll(values, HD // 2, 1) * self.sin_ref[...]).astype(LOW)

    def keys(self):
        self.xa_landing().wait_recv()
        both_kv = self.columns(self.q_width, 2 * HD)
        self.k_ref[...] = self.rope(both_kv[:, :HD])
        self.v_ref[...] = both_kv[:, HD:].astype(LOW)

    def heads(self, first):
        lin = self.columns(first * HD, 2 * HD)
        for number in range(2):
            head = first + number
            low = head * HD
            query = self.rope(lin[:, number * HD : (number + 1) * HD])
            self.q_ref[:, low : low + HD] = query
            raw = lax.dot_general(
                query, self.k_ref[...], (((1,), (1,)), ((), ())), preferred_element_type=F32
            )
            scores = jnp.where(self.mask_ref[...] > 0, raw * (1.0 / math.sqrt(HD)), -1e30)
            top = jnp.max(scores, axis=-1, keepdims=True)
            expo = jnp.exp(scores - top)
            whole = jnp.sum(expo, axis=-1, keepdims=True)
            probs = (expo / whole).astype(LOW)
            self.lse_ref[head] = top + jnp.log(whole)
            out = jnp.dot(probs, self.v_ref[...], preferred_element_type=F32).astype(LOW)
            self.o_ref[0, :, low : low + HD] = out[: self.count]
            self.o_ref[1, :, low : low + HD] = out[self.count :]

    def projected(self, half, step):
        left = self.o_ref[half]
        for low in range(0, self.slots, step):
            weight = self.w_ref[low : low + step, :, self.width :].reshape(step * self.few, self.q_width)
            yield low * self.few, lax.dot_general(
                left, weight, (((1,), (1,)), ((), ())), preferred_element_type=F32
            )

    def other_half(self):
        for low, part in self.projected(1 - self.t, self.slots // 4):
            self.send_buf[:, low : low + part.shape[1]] = part.astype(LOW)
        self.half_copy().start()

    def own_half(self):
        for low, part in self.projected(self.t, self.slots // 4):
            where = slice(low, low + part.shape[1])
            self.middle_ref[:, where] = self.state_ref[:, where] + part

    def finish(self, gain_ref, xf_ref):
        self.half_copy().wait_recv()
        middle = self.middle_ref[...] + self.land_buf[...].astype(F32)
        self.middle_ref[...] = middle
        xf_ref[...] = self.normed(middle, gain_ref)

    def end(self):
        self.xa_copy().wait_send()
        self.half_copy().wait_send()


def front_kernel(size, bits, block, half, layer, width, *refs):
    first = layer == 0
    inputs, far_rows, outs, refs = in_groups(
        refs, [11, 1 if first else 0, 14 if first else 11, len(refs)]
    )
    (x_ref, more_ref, ga_ref, gf_ref, bias_ref, cos_ref, sin_ref, mask_ref, at_ref, gu_ref, dn_ref) = inputs
    xf_out, gu_out, dn_out = outs[8:11]
    (w_ref, xf_ref, at_sem), pair, feed_sems, rows_sems, rest = in_groups(refs, [3, 4, 4, 4, len(refs)])
    greet_all(size, ("t", *bits))
    work = Attend(
        x_ref, ga_ref, bias_ref, cos_ref, sin_ref, mask_ref, w_ref, outs[:8], pair, width
    )
    feed = Exchange(
        size, bits, block, half, gu_ref.at[layer], dn_ref.at[layer], gu_out, dn_out, feed_sems
    )
    rows = Gather(size, ("t",), xf_ref, xf_out, *rows_sems)
    if first:
        at_sems, next_sems, side_sems = in_groups(rest, [4, 4, 4])
        side = Gather(size, ("t",), far_rows[0], outs[13], *side_sems)
        attention = Gather(size, bits, at_ref, w_ref, *at_sems)
        ahead = Gather(size, bits, more_ref, outs[12], *next_sems)
        moved = pltpu.make_async_copy(w_ref, outs[11], at_sem)
        attention.begin()
        side.begin()
        feed.begin()
        work.begin(x_ref[...].astype(F32))
        attention.step(1)
        side.step(1)
        attention.step(2)
        attention.on_bits(0)
        side.on_bits(0)
        side.step(2)
        feed.send(1)
        attention.step(3)
        attention.on_bits(1)
        side.on_bits(1)
        side.step(3)
        attention.on_bits(2)
        attention.on_bits(3)
        attention.settle()
        moved.start()
        feed.on_bits(0)
        feed.sent(1)
        feed.send(3)
        feed.step(1)
        side.on_bits(2)
        side.on_bits(3)
        steps = (attention, ahead, side)
    else:
        total_ref, *rest = rest
        side = Relay(size, ("t",), more_ref, total_ref, *rest)
        moved = pltpu.make_async_copy(at_ref, w_ref, at_sem)
        moved.start()
        side.begin()
        feed.begin()
        for place in range(size):
            side.place(place)
        feed.send(1)
        side.finish()
        work.begin(x_ref[...] + total_ref[...])
        moved.wait()
        feed.on_bits(0)
        feed.sent(1)
        feed.send(3)
        feed.step(1)
        steps = (side,)
    work.keys()
    work.heads(0)
    work.heads(2)
    work.heads(4)
    work.other_half()
    work.own_half()
    feed.sent(3)
    feed.send(2)
    feed.step(3)
    feed.on_bits(1)
    work.finish(gf_ref, xf_ref)
    rows.begin()
    if first:
        ahead.begin()
    rows.step(1)
    rows.on_bits(0)
    if first:
        ahead.step(1)
    rows.step(2)
    feed.sent(2)
    feed.step(2)
    rows.on_bits(1)
    if first:
        ahead.on_bits(0)
    feed.on_bits(3)
    rows.step(3)
    if first:
        ahead.step(2)
    rows.on_bits(2)
    feed.on_bits(2)
    rows.on_bits(3)
    if first:
        ahead.on_bits(1)
        ahead.step(3)
        ahead.on_bits(2)
        ahead.on_bits(3)
        moved.wait()
    for item in (*steps, feed, work, rows):
        item.end()


def front(x, more, gains, bias, tables, at, gu, dn, late, layer, size, bits, block, width, collective_id):
    slots = size * 2 ** len(bits)
    count, model = x.shape
    few, half = dn.shape[1:]
    length = 2 * count
    q_width = at.shape[-1] - width
    first = layer == 0
    held, far = pl.BlockSpec(memory_space=pltpu.VMEM), pl.BlockSpec(memory_space=pl.ANY)
    shape = jax.ShapeDtypeStruct
    weight = (slots, few, at.shape[-1])
    more_scratch = (
        [*gather_semaphores(size, bits) * 2, *gather_semaphores(size, ("t",))]
        if first
        else [pltpu.VMEM((count, model), F32), *scatter_scratch(size, ("t",), count, model)]
    )
    return pl.pallas_call(
        functools.partial(front_kernel, size, bits, block, half, layer, width),
        out_shape=(
            shape((count, model), F32),
            shape((count, model), F32),
            shape((2, count, model), LOW),
            shape((length, q_width), LOW),
            shape((length, HD), LOW),
            shape((length, HD), LOW),
            shape((q_width // HD, length, 1), F32),
            shape((2, count, q_width), LOW),
            shape((2 * size, count, model), LOW),
            shape((slots, few, 2 * block), LOW),
            shape((slots, few, block), LOW),
            *([shape(weight, LOW)] * 2 if first else []),
            *([shape((2 * size, count, model), LOW)] if first else []),
        ),
        in_specs=[held, far] + [held] * 6 + [far] * (3 + len(late)),
        out_specs=[held] * 8 + [far] * (6 if first else 3),
        scratch_shapes=[
            pltpu.VMEM(weight, LOW),
            pltpu.VMEM((count, model), LOW),
            pltpu.SemaphoreType.DMA,
            pltpu.VMEM((count, model), LOW),
            pltpu.VMEM((count, model), LOW),
            pltpu.SemaphoreType.DMA((2,)),
            pltpu.SemaphoreType.DMA((2,)),
            pltpu.SemaphoreType.DMA((3,)),
            pltpu.SemaphoreType.DMA((size - 1, 3)),
            pltpu.SemaphoreType.DMA((size, 2 ** len(bits), len(bits), 3)),
            pltpu.SemaphoreType.DMA((slots, 3)),
            *gather_semaphores(size, ("t",)),
            *more_scratch,
        ],
        compiler_params=comm_params(collective_id),
        cost_estimate=at_microseconds(150),
    )(x, more, *gains, bias, *tables, at, gu, dn, *late)


class AttendBack:
    def __init__(self, ins, outs, scratch, width, epsilon=1e-06):
        (self.g_ref, self.state_ref, self.middle_ref, self.ga_gain, self.gf_gain, self.cos_ref, self.sin_ref) = ins[:7]
        (self.mask_ref, self.q_ref, self.k_ref, self.v_ref, self.lse_ref, self.xa_ref, self.o_ref, self.far_w) = ins[7:]
        (self.grad_ref, self.ga_ref, self.lin_ref, self.bias_ref, self.pa_ref, self.pf_ref) = outs
        (self.w_ref, self.w_sem, self.dk, self.dv, self.sum_buf, self.send_buf, self.land_buf) = scratch[:7]
        (self.send_sems, self.recv_sems) = scratch[7:]
        self.t = lax.axis_index("t")
        self.slots, self.few = self.w_ref.shape[:2]
        self.model = self.slots * self.few
        self.count = self.state_ref.shape[0]
        self.q_width = self.q_ref.shape[1]
        self.width, self.epsilon = width, epsilon

    def pair_copy(self, number, source, landing):
        return pltpu.make_async_remote_copy(
            src_ref=source,
            dst_ref=landing,
            send_sem=self.send_sems.at[number],
            recv_sem=self.recv_sems.at[number],
            device_id={"t": 1 - self.t},
            device_id_type=MESH,
        )

    def ga_copy(self, side):
        return self.pair_copy(0, self.ga_ref.at[side], self.ga_ref.at[side])

    def half_copy(self):
        return self.pair_copy(1, self.send_buf, self.land_buf)

    def weight_copy(self):
        return pltpu.make_async_copy(self.far_w, self.w_ref, self.w_sem)

    def norm_back(self, upstream, rows, gain):
        factor = lax.rsqrt(jnp.mean(rows * rows, axis=-1, keepdims=True) + self.epsilon)
        scaled = upstream * gain
        part = jnp.sum(upstream * rows * factor, axis=0, keepdims=True)
        inner = jnp.mean(scaled * rows, axis=-1, keepdims=True)
        return factor * scaled - rows * factor**3 * inner, part

    def prepare(self):
        self.weight_copy().start()

    def begin(self, d_xf):
        d_mid, part = self.norm_back(d_xf, self.middle_ref[...], self.gf_gain[...])
        self.pf_ref[...] = part
        grad = self.g_ref[...].astype(F32) + d_mid
        self.grad_ref[...] = grad
        self.ga_ref[self.t] = grad.astype(LOW)
        self.ga_copy(self.t).start()
        self.dk[...] = jnp.zeros_like(self.dk)
        self.dv[...] = jnp.zeros_like(self.dv)

    def arrive(self):
        self.weight_copy().wait()
        self.ga_copy(1 - self.t).wait_recv()

    def unrope(self, values):
        return values * self.cos_ref[...] - pltpu.roll(values, HD // 2, 1) * self.sin_ref[...]

    def keep(self, low, values):
        count = values.shape[1]
        self.bias_ref[:, low : low + count] = jnp.sum(values, axis=0, keepdims=True)
        values = values.astype(LOW)
        self.lin_ref[0, :, low : low + count] = values[: self.count]
        self.lin_ref[1, :, low : low + count] = values[self.count :]

    def heads(self, first):
        low, count = self.width + first * HD, 2 * HD
        weight = self.w_ref[:, :, low : low + count].reshape(self.model, count)
        above = self.ga_ref[...].reshape(2 * self.count, self.model)
        d_out = jnp.dot(above, weight, preferred_element_type=F32).astype(LOW)
        key, value = self.k_ref[...], self.v_ref[...]
        last = (((1,), (1,)), ((), ()))
        early = (((0,), (0,)), ((), ()))
        scale = 1.0 / math.sqrt(HD)
        for number in range(2):
            head = first + number
            query = self.q_ref[:, head * HD : (head + 1) * HD]
            d_head = d_out[:, number * HD : (number + 1) * HD]
            raw = lax.dot_general(query, key, last, preferred_element_type=F32)
            scores = jnp.where(self.mask_ref[...] > 0, raw * scale, -1e30)
            probs = jnp.exp(scores - self.lse_ref[head])
            d_probs = lax.dot_general(d_head, value, last, preferred_element_type=F32)
            centre = jnp.sum(probs * d_probs, axis=-1, keepdims=True)
            d_raw = (probs * (d_probs - centre) * scale).astype(LOW)
            d_query = jnp.dot(d_raw, key, preferred_element_type=F32)
            self.dk[...] += lax.dot_general(d_raw, query, early, preferred_element_type=F32)
            self.dv[...] += lax.dot_general(
                probs.astype(LOW), d_head, early, preferred_element_type=F32
            )
            self.keep(head * HD, self.unrope(d_query))

    def keys(self):
        self.keep(self.q_width, self.unrope(self.dk[...]))
        self.keep(self.q_width + HD, self.dv[...])

    def projected(self, half):
        left, step = self.lin_ref[half], self.slots // 4
        for low in range(0, self.slots, step):
            weight = self.w_ref[low : low + step, :, : self.width].reshape(step * self.few, self.width)
            yield slice(low * self.few, (low + step) * self.few), lax.dot_general(
                left, weight, (((1,), (1,)), ((), ())), preferred_element_type=F32
            )

    def other_half(self):
        for where, part in self.projected(1 - self.t):
            self.send_buf[:, where] = part.astype(LOW)
        self.half_copy().start()

    def own_half(self):
        for where, part in self.projected(self.t):
            self.sum_buf[:, where] = part

    def gradients(self):
        step = self.slots // 4
        early = (((0,), (0,)), ((), ()))
        pairs = ((self.xa_ref, self.lin_ref, 0, self.width), (self.ga_ref, self.o_ref, self.width, self.q_width))
        for left_ref, right_ref, low, count in pairs:
            right = right_ref[...].reshape(2 * self.count, count)
            for slot in range(0, self.slots, step):
                where = slice(slot * self.few, (slot + step) * self.few)
                left = left_ref[:, :, where].reshape(2 * self.count, step * self.few)
                part = lax.dot_general(left, right, early, preferred_element_type=F32)
                self.w_ref[slot : slot + step, :, low : low + count] = part.astype(LOW).reshape(
                    step, self.few, count
                )

    def finish(self):
        self.half_copy().wait_recv()
        d_xa = self.sum_buf[...] + self.land_buf[...].astype(F32)
        d_in, part = self.norm_back(d_xa, self.state_ref[...], self.ga_gain[...])
        self.pa_ref[...] = part
        grad = self.grad_ref[...] + d_in
        self.grad_ref[...] = grad
        return grad

    def end(self):
        self.ga_copy(self.t).wait_send()
        self.half_copy().wait_send()


class Blocks:
    def __init__(self, size, bits, gu_ref, dn_ref, outs, gu_fold, dn_fold, done, sems):
        self.size, self.outs, self.sending = size, outs, len(outs) == 1
        order = list(range(1, size)) + [0]
        self.folds = [Fold(size, bits, order, gu_ref, *gu_fold), Fold(size, bits, order, dn_ref, *dn_fold)]
        self.done = done
        self.own_sems, self.send_sems, self.recv_sems = sems
        self.width, self.narrow = gu_ref.shape[2], dn_ref.shape[2]
        self.z = lax.axis_index("z")

    def columns(self, number):
        return pl.ds(*((0, self.width), (self.width, self.narrow))[number])

    def landing(self, number, slot):
        return self.outs[0].at[slot, :, self.columns(number)]

    def line_copy(self, number, place, slot):
        return pltpu.make_async_remote_copy(
            src_ref=self.done[number].at[place],
            dst_ref=self.landing(number, slot),
            send_sem=self.send_sems.at[number, place],
            recv_sem=self.recv_sems.at[number, slot],
            device_id={"z": self.folds[0].line(place)},
            device_id_type=MESH,
        )

    def own_copy(self, number, place):
        landing = (
            self.landing(number, self.z)
            if self.sending
            else self.outs[place].at[:, self.columns(number)]
        )
        return pltpu.make_async_copy(
            self.done[number].at[place], landing, self.own_sems.at[number, place]
        )

    def begin(self):
        for fold in self.folds:
            fold.begin()

    def inner(self, place):
        for stage in reversed(range(1, self.folds[0].count)):
            for fold in self.folds:
                fold.stage(place, stage)

    def send(self, place):
        for number, fold in enumerate(self.folds):

            def keep(place, total, number=number):
                self.done[number][place] = total.astype(LOW)
                if self.sending and place < self.size - 1:
                    self.line_copy(number, place, self.z).start()
                else:
                    self.own_copy(number, place).start()

            fold.stage(place, 0, keep)

    def end(self):
        for number, fold in enumerate(self.folds):
            for place in range(self.size):
                if not self.sending or place == self.size - 1:
                    self.own_copy(number, place).wait()
                    continue
                slot = lax.rem(self.z - place - 1 + self.size, self.size)
                self.line_copy(number, 0, slot).wait_recv()
                self.line_copy(number, place, self.z).wait_send()
            fold.end()


def back_kernel(size, bits, width, final, *refs):
    top, bottom = final
    counts = [1, 1 if top else 0, 2, 15, 3 if bottom else 0, 6, 1 if bottom else size, 1, 1 if top else 0, 1]
    p_ref, branch_ref, wide, ins, above, outs, folded, (attn_ref,), branch_out, more_out, refs = (
        in_groups(refs, counts + [len(refs)])
    )
    (dxf_ref,), dxf_scratch, gu_fold, dn_fold, done, sems, work_scratch, refs = in_groups(
        refs, [1, SCATTER_REFS, 7, 7, 2, 3, 9, len(refs)]
    )
    greet_all(size, ("t", *bits))
    rows = Relay(size, ("t",), p_ref[0], dxf_ref, *dxf_scratch)
    blocks = Blocks(size, bits, *wide, folded, gu_fold, dn_fold, done, sems)
    work = AttendBack(ins, outs, work_scratch, width)
    branch = None
    if top:
        branch_scratch, refs = in_groups(refs, [SCATTER_REFS, len(refs)])
        branch = Relay(size, ("t",), branch_ref[0], branch_out[0], *branch_scratch)
    if not bottom:
        gm_ref, kept_sem, *gm_sems = refs
        onward = Gather(size, ("t",), gm_ref, more_out[0], *gm_sems)
        kept = pltpu.make_async_copy(work.w_ref, attn_ref, kept_sem)
    else:
        attn_scratch, (x_ref, *small_scratch) = in_groups(refs, [SCATTER_REFS, len(refs)])
        final = Relay(size, bits, work.w_ref, attn_ref, *attn_scratch)
        small = Total(size, ("t", *bits), x_ref, more_out[0], *small_scratch)
    rows.begin()
    blocks.begin()
    work.prepare()
    blocks.inner(0)
    rows.place(0)
    blocks.inner(1)
    blocks.inner(2)
    rows.place(1)
    blocks.inner(3)
    rows.place(2)
    rows.place(3)
    if top:
        branch.begin([0])
    rows.finish()
    work.begin(dxf_ref[...])
    blocks.send(0)
    blocks.send(1)
    if top:
        branch.begin([1])
    work.arrive()
    work.heads(0)
    if top:
        branch.place(0)
    work.heads(2)
    blocks.send(2)
    work.heads(4)
    work.keys()
    work.other_half()
    if top:
        branch.place(1)
        branch.begin([2])
    work.own_half()
    blocks.send(3)
    work.gradients()
    if bottom:
        final.begin()
    else:
        kept.start()
    grad = work.finish()
    if bottom:
        pa_above, pf_above, bias_above = above
        x_ref[...] = jnp.zeros_like(x_ref)
        x_ref[0:1, :] = work.pa_ref[...]
        x_ref[1:2, :] = pa_above[...]
        x_ref[2:3, :] = work.pf_ref[...]
        x_ref[3:4, :] = pf_above[...]
        for side in range(2):
            mine = (work.t == side).astype(F32)
            x_ref[4 + 2 * side : 5 + 2 * side, : work.width] = work.bias_ref[...] * mine
            x_ref[5 + 2 * side : 6 + 2 * side, : work.width] = bias_above[...] * mine
        small.begin()
        for place in range(size):
            final.place(place)
            if place <= len(bits):
                small.pair(place)
        for number in range(size, len(bits) + 1):
            small.pair(number)
        final.finish()
        small.finish()
    if not bottom:
        gm_ref[...] = grad.astype(LOW)
        onward.begin()
    if top:
        branch.begin([3])
        branch.place(2)
    if not bottom:
        onward.step(1)
        onward.on_bits(0)
    if top:
        branch.place(3)
    if not bottom:
        onward.step(2)
        onward.on_bits(1)
        onward.step(3)
        onward.on_bits(2)
        onward.on_bits(3)
    if top:
        branch.finish()
    for steps in (rows, blocks, work, *((final, small) if bottom else (onward,)), branch):
        if steps is not None:
            steps.end()
    if not bottom:
        kept.wait()


def back(partial, branch, gu, dn, ins, above, size, bits, width, collective_id):
    count, model = ins[1].shape
    length, q_width = ins[8].shape
    slots, few, wide = gu.shape
    narrow = dn.shape[2]
    top, bottom = branch is not None, bool(above)
    number = len(bits) + 1
    weight = ins[14].shape
    held, far = pl.BlockSpec(memory_space=pltpu.VMEM), pl.BlockSpec(memory_space=pl.ANY)
    shape = jax.ShapeDtypeStruct
    rows_scratch = scatter_scratch(size, ("t",), count, model)
    return pl.pallas_call(
        functools.partial(back_kernel, size, bits, width, (top, bottom)),
        out_shape=(
            shape((count, model), F32),
            shape((2, count, model), LOW),
            shape((2, count, width), LOW),
            shape((1, width), F32),
            shape((1, model), F32),
            shape((1, model), F32),
            *(
                [shape((size, few, wide + narrow), LOW)]
                if bottom
                else [shape((few, wide + narrow), LOW)] * size
            ),
            shape(weight[1:], F32) if bottom else shape(weight, LOW),
            *([shape((count, model), F32)] if top else []),
            shape((8, model), F32) if bottom else shape((2 * size, count, model), LOW),
        ),
        in_specs=[far] * (4 if top else 3) + [held] * 14 + [far] + [held] * len(above),
        out_specs=[held] * 6
        + ([far, held] if bottom else [far] * (size + 1))
        + [held] * top + [held if bottom else far],
        scratch_shapes=[
            pltpu.VMEM((count, model), F32),
            *rows_scratch,
            *fold_scratch(size, bits, few, wide),
            *fold_scratch(size, bits, few, narrow),
            pltpu.VMEM((size, few, wide), LOW),
            pltpu.VMEM((size, few, narrow), LOW),
            *([pltpu.SemaphoreType.DMA((2, size))] * 3),
            pltpu.VMEM(weight, LOW),
            pltpu.SemaphoreType.DMA,
            pltpu.VMEM((length, HD), F32),
            pltpu.VMEM((length, HD), F32),
            pltpu.VMEM((count, model), F32),
            pltpu.VMEM((count, model), LOW),
            pltpu.VMEM((count, model), LOW),
            pltpu.SemaphoreType.DMA((2,)),
            pltpu.SemaphoreType.DMA((2,)),
            *(rows_scratch if top else []),
            *(
                [
                    *scatter_scratch(size, bits, *weight[1:]),
                    pltpu.VMEM((8, model), F32),
                    pltpu.VMEM((number + 1, 8, model), F32),
                    pltpu.VMEM((number + size - 1, 8, model), F32),
                    pltpu.SemaphoreType.DMA((number + size - 1,)),
                    pltpu.SemaphoreType.DMA((number + size - 1,)),
                ]
                if bottom
                else [
                    pltpu.VMEM((count, model), LOW),
                    pltpu.SemaphoreType.DMA,
                    *gather_semaphores(size, ("t",)),
                ]
            ),
        ],
        compiler_params=comm_params(collective_id),
        cost_estimate=at_microseconds(5 if bottom else 150),
    )(partial, *([branch] if top else []), gu, dn, *ins, *above)


def settle_kernel(half, width, *refs):
    low_ref, *high_refs = refs[: LINE + 1]
    attn_low, attn_high, gu_ref, dn_ref, qkv_ref, out_ref = refs[LINE + 1 :]
    block = low_ref.shape[2] // 3
    z = lax.axis_index("z")
    for layer in range(2):
        for line in range(LINE):
            low = block_start(line, block, half)
            skip = line * block - low
            for part in range(3):
                where = slice(part * block + skip, (part + 1) * block)
                if layer == 0:
                    piece = low_ref[line, :, where]
                else:
                    offset = lax.rem(z - line + LINE, LINE)
                    piece = high_refs[LINE - 1][:, where]
                    for o in range(1, LINE):
                        piece = jnp.where(offset == o, high_refs[o - 1][:, where], piece)
                piece = piece.astype(F32)
                if part < 2:
                    gu_ref[layer, :, part * half + low + skip : part * half + low + block] = piece
                else:
                    dn_ref[layer, :, low + skip : low + block] = piece
    for layer, ref in enumerate((attn_low, attn_high)):
        qkv_ref[layer] = ref[:, :width].astype(F32)
        out_ref[layer] = ref[:, width:].astype(F32)


def settle(blocks, arrived, attn, half, width):
    few = attn[0].shape[0]
    shape = jax.ShapeDtypeStruct
    return pl.pallas_call(
        functools.partial(settle_kernel, half, width),
        out_shape=(
            shape((2, few, 2 * half), F32),
            shape((2, few, half), F32),
            shape((2, few, width), F32),
            shape((2, few, attn[0].shape[1] - width), F32),
        ),
        compiler_params=pltpu.CompilerParams(vmem_limit_bytes=56 * 2**20),
    )(blocks, *arrived, *attn)


def in_slots(partial, slots):
    return partial.reshape(slots, -1, partial.shape[1])


def block_width(half):
    return -(-half // (LINE * LANES)) * LANES


def block_start(line, block, half):
    return min(line * block, half - block)


def local(
    bits, tokens, cotangent, doc_lengths, norm_attn, norm_ffn, w_qkv, b_qkv, w_out, w_gateup, w_down
):
    dp = ("z", *bits)
    tensor_size = lax.axis_size("t")
    count = tokens.shape[0]
    length = count * tensor_size
    layers = w_qkv.shape[0]
    qkv_width = w_qkv.shape[2]
    rows = w_qkv.shape[1]
    half = w_down.shape[2]
    block = block_width(half)
    positions, allowed = doc_layout(doc_lengths[0], length)
    cosine, sine = rope_tables(positions, HD)
    turned = jnp.where(jnp.arange(HD) < HD // 2, -sine, sine)
    tables = (cosine, turned, allowed.astype(F32))
    gain_attn = norm_attn.astype(F32)
    gain_ffn = norm_ffn.astype(F32)
    bias_all = b_qkv.astype(F32)
    line = lax.axis_index("z")
    valid = jnp.arange(block) >= line * block - jnp.minimum(line * block, half - block)
    flats = [jnp.concatenate([w_qkv[layer], w_out[layer]], axis=1) for layer in range(layers)]
    saved = []
    for layer in range(layers):
        gains = (gain_attn[layer : layer + 1], gain_ffn[layer : layer + 1])
        if layer == 0:
            start, more, weight = tokens, flats[1], flats[0]
        else:
            start, more, weight = middle, in_slots(partial, 2 * LINE), attn_weights[layer]
        out = front(
            start, more, gains, bias_all[layer : layer + 1], tables, weight, w_gateup, w_down,
            [cotangent] if layer == 0 else [], layer, LINE, bits, block, qkv_width, 8 + layer,
        )
        (state, middle, xa_all, query, key, value, log_total, attended) = out[:8]
        xf_all, gu_w, down_w = (item.reshape(-1, item.shape[2]) for item in out[8:11])
        if layer == 0:
            attn_weights = out[11:13]
            gm_all = out[13].reshape(-1, cotangent.shape[1])
        both_w = attn_weights[layer]
        gate_up = jnp.dot(xf_all, gu_w, preferred_element_type=F32)
        gate = gate_up[:, :block]
        up = gate_up[:, block:]
        act = jnp.where(valid, jax.nn.silu(gate) * up, 0.0).astype(LOW)
        partial = contract_last(act, down_w, LOW)
        saved.append(
            (state, xa_all, query, key, value, log_total, attended)
            + (middle, xf_all, gate, up, act, gu_w, down_w, both_w)
        )
    grad, branch, above = cotangent, in_slots(partial, 2 * LINE), []
    grads_attn = []
    for layer in reversed(range(layers)):
        (state_in, xa_all, query, key, value, log_total, attended) = saved[layer][:7]
        (middle, xf_all, gate, up, act, gu_w, down_w, both_w) = saved[layer][7:]
        d_down = contract_first(gm_all, act, LOW)
        d_act = jnp.dot(gm_all, down_w, preferred_element_type=F32)
        sig = jax.nn.sigmoid(gate)
        d_gate = d_act * up * sig * (1.0 + gate * (1.0 - sig))
        d_up = d_act * gate * sig
        d_gu = jnp.concatenate(
            [jnp.where(valid, d_gate, 0.0), jnp.where(valid, d_up, 0.0)], axis=1
        ).astype(LOW)
        d_gateup = contract_first(xf_all, d_gu, LOW)
        partial = in_slots(contract_last(d_gu, gu_w, LOW), 2 * LINE)
        wide = (in_slots(d_gateup, d_gateup.shape[0] // rows), in_slots(d_down, d_down.shape[0] // rows))
        gains = (gain_attn[layer : layer + 1], gain_ffn[layer : layer + 1])
        ins = (grad, state_in, middle, *gains, *tables, query, key, value, log_total, xa_all, attended, both_w)
        out = back(
            partial, branch, *wide, ins, above if layer == 0 else [], LINE, bits, qkv_width, 16 + layer
        )
        (grad, _, _, d_bias, part_a, part_f), rest = out[:6], out[6:]
        if layer > 0:
            (*folded, d_attn), rest = rest[: LINE + 1], rest[LINE + 1 :]
            arrived = [
                lax.ppermute(folded[o - 1], "z", [(i, (i + o) % LINE) for i in range(LINE)])
                for o in range(1, LINE)
            ]
            arrived.append(folded[LINE - 1])
        else:
            (blocks, d_attn), rest = rest[:2], rest[2:]
        if branch is not None:
            output = (middle + rest[0]).astype(LOW)
            branch = None
        if layer > 0:
            gm_all = rest[-1].reshape(-1, rest[-1].shape[2])
            above = [part_a, part_f, d_bias]
            d_attn = lax.psum_scatter(
                d_attn.reshape(-1, d_attn.shape[2]), dp, scatter_dimension=0, tiled=True
            )
        grads_attn.append(d_attn)
    sums = rest[-1]
    side = lax.axis_index("t")
    d_gu_all, d_dn_all, d_qkv_all, d_out_all = settle(blocks, arrived, grads_attn[::-1], half, qkv_width)
    return (
        output,
        grad,
        sums[0:2],
        sums[2:4],
        d_qkv_all,
        lax.dynamic_slice_in_dim(sums, 4 + 2 * side, 2, 0)[:, :qkv_width],
        d_out_all,
        d_gu_all,
        d_dn_all,
    )


def solution(mesh):
    dp_size, tensor_size = mesh.devices.shape
    rest = dp_size // LINE
    bits = tuple(f"r{number}" for number in range(rest.bit_length() - 1))
    shape = (LINE, *([2] * len(bits)), tensor_size)
    fine = Mesh(mesh.devices.reshape(shape), ("z", *bits, "t"))
    dp = ("z", *bits)
    rows = P((*dp, "t"), None)
    weight = P(None, dp, "t")

    def step(*args):
        return local(bits, *args)

    return jax.shard_map(
        step,
        mesh=fine,
        in_specs=(rows, rows, P(dp, None), P(), P(), weight, P(None, "t"), weight, weight, weight),
        out_specs=(rows, rows, P(), P(), weight, P(None, "t"), weight, weight, weight),
        check_vma=False,
    )
```

```python
import functools
import math

import jax
import jax.numpy as jnp
from jax import lax
from jax.experimental import pallas as pl
from jax.experimental.pallas import tpu as pltpu
from jax.sharding import Mesh
from jax.sharding import PartitionSpec as P

HD = 128
LINE = 4
LANES = 128
LOW = jnp.bfloat16
F32 = jnp.float32
MESH = pl.DeviceIdType.MESH


def doc_layout(lens, count):
    rows = jnp.arange(count, dtype=jnp.int32)
    doc = jnp.zeros((count,), jnp.int32)
    start = jnp.zeros((count,), jnp.int32)
    bound = jnp.int32(0)
    for number in range(lens.shape[0]):
        bound = bound + lens[number]
        after = (rows >= bound).astype(jnp.int32)
        doc = doc + after
        start = start + after * lens[number]
    positions = rows - start
    allowed = (doc[:, None] == doc[None, :]) & (rows[:, None] >= rows[None, :])
    return (positions, allowed)


def rope_tables(positions, width):
    index = jnp.arange(width // 2, dtype=F32)
    freq = jnp.exp(-(2.0 * index / width) * math.log(1000000.0))
    angle = positions.astype(F32)[:, None] * freq[None, :]
    return (
        jnp.concatenate([jnp.cos(angle)] * 2, axis=1),
        jnp.concatenate([jnp.sin(angle)] * 2, axis=1),
    )


def contract_last(left, right, out=F32):
    return lax.dot_general(left, right, (((1,), (1,)), ((), ())), preferred_element_type=out)


def contract_first(left, right, out=F32):
    return lax.dot_general(left, right, (((0,), (0,)), ((), ())), preferred_element_type=out)


def take(array, index, axis):
    return lax.dynamic_index_in_dim(array, index, axis, keepdims=False)


def greet(axes_targets, conditions):
    barrier = pltpu.get_barrier_semaphore()
    for (axis, target), condition in zip(axes_targets, conditions):
        def signal(axis=axis, target=target):
            pl.semaphore_signal(barrier, inc=1, device_id={axis: target}, device_id_type=MESH)
        if condition is None:
            signal()
        else:
            pl.when(condition)(signal)
    amount = sum(1 if c is None else c.astype(jnp.int32) for c in conditions)
    pl.semaphore_wait(barrier, amount)


def slot_of(line, values):
    slot = line
    for value in values:
        slot = slot * 2 + value
    return slot


def both(*conditions):
    given = [c for c in conditions if c is not None]
    return functools.reduce(jnp.logical_and, given) if given else None


def guarded(condition, action):
    if condition is None:
        action()
    else:
        pl.when(condition)(action)


def bit_flips(variant, stage, count):
    return [(variant >> b) & 1 for b in range(stage)] + [1] + [0] * (count - stage - 1)


class Gather:
    def __init__(self, size, bits, x_ref, out_ref, own_sem, line_sems, bit_sems, recv_sems):
        self.size, self.bits, self.count = size, bits, len(bits)
        self.x_ref, self.out_ref, self.own_sem = x_ref, out_ref, own_sem
        self.line_sems, self.bit_sems, self.recv_sems = line_sems, bit_sems, recv_sems
        self.z = lax.axis_index("z")
        self.mine = [lax.axis_index(bit) for bit in bits]
        self.own = slot_of(self.z, self.mine)
        self.pending, self.settled = [], False

    def copy(self, slot, first, axis, target, send_sem):
        return pltpu.make_async_remote_copy(
            src_ref=self.x_ref if first else self.out_ref.at[slot],
            dst_ref=self.out_ref.at[slot],
            send_sem=send_sem,
            recv_sem=self.recv_sems.at[slot],
            device_id={axis: target},
            device_id_type=MESH,
        )

    def start(self, condition, make):
        self.pending.append((condition, make))
        guarded(condition, lambda: make().start())

    def arrived(self, condition, slot, axis, target):
        guarded(
            condition,
            lambda: self.copy(slot, False, axis, target, self.line_sems.at[0, 0]).wait_recv(),
        )

    def spread(self, condition, slot, first, number, side, variant, after):
        for stage in range(after, self.count):
            self.start(
                condition,
                functools.partial(
                    self.copy,
                    slot,
                    first,
                    self.bits[stage],
                    1 - self.mine[stage],
                    self.bit_sems.at[number, side, variant, stage],
                ),
            )

    def line_of(self, number, side):
        line = self.z - number if side == 0 else self.z + number
        if number == 0:
            return line, None
        return line, (line >= 0 if side == 0 else line < self.size)

    def on_bits(self, number):
        for side in range(1 if number == 0 else 2):
            line, condition = self.line_of(number, side)
            for stage in range(self.count):
                for variant in range(2**stage):
                    flips = bit_flips(variant, stage, self.count)
                    slot = slot_of(line, [1 - m if f else m for m, f in zip(self.mine, flips)])
                    self.arrived(condition, slot, self.bits[stage], 1 - self.mine[stage])
                    code = sum(f << b for b, f in enumerate(flips))
                    self.spread(condition, slot, False, number, side, code, stage + 1)

    def begin(self):
        pltpu.make_async_copy(self.x_ref, self.out_ref.at[self.own], self.own_sem).start()
        z, size = self.z, self.size
        first = functools.partial(self.copy, self.own, True, "z")
        self.start(z < size - 1, functools.partial(first, z + 1, self.line_sems.at[0, 0]))
        self.start(z > 0, functools.partial(first, z - 1, self.line_sems.at[0, 1]))
        self.spread(None, self.own, True, 0, 0, 0, 0)

    def step(self, number):
        z, size = self.z, self.size
        for side in range(2):
            line, condition = self.line_of(number, side)
            slot = slot_of(line, self.mine)
            back = z - 1 if side == 0 else z + 1
            onto = z + 1 if side == 0 else z - 1
            self.arrived(condition, slot, "z", back)
            self.start(
                both(condition, onto < size if side == 0 else onto >= 0),
                functools.partial(self.copy, slot, False, "z", onto, self.line_sems.at[number, side]),
            )
            self.spread(condition, slot, False, number, side, 0, 0)

    def middle(self):
        for number in range(1, self.size):
            self.step(number)
            self.on_bits(number - 1)
        self.on_bits(self.size - 1)

    def settle(self):
        if not self.settled:
            pltpu.make_async_copy(self.x_ref, self.out_ref.at[self.own], self.own_sem).wait()
            self.settled = True

    def end(self):
        self.settle()
        for condition, make in self.pending:
            guarded(condition, lambda make=make: make().wait_send())


def gather_semaphores(size, bits):
    slots = size * 2 ** len(bits)
    return [
        pltpu.SemaphoreType.DMA,
        pltpu.SemaphoreType.DMA((size, 2)),
        pltpu.SemaphoreType.DMA((size, 2, 2 ** len(bits), len(bits))),
        pltpu.SemaphoreType.DMA((slots,)),
    ]


class Exchange:
    def __init__(self, size, bits, block, half, gu_ref, dn_ref, gu_out, dn_out, sems):
        self.size, self.bits, self.count = size, bits, len(bits)
        self.block, self.half = block, half
        self.gu_ref, self.dn_ref, self.gu_out, self.dn_out = gu_ref, dn_ref, gu_out, dn_out
        self.own_sems, self.line_sems, self.bit_sems, self.recv_sems = sems
        self.z = lax.axis_index("z")
        self.mine = [lax.axis_index(bit) for bit in bits]
        self.own = slot_of(self.z, self.mine)
        self.others = [lax.rem(self.z + o, size) for o in range(1, size)]
        self.pending = []

    def pieces(self, target, slot):
        low = pl.multiple_of(jnp.minimum(target * self.block, self.half - self.block), LANES)
        high = pl.multiple_of(low + self.half, LANES)
        width = self.block
        return [
            (self.gu_ref.at[:, pl.ds(low, width)], self.gu_out.at[slot, :, pl.ds(0, width)]),
            (self.gu_ref.at[:, pl.ds(high, width)], self.gu_out.at[slot, :, pl.ds(width, width)]),
            (self.dn_ref.at[:, pl.ds(low, width)], self.dn_out.at[slot]),
        ]

    def line_copy(self, place, piece, slot):
        source, landing = self.pieces(self.others[place], slot)[piece]
        return pltpu.make_async_remote_copy(
            src_ref=source,
            dst_ref=landing,
            send_sem=self.line_sems.at[place, piece],
            recv_sem=self.recv_sems.at[slot, piece],
            device_id={"z": self.others[place]},
            device_id_type=MESH,
        )

    def own_copy(self, piece):
        source, landing = self.pieces(self.z, self.own)[piece]
        return pltpu.make_async_copy(source, landing, self.own_sems.at[piece])

    def bit_copy(self, slot, piece, stage, send_sem):
        ref = (self.gu_out, None, self.dn_out)[piece]
        return pltpu.make_async_remote_copy(
            src_ref=ref.at[slot],
            dst_ref=ref.at[slot],
            send_sem=send_sem,
            recv_sem=self.recv_sems.at[slot, piece],
            device_id={self.bits[stage]: 1 - self.mine[stage]},
            device_id_type=MESH,
        )

    def first_copy(self, slot, piece, stage, send_sem):
        source, landing = self.pieces(self.z, slot)[piece]
        return pltpu.make_async_remote_copy(
            src_ref=source,
            dst_ref=landing,
            send_sem=send_sem,
            recv_sem=self.recv_sems.at[slot, piece],
            device_id={self.bits[stage]: 1 - self.mine[stage]},
            device_id_type=MESH,
        )

    def spread(self, slot, number, variant, after):
        for stage in range(after, self.count):
            for piece in (0, 2):
                make = functools.partial(
                    self.bit_copy, slot, piece, stage, self.bit_sems.at[number, variant, stage, piece]
                )
                self.pending.append(make)
                make().start()

    def on_bits(self, number):
        line = lax.rem(self.z - number + self.size, self.size)
        for stage in range(self.count):
            for variant in range(2**stage):
                flips = bit_flips(variant, stage, self.count)
                slot = slot_of(line, [1 - m if f else m for m, f in zip(self.mine, flips)])
                if number == 0 and variant == 0:
                    for piece in range(3):
                        self.first_copy(slot, piece, stage, self.own_sems.at[0]).wait_recv()
                else:
                    for piece in (0, 2):
                        self.bit_copy(slot, piece, stage, self.own_sems.at[0]).wait_recv()
                self.spread(slot, number, sum(f << b for b, f in enumerate(flips)), stage + 1)

    def begin(self):
        for stage in range(self.count):
            for piece in range(3):
                make = functools.partial(
                    self.first_copy, self.own, piece, stage, self.bit_sems.at[0, 0, stage, piece]
                )
                self.pending.append(make)
                make().start()
        for piece in range(3):
            self.own_copy(piece).start()

    def send(self, offset):
        for piece in range(3):
            self.line_copy(offset - 1, piece, self.own).start()

    def sent(self, offset):
        for piece in range(3):
            self.line_copy(offset - 1, piece, self.own).wait_send()

    def step(self, offset):
        slot = slot_of(lax.rem(self.z - offset + self.size, self.size), self.mine)
        for piece in range(3):
            self.line_copy(0, piece, slot).wait_recv()
        self.spread(slot, offset, 0, 0)

    def end(self):
        for piece in range(3):
            self.own_copy(piece).wait()
        for make in self.pending:
            make().wait_send()


class Fold:
    def __init__(self, size, bits, order, p_ref, own_buf, sums, stage_in, stage_out, own_sems, send_sems, recv_sems):
        self.size, self.bits, self.count, self.order = size, bits, len(bits), order
        self.last = self.count - 1
        self.p_ref, self.own_buf, self.sums = p_ref, own_buf, sums
        self.stage_in, self.stage_out = stage_in, stage_out
        self.own_sems, self.send_sems, self.recv_sems = own_sems, send_sems, recv_sems
        self.z = lax.axis_index("z")
        self.mine = [lax.axis_index(bit) for bit in bits]

    def line(self, place):
        if self.order is None:
            return relay_line(self.z, place, self.size)
        return lax.rem(self.z + self.order[place], self.size)

    def index(self, place, stage, variant):
        return place * (2**self.count - 1) + 2**stage - 1 + variant

    def slot(self, place, variant, flip):
        flips = [(variant >> b) & 1 for b in range(self.last)] + [flip]
        return slot_of(self.line(place), [1 - m if f else m for m, f in zip(self.mine, flips)])

    def copy(self, place, stage, variant):
        index = self.index(place, stage, variant)
        if stage == self.last:
            source = self.p_ref.at[self.slot(place, variant, 1)]
        else:
            source = self.stage_out.at[place * (2**self.last - 1) + 2**stage - 1 + variant]
        return pltpu.make_async_remote_copy(
            src_ref=source,
            dst_ref=self.stage_in.at[index],
            send_sem=self.send_sems.at[index],
            recv_sem=self.recv_sems.at[index],
            device_id={self.bits[stage]: 1 - self.mine[stage]},
            device_id_type=MESH,
        )

    def own_copy(self, place, variant):
        number = place * 2**self.last + variant
        return pltpu.make_async_copy(
            self.p_ref.at[self.slot(place, variant, 0)], self.own_buf.at[number], self.own_sems.at[number]
        )

    def begin(self, places=None):
        for place in range(self.size) if places is None else places:
            for variant in reversed(range(2**self.last)):
                self.copy(place, self.last, variant).start()
                self.own_copy(place, variant).start()

    def stage(self, place, stage, done=None):
        for variant in reversed(range(2**stage)):
            if stage == self.last:
                self.own_copy(place, variant).wait()
                held = self.own_buf[place * 2**self.last + variant].astype(F32)
            else:
                held = self.sums[place * (2**self.last - 1) + 2**stage - 1 + variant].astype(F32)
            self.copy(place, stage, variant).wait_recv()
            total = held + self.stage_in[self.index(place, stage, variant)].astype(F32)
            if stage == 0:
                done(place, total)
                continue
            lower = variant & (2 ** (stage - 1) - 1)
            number = place * (2**self.last - 1) + 2 ** (stage - 1) - 1 + lower
            if variant >> (stage - 1):
                self.stage_out[number] = total.astype(LOW)
                self.copy(place, stage - 1, lower).start()
            else:
                self.sums[number] = total.astype(LOW)

    def end(self):
        for place in range(self.size):
            for stage in range(self.count):
                for variant in range(2**stage):
                    self.copy(place, stage, variant).wait_send()


def fold_scratch(size, bits, rows, columns):
    count = len(bits)
    inner, lower = size * (2**count - 1), size * (2 ** (count - 1) - 1)
    return [
        pltpu.VMEM((size * 2 ** (count - 1), rows, columns), LOW),
        pltpu.VMEM((max(lower, 1), rows, columns) if lower else (1, 16, LANES), LOW),
        pltpu.VMEM((inner, rows, columns), LOW),
        pltpu.VMEM((max(lower, 1), rows, columns) if lower else (1, 16, LANES), LOW),
        pltpu.SemaphoreType.DMA((size * 2 ** (count - 1),)),
        pltpu.SemaphoreType.DMA((inner,)),
        pltpu.SemaphoreType.DMA((inner,)),
    ]


def relay_line(z, place, size):
    order = []
    for line in range(size):
        others = sorted((other for other in range(size) if other != line), key=lambda other: -abs(other - line))
        order.append([*others, line])
    return sum(jnp.where(z == line, order[line][place], 0) for line in range(size))


class Relay:
    def __init__(self, size, bits, p_ref, out_ref, line_out, line_in, line_send, line_recv, *fold):
        self.fold = Fold(size, bits, None, p_ref, *fold)
        self.size, self.out_ref, self.z = size, out_ref, lax.axis_index("z")
        self.line_out, self.line_in, self.line_send, self.line_recv = line_out, line_in, line_send, line_recv

    def line_copy(self, place, line):
        right = (line > self.z).astype(jnp.int32)
        slot = (1 - right) * (self.size - 1) + jnp.abs(line - self.z) - 1
        return pltpu.make_async_remote_copy(
            src_ref=self.line_out.at[place],
            dst_ref=self.line_in.at[slot],
            send_sem=self.line_send.at[place],
            recv_sem=self.line_recv.at[slot],
            device_id={"z": self.z + 2 * right - 1},
            device_id_type=MESH,
        )

    def landed(self, slot):
        pltpu.make_async_remote_copy(
            src_ref=self.line_in.at[slot],
            dst_ref=self.line_in.at[slot],
            send_sem=self.line_send.at[0],
            recv_sem=self.line_recv.at[slot],
            device_id={"z": lax.rem(self.z + 1, self.size)},
            device_id_type=MESH,
        ).wait_recv()

    def done(self, place, total):
        if place == self.size - 1:
            self.out_ref[...] = total
            return
        line = self.fold.line(place)
        right = line > self.z
        self.line_out[place] = total.astype(LOW)
        slot = (1 - right.astype(jnp.int32)) * (self.size - 1) + jnp.abs(line - self.z)

        @pl.when(jnp.where(right, self.z > 0, self.z < self.size - 1))
        def _():
            self.landed(slot)
            self.line_out[place] = (total + self.line_in[slot].astype(F32)).astype(LOW)

        self.line_copy(place, line).start()

    def begin(self, places=None):
        self.fold.begin(places)

    def place(self, place):
        for stage in reversed(range(self.fold.count)):
            self.fold.stage(place, stage, self.done)

    def finish(self):
        for slot, there in ((0, self.z > 0), (self.size - 1, self.z < self.size - 1)):

            @pl.when(there)
            def _(slot=slot):
                self.landed(slot)
                self.out_ref[...] += self.line_in[slot].astype(F32)

    def end(self):
        self.fold.end()
        for place in range(self.size - 1):
            self.line_copy(place, self.fold.line(place)).wait_send()


def scatter_scratch(size, bits, rows, columns):
    lands = 2 * (size - 1)
    return [
        pltpu.VMEM((size - 1, rows, columns), LOW),
        pltpu.VMEM((lands, rows, columns), LOW),
        pltpu.SemaphoreType.DMA((size - 1,)),
        pltpu.SemaphoreType.DMA((lands,)),
        *fold_scratch(size, bits, rows, columns),
    ]


SCATTER_REFS = 11


class Total:
    def __init__(self, size, bits, x_ref, out_ref, held, landed, send_sems, recv_sems):
        self.size, self.bits, self.count = size, bits, len(bits)
        self.x_ref, self.out_ref, self.held, self.landed = x_ref, out_ref, held, landed
        self.send_sems, self.recv_sems = send_sems, recv_sems
        self.z = lax.axis_index("z")
        self.others = [lax.rem(self.z + o, size) for o in range(1, size)]

    def copy(self, number):
        if number < self.count:
            axis = self.bits[number]
            source, target = self.held.at[number], {axis: 1 - lax.axis_index(axis)}
        else:
            source, target = self.held.at[self.count], {"z": self.others[number - self.count]}
        return pltpu.make_async_remote_copy(
            src_ref=source,
            dst_ref=self.landed.at[number],
            send_sem=self.send_sems.at[number],
            recv_sem=self.recv_sems.at[number],
            device_id=target,
            device_id_type=MESH,
        )

    def begin(self):
        self.held[0] = self.x_ref[...]
        self.copy(0).start()

    def pair(self, number):
        self.copy(number).wait_recv()
        self.held[number + 1] = self.held[number] + self.landed[number]
        if number + 1 < self.count:
            self.copy(number + 1).start()
        else:
            for place in range(self.size - 1):
                self.copy(self.count + place).start()

    def finish(self):
        for place in range(self.size - 1):
            self.copy(self.count + place).wait_recv()
        total = jnp.zeros(self.out_ref.shape, self.out_ref.dtype)
        for line in range(self.size):
            offset = lax.rem(line - self.z + self.size, self.size)
            part = self.held[self.count]
            for o in range(1, self.size):
                part = jnp.where(offset == o, self.landed[self.count + self.size - o - 1], part)
            total = total + part
        self.out_ref[...] = total

    def end(self):
        for number in range(self.count + self.size - 1):
            self.copy(number).wait_send()


def greet_all(size, axes):
    z = lax.axis_index("z")
    greet(
        [("z", lax.rem(z + o, size)) for o in range(1, size)]
        + [(axis, 1 - lax.axis_index(axis)) for axis in axes],
        [None] * (size - 1 + len(axes)),
    )


def in_groups(refs, sizes):
    groups, at = [], 0
    for number in sizes:
        groups.append(refs[at : at + number])
        at += number
    return groups


def comm_params(collective_id):
    return pltpu.CompilerParams(
        collective_id=collective_id, has_side_effects=True, vmem_limit_bytes=61 * 2**20
    )


def at_microseconds(time):
    return pl.CostEstimate(flops=0, transcendentals=0, bytes_accessed=time * 3500000)


class Attend:
    def __init__(self, rows_ref, gain_ref, bias_ref, cos_ref, sin_ref, mask_ref, w_ref, outs, scratch, width, epsilon=1e-06):
        self.gain_ref, self.bias_ref, self.w_ref = gain_ref, bias_ref, w_ref
        self.cos_ref, self.sin_ref, self.mask_ref = cos_ref, sin_ref, mask_ref
        self.state_ref, self.middle_ref, self.xa_ref, self.q_ref, self.k_ref, self.v_ref, self.lse_ref, self.o_ref = outs
        self.send_buf, self.land_buf, self.send_sems, self.recv_sems = scratch
        self.rows_ref = rows_ref
        self.t = lax.axis_index("t")
        self.slots, self.few = w_ref.shape[0], w_ref.shape[1]
        self.model = self.slots * self.few
        self.count = rows_ref.shape[0]
        self.q_width = self.q_ref.shape[1]
        self.width = width
        self.epsilon = epsilon

    def normed(self, rows, gain_ref):
        factor = lax.rsqrt(jnp.mean(rows * rows, axis=-1, keepdims=True) + self.epsilon)
        return (rows * factor * gain_ref[...]).astype(LOW)

    def xa_copy(self):
        return pltpu.make_async_remote_copy(
            src_ref=self.xa_ref.at[self.t],
            dst_ref=self.xa_ref.at[self.t],
            send_sem=self.send_sems.at[0],
            recv_sem=self.recv_sems.at[0],
            device_id={"t": 1 - self.t},
            device_id_type=MESH,
        )

    def xa_landing(self):
        return pltpu.make_async_remote_copy(
            src_ref=self.xa_ref.at[1 - self.t],
            dst_ref=self.xa_ref.at[1 - self.t],
            send_sem=self.send_sems.at[0],
            recv_sem=self.recv_sems.at[0],
            device_id={"t": 1 - self.t},
            device_id_type=MESH,
        )

    def half_copy(self):
        return pltpu.make_async_remote_copy(
            src_ref=self.send_buf,
            dst_ref=self.land_buf,
            send_sem=self.send_sems.at[1],
            recv_sem=self.recv_sems.at[1],
            device_id={"t": 1 - self.t},
            device_id_type=MESH,
        )

    def begin(self, state):
        self.state_ref[...] = state
        self.xa_ref[self.t] = self.normed(state, self.gain_ref)
        self.xa_copy().start()

    def columns(self, low, count):
        weight = self.w_ref[:, :, low : low + count].reshape(self.model, count)
        xa = self.xa_ref[...].reshape(2 * self.count, self.model)
        return jnp.dot(xa, weight, preferred_element_type=F32) + self.bias_ref[:, low : low + count]

    def rope(self, values):
        return (values * self.cos_ref[...] + pltpu.roll(values, HD // 2, 1) * self.sin_ref[...]).astype(LOW)

    def keys(self):
        self.xa_landing().wait_recv()
        both_kv = self.columns(self.q_width, 2 * HD)
        self.k_ref[...] = self.rope(both_kv[:, :HD])
        self.v_ref[...] = both_kv[:, HD:].astype(LOW)

    def heads(self, first):
        lin = self.columns(first * HD, 2 * HD)
        for number in range(2):
            head = first + number
            low = head * HD
            query = self.rope(lin[:, number * HD : (number + 1) * HD])
            self.q_ref[:, low : low + HD] = query
            raw = lax.dot_general(
                query, self.k_ref[...], (((1,), (1,)), ((), ())), preferred_element_type=F32
            )
            scores = jnp.where(self.mask_ref[...] > 0, raw * (1.0 / math.sqrt(HD)), -1e30)
            top = jnp.max(scores, axis=-1, keepdims=True)
            expo = jnp.exp(scores - top)
            whole = jnp.sum(expo, axis=-1, keepdims=True)
            probs = (expo / whole).astype(LOW)
            self.lse_ref[head] = top + jnp.log(whole)
            out = jnp.dot(probs, self.v_ref[...], preferred_element_type=F32).astype(LOW)
            self.o_ref[0, :, low : low + HD] = out[: self.count]
            self.o_ref[1, :, low : low + HD] = out[self.count :]

    def projected(self, half, step):
        left = self.o_ref[half]
        for low in range(0, self.slots, step):
            weight = self.w_ref[low : low + step, :, self.width :].reshape(step * self.few, self.q_width)
            yield low * self.few, lax.dot_general(
                left, weight, (((1,), (1,)), ((), ())), preferred_element_type=F32
            )

    def other_half(self):
        for low, part in self.projected(1 - self.t, self.slots // 4):
            self.send_buf[:, low : low + part.shape[1]] = part.astype(LOW)
        self.half_copy().start()

    def own_half(self):
        for low, part in self.projected(self.t, self.slots // 4):
            where = slice(low, low + part.shape[1])
            self.middle_ref[:, where] = self.state_ref[:, where] + part

    def finish(self, gain_ref, xf_ref):
        self.half_copy().wait_recv()
        middle = self.middle_ref[...] + self.land_buf[...].astype(F32)
        self.middle_ref[...] = middle
        xf_ref[...] = self.normed(middle, gain_ref)

    def end(self):
        self.xa_copy().wait_send()
        self.half_copy().wait_send()


def front_kernel(size, bits, block, half, layer, width, *refs):
    first = layer == 0
    inputs, outs, refs = in_groups(refs, [11, 13 if first else 11, len(refs)])
    (x_ref, more_ref, ga_ref, gf_ref, bias_ref, cos_ref, sin_ref, mask_ref, at_ref, gu_ref, dn_ref) = inputs
    xf_out, gu_out, dn_out = outs[8:11]
    (w_ref, xf_ref, at_sem), pair, feed_sems, rows_sems, rest = in_groups(refs, [3, 4, 4, 4, len(refs)])
    greet_all(size, ("t", *bits))
    work = Attend(
        x_ref, ga_ref, bias_ref, cos_ref, sin_ref, mask_ref, w_ref, outs[:8], pair, width
    )
    feed = Exchange(
        size, bits, block, half, gu_ref.at[layer], dn_ref.at[layer], gu_out, dn_out, feed_sems
    )
    rows = Gather(size, ("t",), xf_ref, xf_out, *rows_sems)
    if first:
        at_sems, next_sems = in_groups(rest, [4, 4])
        attention = Gather(size, bits, at_ref, w_ref, *at_sems)
        ahead = Gather(size, bits, more_ref, outs[12], *next_sems)
        moved = pltpu.make_async_copy(w_ref, outs[11], at_sem)
        attention.begin()
        feed.begin()
        work.begin(x_ref[...].astype(F32))
        attention.step(1)
        attention.step(2)
        attention.on_bits(0)
        attention.step(3)
        feed.send(1)
        attention.on_bits(1)
        attention.on_bits(2)
        attention.on_bits(3)
        attention.settle()
        moved.start()
        feed.on_bits(0)
        feed.sent(1)
        feed.send(3)
        feed.step(1)
        steps = (attention, ahead)
    else:
        total_ref, *rest = rest
        side = Relay(size, ("t",), more_ref, total_ref, *rest)
        moved = pltpu.make_async_copy(at_ref, w_ref, at_sem)
        moved.start()
        side.begin()
        feed.begin()
        for place in range(size):
            side.place(place)
        feed.send(1)
        side.finish()
        work.begin(x_ref[...] + total_ref[...])
        moved.wait()
        feed.on_bits(0)
        feed.sent(1)
        feed.send(3)
        feed.step(1)
        steps = (side,)
    work.keys()
    work.heads(0)
    work.heads(2)
    work.heads(4)
    work.other_half()
    work.own_half()
    feed.sent(3)
    feed.send(2)
    feed.step(3)
    feed.on_bits(1)
    work.finish(gf_ref, xf_ref)
    rows.begin()
    if first:
        ahead.begin()
    rows.step(1)
    rows.on_bits(0)
    if first:
        ahead.step(1)
    rows.step(2)
    feed.sent(2)
    feed.step(2)
    rows.on_bits(1)
    if first:
        ahead.on_bits(0)
    feed.on_bits(3)
    rows.step(3)
    if first:
        ahead.step(2)
    rows.on_bits(2)
    feed.on_bits(2)
    rows.on_bits(3)
    if first:
        ahead.on_bits(1)
        ahead.step(3)
        ahead.on_bits(2)
        ahead.on_bits(3)
        moved.wait()
    for item in (*steps, feed, work, rows):
        item.end()


def front(x, more, gains, bias, tables, at, gu, dn, layer, size, bits, block, width, collective_id):
    slots = size * 2 ** len(bits)
    count, model = x.shape
    few, half = dn.shape[1:]
    length = 2 * count
    q_width = at.shape[-1] - width
    first = layer == 0
    held, far = pl.BlockSpec(memory_space=pltpu.VMEM), pl.BlockSpec(memory_space=pl.ANY)
    shape = jax.ShapeDtypeStruct
    weight = (slots, few, at.shape[-1])
    more_scratch = (
        gather_semaphores(size, bits) * 2
        if first
        else [pltpu.VMEM((count, model), F32), *scatter_scratch(size, ("t",), count, model)]
    )
    return pl.pallas_call(
        functools.partial(front_kernel, size, bits, block, half, layer, width),
        out_shape=(
            shape((count, model), F32),
            shape((count, model), F32),
            shape((2, count, model), LOW),
            shape((length, q_width), LOW),
            shape((length, HD), LOW),
            shape((length, HD), LOW),
            shape((q_width // HD, length, 1), F32),
            shape((2, count, q_width), LOW),
            shape((2 * size, count, model), LOW),
            shape((slots, few, 2 * block), LOW),
            shape((slots, few, block), LOW),
            *([shape(weight, LOW)] * 2 if first else []),
        ),
        in_specs=[held, far] + [held] * 6 + [far] * 3,
        out_specs=[held] * 8 + [far] * (5 if first else 3),
        scratch_shapes=[
            pltpu.VMEM(weight, LOW),
            pltpu.VMEM((count, model), LOW),
            pltpu.SemaphoreType.DMA,
            pltpu.VMEM((count, model), LOW),
            pltpu.VMEM((count, model), LOW),
            pltpu.SemaphoreType.DMA((2,)),
            pltpu.SemaphoreType.DMA((2,)),
            pltpu.SemaphoreType.DMA((3,)),
            pltpu.SemaphoreType.DMA((size - 1, 3)),
            pltpu.SemaphoreType.DMA((size, 2 ** len(bits), len(bits), 3)),
            pltpu.SemaphoreType.DMA((slots, 3)),
            *gather_semaphores(size, ("t",)),
            *more_scratch,
        ],
        compiler_params=comm_params(collective_id),
        cost_estimate=at_microseconds(150),
    )(x, more, *gains, bias, *tables, at, gu, dn)


class AttendBack:
    def __init__(self, ins, outs, scratch, width, epsilon=1e-06):
        (self.g_ref, self.state_ref, self.middle_ref, self.ga_gain, self.gf_gain, self.cos_ref, self.sin_ref) = ins[:7]
        (self.mask_ref, self.q_ref, self.k_ref, self.v_ref, self.lse_ref, self.xa_ref, self.o_ref, self.far_w) = ins[7:]
        (self.grad_ref, self.ga_ref, self.lin_ref, self.bias_ref, self.pa_ref, self.pf_ref) = outs
        (self.w_ref, self.w_sem, self.dk, self.dv, self.sum_buf, self.send_buf, self.land_buf) = scratch[:7]
        (self.send_sems, self.recv_sems) = scratch[7:]
        self.t = lax.axis_index("t")
        self.slots, self.few = self.w_ref.shape[:2]
        self.model = self.slots * self.few
        self.count = self.state_ref.shape[0]
        self.q_width = self.q_ref.shape[1]
        self.width, self.epsilon = width, epsilon

    def pair_copy(self, number, source, landing):
        return pltpu.make_async_remote_copy(
            src_ref=source,
            dst_ref=landing,
            send_sem=self.send_sems.at[number],
            recv_sem=self.recv_sems.at[number],
            device_id={"t": 1 - self.t},
            device_id_type=MESH,
        )

    def ga_copy(self, side):
        return self.pair_copy(0, self.ga_ref.at[side], self.ga_ref.at[side])

    def half_copy(self):
        return self.pair_copy(1, self.send_buf, self.land_buf)

    def weight_copy(self):
        return pltpu.make_async_copy(self.far_w, self.w_ref, self.w_sem)

    def norm_back(self, upstream, rows, gain):
        factor = lax.rsqrt(jnp.mean(rows * rows, axis=-1, keepdims=True) + self.epsilon)
        scaled = upstream * gain
        part = jnp.sum(upstream * rows * factor, axis=0, keepdims=True)
        inner = jnp.mean(scaled * rows, axis=-1, keepdims=True)
        return factor * scaled - rows * factor**3 * inner, part

    def prepare(self):
        self.weight_copy().start()

    def begin(self, d_xf):
        d_mid, part = self.norm_back(d_xf, self.middle_ref[...], self.gf_gain[...])
        self.pf_ref[...] = part
        grad = self.g_ref[...].astype(F32) + d_mid
        self.grad_ref[...] = grad
        self.ga_ref[self.t] = grad.astype(LOW)
        self.ga_copy(self.t).start()
        self.dk[...] = jnp.zeros_like(self.dk)
        self.dv[...] = jnp.zeros_like(self.dv)

    def arrive(self):
        self.weight_copy().wait()
        self.ga_copy(1 - self.t).wait_recv()

    def unrope(self, values):
        return values * self.cos_ref[...] - pltpu.roll(values, HD // 2, 1) * self.sin_ref[...]

    def keep(self, low, values):
        count = values.shape[1]
        self.bias_ref[:, low : low + count] = jnp.sum(values, axis=0, keepdims=True)
        values = values.astype(LOW)
        self.lin_ref[0, :, low : low + count] = values[: self.count]
        self.lin_ref[1, :, low : low + count] = values[self.count :]

    def heads(self, first):
        low, count = self.width + first * HD, 2 * HD
        weight = self.w_ref[:, :, low : low + count].reshape(self.model, count)
        above = self.ga_ref[...].reshape(2 * self.count, self.model)
        d_out = jnp.dot(above, weight, preferred_element_type=F32).astype(LOW)
        key, value = self.k_ref[...], self.v_ref[...]
        last = (((1,), (1,)), ((), ()))
        early = (((0,), (0,)), ((), ()))
        scale = 1.0 / math.sqrt(HD)
        for number in range(2):
            head = first + number
            query = self.q_ref[:, head * HD : (head + 1) * HD]
            d_head = d_out[:, number * HD : (number + 1) * HD]
            raw = lax.dot_general(query, key, last, preferred_element_type=F32)
            scores = jnp.where(self.mask_ref[...] > 0, raw * scale, -1e30)
            probs = jnp.exp(scores - self.lse_ref[head])
            d_probs = lax.dot_general(d_head, value, last, preferred_element_type=F32)
            centre = jnp.sum(probs * d_probs, axis=-1, keepdims=True)
            d_raw = (probs * (d_probs - centre) * scale).astype(LOW)
            d_query = jnp.dot(d_raw, key, preferred_element_type=F32)
            self.dk[...] += lax.dot_general(d_raw, query, early, preferred_element_type=F32)
            self.dv[...] += lax.dot_general(
                probs.astype(LOW), d_head, early, preferred_element_type=F32
            )
            self.keep(head * HD, self.unrope(d_query))

    def keys(self):
        self.keep(self.q_width, self.unrope(self.dk[...]))
        self.keep(self.q_width + HD, self.dv[...])

    def projected(self, half):
        left, step = self.lin_ref[half], self.slots // 4
        for low in range(0, self.slots, step):
            weight = self.w_ref[low : low + step, :, : self.width].reshape(step * self.few, self.width)
            yield slice(low * self.few, (low + step) * self.few), lax.dot_general(
                left, weight, (((1,), (1,)), ((), ())), preferred_element_type=F32
            )

    def other_half(self):
        for where, part in self.projected(1 - self.t):
            self.send_buf[:, where] = part.astype(LOW)
        self.half_copy().start()

    def own_half(self):
        for where, part in self.projected(self.t):
            self.sum_buf[:, where] = part

    def gradients(self):
        step = self.slots // 4
        early = (((0,), (0,)), ((), ()))
        pairs = ((self.xa_ref, self.lin_ref, 0, self.width), (self.ga_ref, self.o_ref, self.width, self.q_width))
        for left_ref, right_ref, low, count in pairs:
            right = right_ref[...].reshape(2 * self.count, count)
            for slot in range(0, self.slots, step):
                where = slice(slot * self.few, (slot + step) * self.few)
                left = left_ref[:, :, where].reshape(2 * self.count, step * self.few)
                part = lax.dot_general(left, right, early, preferred_element_type=F32)
                self.w_ref[slot : slot + step, :, low : low + count] = part.astype(LOW).reshape(
                    step, self.few, count
                )

    def finish(self):
        self.half_copy().wait_recv()
        d_xa = self.sum_buf[...] + self.land_buf[...].astype(F32)
        d_in, part = self.norm_back(d_xa, self.state_ref[...], self.ga_gain[...])
        self.pa_ref[...] = part
        grad = self.grad_ref[...] + d_in
        self.grad_ref[...] = grad
        return grad

    def end(self):
        self.ga_copy(self.t).wait_send()
        self.half_copy().wait_send()


class Blocks:
    def __init__(self, size, bits, gu_ref, dn_ref, outs, gu_fold, dn_fold, done, sems):
        self.size, self.outs, self.sending = size, outs, len(outs) == 1
        order = list(range(1, size)) + [0]
        self.folds = [Fold(size, bits, order, gu_ref, *gu_fold), Fold(size, bits, order, dn_ref, *dn_fold)]
        self.done = done
        self.own_sems, self.send_sems, self.recv_sems = sems
        self.width, self.narrow = gu_ref.shape[2], dn_ref.shape[2]
        self.z = lax.axis_index("z")

    def columns(self, number):
        return pl.ds(*((0, self.width), (self.width, self.narrow))[number])

    def landing(self, number, slot):
        return self.outs[0].at[slot, :, self.columns(number)]

    def line_copy(self, number, place, slot):
        return pltpu.make_async_remote_copy(
            src_ref=self.done[number].at[place],
            dst_ref=self.landing(number, slot),
            send_sem=self.send_sems.at[number, place],
            recv_sem=self.recv_sems.at[number, slot],
            device_id={"z": self.folds[0].line(place)},
            device_id_type=MESH,
        )

    def own_copy(self, number, place):
        landing = (
            self.landing(number, self.z)
            if self.sending
            else self.outs[place].at[:, self.columns(number)]
        )
        return pltpu.make_async_copy(
            self.done[number].at[place], landing, self.own_sems.at[number, place]
        )

    def begin(self):
        for fold in self.folds:
            fold.begin()

    def inner(self, place):
        for stage in reversed(range(1, self.folds[0].count)):
            for fold in self.folds:
                fold.stage(place, stage)

    def send(self, place):
        for number, fold in enumerate(self.folds):

            def keep(place, total, number=number):
                self.done[number][place] = total.astype(LOW)
                if self.sending and place < self.size - 1:
                    self.line_copy(number, place, self.z).start()
                else:
                    self.own_copy(number, place).start()

            fold.stage(place, 0, keep)

    def end(self):
        for number, fold in enumerate(self.folds):
            for place in range(self.size):
                if not self.sending or place == self.size - 1:
                    self.own_copy(number, place).wait()
                    continue
                slot = lax.rem(self.z - place - 1 + self.size, self.size)
                self.line_copy(number, 0, slot).wait_recv()
                self.line_copy(number, place, self.z).wait_send()
            fold.end()


def back_kernel(size, bits, width, final, *refs):
    top, bottom = final
    counts = [1, 1 if top else 0, 2, 15, 3 if bottom else 0, 6, 1 if bottom else size, 1, 1 if top else 0, 1]
    p_ref, branch_ref, wide, ins, above, outs, folded, (attn_ref,), branch_out, more_out, refs = (
        in_groups(refs, counts + [len(refs)])
    )
    (dxf_ref,), dxf_scratch, gu_fold, dn_fold, done, sems, work_scratch, refs = in_groups(
        refs, [1, SCATTER_REFS, 7, 7, 2, 3, 9, len(refs)]
    )
    greet_all(size, ("t", *bits))
    rows = Relay(size, ("t",), p_ref[0], dxf_ref, *dxf_scratch)
    blocks = Blocks(size, bits, *wide, folded, gu_fold, dn_fold, done, sems)
    work = AttendBack(ins, outs, work_scratch, width)
    branch = None
    if top:
        branch_scratch, refs = in_groups(refs, [SCATTER_REFS, len(refs)])
        branch = Relay(size, ("t",), branch_ref[0], branch_out[0], *branch_scratch)
    if not bottom:
        gm_ref, kept_sem, *gm_sems = refs
        onward = Gather(size, ("t",), gm_ref, more_out[0], *gm_sems)
        kept = pltpu.make_async_copy(work.w_ref, attn_ref, kept_sem)
    else:
        attn_scratch, (x_ref, *small_scratch) = in_groups(refs, [SCATTER_REFS, len(refs)])
        final = Relay(size, bits, work.w_ref, attn_ref, *attn_scratch)
        small = Total(size, ("t", *bits), x_ref, more_out[0], *small_scratch)
    rows.begin()
    blocks.begin()
    work.prepare()
    blocks.inner(0)
    rows.place(0)
    blocks.inner(1)
    blocks.inner(2)
    rows.place(1)
    blocks.inner(3)
    rows.place(2)
    rows.place(3)
    if top:
        branch.begin([0])
    rows.finish()
    work.begin(dxf_ref[...])
    blocks.send(0)
    blocks.send(1)
    if top:
        branch.begin([1])
    work.arrive()
    work.heads(0)
    if top:
        branch.place(0)
    work.heads(2)
    blocks.send(2)
    work.heads(4)
    work.keys()
    work.other_half()
    if top:
        branch.place(1)
        branch.begin([2])
    work.own_half()
    blocks.send(3)
    work.gradients()
    if bottom:
        final.begin()
    else:
        kept.start()
    grad = work.finish()
    if bottom:
        pa_above, pf_above, bias_above = above
        x_ref[...] = jnp.zeros_like(x_ref)
        x_ref[0:1, :] = work.pa_ref[...]
        x_ref[1:2, :] = pa_above[...]
        x_ref[2:3, :] = work.pf_ref[...]
        x_ref[3:4, :] = pf_above[...]
        for side in range(2):
            mine = (work.t == side).astype(F32)
            x_ref[4 + 2 * side : 5 + 2 * side, : work.width] = work.bias_ref[...] * mine
            x_ref[5 + 2 * side : 6 + 2 * side, : work.width] = bias_above[...] * mine
        small.begin()
        for place in range(size):
            final.place(place)
            if place <= len(bits):
                small.pair(place)
        for number in range(size, len(bits) + 1):
            small.pair(number)
        final.finish()
        small.finish()
    if not bottom:
        gm_ref[...] = grad.astype(LOW)
        onward.begin()
    if top:
        branch.begin([3])
        branch.place(2)
    if not bottom:
        onward.step(1)
        onward.on_bits(0)
    if top:
        branch.place(3)
    if not bottom:
        onward.step(2)
        onward.on_bits(1)
        onward.step(3)
        onward.on_bits(2)
        onward.on_bits(3)
    if top:
        branch.finish()
    for steps in (rows, blocks, work, *((final, small) if bottom else (onward,)), branch):
        if steps is not None:
            steps.end()
    if not bottom:
        kept.wait()


def back(partial, branch, gu, dn, ins, above, size, bits, width, collective_id):
    count, model = ins[1].shape
    length, q_width = ins[8].shape
    slots, few, wide = gu.shape
    narrow = dn.shape[2]
    top, bottom = branch is not None, bool(above)
    number = len(bits) + 1
    weight = ins[14].shape
    held, far = pl.BlockSpec(memory_space=pltpu.VMEM), pl.BlockSpec(memory_space=pl.ANY)
    shape = jax.ShapeDtypeStruct
    rows_scratch = scatter_scratch(size, ("t",), count, model)
    return pl.pallas_call(
        functools.partial(back_kernel, size, bits, width, (top, bottom)),
        out_shape=(
            shape((count, model), F32),
            shape((2, count, model), LOW),
            shape((2, count, width), LOW),
            shape((1, width), F32),
            shape((1, model), F32),
            shape((1, model), F32),
            *(
                [shape((size, few, wide + narrow), LOW)]
                if bottom
                else [shape((few, wide + narrow), LOW)] * size
            ),
            shape(weight[1:], F32) if bottom else shape(weight, LOW),
            *([shape((count, model), F32)] if top else []),
            shape((8, model), F32) if bottom else shape((2 * size, count, model), LOW),
        ),
        in_specs=[far] * (4 if top else 3) + [held] * 14 + [far] + [held] * len(above),
        out_specs=[held] * 6
        + ([far, held] if bottom else [far] * (size + 1))
        + [held] * top + [held if bottom else far],
        scratch_shapes=[
            pltpu.VMEM((count, model), F32),
            *rows_scratch,
            *fold_scratch(size, bits, few, wide),
            *fold_scratch(size, bits, few, narrow),
            pltpu.VMEM((size, few, wide), LOW),
            pltpu.VMEM((size, few, narrow), LOW),
            *([pltpu.SemaphoreType.DMA((2, size))] * 3),
            pltpu.VMEM(weight, LOW),
            pltpu.SemaphoreType.DMA,
            pltpu.VMEM((length, HD), F32),
            pltpu.VMEM((length, HD), F32),
            pltpu.VMEM((count, model), F32),
            pltpu.VMEM((count, model), LOW),
            pltpu.VMEM((count, model), LOW),
            pltpu.SemaphoreType.DMA((2,)),
            pltpu.SemaphoreType.DMA((2,)),
            *(rows_scratch if top else []),
            *(
                [
                    *scatter_scratch(size, bits, *weight[1:]),
                    pltpu.VMEM((8, model), F32),
                    pltpu.VMEM((number + 1, 8, model), F32),
                    pltpu.VMEM((number + size - 1, 8, model), F32),
                    pltpu.SemaphoreType.DMA((number + size - 1,)),
                    pltpu.SemaphoreType.DMA((number + size - 1,)),
                ]
                if bottom
                else [
                    pltpu.VMEM((count, model), LOW),
                    pltpu.SemaphoreType.DMA,
                    *gather_semaphores(size, ("t",)),
                ]
            ),
        ],
        compiler_params=comm_params(collective_id),
        cost_estimate=at_microseconds(5 if bottom else 150),
    )(partial, *([branch] if top else []), gu, dn, *ins, *above)


def settle_kernel(half, width, *refs):
    low_ref, *high_refs = refs[: LINE + 1]
    attn_low, attn_high, gu_ref, dn_ref, qkv_ref, out_ref = refs[LINE + 1 :]
    block = low_ref.shape[2] // 3
    z = lax.axis_index("z")
    for layer in range(2):
        for line in range(LINE):
            low = block_start(line, block, half)
            skip = line * block - low
            for part in range(3):
                where = slice(part * block + skip, (part + 1) * block)
                if layer == 0:
                    piece = low_ref[line, :, where]
                else:
                    offset = lax.rem(z - line + LINE, LINE)
                    piece = high_refs[LINE - 1][:, where]
                    for o in range(1, LINE):
                        piece = jnp.where(offset == o, high_refs[o - 1][:, where], piece)
                piece = piece.astype(F32)
                if part < 2:
                    gu_ref[layer, :, part * half + low + skip : part * half + low + block] = piece
                else:
                    dn_ref[layer, :, low + skip : low + block] = piece
    for layer, ref in enumerate((attn_low, attn_high)):
        qkv_ref[layer] = ref[:, :width].astype(F32)
        out_ref[layer] = ref[:, width:].astype(F32)


def settle(blocks, arrived, attn, half, width):
    few = attn[0].shape[0]
    shape = jax.ShapeDtypeStruct
    return pl.pallas_call(
        functools.partial(settle_kernel, half, width),
        out_shape=(
            shape((2, few, 2 * half), F32),
            shape((2, few, half), F32),
            shape((2, few, width), F32),
            shape((2, few, attn[0].shape[1] - width), F32),
        ),
        compiler_params=pltpu.CompilerParams(vmem_limit_bytes=56 * 2**20),
    )(blocks, *arrived, *attn)


def in_slots(partial, slots):
    return partial.reshape(slots, -1, partial.shape[1])


def block_width(half):
    return -(-half // (LINE * LANES)) * LANES


def block_start(line, block, half):
    return min(line * block, half - block)


def local(
    bits, tokens, cotangent, doc_lengths, norm_attn, norm_ffn, w_qkv, b_qkv, w_out, w_gateup, w_down
):
    dp = ("z", *bits)
    tensor_size = lax.axis_size("t")
    count = tokens.shape[0]
    length = count * tensor_size
    layers = w_qkv.shape[0]
    qkv_width = w_qkv.shape[2]
    rows = w_qkv.shape[1]
    half = w_down.shape[2]
    block = block_width(half)
    positions, allowed = doc_layout(doc_lengths[0], length)
    cosine, sine = rope_tables(positions, HD)
    turned = jnp.where(jnp.arange(HD) < HD // 2, -sine, sine)
    tables = (cosine, turned, allowed.astype(F32))
    gain_attn = norm_attn.astype(F32)
    gain_ffn = norm_ffn.astype(F32)
    bias_all = b_qkv.astype(F32)
    line = lax.axis_index("z")
    valid = jnp.arange(block) >= line * block - jnp.minimum(line * block, half - block)
    flats = [jnp.concatenate([w_qkv[layer], w_out[layer]], axis=1) for layer in range(layers)]
    saved = []
    for layer in range(layers):
        gains = (gain_attn[layer : layer + 1], gain_ffn[layer : layer + 1])
        if layer == 0:
            start, more, weight = tokens, flats[1], flats[0]
        else:
            start, more, weight = middle, in_slots(partial, 2 * LINE), attn_weights[layer]
        out = front(
            start, more, gains, bias_all[layer : layer + 1], tables, weight, w_gateup, w_down,
            layer, LINE, bits, block, qkv_width, 8 + layer,
        )
        (state, middle, xa_all, query, key, value, log_total, attended) = out[:8]
        xf_all, gu_w, down_w = (item.reshape(-1, item.shape[2]) for item in out[8:11])
        if layer == 0:
            attn_weights = out[11:]
            gm_all = lax.all_gather(cotangent, ("z", "t"), axis=0, tiled=True)
        both_w = attn_weights[layer]
        gate_up = jnp.dot(xf_all, gu_w, preferred_element_type=F32)
        gate = gate_up[:, :block]
        up = gate_up[:, block:]
        act = jnp.where(valid, jax.nn.silu(gate) * up, 0.0).astype(LOW)
        partial = contract_last(act, down_w, LOW)
        if layer == 0:
            partial, gm_all = lax.optimization_barrier((partial, gm_all))
        saved.append(
            (state, xa_all, query, key, value, log_total, attended)
            + (middle, xf_all, gate, up, act, gu_w, down_w, both_w)
        )
    grad, branch, above = cotangent, in_slots(partial, 2 * LINE), []
    grads_attn = []
    for layer in reversed(range(layers)):
        (state_in, xa_all, query, key, value, log_total, attended) = saved[layer][:7]
        (middle, xf_all, gate, up, act, gu_w, down_w, both_w) = saved[layer][7:]
        d_down = contract_first(gm_all, act, LOW)
        d_act = jnp.dot(gm_all, down_w, preferred_element_type=F32)
        sig = jax.nn.sigmoid(gate)
        d_gate = d_act * up * sig * (1.0 + gate * (1.0 - sig))
        d_up = d_act * gate * sig
        d_gu = jnp.concatenate(
            [jnp.where(valid, d_gate, 0.0), jnp.where(valid, d_up, 0.0)], axis=1
        ).astype(LOW)
        d_gateup = contract_first(xf_all, d_gu, LOW)
        partial = in_slots(contract_last(d_gu, gu_w, LOW), 2 * LINE)
        wide = (in_slots(d_gateup, d_gateup.shape[0] // rows), in_slots(d_down, d_down.shape[0] // rows))
        gains = (gain_attn[layer : layer + 1], gain_ffn[layer : layer + 1])
        ins = (grad, state_in, middle, *gains, *tables, query, key, value, log_total, xa_all, attended, both_w)
        out = back(
            partial, branch, *wide, ins, above if layer == 0 else [], LINE, bits, qkv_width, 16 + layer
        )
        (grad, _, _, d_bias, part_a, part_f), rest = out[:6], out[6:]
        if layer > 0:
            (*folded, d_attn), rest = rest[: LINE + 1], rest[LINE + 1 :]
            arrived = [
                lax.ppermute(folded[o - 1], "z", [(i, (i + o) % LINE) for i in range(LINE)])
                for o in range(1, LINE)
            ]
            arrived.append(folded[LINE - 1])
        else:
            (blocks, d_attn), rest = rest[:2], rest[2:]
        if branch is not None:
            output = (middle + rest[0]).astype(LOW)
            branch = None
        if layer > 0:
            gm_all = rest[-1].reshape(-1, rest[-1].shape[2])
            above = [part_a, part_f, d_bias]
            d_attn = lax.psum_scatter(
                d_attn.reshape(-1, d_attn.shape[2]), dp, scatter_dimension=0, tiled=True
            )
        grads_attn.append(d_attn)
    sums = rest[-1]
    side = lax.axis_index("t")
    d_gu_all, d_dn_all, d_qkv_all, d_out_all = settle(blocks, arrived, grads_attn[::-1], half, qkv_width)
    return (
        output,
        grad,
        sums[0:2],
        sums[2:4],
        d_qkv_all,
        lax.dynamic_slice_in_dim(sums, 4 + 2 * side, 2, 0)[:, :qkv_width],
        d_out_all,
        d_gu_all,
        d_dn_all,
    )


def solution(mesh):
    dp_size, tensor_size = mesh.devices.shape
    rest = dp_size // LINE
    bits = tuple(f"r{number}" for number in range(rest.bit_length() - 1))
    shape = (LINE, *([2] * len(bits)), tensor_size)
    fine = Mesh(mesh.devices.reshape(shape), ("z", *bits, "t"))
    dp = ("z", *bits)
    rows = P((*dp, "t"), None)
    weight = P(None, dp, "t")

    def step(*args):
        return local(bits, *args)

    return jax.shard_map(
        step,
        mesh=fine,
        in_specs=(rows, rows, P(dp, None), P(), P(), weight, P(None, "t"), weight, weight, weight),
        out_specs=(rows, rows, P(), P(), weight, P(None, "t"), weight, weight, weight),
        check_vma=False,
    )
```
